32 devices in a mesh: dp: 4 (over z), row: 2 (over y), col: 4 (over x, core).
Axes of the slice: x: 2, y: 2, z: 4, core: 2. Of those that a mesh axis runs over, the one named last changes fastest.
Arguments:
- tokens: bfloat16 [8192, 2048], P(('dp', 'row'), 'col'), may hold values from -6 to 6
- cotangent: bfloat16 [8192, 2048], P(('dp', 'row'), 'col'), may hold values from -6 to 6
- segment_ids: int32 [8, 1024], P('dp'), may hold values from 0 to 4, never falling along the last dimension, each value on 1 to 800 neighbouring positions
- norm1_gain: float32 [2048], P('col'), may hold values from 0.1 to 1.9
- proj_gate: bfloat16 [2048, 3072], P('col', 'row'), may hold values from -0.125 to 0.125
- proj_conv: bfloat16 [2048, 3072], P('col', 'row'), may hold values from -0.125 to 0.125
- proj_step: bfloat16 [2048, 48], P('col', 'row'), may hold values from -0.125 to 0.125
- proj_shared: bfloat16 [2048, 512], P('col', 'row'), may hold values from -0.125 to 0.125
- proj_query: bfloat16 [2048, 1024], P('col', 'row'), may hold values from -0.125 to 0.125
- proj_key: bfloat16 [2048, 256], P('col', 'row'), may hold values from -0.125 to 0.125
- proj_value: bfloat16 [2048, 256], P('col', 'row'), may hold values from -0.125 to 0.125
- conv_weight: float32 [4, 3072], P(None, ('row', 'col')), may hold values from -3 to 3
- conv_bias: float32 [3072], P(('row', 'col')), may hold values from -3 to 3
- shared_conv: float32 [4, 512], replicated, may hold values from -3 to 3
- shared_bias: float32 [512], replicated, may hold values from -3 to 3
- step_bias: float32 [48], P(('row', 'col')), may hold values from -7 to -2.3
- decay_log: float32 [48], P(('row', 'col')), may hold values from 0 to 2.77
- skip_gain: float32 [48], P(('row', 'col')), may hold values from 0.5 to 1.5
- mamba_out_proj: bfloat16 [3072, 2048], P('row', 'col'), may hold values from -0.109375 to 0.109375
- attn_out_proj: bfloat16 [1024, 2048], P('row', 'col'), may hold values from -0.75 to 0.75
- norm2_gain: float32 [2048], P('col'), may hold values from 0.1 to 1.9
- ffn_gate: bfloat16 [2048, 4096], P('col', 'row'), may hold values from -0.125 to 0.125
- ffn_up: bfloat16 [2048, 4096], P('col', 'row'), may hold values from -0.125 to 0.125
- ffn_down: bfloat16 [4096, 2048], P('row', 'col'), may hold values from -0.09375 to 0.09375
Outputs:
- output: bfloat16 [8192, 2048], P(('dp', 'row'), 'col')
- tokens_grad: bfloat16 [8192, 2048], P(('dp', 'row'), 'col')
- norm1_gain_grad: float32 [2048], P('col')
- proj_gate_grad: float32 [2048, 3072], P('col', 'row')
- proj_conv_grad: float32 [2048, 3072], P('col', 'row')
- proj_step_grad: float32 [2048, 48], P('col', 'row')
- proj_shared_grad: float32 [2048, 512], P('col', 'row')
- proj_query_grad: float32 [2048, 1024], P('col', 'row')
- proj_key_grad: float32 [2048, 256], P('col', 'row')
- proj_value_grad: float32 [2048, 256], P('col', 'row')
- conv_weight_grad: float32 [4, 3072], P(None, ('row', 'col'))
- conv_bias_grad: float32 [3072], P(('row', 'col'))
- shared_conv_grad: float32 [4, 512], replicated
- shared_bias_grad: float32 [512], replicated
- step_bias_grad: float32 [48], P(('row', 'col'))
- decay_log_grad: float32 [48], P(('row', 'col'))
- skip_gain_grad: float32 [48], P(('row', 'col'))
- mamba_out_proj_grad: float32 [3072, 2048], P('row', 'col')
- attn_out_proj_grad: float32 [1024, 2048], P('row', 'col')
- norm2_gain_grad: float32 [2048], P('col')
- ffn_gate_grad: float32 [2048, 4096], P('col', 'row')
- ffn_up_grad: float32 [2048, 4096], P('col', 'row')
- ffn_down_grad: float32 [4096, 2048], P('row', 'col')
The draws below stay inside these ranges and needn't reach their ends.
Inputs may be any that keep to these rules, and one draw needn't show every extreme that they name: `segment_ids`: along each sequence the ids never fall; a run of equal ids is one document of 1 to 800 tokens, and some document has exactly 800.
All inputs are finite; a program needn't handle non-finite values.
Results may differ from the reference program's by a relative error of at most 0.018.
Values may be sent and summed in bfloat16 or wider, within the bound.
No kernel may reach another device: no remote copies, remote signals or barrier semaphores. Data moves between devices by JAX's collectives and lax.ppermute only.
A program may use at most 384 MiB of HBM per device.

```python
import math
from functools import partial
import jax
import jax.numpy as jnp
import numpy as np
from jax import lax

D = 2048
FF = 4096
MH = 48
P_SIZE = 64
NS = 256
KC = 4
QH = 8
KVH = 2
HD = 128
DI = 3072
LEN = 1024
DOCS = 5
DOC_MOST = 800
TOKENS = 8192
SEQ_ALL = 8


def steps_of(stream_key, shape, cuts, smallest, top_value):
    level = 1.0
    for axis_at, shards_of in cuts:
        draws = jax.random.uniform(jax.random.fold_in(jax.random.fold_in(stream_key, 6), axis_at), (shards_of,), jnp.float32, smallest / len(cuts), top_value / len(cuts))
        level = level * jnp.repeat(jnp.exp(draws), shape[axis_at] // shards_of).reshape((-1,) + (1,) * (len(shape) - 1 - axis_at))
    return level


def length_profile(count, total, bound, lean):
    portions = [(1 << 20) // math.isqrt(standing ** lean) + 1 for standing in range(2, count + 1)]
    surplus, holding = total - bound - (count - 1), [1] * (count - 1)
    while surplus > 0:
        free = [i for i in range(count - 1) if holding[i] < bound]
        whole, remaining = sum([portions[i] for i in free]), surplus
        for i in free:
            extra = min(bound - holding[i], max(1, remaining * portions[i] // whole), surplus)
            holding[i] = holding[i] + extra
            surplus = surplus - extra
    return np.array([bound] + holding)


def uneven(rng, amount, total, reach, slope):
    if amount == 2:
        one = jax.random.randint(rng, (), max(1, total - reach), min(reach, total - 1) + 1)
        return jnp.stack([one, total - one])
    tallies = jnp.asarray(length_profile(amount, total, reach, slope), jnp.int32)
    pairs = (amount - 1) // 2
    donor, taker = tallies[1:1 + 2 * pairs:2], tallies[2:2 + 2 * pairs:2]
    margin = jnp.minimum(donor - 1, reach - taker)
    moved = jax.random.randint(jax.random.fold_in(rng, 1), (pairs,), 0, 1 << 20) % (margin + 1)
    tallies = tallies.at[1:1 + 2 * pairs:2].set(donor - moved).at[2:2 + 2 * pairs:2].set(taker + moved)
    return tallies[jax.random.permutation(jax.random.fold_in(rng, 2), amount)]


def noise(own_key, shape, spread, bound, shards=(), kind=jnp.bfloat16):
    drawn = jax.random.normal(own_key, shape, jnp.float32) * spread
    if len(shards) > 0:
        drawn = steps_of(own_key, shape, shards, -0.22, 0.18) * drawn
    return jnp.clip(drawn, min=-bound, max=bound).astype(kind)


def setup_inputs(seed: int = 0) -> dict:
    arg_keys = jax.random.split(jax.random.key(seed), 25)
    tokens = noise(arg_keys[0], (TOKENS, D), 1.0, 6.0, ((0, 8), (1, 4)))
    cotangent = noise(arg_keys[1], (TOKENS, D), 1.0, 6.0, ((0, 8), (1, 4)))
    segment_ids = jax.vmap(lambda own: jnp.searchsorted(jnp.cumsum(uneven(own, DOCS, LEN, DOC_MOST, 0)), jnp.arange(LEN), side="right"))(jax.random.split(arg_keys[2], SEQ_ALL)).reshape((SEQ_ALL, LEN)).astype(jnp.int32)
    norm1_gain = jnp.clip(1.0 + 0.18 * jax.random.normal(arg_keys[3], (D,), jnp.float32), 0.1, 1.9)
    proj_gate = noise(arg_keys[4], (D, DI), D ** -0.5, 0.125, ((0, 4), (1, 2)))
    proj_conv = noise(arg_keys[5], (D, DI), D ** -0.5, 0.125, ((0, 4), (1, 2)))
    proj_step = noise(arg_keys[6], (D, MH), D ** -0.5, 0.125, ((0, 4), (1, 2)))
    proj_shared = noise(arg_keys[7], (D, 2 * NS), D ** -0.5, 0.125, ((0, 4), (1, 2)))
    proj_query = noise(arg_keys[8], (D, QH * HD), D ** -0.5, 0.125, ((0, 4), (1, 2)))
    proj_key = noise(arg_keys[9], (D, KVH * HD), D ** -0.5, 0.125, ((0, 4), (1, 2)))
    proj_value = noise(arg_keys[10], (D, KVH * HD), D ** -0.5, 0.125, ((0, 4), (1, 2)))
    conv_weight = noise(arg_keys[11], (KC, DI), KC ** -0.5, 3.0, ((1, 8),), jnp.float32)
    conv_bias = noise(arg_keys[12], (DI,), 0.5, 3.0, ((0, 8),), jnp.float32)
    shared_conv = noise(arg_keys[13], (KC, 2 * NS), KC ** -0.5, 3.0, (), jnp.float32)
    shared_bias = noise(arg_keys[14], (2 * NS,), 0.5, 3.0, (), jnp.float32)
    step_bias = jnp.clip(-7.0 + 4.7 * jax.random.uniform(arg_keys[15], (MH,), jnp.float32) ** steps_of(arg_keys[15], (MH,), ((0, 8),), -0.2, 0.2), -7.0, -2.3)
    decay_log = jnp.clip(2.77 * jax.random.uniform(arg_keys[16], (MH,), jnp.float32) ** steps_of(arg_keys[16], (MH,), ((0, 8),), -0.2, 0.2), 0.0, 2.77)
    skip_gain = jnp.clip(0.5 + 1.0 * jax.random.uniform(arg_keys[17], (MH,), jnp.float32) ** steps_of(arg_keys[17], (MH,), ((0, 8),), -0.2, 0.2), 0.5, 1.5)
    mamba_out_proj = noise(arg_keys[18], (DI, D), DI ** -0.5, 0.109375, ((0, 2), (1, 4)))
    attn_out_proj = noise(arg_keys[19], (QH * HD, D), (QH * HD // 16) ** -0.5, 0.75, ((0, 2), (1, 4)))
    norm2_gain = jnp.clip(1.0 + 0.18 * jax.random.normal(arg_keys[20], (D,), jnp.float32), 0.1, 1.9)
    ffn_gate = noise(arg_keys[21], (D, FF), D ** -0.5, 0.125, ((0, 4), (1, 2)))
    ffn_up = noise(arg_keys[22], (D, FF), D ** -0.5, 0.125, ((0, 4), (1, 2)))
    ffn_down = noise(arg_keys[23], (FF, D), FF ** -0.5, 0.09375, ((0, 2), (1, 4)))
    return dict(tokens=tokens, cotangent=cotangent, segment_ids=segment_ids, norm1_gain=norm1_gain, proj_gate=proj_gate, proj_conv=proj_conv, proj_step=proj_step, proj_shared=proj_shared, proj_query=proj_query, proj_key=proj_key, proj_value=proj_value, conv_weight=conv_weight, conv_bias=conv_bias, shared_conv=shared_conv, shared_bias=shared_bias, step_bias=step_bias, decay_log=decay_log, skip_gain=skip_gain, mamba_out_proj=mamba_out_proj, attn_out_proj=attn_out_proj, norm2_gain=norm2_gain, ffn_gate=ffn_gate, ffn_up=ffn_up, ffn_down=ffn_down)


EPS = 1e-05
ROPE_BASE = 100000000000.0
NEG_DECAY = -10000.0
MASKED = -1e+30
HIGHEST = lax.Precision.HIGHEST

@jax.custom_vjp
def low(v):
    return lax.optimization_barrier(v.astype(jnp.bfloat16)).astype(jnp.float32)

@jax.custom_vjp
def low_back(v):
    return v

def low_keep(v):
    return (low(v), None)

def low_pass(kept, grad):
    return (grad,)

def back_keep(v):
    return (v, None)

def back_low(kept, grad):
    return (low(grad),)
low.defvjp(low_keep, low_pass)
low_back.defvjp(back_keep, back_low)

def matmul(former, latter):
    return jnp.dot(former, latter, precision=HIGHEST, preferred_element_type=jnp.float32)

def rms_norm(values, gain):
    factor = lax.rsqrt(lax.optimization_barrier(jnp.mean(values * values, axis=-1, keepdims=True)) + EPS)
    return values * factor * gain

def doc_layout(segment_ids):
    seq_len = segment_ids.shape[1]
    indices = jnp.arange(seq_len, dtype=jnp.int32)
    earlier = jnp.concatenate([segment_ids[:, :1], segment_ids[:, :-1]], axis=1)
    starts = (indices[None, :] == 0) | (segment_ids != earlier)
    latest = lax.cummax(jnp.where(starts, indices[None, :], 0).astype(jnp.int32), axis=1)
    return (starts, indices[None, :] - latest)

def doc_conv(inputs, weight, conv_offset, segment_ids):
    taps = weight.shape[0]
    seq_len = inputs.shape[1]
    running = conv_offset + weight[taps - 1] * inputs
    for offset in range(1, taps):
        shifted = jnp.pad(inputs, ((0, 0), (offset, 0), (0, 0)))[:, :seq_len]
        earlier = jnp.pad(segment_ids, ((0, 0), (offset, 0)), constant_values=-1)[:, :seq_len]
        running = running + weight[taps - 1 - offset] * jnp.where((earlier == segment_ids)[..., None], shifted, 0.0)
    return running

def rotate(values, positions, sign):
    half_dim = values.shape[-1] // 2
    frequency = ROPE_BASE ** (-2.0 * jnp.arange(half_dim, dtype=jnp.float32) / values.shape[-1])
    angles = positions.astype(jnp.float32)[..., None] * frequency
    cosine = jnp.cos(angles)[..., None, :]
    sine_term = sign * jnp.sin(angles)[..., None, :]
    front_half = values[..., :half_dim]
    back_half = values[..., half_dim:]
    return jnp.concatenate([front_half * cosine - back_half * sine_term, back_half * cosine + front_half * sine_term], axis=-1)

def sequence_mixer(inputs):
    conv_out, b_map, c_map, step_size, log_decay, query_heads, key_heads, value_heads, segments = inputs
    indices = jnp.arange(LEN, dtype=jnp.int32)
    strictly_below = indices[:, None] > indices[None, :]
    causal = indices[:, None] >= indices[None, :]
    gram_matrix = matmul(c_map, b_map.T)

    def one_head(head_inputs):
        head_decay, head_step, head_values = head_inputs
        segsum = jnp.cumsum(jnp.where(strictly_below, head_decay[:, None], 0.0), axis=0)
        weights = jnp.where(causal, gram_matrix * jnp.exp(segsum), 0.0) * head_step[None, :]
        return matmul(weights, head_values)
    scanned = lax.map(one_head, (log_decay.T, step_size.T, jnp.transpose(conv_out, (1, 0, 2))))
    allowed_mask = causal & (segments[:, None] == segments[None, :])
    grouped = query_heads.reshape(LEN, KVH, QH // KVH, HD)
    scores = jnp.einsum('tkgd,skd->kgts', grouped, key_heads, precision=HIGHEST) * (1.0 / math.sqrt(HD))
    scores = jnp.where(allowed_mask, low_back(scores), MASKED)
    attn_probs = low(jax.nn.softmax(scores, axis=-1))
    attended = jnp.einsum('kgts,skd->tkgd', attn_probs, value_heads, precision=HIGHEST)
    return (jnp.transpose(scanned, (1, 0, 2)), attended.reshape(LEN, QH * HD))

def block_forward(segment_ids, starts, positions, residual, norm1_gain, proj_gate, proj_conv, proj_step, proj_shared, proj_query, proj_key, proj_value, conv_weight, conv_bias, shared_conv, shared_bias, step_bias, decay_log, skip_gain, mamba_out_proj, attn_out_proj, norm2_gain, ffn_gate, ffn_up, ffn_down):
    normed1 = low(rms_norm(residual, norm1_gain))
    mixer_gate = low_back(matmul(normed1, proj_gate))
    conv_input = low_back(matmul(normed1, proj_conv))
    step_raw = low_back(matmul(normed1, proj_step))
    shared_raw = low_back(matmul(normed1, proj_shared))
    query_raw = low_back(matmul(normed1, proj_query))
    key_raw = low_back(matmul(normed1, proj_key))
    value_in = low(low_back(matmul(normed1, proj_value)))
    conv_out = jax.nn.silu(doc_conv(conv_input.reshape(SEQ_ALL, LEN, DI), conv_weight, conv_bias, segment_ids))
    conv_out = conv_out.reshape(SEQ_ALL, LEN, MH, P_SIZE)
    shared = jax.nn.silu(doc_conv(shared_raw.reshape(SEQ_ALL, LEN, 2 * NS), shared_conv, shared_bias, segment_ids))
    step_size = jax.nn.softplus(step_raw.reshape(SEQ_ALL, LEN, MH) + step_bias)
    log_decay = jnp.where(starts[..., None], NEG_DECAY, step_size * -jnp.exp(decay_log))
    query_heads = low(rotate(query_raw.reshape(SEQ_ALL, LEN, QH, HD), positions, 1.0))
    key_heads = low(rotate(key_raw.reshape(SEQ_ALL, LEN, KVH, HD), positions, 1.0))
    value_heads = value_in.reshape(SEQ_ALL, LEN, KVH, HD)
    scanned, attended = lax.map(jax.checkpoint(sequence_mixer), (conv_out, shared[..., :NS], shared[..., NS:], step_size, log_decay, query_heads, key_heads, value_heads, segment_ids))
    mamba_out = (scanned + skip_gain[:, None] * conv_out).reshape(TOKENS, DI) * jax.nn.silu(mixer_gate)
    mamba_out = low(mamba_out)
    attended = low(low_back(attended.reshape(TOKENS, QH * HD)))
    mixer_sum = low_back(matmul(mamba_out, mamba_out_proj) + matmul(attended, attn_out_proj))
    hidden1 = residual + mixer_sum
    normed2 = low(rms_norm(hidden1, norm2_gain))
    gate_pre = low_back(matmul(normed2, ffn_gate))
    up_pre = low_back(matmul(normed2, ffn_up))
    hidden = low(jax.nn.silu(gate_pre) * up_pre)
    return hidden1 + matmul(hidden, ffn_down)

def reference(tokens, cotangent, segment_ids, norm1_gain, proj_gate, proj_conv, proj_step, proj_shared, proj_query, proj_key, proj_value, conv_weight, conv_bias, shared_conv, shared_bias, step_bias, decay_log, skip_gain, mamba_out_proj, attn_out_proj, norm2_gain, ffn_gate, ffn_up, ffn_down):
    starts, positions = doc_layout(segment_ids)
    arguments = [tokens, norm1_gain, proj_gate, proj_conv, proj_step, proj_shared, proj_query, proj_key, proj_value, conv_weight, conv_bias, shared_conv, shared_bias, step_bias, decay_log, skip_gain, mamba_out_proj, attn_out_proj, norm2_gain, ffn_gate, ffn_up, ffn_down]
    arguments = [argument.astype(jnp.float32) for argument in arguments]
    forward = partial(block_forward, segment_ids, starts, positions)
    output, pullback = jax.vjp(forward, *arguments)
    gradients = pullback(cotangent.astype(jnp.float32))
    return (output.astype(jnp.bfloat16), gradients[0].astype(jnp.bfloat16), gradients[1], gradients[2], gradients[3], gradients[4], gradients[5], gradients[6], gradients[7], gradients[8], gradients[9], gradients[10], gradients[11], gradients[12], gradients[13], gradients[14], gradients[15], gradients[16], gradients[17], gradients[18], gradients[19], gradients[20], gradients[21])
```

```python
from functools import partial
import math

import jax
import jax.numpy as jnp
from jax import lax
from jax.experimental import pallas as pl
from jax.experimental.pallas import tpu as pltpu
from jax.sharding import PartitionSpec as P

EPS = 1e-05
ROPE_BASE = 100000000000.0
MASKED = -1e30
HIGHEST = lax.Precision.HIGHEST
DISTANCES = (0, 2, 1, 3)
LANES = 128
CHUNK = 128
TAIL = 8


def dot_any(former, latter, dims, precision=None):
    return lax.dot_general(
        former, latter, (dims, ((), ())), precision=precision, preferred_element_type=jnp.float32
    )


def nn(former, latter):
    return dot_any(former, latter, ((1,), (0,)))


def nt(former, latter):
    return dot_any(former, latter, ((1,), (1,)))


def tn(former, latter):
    return dot_any(former, latter, ((0,), (0,)))


def exact(former, latter):
    return dot_any(former, latter, ((1,), (0,)), HIGHEST)


def sigmoid_of(values):
    return 1.0 / (1.0 + jnp.exp(-values))


def softplus_of(values):
    return jnp.maximum(values, 0.0) + jnp.log1p(jnp.exp(-jnp.abs(values)))


def head_spread(head_width, width):
    heads = lax.broadcasted_iota(jnp.int32, (LANES, width), 0)
    columns = lax.broadcasted_iota(jnp.int32, (LANES, width), 1)
    return (columns // head_width == heads).astype(jnp.float32)


def head_gather(head_width, width):
    columns = lax.broadcasted_iota(jnp.int32, (width, LANES), 0)
    heads = lax.broadcasted_iota(jnp.int32, (width, LANES), 1)
    return (columns // head_width == heads).astype(jnp.float32)


def causal_conv(ext_ref, columns, weight_ref, bias_ref, position, taps):
    length = ext_ref.shape[0] - TAIL
    running = bias_ref[...] + weight_ref[taps - 1 : taps, :] * ext_ref[TAIL:, columns]
    for offset in range(1, taps):
        earlier = ext_ref[TAIL - offset : TAIL - offset + length, columns]
        running = running + weight_ref[taps - 1 - offset : taps - offset, :] * jnp.where(
            position >= offset, earlier, 0.0
        )
    return running


def chunk_decay(step_in, position, decay_rate):
    length = step_in.shape[0]
    step_size = softplus_of(step_in)
    log_decay = jnp.where(position == 0.0, 0.0, -step_size * decay_rate)
    rows = lax.broadcasted_iota(jnp.int32, (length, length), 0)
    columns = lax.broadcasted_iota(jnp.int32, (length, length), 1)
    causal = rows >= columns
    running = exact(causal.astype(jnp.float32), log_decay)
    return step_size, log_decay, running, jnp.transpose(running), causal


def split_pair(values, head_width):
    lane = lax.broadcasted_iota(jnp.int32, values.shape, 1)
    zero = jnp.zeros_like(values)
    return jnp.concatenate(
        [jnp.where(lane < head_width, values, zero), jnp.where(lane < head_width, zero, values)],
        axis=0,
    )


def mamba_forward_kernel(
    shared_ref, gate_ref, conv_ref, step_ref, info_ref, row_ref, weight_ref, bias_ref,
    shared_weight_ref, shared_bias_ref, head_ref, skip_ref, attended_ref,
    mixed_ref, combined_ref, states_ref,
    state, ext, *, head_width
):
    chunk = pl.program_id(0)
    length, width = conv_ref.shape
    states = shared_ref.shape[1] // 2
    taps = weight_ref.shape[0]
    low = jnp.bfloat16

    @pl.when(chunk == 0)
    def _():
        state[...] = jnp.zeros_like(state)
        ext[...] = jnp.zeros_like(ext)

    ext[:TAIL, :] = ext[length : length + TAIL, :]
    ext[TAIL:, :width] = conv_ref[...].astype(jnp.float32)
    ext[TAIL:, width:] = shared_ref[...].astype(jnp.float32)
    segment = info_ref[:, 0:1]
    position = info_ref[:, 1:2]
    pre = causal_conv(ext, slice(0, width), weight_ref, bias_ref, position, taps)
    conv_out = pre * sigmoid_of(pre)
    pre = causal_conv(
        ext, slice(width, None), shared_weight_ref, shared_bias_ref, position, taps
    )
    shared = (pre * sigmoid_of(pre)).astype(low)
    b_map = shared[:, :states]
    c_map = shared[:, states:]
    step_size, _, running, running_t, causal = chunk_decay(
        step_ref[...] + head_ref[0:1, :], position, head_ref[1:2, :]
    )
    segment_row = row_ref[0:1, :]
    allowed = causal & (segment == segment_row)
    local = lax.broadcasted_iota(jnp.int32, (length, 1), 0).astype(jnp.float32)
    enters = jnp.where(position > local, jnp.exp(running), 0.0)
    last = running[length - 1 : length, :]
    leaves = jnp.where(segment == segment_row[:, length - 1 :], jnp.exp(last - running), 0.0)
    spread = head_spread(head_width, width)
    wide = exact(jnp.concatenate([step_size, enters, leaves], axis=0), spread)
    weighted = conv_out * wide[:length]
    gram = nt(c_map, b_map)
    weighted_low = weighted.astype(low)
    parts = []
    for pair in range(width // (2 * head_width)):
        weights = []
        for head in (2 * pair, 2 * pair + 1):
            gap = jnp.where(allowed, running[:, head : head + 1] - running_t[head : head + 1, :], MASKED)
            weights.append((gram * jnp.exp(gap)).astype(low))
        columns = slice(2 * pair * head_width, 2 * (pair + 1) * head_width)
        parts.append(
            nn(jnp.concatenate(weights, axis=1), split_pair(weighted_low[:, columns], head_width))
        )
    held = state[...]
    held_low = held.astype(low)
    states_ref[...] = held_low
    scanned = jnp.concatenate(parts, axis=1) + nn(c_map, held_low) * wide[length : 2 * length]
    fade = wide[2 * length - 1 : 2 * length]
    state[...] = held * fade + tn(b_map, (weighted * wide[2 * length :]).astype(low))
    combined = scanned + skip_ref[...] * conv_out
    combined_ref[...] = combined.astype(low)
    gate = gate_ref[...].astype(jnp.float32)
    mixed_ref[:, :width] = (combined * (gate * sigmoid_of(gate))).astype(low)
    mixed_ref[:, width:] = attended_ref[...]


def mamba_backward_kernel(
    raw_ref, tail_ref, step_ref, info_ref, row_ref, weight_ref, bias_ref,
    shared_weight_ref, shared_bias_ref, head_ref, skip_ref, combined_ref, states_ref, grad_ref,
    query_ref, key_ref, value_ref,
    out_ref, inner_ref, sums_ref,
    grad_state, ext, ext_grad, *, head_width, places
):
    count = pl.num_programs(0)
    step = pl.program_id(0)
    length = grad_ref.shape[0]
    at_shared, at_query, at_key, at_gate, at_conv, at_value, at_step = places
    width = at_conv - at_gate
    states = (at_query - at_shared) // 2
    taps = weight_ref.shape[0]
    low = jnp.bfloat16
    f32 = jnp.float32
    gate_columns = slice(at_gate, at_gate + width)
    conv_columns = slice(at_conv, at_conv + width)
    shared_columns = slice(at_shared, at_shared + 2 * states)

    @pl.when(step == 0)
    def _():
        grad_state[...] = jnp.zeros_like(grad_state)
        ext_grad[...] = jnp.zeros_like(ext_grad)
        sums_ref[...] = jnp.zeros_like(sums_ref)

    ext[:TAIL, :width] = tail_ref[tail_ref.shape[0] - TAIL :, conv_columns].astype(f32)
    ext[:TAIL, width:] = tail_ref[tail_ref.shape[0] - TAIL :, shared_columns].astype(f32)
    ext[TAIL:, :width] = raw_ref[:, conv_columns].astype(f32)
    ext[TAIL:, width:] = raw_ref[:, shared_columns].astype(f32)
    segment = info_ref[:, 0:1]
    position = info_ref[:, 1:2]
    remaining = info_ref[:, 2:3]
    pre = causal_conv(ext, slice(0, width), weight_ref, bias_ref, position, taps)
    sig = sigmoid_of(pre)
    conv_out = pre * sig
    conv_slope = sig * (1.0 + pre * (1.0 - sig))
    pre = causal_conv(
        ext, slice(width, None), shared_weight_ref, shared_bias_ref, position, taps
    )
    sig = sigmoid_of(pre)
    shared = (pre * sig).astype(low)
    shared_slope = sig * (1.0 + pre * (1.0 - sig))
    b_map = shared[:, :states]
    c_map = shared[:, states:]
    step_in = step_ref[...] + head_ref[0:1, :]
    rate = head_ref[1:2, :]
    step_size, log_decay, running, running_t, causal = chunk_decay(step_in, position, rate)
    segment_row = row_ref[0:1, :]
    allowed = causal & (segment == segment_row)
    local = lax.broadcasted_iota(jnp.int32, (length, 1), 0).astype(f32)
    enters = jnp.where(position > local, jnp.exp(running), 0.0)
    last = running[length - 1 : length, :]
    leaves = jnp.where(segment == segment_row[:, length - 1 :], jnp.exp(last - running), 0.0)
    spread = head_spread(head_width, width)
    wide = exact(jnp.concatenate([step_size, enters, leaves], axis=0), spread)
    step_wide = wide[:length]
    enters_wide = wide[length : 2 * length]
    leaves_wide = wide[2 * length :]
    fade = wide[2 * length - 1 : 2 * length]
    weighted = conv_out * step_wide

    gate = raw_ref[:, gate_columns].astype(f32)
    sig = sigmoid_of(gate)
    grad_out = grad_ref[:, :width].astype(f32)
    grad_gate = grad_out * combined_ref[...].astype(f32) * (sig * (1.0 + gate * (1.0 - sig)))
    grad_scan = grad_out * (gate * sig)

    gram = nt(c_map, b_map)
    weighted_low = weighted.astype(low)
    grad_low = grad_scan.astype(low)
    lane = lax.broadcasted_iota(jnp.int32, (length, LANES), 1)
    sub = lax.broadcasted_iota(jnp.int32, (LANES, length), 0)
    grad_gram = jnp.zeros((length, length), f32)
    by_row = jnp.zeros((length, LANES), f32)
    by_column = jnp.zeros((LANES, length), f32)
    parts = []
    for pair in range(width // (2 * head_width)):
        columns = slice(2 * pair * head_width, 2 * (pair + 1) * head_width)
        split_grad = split_pair(grad_low[:, columns], head_width)
        products = nt(split_grad, weighted_low[:, columns])
        weights = []
        for place, head in enumerate((2 * pair, 2 * pair + 1)):
            gap = jnp.where(allowed, running[:, head : head + 1] - running_t[head : head + 1, :], MASKED)
            fading = jnp.exp(gap)
            weight = gram * fading
            product = products[place * length : (place + 1) * length]
            grad_gram = grad_gram + fading * product
            meeting = weight * product
            by_row = jnp.where(lane == head, jnp.sum(meeting, axis=1, keepdims=True), by_row)
            by_column = jnp.where(sub == head, jnp.sum(meeting, axis=0, keepdims=True), by_column)
            weights.append(weight.astype(low))
        parts.append(tn(jnp.concatenate(weights, axis=0), split_grad))
    held = states_ref[...]
    entering = (grad_scan * enters_wide).astype(low)
    leaving = (weighted * leaves_wide).astype(low)
    grad_held = grad_state[...]
    grad_held_low = grad_held.astype(low)
    from_state = nn(b_map, grad_held_low) * leaves_wide
    grad_weighted = jnp.concatenate(parts, axis=1) + from_state
    grad_gram_low = grad_gram.astype(low)
    grad_c = nn(grad_gram_low, b_map) + nt(entering, held)
    grad_b = tn(grad_gram_low, c_map) + nt(leaving, grad_held_low)
    met_in = grad_scan * enters_wide * nn(c_map, held)
    met_out = weighted * from_state
    met_state = fade * jnp.sum(held.astype(f32) * grad_held, axis=0, keepdims=True)
    grad_state[...] = grad_held * fade + tn(c_map, entering)
    grad_conv_out = grad_weighted * step_wide + skip_ref[...] * grad_scan
    gathered = exact(
        jnp.concatenate(
            [met_in, met_out, conv_out * grad_weighted, jnp.broadcast_to(met_state, (TAIL, width))],
            axis=0,
        ),
        head_gather(head_width, width),
    )
    out_rows = gathered[length : 2 * length]
    at_last = jnp.sum(out_rows, axis=0, keepdims=True) + gathered[3 * length : 3 * length + 1]
    grad_running = by_row - jnp.transpose(by_column) + gathered[:length] - out_rows
    grad_running = grad_running + jnp.where(local == length - 1.0, at_last, 0.0)
    rows = lax.broadcasted_iota(jnp.int32, (length, length), 0)
    later = lax.broadcasted_iota(jnp.int32, (length, length), 1) >= rows
    grad_decay = jnp.where(position == 0.0, 0.0, exact(later.astype(f32), grad_running))
    grad_step = (gathered[2 * length : 3 * length] - grad_decay * rate) * sigmoid_of(step_in)

    ext_grad[length : length + TAIL, :] = ext_grad[:TAIL, :]
    ext_grad[:length, :width] = grad_conv_out * conv_slope
    ext_grad[:length, width : width + states] = grad_b * shared_slope[:, :states]
    ext_grad[:length, width + states :] = grad_c * shared_slope[:, states:]

    def conv_back(columns, weights, row_at):
        now = ext_grad[:length, columns]
        running = weights[taps - 1 : taps, :] * now
        wide_columns = slice(0, now.shape[1])
        sums_ref[row_at + taps : row_at + taps + 1, wide_columns] += jnp.sum(now, axis=0, keepdims=True)
        sums_ref[row_at + taps - 1 : row_at + taps, wide_columns] += jnp.sum(
            now * ext[TAIL:, columns], axis=0, keepdims=True
        )
        for offset in range(1, taps):
            at = taps - 1 - offset
            running = running + weights[at : at + 1, :] * jnp.where(
                remaining >= offset, ext_grad[offset : offset + length, columns], 0.0
            )
            earlier = jnp.where(
                position >= offset, ext[TAIL - offset : TAIL - offset + length, columns], 0.0
            )
            sums_ref[row_at + at : row_at + at + 1, wide_columns] += jnp.sum(
                now * earlier, axis=0, keepdims=True
            )
        return running

    grad_conv = conv_back(slice(0, width), weight_ref, 0).astype(low)
    grad_shared = conv_back(slice(width, None), shared_weight_ref, taps + 1).astype(low)
    row_at = 2 * (taps + 1)
    sums_ref[row_at : row_at + 1, :width] += jnp.sum(grad_scan * conv_out, axis=0, keepdims=True)
    sums_ref[row_at + 1 : row_at + 2, :LANES] += jnp.sum(grad_step, axis=0, keepdims=True)
    sums_ref[row_at + 2 : row_at + 3, :LANES] += jnp.sum(
        grad_decay * log_decay, axis=0, keepdims=True
    )
    grad_step = grad_step.astype(low)
    out_ref[:, shared_columns] = grad_shared
    out_ref[:, at_query:at_key] = query_ref[...]
    out_ref[:, at_key:at_gate] = key_ref[...]
    out_ref[:, gate_columns] = grad_gate.astype(low)
    out_ref[:, conv_columns] = grad_conv
    out_ref[:, at_value:at_step] = value_ref[...]
    out_ref[:, at_step:] = grad_step
    inner = grad_step.astype(f32) * step_ref[...]
    for at in range(0, at_step, LANES):
        inner = inner + out_ref[:, at : at + LANES].astype(f32) * raw_ref[:, at : at + LANES].astype(f32)
    inner_ref[...] = inner


def rope(values, cosine, sine):
    return values * cosine + pltpu.roll(values, values.shape[1] // 2, 1) * sine


def attention_rows(query, key, begin, size, info_ref, row_ref, factor):
    seen = begin + size
    scores = nt(query, key) * factor
    rows = begin + lax.broadcasted_iota(jnp.int32, (size, seen), 0)
    columns = lax.broadcasted_iota(jnp.int32, (size, seen), 1)
    allowed = (rows >= columns) & (info_ref[begin:seen, 0:1] == row_ref[0:1, :seen])
    scores = jnp.where(allowed, scores, MASKED)
    raised = jnp.exp(scores - jnp.max(scores, axis=1, keepdims=True))
    return raised * (1.0 / jnp.sum(raised, axis=1, keepdims=True))


def attention_forward_kernel(
    query_ref, key_ref, value_ref, cosine_ref, sine_ref, info_ref, row_ref, out_ref, *, block
):
    low = jnp.bfloat16
    length, head_dim = query_ref.shape
    factor = 1.0 / math.sqrt(head_dim)
    cosine, sine = cosine_ref[...], sine_ref[...]
    query = rope(query_ref[...].astype(jnp.float32), cosine, sine).astype(low)
    key = rope(key_ref[...].astype(jnp.float32), cosine, sine).astype(low)
    value = value_ref[...]
    for begin in range(0, length, block):
        seen = begin + block
        probs = attention_rows(
            query[begin:seen], key[:seen], begin, block, info_ref, row_ref, factor
        )
        out_ref[begin:seen, :] = nn(probs.astype(low), value[:seen]).astype(low)


def attention_backward_kernel(
    query_ref, key_ref, value_ref, cosine_ref, sine_ref, info_ref, row_ref, grad_ref,
    grad_query_ref, grad_key_ref, grad_value_ref, key_total, value_total, *, block
):
    low = jnp.bfloat16
    length, head_dim = query_ref.shape
    factor = 1.0 / math.sqrt(head_dim)
    cosine, sine = cosine_ref[...], sine_ref[...]
    query = rope(query_ref[...].astype(jnp.float32), cosine, sine).astype(low)
    key = rope(key_ref[...].astype(jnp.float32), cosine, sine).astype(low)
    value = value_ref[...]
    key_total[...] = jnp.zeros_like(key_total)
    value_total[...] = jnp.zeros_like(value_total)
    for begin in range(0, length, block):
        seen = begin + block
        probs = attention_rows(
            query[begin:seen], key[:seen], begin, block, info_ref, row_ref, factor
        )
        grad_out = grad_ref[begin:seen, :]
        grad_probs = nt(grad_out, value[:seen])
        inner = jnp.sum(probs * grad_probs, axis=1, keepdims=True)
        grad_scores = (probs * (grad_probs - inner)).astype(low)
        grad_query = nn(grad_scores, key[:seen]) * factor
        grad_query_ref[begin:seen, :] = rope(
            grad_query, cosine[begin:seen], -sine[begin:seen]
        ).astype(low)
        key_total[:seen, :] += tn(grad_scores, query[begin:seen])
        value_total[:seen, :] += tn(probs.astype(low), grad_out)
    grad_key_ref[...] = rope(key_total[...] * factor, cosine, -sine).astype(low)
    grad_value_ref[...] = value_total[...].astype(low)


def whole(shape):
    return pl.BlockSpec(shape, lambda i: (0,) * len(shape))


def limits(megabytes):
    return pltpu.CompilerParams(vmem_limit_bytes=megabytes * 1024 * 1024)


def column_block(rows, width, at):
    return pl.BlockSpec((rows, width), lambda i: (0, at // width))


def attention_forward(raw, places, cosine, sine, info, row):
    length = raw.shape[0]
    _, at_query, at_key, _, _, at_value, _ = places
    width = cosine.shape[1]
    return pl.pallas_call(
        partial(attention_forward_kernel, block=256),
        grid=(1,),
        in_specs=[
            column_block(length, width, at_query),
            column_block(length, width, at_key),
            column_block(length, width, at_value),
            whole(cosine.shape), whole(sine.shape), whole(info.shape), whole(row.shape),
        ],
        out_specs=whole((length, width)),
        out_shape=jax.ShapeDtypeStruct((length, width), jnp.bfloat16),
        compiler_params=limits(48),
        name="attention_forward",
    )(raw, raw, raw, cosine, sine, info, row)


def attention_backward(raw, places, cosine, sine, info, row, grad_mixed):
    length = raw.shape[0]
    _, at_query, at_key, at_gate, at_conv, at_value, _ = places
    width = cosine.shape[1]
    out = jax.ShapeDtypeStruct((length, width), jnp.bfloat16)
    return pl.pallas_call(
        partial(attention_backward_kernel, block=256),
        grid=(1,),
        in_specs=[
            column_block(length, width, at_query),
            column_block(length, width, at_key),
            column_block(length, width, at_value),
            whole(cosine.shape), whole(sine.shape), whole(info.shape), whole(row.shape),
            column_block(length, width, at_conv - at_gate),
        ],
        out_specs=[whole((length, width))] * 3,
        out_shape=[out] * 3,
        scratch_shapes=[pltpu.VMEM((length, width), jnp.float32)] * 2,
        compiler_params=limits(48),
        name="attention_backward",
    )(raw, raw, raw, cosine, sine, info, row, grad_mixed)


def mamba_forward(raw, places, step_raw, info, row, params, attended, head_width):
    length = raw.shape[0]
    at_shared, at_query, at_key, at_gate, at_conv, at_value, at_step = places
    width = at_conv - at_gate
    shared = at_query - at_shared
    head_dim = attended.shape[1]
    chunks = length // CHUNK

    def block(columns, at=0):
        return pl.BlockSpec((CHUNK, columns), lambda i: (i, at // columns))

    return pl.pallas_call(
        partial(mamba_forward_kernel, head_width=head_width),
        grid=(chunks,),
        in_specs=[
            block(shared, at_shared), block(width, at_gate), block(width, at_conv),
            block(LANES), block(LANES), pl.BlockSpec((8, CHUNK), lambda i: (0, i)),
            *[whole(p.shape) for p in params],
            block(head_dim),
        ],
        out_specs=[
            block(width + head_dim), block(width),
            pl.BlockSpec((None, shared // 2, width), lambda i: (i, 0, 0)),
        ],
        out_shape=[
            jax.ShapeDtypeStruct((length, width + head_dim), jnp.bfloat16),
            jax.ShapeDtypeStruct((length, width), jnp.bfloat16),
            jax.ShapeDtypeStruct((chunks, shared // 2, width), jnp.bfloat16),
        ],
        scratch_shapes=[
            pltpu.VMEM((shared // 2, width), jnp.float32),
            pltpu.VMEM((TAIL + CHUNK, width + shared), jnp.float32),
        ],
        compiler_params=limits(48),
        name="mamba_forward",
    )(raw, raw, raw, step_raw, info, row, *params, attended)


def mamba_backward(
    raw, places, step_raw, info, row, params, combined, states, grad_mixed, grads, head_width
):
    length = raw.shape[0]
    at_shared, at_query, at_key, at_gate, at_conv, at_value, at_step = places
    width = at_conv - at_gate
    shared = at_query - at_shared
    head_dim = grads[0].shape[1]
    chunks = length // CHUNK
    total = at_step + LANES
    tail = 16

    def block(columns, at=0):
        return pl.BlockSpec((CHUNK, columns), lambda i: (chunks - 1 - i, at // columns))

    return pl.pallas_call(
        partial(mamba_backward_kernel, head_width=head_width, places=places),
        grid=(chunks,),
        in_specs=[
            block(at_step),
            pl.BlockSpec(
                (tail, at_step),
                lambda i: (jnp.maximum((chunks - 1 - i) * (CHUNK // tail) - 1, 0), 0),
            ),
            block(LANES), block(LANES),
            pl.BlockSpec((8, CHUNK), lambda i: (0, chunks - 1 - i)),
            *[whole(p.shape) for p in params],
            block(width),
            pl.BlockSpec((None, shared // 2, width), lambda i: (chunks - 1 - i, 0, 0)),
            block(grad_mixed.shape[1]),
            block(head_dim), block(head_dim), block(head_dim),
        ],
        out_specs=[block(total), block(LANES), whole((16, shared))],
        out_shape=[
            jax.ShapeDtypeStruct((length, total), jnp.bfloat16),
            jax.ShapeDtypeStruct((length, LANES), jnp.float32),
            jax.ShapeDtypeStruct((16, shared), jnp.float32),
        ],
        scratch_shapes=[
            pltpu.VMEM((shared // 2, width), jnp.float32),
            pltpu.VMEM((TAIL + CHUNK, width + shared), jnp.float32),
            pltpu.VMEM((TAIL + CHUNK, width + shared), jnp.float32),
        ],
        compiler_params=limits(48),
        name="mamba_backward",
    )(raw, raw, step_raw, info, row, *params, combined, states, grad_mixed, *grads)


def matmul(former, latter):
    return jnp.dot(former, latter, preferred_element_type=jnp.float32)


def matmul_left(former, latter):
    return lax.dot_general(
        former, latter, (((0,), (0,)), ((), ())), preferred_element_type=jnp.float32
    )


def matmul_right(former, latter):
    return lax.dot_general(
        former, latter, (((1,), (1,)), ((), ())), preferred_element_type=jnp.float32
    )


def col_swap(values, distance):
    count = lax.axis_size("col")
    return lax.ppermute(values, "col", [(i, i ^ distance) for i in range(count)])


def row_swap(values):
    return lax.ppermute(values, "row", [(0, 1), (1, 0)])


def gather_pieces(block):
    half = block.shape[0] // 2
    along_x = col_swap(block, 2)
    along_y = row_swap(block)
    core = col_swap(block, 1)
    top = col_swap(along_y[:half], 2)
    low = row_swap(along_x[half:])
    own = [block, along_x, core, col_swap(along_x, 1)]
    other = [along_y, (top, low), col_swap(along_y, 1), (col_swap(top, 1), col_swap(low, 1))]
    return own, other


def add_low(former, latter):
    return (former.astype(jnp.float32) + latter.astype(jnp.float32)).astype(jnp.bfloat16)


def scatter_sum(shares):
    (own, own_far), (other, other_far) = shares
    tokens = own.shape[0]
    half = tokens // 2
    width = own.shape[1] // 2
    other = add_low(other, col_swap(other_far, 1))
    own = add_low(own, col_swap(own_far, 1))
    top_got = col_swap(jnp.concatenate([own[:half, width:], other[:half, width:]], axis=0), 2)
    low_got = row_swap(other[half:])
    top_last = row_swap(add_low(other[:half, :width], top_got[half:]))
    low_last = col_swap(add_low(own[half:, width:], low_got[:, width:]), 2)
    wide = jnp.float32
    top = own[:half, :width].astype(wide) + top_got[:half].astype(wide) + top_last.astype(wide)
    low = own[half:, :width].astype(wide) + low_got[:, :width].astype(wide) + low_last.astype(wide)
    return jnp.concatenate([top, low], axis=0)


def token_total(own, other):
    total = own + row_swap(other)
    total = total + col_swap(total, 1)
    return total + col_swap(total, 2)


def dp_sum(values):
    if lax.axis_size("dp") != 4:
        return lax.psum(values, "dp")
    place = lax.axis_index("dp")
    pair = add_low(values, lax.ppermute(values, "dp", [(0, 1), (3, 2)]))
    total = add_low(pair, lax.ppermute(pair, "dp", [(1, 2), (2, 1)]))
    final = lax.ppermute(total, "dp", [(1, 0), (2, 3)])
    return jnp.where((place == 1) | (place == 2), total, final)


def dp_total(values):
    count = lax.axis_size("dp")
    if count & (count - 1):
        return lax.psum(values, "dp")
    distance = 1
    while distance < count:
        values = values + lax.ppermute(values, "dp", [(i, i ^ distance) for i in range(count)])
        distance *= 2
    return values


def exchange_blocks(blocks):
    return [col_swap(block, d) if d else block for block, d in zip(blocks, DISTANCES)]


def in_order(pieces, index, axis):
    stacked = jnp.stack([pieces[DISTANCES.index(d)] for d in range(len(DISTANCES))])
    return jnp.concatenate(
        [lax.dynamic_index_in_dim(stacked, index ^ b, 0, keepdims=False) for b in range(len(pieces))],
        axis=axis,
    )


def own_first(values, row_index):
    return jnp.where(row_index == 0, values, jnp.flip(values, 0))


def assemble_kernel(*refs, split, normed):
    tile = pl.program_id(0)
    tiles = pl.num_programs(0)
    count = len(split) + sum(split)
    pieces = list(refs[:count])
    rest = refs[count:]
    columns = []
    for halves in split:
        if halves:
            top, low = pieces.pop(0), pieces.pop(0)
            columns.append(jnp.where(tile < tiles // 2, top[...], low[...]))
        else:
            columns.append(pieces.pop(0)[...])
    width = columns[0].shape[1]
    if not normed:
        for at, piece in enumerate(columns):
            rest[0][:, at * width : (at + 1) * width] = piece
        return
    gain_ref, out_ref, factor_ref = rest
    total = jnp.zeros((columns[0].shape[0], 1), jnp.float32)
    for piece in columns:
        values = piece.astype(jnp.float32)
        total = total + jnp.sum(values * values, axis=1, keepdims=True)
    factor = lax.rsqrt(total * (1.0 / (width * len(columns))) + EPS)
    for at, piece in enumerate(columns):
        span = slice(at * width, (at + 1) * width)
        out_ref[:, span] = (piece.astype(jnp.float32) * factor * gain_ref[:, span]).astype(jnp.bfloat16)
    factor_ref[...] = jnp.broadcast_to(factor, factor_ref.shape)


def assemble(pieces, gain=None):
    tokens, width = pieces[0].shape
    tiles = 4
    size = tokens // tiles
    total = width * len(pieces)
    split = [isinstance(piece, tuple) for piece in pieces]
    specs, operands = [], []
    for piece, halves in zip(pieces, split):
        if halves:
            specs.append(pl.BlockSpec((size, width), lambda i: (jnp.minimum(i, tiles // 2 - 1), 0)))
            specs.append(pl.BlockSpec((size, width), lambda i: (jnp.maximum(i - tiles // 2, 0), 0)))
            operands.extend(piece)
        else:
            specs.append(pl.BlockSpec((size, width), lambda i: (i, 0)))
            operands.append(piece)
    out_specs = [pl.BlockSpec((size, total), lambda i: (i, 0))]
    out_shape = [jax.ShapeDtypeStruct((tokens, total), jnp.bfloat16)]
    if gain is not None:
        specs.append(whole((1, total)))
        operands.append(gain)
        out_specs.append(pl.BlockSpec((size, LANES), lambda i: (i, 0)))
        out_shape.append(jax.ShapeDtypeStruct((tokens, LANES), jnp.float32))
    out = pl.pallas_call(
        partial(assemble_kernel, split=split, normed=gain is not None),
        grid=(tiles,),
        in_specs=specs,
        out_specs=out_specs,
        out_shape=out_shape,
        compiler_params=limits(32),
        name="assemble",
    )(*operands)
    return out if gain is not None else out[0]


def on_device(
    tokens,
    cotangent,
    segment_ids,
    norm1_gain,
    proj_gate,
    proj_conv,
    proj_step,
    proj_shared,
    proj_query,
    proj_key,
    proj_value,
    conv_weight,
    conv_bias,
    shared_conv,
    shared_bias,
    step_bias,
    decay_log,
    skip_gain,
    mamba_out_proj,
    attn_out_proj,
    norm2_gain,
    ffn_gate,
    ffn_up,
    ffn_down,
):
    low = jnp.bfloat16
    wide = jnp.float32
    me = lax.axis_index("col")
    row_index = lax.axis_index("row")
    length = segment_ids.shape[1]
    width = tokens.shape[1]
    model = width * len(DISTANCES)
    head_dim = proj_key.shape[1]
    channels = proj_gate.shape[1] // 4
    steps = proj_step.shape[1] // 4
    head_width = channels // steps
    units = ffn_gate.shape[1] // 4
    query_width = proj_query.shape[1] // 4
    part = proj_shared.shape[1]
    at_query = 2 * part
    at_key = at_query + query_width
    at_gate = at_key + head_dim
    at_conv = at_gate + channels
    at_value = at_conv + channels
    at_step = at_value + head_dim
    places = (0, at_query, at_key, at_gate, at_conv, at_value, at_step)

    def cols(weight, place, count):
        return lax.dynamic_slice_in_dim(weight, place * count, count, 1)

    def rows(weight, place, count):
        return lax.dynamic_slice_in_dim(weight, place * count, count, 0)

    def first_block(place):
        step = jnp.pad(cols(proj_step, place, steps), ((0, 0), (0, LANES - steps)))
        return jnp.concatenate(
            [
                proj_shared,
                cols(proj_query, place, query_width),
                proj_key,
                cols(proj_gate, place, channels),
                cols(proj_conv, place, channels),
                proj_value,
                step,
            ],
            axis=1,
        )

    token_own, token_other = gather_pieces(tokens)
    blocks = exchange_blocks([first_block(me ^ d) for d in DISTANCES])
    shared_own = jnp.concatenate([b[:, :part] for b in blocks], axis=0)
    shared_other = row_swap(shared_own)
    weight_first = jnp.concatenate(
        [
            jnp.where(row_index == 0, shared_own, shared_other),
            jnp.where(row_index == 0, shared_other, shared_own),
            jnp.concatenate([b[:, part:] for b in blocks], axis=0),
        ],
        axis=1,
    )
    gains = jnp.stack([norm1_gain, norm2_gain])
    gains = jnp.concatenate(exchange_blocks([gains] * 4), axis=1)
    gain1, gain2 = gains[0:1], gains[1:2]
    weight_out = jnp.concatenate(
        exchange_blocks(
            [
                jnp.concatenate(
                    [rows(mamba_out_proj, me ^ d, channels), rows(attn_out_proj, me ^ d, query_width)],
                    axis=0,
                )
                for d in DISTANCES
            ]
        ),
        axis=1,
    )
    weight_in = jnp.concatenate(
        exchange_blocks(
            [
                jnp.concatenate([cols(ffn_gate, me ^ d, units), cols(ffn_up, me ^ d, units)], axis=1)
                for d in DISTANCES
            ]
        ),
        axis=0,
    )
    weight_down = jnp.concatenate(
        exchange_blocks([rows(ffn_down, me ^ d, units) for d in DISTANCES]), axis=1
    )

    segments = own_first(segment_ids, row_index)
    indices = jnp.arange(length, dtype=jnp.int32)
    same = segments[:, :, None] == segments[:, None, :]
    position = jnp.sum(same & (indices[:, None] > indices[None, :]), axis=2).astype(wide)
    remaining = jnp.sum(same & (indices[:, None] < indices[None, :]), axis=2).astype(wide)
    lane = jnp.arange(LANES)
    info = jnp.where(
        lane == 0,
        segments.astype(wide)[..., None],
        jnp.where(lane == 1, position[..., None], remaining[..., None]),
    )
    row_info = jnp.broadcast_to(segments.astype(wide)[:, None, :], (2, 8, length))
    half_dim = head_dim // 2
    frequency = ROPE_BASE ** (-2.0 * jnp.arange(half_dim, dtype=wide) / head_dim)
    angles = position[..., None] * frequency
    cosine, sine = jnp.cos(angles), jnp.sin(angles)
    cosine = jnp.concatenate([cosine, cosine], axis=2)
    sine = jnp.concatenate([-sine, sine], axis=2)
    head_rows = jnp.pad(
        jnp.stack([step_bias, jnp.exp(decay_log)]), ((0, 6), (0, LANES - steps))
    )
    params = (
        conv_weight, conv_bias[None], shared_conv, shared_bias[None], head_rows,
        jnp.repeat(skip_gain, head_width)[None],
    )

    both = (0, 1)
    normed1, factor1, raw, step_raw, mixed, combined, states = [], [], [], [], [], [], []
    for s, pieces in enumerate((token_own, token_other)):
        normed, factor = assemble(pieces, gain1)
        normed1.append(normed)
        factor1.append(factor)
        raw.append(matmul(normed, weight_first[:, :at_step]).astype(low))
        step_raw.append(matmul(normed, weight_first[:, at_step:]))
        attended = attention_forward(raw[s], places, cosine[s], sine[s], info[s], row_info[s])
        got = mamba_forward(
            raw[s], places, step_raw[s], info[s], row_info[s], params, attended, head_width
        )
        mixed.append(got[0])
        combined.append(got[1])
        states.append(got[2])

    def spread_out(values, weight):
        return (
            matmul(values, weight[:, : model // 2]).astype(low),
            matmul(values, weight[:, model // 2 :]).astype(low),
        )

    def spread_back(values, weight):
        return (
            matmul_right(values, weight[: model // 2]).astype(low),
            matmul_right(values, weight[model // 2 :]).astype(low),
        )

    hidden1 = tokens.astype(wide) + scatter_sum([spread_out(mixed[s], weight_out) for s in both])
    normed2, factor2, gate_pre, up_pre, hidden = [], [], [], [], []
    for pieces in gather_pieces(hidden1.astype(low)):
        normed, factor = assemble(pieces, gain2)
        normed2.append(normed)
        factor2.append(factor)
        gate_pre.append(matmul(normed, weight_in[:, :units]).astype(low))
        up_pre.append(matmul(normed, weight_in[:, units:]).astype(low))
        gate = gate_pre[-1].astype(wide)
        hidden.append((gate * jax.nn.sigmoid(gate) * up_pre[-1].astype(wide)).astype(low))
    cot = [assemble(pieces) for pieces in gather_pieces(cotangent)]
    grad_in, inner = [], []
    for s in both:
        grad_hidden = matmul_right(cot[s], weight_down)
        gate, up = gate_pre[s].astype(wide), up_pre[s].astype(wide)
        sigmoid = jax.nn.sigmoid(gate)
        grad_gate = (grad_hidden * up * sigmoid * (1.0 + gate * (1.0 - sigmoid))).astype(low)
        grad_up = (grad_hidden * gate * sigmoid).astype(low)
        inner.append(
            jnp.sum(grad_gate.astype(wide) * gate + grad_up.astype(wide) * up, axis=1)
            .reshape(length // LANES, LANES)
        )
        grad_in.append(jnp.concatenate([grad_gate, grad_up], axis=1))
    inner2 = token_total(*inner).reshape(length, 1)
    grad_normed2 = scatter_sum([spread_back(grad_in[s], weight_in) for s in both])
    output = (hidden1 + scatter_sum([spread_out(hidden[s], weight_down) for s in both])).astype(low)

    def token_grad(former, latter):
        return (matmul_left(former[0], latter[0]) + matmul_left(former[1], latter[1])).astype(low)

    grad_down = token_grad(hidden, cot)
    grad_weight_in = token_grad(normed2, grad_in)
    own_factor = factor2[0][:, :1]
    back2 = (
        own_factor * norm2_gain * grad_normed2
        - hidden1 * (own_factor * own_factor * inner2 / model)
    )
    grad_gain2 = jnp.sum(grad_normed2 * hidden1 * own_factor, axis=0)
    grad_hidden1 = cotangent.astype(wide) + back2
    mix_grad = [assemble(pieces) for pieces in gather_pieces(grad_hidden1.astype(low))]
    grad_weight_out = token_grad(mixed, mix_grad)
    grad_first, inner, sums = [], [], []
    for s in both:
        grad_mixed = matmul_right(mix_grad[s], weight_out).astype(low)
        grads = attention_backward(
            raw[s], places, cosine[s], sine[s], info[s], row_info[s], grad_mixed
        )
        got = mamba_backward(
            raw[s], places, step_raw[s], info[s], row_info[s], params, combined[s], states[s],
            grad_mixed, grads, head_width,
        )
        grad_first.append(got[0])
        inner.append(jnp.sum(got[1], axis=1).reshape(length // LANES, LANES))
        sums.append(got[2])
    inner1 = token_total(*inner).reshape(length, 1)
    grad_normed1 = scatter_sum([spread_back(grad_first[s], weight_first) for s in both])
    grad_weight_first = token_grad(normed1, grad_first)
    own_factor = factor1[0][:, :1]
    own_tokens = tokens.astype(wide)
    back1 = (
        own_factor * norm1_gain * grad_normed1
        - own_tokens * (own_factor * own_factor * inner1 / model)
    )
    grad_gain1 = jnp.sum(grad_normed1 * own_tokens * own_factor, axis=0)
    tokens_grad = (grad_hidden1 + back1).astype(low)

    four = range(4)
    down = exchange_blocks([grad_down[:, p * width : (p + 1) * width] for p in four])
    down = dp_sum(jnp.stack(down))
    d_ffn_down = in_order([down[p] for p in four], me, 0).astype(wide)
    into = exchange_blocks([grad_weight_in[p * width : (p + 1) * width] for p in four])
    into = dp_sum(jnp.stack(into))
    d_ffn_gate = in_order([into[p, :, :units] for p in four], me, 1).astype(wide)
    d_ffn_up = in_order([into[p, :, units:] for p in four], me, 1).astype(wide)
    outs = exchange_blocks([grad_weight_out[:, p * width : (p + 1) * width] for p in four])
    outs = dp_sum(jnp.stack(outs))
    d_mamba_out = in_order([outs[p, :channels] for p in four], me, 0).astype(wide)
    d_attn_out = in_order([outs[p, channels:] for p in four], me, 0).astype(wide)
    first = exchange_blocks([grad_weight_first[p * width : (p + 1) * width] for p in four])
    lone = dp_sum(jnp.stack([f[:, at_gate:at_value] for f in first]))
    d_gate = in_order([lone[p, :, :channels] for p in four], me, 1).astype(wide)
    d_conv = in_order([lone[p, :, channels:] for p in four], me, 1).astype(wide)

    def over_devices(begin, end):
        return sum(f[:, begin:end].astype(wide) for f in first).astype(low)

    shared_sum = over_devices(0, at_query)
    shared_keep = jnp.where(row_index == 0, shared_sum[:, :part], shared_sum[:, part:])
    shared_send = jnp.where(row_index == 0, shared_sum[:, part:], shared_sum[:, :part])
    shared_total = add_low(shared_keep, row_swap(shared_send))
    step_all = in_order([f[:, at_step : at_step + steps] for f in first], me, 1)
    query_all = in_order([f[:, at_query:at_key] for f in first], me, 1)
    common = dp_sum(
        jnp.concatenate(
            [
                query_all, over_devices(at_key, at_gate), over_devices(at_value, at_step),
                shared_total, jnp.pad(step_all, ((0, 0), (0, LANES - 4 * steps))),
            ],
            axis=1,
        )
    ).astype(wide)
    d_query = common[:, : 4 * query_width]
    at = 4 * query_width
    d_key = common[:, at : at + head_dim]
    d_value = common[:, at + head_dim : at + 2 * head_dim]
    at = at + 2 * head_dim
    d_shared = common[:, at : at + part]
    d_step = common[:, at + part : at + part + 4 * steps]

    sums = sums[0] + sums[1]
    sums = jnp.concatenate(
        [sums[:13], jnp.stack([grad_gain1, grad_gain2]), jnp.zeros((1, width), wide)], axis=0
    )
    line = jnp.arange(16)[:, None]
    taps = conv_weight.shape[0]
    is_shared = (line > taps) & (line < 2 * taps + 2)
    sums = sums + jnp.where(is_shared | (line >= 13), row_swap(sums), 0.0)
    sums = sums + jnp.where(is_shared, col_swap(sums, 1), 0.0)
    sums = sums + jnp.where(is_shared, col_swap(sums, 2), 0.0)
    sums = dp_total(sums)
    return (
        output, tokens_grad, sums[13], d_gate, d_conv, d_step, d_shared, d_query, d_key, d_value,
        sums[:taps, :channels], sums[taps, :channels], sums[taps + 1 : 2 * taps + 1],
        sums[2 * taps + 1],
        sums[11, :steps], sums[12, :steps],
        jnp.sum(sums[10, :channels].reshape(steps, head_width), axis=1),
        d_mamba_out, d_attn_out, sums[14], d_ffn_gate, d_ffn_up, d_ffn_down,
    )


def solution(mesh):
    return jax.shard_map(
        on_device,
        mesh=mesh,
        in_specs=(
            P(("dp", "row"), "col"),
            P(("dp", "row"), "col"),
            P("dp", None),
            P("col"),
            P("col", "row"),
            P("col", "row"),
            P("col", "row"),
            P("col", "row"),
            P("col", "row"),
            P("col", "row"),
            P("col", "row"),
            P(None, ("row", "col")),
            P(("row", "col")),
            P(),
            P(),
            P(("row", "col")),
            P(("row", "col")),
            P(("row", "col")),
            P("row", "col"),
            P("row", "col"),
            P("col"),
            P("col", "row"),
            P("col", "row"),
            P("row", "col"),
        ),
        out_specs=(
            P(("dp", "row"), "col"),
            P(("dp", "row"), "col"),
            P("col"),
            P("col", "row"),
            P("col", "row"),
            P("col", "row"),
            P("col", "row"),
            P("col", "row"),
            P("col", "row"),
            P("col", "row"),
            P(None, ("row", "col")),
            P(("row", "col")),
            P(),
            P(),
            P(("row", "col")),
            P(("row", "col")),
            P(("row", "col")),
            P("row", "col"),
            P("row", "col"),
            P("col"),
            P("col", "row"),
            P("col", "row"),
            P("row", "col"),
        ),
        check_vma=False,
    )
```

```python
from functools import partial
import math
from typing import NamedTuple

import jax
import jax.numpy as jnp
from jax import lax
from jax.experimental import pallas as pl
from jax.experimental.pallas import tpu as pltpu
from jax.sharding import PartitionSpec as P

EPS = 1e-05
ROPE_BASE = 100000000000.0
MASKED = -1e30
HIGHEST = lax.Precision.HIGHEST
DISTANCES = (0, 2, 1, 3)
LANES = 128
CHUNK = 128
TAIL = 8


class Places(NamedTuple):
    query: int
    key: int
    gate: int
    value: int
    shared: int
    conv: int
    step: int


def dot_any(former, latter, dims, precision=None):
    return lax.dot_general(
        former, latter, (dims, ((), ())), precision=precision, preferred_element_type=jnp.float32
    )


def nn(former, latter):
    return dot_any(former, latter, ((1,), (0,)))


def nt(former, latter):
    return dot_any(former, latter, ((1,), (1,)))


def tn(former, latter):
    return dot_any(former, latter, ((0,), (0,)))


def exact(former, latter):
    return dot_any(former, latter, ((1,), (0,)), HIGHEST)


def sigmoid_of(values):
    return 1.0 / (1.0 + jnp.exp(-values))


def softplus_of(values):
    return jnp.maximum(values, 0.0) + jnp.log1p(jnp.exp(-jnp.abs(values)))


def head_spread(head_width, width):
    heads = lax.broadcasted_iota(jnp.int32, (LANES, width), 0)
    columns = lax.broadcasted_iota(jnp.int32, (LANES, width), 1)
    return (columns // head_width == heads).astype(jnp.float32)


def head_gather(head_width, width):
    columns = lax.broadcasted_iota(jnp.int32, (width, LANES), 0)
    heads = lax.broadcasted_iota(jnp.int32, (width, LANES), 1)
    return (columns // head_width == heads).astype(jnp.float32)


def causal_conv(ext_ref, columns, weight_ref, bias_ref, position, taps):
    length = ext_ref.shape[0] - TAIL
    running = bias_ref[...] + weight_ref[taps - 1 : taps, :] * ext_ref[TAIL:, columns]
    for offset in range(1, taps):
        earlier = ext_ref[TAIL - offset : TAIL - offset + length, columns]
        running = running + weight_ref[taps - 1 - offset : taps - offset, :] * jnp.where(
            position >= offset, earlier, 0.0
        )
    return running


def chunk_decay(step_in, position, decay_rate):
    length = step_in.shape[0]
    step_size = softplus_of(step_in)
    log_decay = jnp.where(position == 0.0, 0.0, -step_size * decay_rate)
    rows = lax.broadcasted_iota(jnp.int32, (length, length), 0)
    columns = lax.broadcasted_iota(jnp.int32, (length, length), 1)
    causal = rows >= columns
    running = exact(causal.astype(jnp.float32), log_decay)
    return step_size, log_decay, running, jnp.transpose(running), causal


def split_pair(values, head_width):
    lane = lax.broadcasted_iota(jnp.int32, values.shape, 1)
    zero = jnp.zeros_like(values)
    return jnp.concatenate(
        [jnp.where(lane < head_width, values, zero), jnp.where(lane < head_width, zero, values)],
        axis=0,
    )


def mamba_forward_kernel(
    raw_ref, step_ref, info_ref, row_ref, weight_ref, bias_ref,
    shared_weight_ref, shared_bias_ref, head_ref, skip_ref, attended_ref,
    mixed_ref, combined_ref, states_ref,
    state, ext, *, head_width, places
):
    chunk = pl.program_id(0)
    length, width = combined_ref.shape
    gate_columns = slice(places.gate, places.value)
    conv_columns = slice(places.conv, places.step)
    shared_columns = slice(places.shared, places.conv)
    states = (places.conv - places.shared) // 2
    taps = weight_ref.shape[0]
    low = jnp.bfloat16

    @pl.when(chunk == 0)
    def _():
        state[...] = jnp.zeros_like(state)
        ext[...] = jnp.zeros_like(ext)

    ext[:TAIL, :] = ext[length : length + TAIL, :]
    ext[TAIL:, :width] = raw_ref[:, conv_columns].astype(jnp.float32)
    ext[TAIL:, width:] = raw_ref[:, shared_columns].astype(jnp.float32)
    segment = info_ref[:, 0:1]
    position = info_ref[:, 1:2]
    pre = causal_conv(ext, slice(0, width), weight_ref, bias_ref, position, taps)
    conv_out = pre * sigmoid_of(pre)
    pre = causal_conv(
        ext, slice(width, None), shared_weight_ref, shared_bias_ref, position, taps
    )
    shared = (pre * sigmoid_of(pre)).astype(low)
    b_map = shared[:, :states]
    c_map = shared[:, states:]
    step_size, _, running, running_t, causal = chunk_decay(
        step_ref[...] + head_ref[0:1, :], position, head_ref[1:2, :]
    )
    segment_row = row_ref[0:1, :]
    allowed = causal & (segment == segment_row)
    local = lax.broadcasted_iota(jnp.int32, (length, 1), 0).astype(jnp.float32)
    enters = jnp.where(position > local, jnp.exp(running), 0.0)
    last = running[length - 1 : length, :]
    leaves = jnp.where(segment == segment_row[:, length - 1 :], jnp.exp(last - running), 0.0)
    spread = head_spread(head_width, width)
    wide = exact(jnp.concatenate([step_size, enters, leaves], axis=0), spread)
    weighted = conv_out * wide[:length]
    gram = nt(c_map, b_map)
    weighted_low = weighted.astype(low)
    parts = []
    for pair in range(width // (2 * head_width)):
        weights = []
        for head in (2 * pair, 2 * pair + 1):
            gap = jnp.where(allowed, running[:, head : head + 1] - running_t[head : head + 1, :], MASKED)
            weights.append((gram * jnp.exp(gap)).astype(low))
        columns = slice(2 * pair * head_width, 2 * (pair + 1) * head_width)
        parts.append(
            nn(jnp.concatenate(weights, axis=1), split_pair(weighted_low[:, columns], head_width))
        )
    held = state[...]
    held_low = held.astype(low)
    states_ref[...] = held_low
    scanned = jnp.concatenate(parts, axis=1) + nn(c_map, held_low) * wide[length : 2 * length]
    fade = wide[2 * length - 1 : 2 * length]
    state[...] = held * fade + tn(b_map, (weighted * wide[2 * length :]).astype(low))
    combined = scanned + skip_ref[...] * conv_out
    combined_ref[...] = combined.astype(low)
    gate = raw_ref[:, gate_columns].astype(jnp.float32)
    mixed_ref[:, :width] = (combined * (gate * sigmoid_of(gate))).astype(low)
    mixed_ref[:, width:] = attended_ref[...]


def mamba_backward_kernel(
    raw_ref, tail_ref, step_ref, info_ref, row_ref, weight_ref, bias_ref,
    shared_weight_ref, shared_bias_ref, head_ref, skip_ref, states_ref, grad_ref,
    out_ref, inner_ref, sums_ref,
    grad_state, ext, ext_grad, *, head_width, places
):
    count = pl.num_programs(0)
    step = pl.program_id(0)
    length = grad_ref.shape[0]
    width = places.step - places.conv
    states = (places.conv - places.shared) // 2
    taps = weight_ref.shape[0]
    low = jnp.bfloat16
    f32 = jnp.float32
    gate_columns = slice(places.gate, places.value)
    conv_columns = slice(places.conv, places.step)
    shared_columns = slice(places.shared, places.conv)

    @pl.when(step == 0)
    def _():
        grad_state[...] = jnp.zeros_like(grad_state)
        ext_grad[...] = jnp.zeros_like(ext_grad)
        sums_ref[...] = jnp.zeros_like(sums_ref)

    tail_at = tail_ref.shape[0] - TAIL
    ext[:TAIL, :width] = tail_ref[:, conv_columns].astype(f32)[tail_at:]
    ext[:TAIL, width:] = tail_ref[:, shared_columns].astype(f32)[tail_at:]
    ext[TAIL:, :width] = raw_ref[:, conv_columns].astype(f32)
    ext[TAIL:, width:] = raw_ref[:, shared_columns].astype(f32)
    segment = info_ref[:, 0:1]
    position = info_ref[:, 1:2]
    remaining = info_ref[:, 2:3]
    pre = causal_conv(ext, slice(0, width), weight_ref, bias_ref, position, taps)
    sig = sigmoid_of(pre)
    conv_out = pre * sig
    conv_slope = sig * (1.0 + pre * (1.0 - sig))
    pre = causal_conv(
        ext, slice(width, None), shared_weight_ref, shared_bias_ref, position, taps
    )
    sig = sigmoid_of(pre)
    shared = (pre * sig).astype(low)
    shared_slope = sig * (1.0 + pre * (1.0 - sig))
    b_map = shared[:, :states]
    c_map = shared[:, states:]
    step_in = step_ref[...] + head_ref[0:1, :]
    rate = head_ref[1:2, :]
    step_size, log_decay, running, running_t, causal = chunk_decay(step_in, position, rate)
    segment_row = row_ref[0:1, :]
    allowed = causal & (segment == segment_row)
    local = lax.broadcasted_iota(jnp.int32, (length, 1), 0).astype(f32)
    enters = jnp.where(position > local, jnp.exp(running), 0.0)
    last = running[length - 1 : length, :]
    leaves = jnp.where(segment == segment_row[:, length - 1 :], jnp.exp(last - running), 0.0)
    spread = head_spread(head_width, width)
    wide = exact(jnp.concatenate([step_size, enters, leaves], axis=0), spread)
    step_wide = wide[:length]
    enters_wide = wide[length : 2 * length]
    leaves_wide = wide[2 * length :]
    fade = wide[2 * length - 1 : 2 * length]
    weighted = conv_out * step_wide

    gate = raw_ref[:, gate_columns].astype(f32)
    sig = sigmoid_of(gate)
    grad_scan = grad_ref[:, :width].astype(f32) * (gate * sig)

    gram = nt(c_map, b_map)
    weighted_low = weighted.astype(low)
    grad_low = grad_scan.astype(low)
    lane = lax.broadcasted_iota(jnp.int32, (length, LANES), 1)
    sub = lax.broadcasted_iota(jnp.int32, (LANES, length), 0)
    grad_gram = jnp.zeros((length, length), f32)
    by_row = jnp.zeros((length, LANES), f32)
    by_column = jnp.zeros((LANES, length), f32)
    parts = []
    for pair in range(width // (2 * head_width)):
        columns = slice(2 * pair * head_width, 2 * (pair + 1) * head_width)
        split_grad = split_pair(grad_low[:, columns], head_width)
        products = nt(split_grad, weighted_low[:, columns])
        weights = []
        for place, head in enumerate((2 * pair, 2 * pair + 1)):
            gap = jnp.where(allowed, running[:, head : head + 1] - running_t[head : head + 1, :], MASKED)
            fading = jnp.exp(gap)
            weight = gram * fading
            product = products[place * length : (place + 1) * length]
            grad_gram = grad_gram + fading * product
            meeting = weight * product
            by_row = jnp.where(lane == head, jnp.sum(meeting, axis=1, keepdims=True), by_row)
            by_column = jnp.where(sub == head, jnp.sum(meeting, axis=0, keepdims=True), by_column)
            weights.append(weight.astype(low))
        parts.append(tn(jnp.concatenate(weights, axis=0), split_grad))
    held = states_ref[...]
    entering = (grad_scan * enters_wide).astype(low)
    leaving = (weighted * leaves_wide).astype(low)
    grad_held = grad_state[...]
    grad_held_low = grad_held.astype(low)
    from_state = nn(b_map, grad_held_low) * leaves_wide
    grad_weighted = jnp.concatenate(parts, axis=1) + from_state
    grad_gram_low = grad_gram.astype(low)
    grad_c = nn(grad_gram_low, b_map) + nt(entering, held)
    grad_b = tn(grad_gram_low, c_map) + nt(leaving, grad_held_low)
    met_in = grad_scan * enters_wide * nn(c_map, held)
    met_out = weighted * from_state
    met_state = fade * jnp.sum(held.astype(f32) * grad_held, axis=0, keepdims=True)
    grad_state[...] = grad_held * fade + tn(c_map, entering)
    grad_conv_out = grad_weighted * step_wide + skip_ref[...] * grad_scan
    gathered = exact(
        jnp.concatenate(
            [met_in, met_out, conv_out * grad_weighted, jnp.broadcast_to(met_state, (TAIL, width))],
            axis=0,
        ),
        head_gather(head_width, width),
    )
    out_rows = gathered[length : 2 * length]
    at_last = jnp.sum(out_rows, axis=0, keepdims=True) + gathered[3 * length : 3 * length + 1]
    grad_running = by_row - jnp.transpose(by_column) + gathered[:length] - out_rows
    grad_running = grad_running + jnp.where(local == length - 1.0, at_last, 0.0)
    rows = lax.broadcasted_iota(jnp.int32, (length, length), 0)
    later = lax.broadcasted_iota(jnp.int32, (length, length), 1) >= rows
    grad_decay = jnp.where(position == 0.0, 0.0, exact(later.astype(f32), grad_running))
    grad_step = (gathered[2 * length : 3 * length] - grad_decay * rate) * sigmoid_of(step_in)

    ext_grad[length : length + TAIL, :] = ext_grad[:TAIL, :]
    ext_grad[:length, :width] = grad_conv_out * conv_slope
    ext_grad[:length, width : width + states] = grad_b * shared_slope[:, :states]
    ext_grad[:length, width + states :] = grad_c * shared_slope[:, states:]

    def conv_back(columns, weights, row_at):
        now = ext_grad[:length, columns]
        running = weights[taps - 1 : taps, :] * now
        wide_columns = slice(0, now.shape[1])
        sums_ref[row_at + taps : row_at + taps + 1, wide_columns] += jnp.sum(now, axis=0, keepdims=True)
        sums_ref[row_at + taps - 1 : row_at + taps, wide_columns] += jnp.sum(
            now * ext[TAIL:, columns], axis=0, keepdims=True
        )
        for offset in range(1, taps):
            at = taps - 1 - offset
            running = running + weights[at : at + 1, :] * jnp.where(
                remaining >= offset, ext_grad[offset : offset + length, columns], 0.0
            )
            earlier = jnp.where(
                position >= offset, ext[TAIL - offset : TAIL - offset + length, columns], 0.0
            )
            sums_ref[row_at + at : row_at + at + 1, wide_columns] += jnp.sum(
                now * earlier, axis=0, keepdims=True
            )
        return running

    grad_conv = conv_back(slice(0, width), weight_ref, 0).astype(low)
    grad_shared = conv_back(slice(width, None), shared_weight_ref, taps + 1).astype(low)
    row_at = 2 * (taps + 1)
    sums_ref[row_at : row_at + 1, :width] += jnp.sum(grad_scan * conv_out, axis=0, keepdims=True)
    sums_ref[row_at + 1 : row_at + 2, :LANES] += jnp.sum(grad_step, axis=0, keepdims=True)
    sums_ref[row_at + 2 : row_at + 3, :LANES] += jnp.sum(
        grad_decay * log_decay, axis=0, keepdims=True
    )
    grad_step = grad_step.astype(low)
    out_ref[:, : 2 * states] = grad_shared
    out_ref[:, 2 * states : 2 * states + width] = grad_conv
    out_ref[:, 2 * states + width :] = grad_step
    inner = grad_step.astype(f32) * step_ref[...]
    for at in range(0, places.step - places.shared, LANES):
        raw = raw_ref[:, places.shared + at : places.shared + at + LANES]
        inner = inner + out_ref[:, at : at + LANES].astype(f32) * raw.astype(f32)
    inner_ref[...] = inner


def rope(values, cosine, sine):
    return values * cosine + pltpu.roll(values, values.shape[1] // 2, 1) * sine


def attention_rows(query, key, begin, size, info_ref, row_ref, factor):
    seen = begin + size
    scores = nt(query, key) * factor
    rows = begin + lax.broadcasted_iota(jnp.int32, (size, seen), 0)
    columns = lax.broadcasted_iota(jnp.int32, (size, seen), 1)
    allowed = (rows >= columns) & (info_ref[begin:seen, 0:1] == row_ref[0:1, :seen])
    scores = jnp.where(allowed, scores, MASKED)
    raised = jnp.exp(scores - jnp.max(scores, axis=1, keepdims=True))
    return raised * (1.0 / jnp.sum(raised, axis=1, keepdims=True))


def attention_forward_kernel(
    query_ref, key_ref, value_ref, cosine_ref, sine_ref, info_ref, row_ref, out_ref, *, block
):
    low = jnp.bfloat16
    length, head_dim = query_ref.shape
    factor = 1.0 / math.sqrt(head_dim)
    cosine, sine = cosine_ref[...], sine_ref[...]
    query = rope(query_ref[...].astype(jnp.float32), cosine, sine).astype(low)
    key = rope(key_ref[...].astype(jnp.float32), cosine, sine).astype(low)
    value = value_ref[...]
    for begin in range(0, length, block):
        seen = begin + block
        probs = attention_rows(
            query[begin:seen], key[:seen], begin, block, info_ref, row_ref, factor
        )
        out_ref[begin:seen, :] = nn(probs.astype(low), value[:seen]).astype(low)


def attention_backward_kernel(
    raw_ref, cosine_ref, sine_ref, info_ref, row_ref, combined_ref, grad_ref,
    out_ref, inner_ref, key_total, value_total, *, block, places
):
    low = jnp.bfloat16
    length, head_dim = cosine_ref.shape
    channels = combined_ref.shape[1]
    factor = 1.0 / math.sqrt(head_dim)
    cosine, sine = cosine_ref[...], sine_ref[...]
    query = rope(raw_ref[:, : places.key].astype(jnp.float32), cosine, sine).astype(low)
    key = rope(raw_ref[:, places.key : places.gate].astype(jnp.float32), cosine, sine).astype(low)
    value = raw_ref[:, places.value : places.shared]
    key_total[...] = jnp.zeros_like(key_total)
    value_total[...] = jnp.zeros_like(value_total)
    for begin in range(0, length, block):
        seen = begin + block
        probs = attention_rows(
            query[begin:seen], key[:seen], begin, block, info_ref, row_ref, factor
        )
        grad_out = grad_ref[begin:seen, channels:]
        gate = raw_ref[begin:seen, places.gate : places.value].astype(jnp.float32)
        sig = sigmoid_of(gate)
        out_ref[begin:seen, places.gate : places.value] = (
            grad_ref[begin:seen, :channels].astype(jnp.float32)
            * combined_ref[begin:seen, :].astype(jnp.float32)
            * (sig * (1.0 + gate * (1.0 - sig)))
        ).astype(low)
        grad_probs = nt(grad_out, value[:seen])
        inner = jnp.sum(probs * grad_probs, axis=1, keepdims=True)
        grad_scores = (probs * (grad_probs - inner)).astype(low)
        grad_query = nn(grad_scores, key[:seen]) * factor
        out_ref[begin:seen, : places.key] = rope(
            grad_query, cosine[begin:seen], -sine[begin:seen]
        ).astype(low)
        key_total[:seen, :] += tn(grad_scores, query[begin:seen])
        value_total[:seen, :] += tn(probs.astype(low), grad_out)
    out_ref[:, places.key : places.gate] = rope(key_total[...] * factor, cosine, -sine).astype(low)
    out_ref[:, places.value :] = value_total[...].astype(low)
    inner = jnp.zeros(inner_ref.shape, jnp.float32)
    for at in range(0, places.shared, LANES):
        span = slice(at, at + LANES)
        inner = inner + out_ref[:, span].astype(jnp.float32) * raw_ref[:, span].astype(jnp.float32)
    inner_ref[...] = inner


BRIEF = pl.CostEstimate(flops=1, bytes_accessed=1, transcendentals=0)


def whole(shape):
    return pl.BlockSpec(shape, lambda i: (0,) * len(shape))


def limits(megabytes):
    return pltpu.CompilerParams(vmem_limit_bytes=megabytes * 1024 * 1024)


def column_block(rows, width, at):
    return pl.BlockSpec((rows, width), lambda i: (0, at // width))


def attention_forward(raw, places, cosine, sine, info, row):
    length, width = cosine.shape
    return pl.pallas_call(
        partial(attention_forward_kernel, block=256),
        grid=(1,),
        in_specs=[
            column_block(length, width, places.query),
            column_block(length, width, places.key),
            column_block(length, width, places.value),
            whole(cosine.shape), whole(sine.shape), whole(info.shape), whole(row.shape),
        ],
        out_specs=whole((length, width)),
        out_shape=jax.ShapeDtypeStruct((length, width), jnp.bfloat16),
        compiler_params=limits(48),
        cost_estimate=BRIEF,
        name="attention_forward",
    )(raw, raw, raw, cosine, sine, info, row)


def attention_backward(raw, places, cosine, sine, info, row, combined, grad_mixed):
    length, width = cosine.shape
    return pl.pallas_call(
        partial(attention_backward_kernel, block=256, places=places),
        grid=(1,),
        in_specs=[
            column_block(length, places.shared, 0),
            whole(cosine.shape), whole(sine.shape), whole(info.shape), whole(row.shape),
            whole(combined.shape), whole(grad_mixed.shape),
        ],
        out_specs=[whole((length, places.shared)), whole((length, LANES))],
        out_shape=[
            jax.ShapeDtypeStruct((length, places.shared), jnp.bfloat16),
            jax.ShapeDtypeStruct((length, LANES), jnp.float32),
        ],
        scratch_shapes=[pltpu.VMEM((length, width), jnp.float32)] * 2,
        compiler_params=limits(48),
        cost_estimate=BRIEF,
        name="attention_backward",
    )(raw, cosine, sine, info, row, combined, grad_mixed)


def mamba_forward(raw, places, step_raw, info, row, params, attended, head_width):
    length = raw.shape[0]
    width = places.step - places.conv
    states = (places.conv - places.shared) // 2
    head_dim = attended.shape[1]
    chunks = length // CHUNK

    def block(columns):
        return pl.BlockSpec((CHUNK, columns), lambda i: (i, 0))

    return pl.pallas_call(
        partial(mamba_forward_kernel, head_width=head_width, places=places),
        grid=(chunks,),
        in_specs=[
            block(places.step),
            block(LANES), block(LANES), pl.BlockSpec((8, CHUNK), lambda i: (0, i)),
            *[whole(p.shape) for p in params],
            block(head_dim),
        ],
        out_specs=[
            block(width + head_dim), block(width),
            pl.BlockSpec((None, states, width), lambda i: (i, 0, 0)),
        ],
        out_shape=[
            jax.ShapeDtypeStruct((length, width + head_dim), jnp.bfloat16),
            jax.ShapeDtypeStruct((length, width), jnp.bfloat16),
            jax.ShapeDtypeStruct((chunks, states, width), jnp.bfloat16),
        ],
        scratch_shapes=[
            pltpu.VMEM((states, width), jnp.float32),
            pltpu.VMEM((TAIL + CHUNK, width + 2 * states), jnp.float32),
        ],
        compiler_params=limits(48),
        cost_estimate=BRIEF,
        name="mamba_forward",
    )(raw, step_raw, info, row, *params, attended)


def mamba_backward(raw, places, step_raw, info, row, params, states, grad_mixed, head_width):
    length = raw.shape[0]
    width = places.step - places.conv
    shared = places.conv - places.shared
    chunks = length // CHUNK
    total = places.step + LANES - places.shared
    tail = 16

    def block(columns):
        return pl.BlockSpec((CHUNK, columns), lambda i: (chunks - 1 - i, 0))

    return pl.pallas_call(
        partial(mamba_backward_kernel, head_width=head_width, places=places),
        grid=(chunks,),
        in_specs=[
            block(places.step),
            pl.BlockSpec(
                (tail, places.step),
                lambda i: (jnp.maximum((chunks - 1 - i) * (CHUNK // tail) - 1, 0), 0),
            ),
            block(LANES), block(LANES),
            pl.BlockSpec((8, CHUNK), lambda i: (0, chunks - 1 - i)),
            *[whole(p.shape) for p in params],
            pl.BlockSpec((None, shared // 2, width), lambda i: (chunks - 1 - i, 0, 0)),
            block(grad_mixed.shape[1]),
        ],
        out_specs=[block(total), block(LANES), whole((16, shared))],
        out_shape=[
            jax.ShapeDtypeStruct((length, total), jnp.bfloat16),
            jax.ShapeDtypeStruct((length, LANES), jnp.float32),
            jax.ShapeDtypeStruct((16, shared), jnp.float32),
        ],
        scratch_shapes=[
            pltpu.VMEM((shared // 2, width), jnp.float32),
            pltpu.VMEM((TAIL + CHUNK, width + shared), jnp.float32),
            pltpu.VMEM((TAIL + CHUNK, width + shared), jnp.float32),
        ],
        compiler_params=limits(48),
        cost_estimate=BRIEF,
        name="mamba_backward",
    )(raw, raw, step_raw, info, row, *params, states, grad_mixed)


def matmul(former, latter):
    return jnp.dot(former, latter, preferred_element_type=jnp.float32)


def matmul_left(former, latter):
    return lax.dot_general(
        former, latter, (((0,), (0,)), ((), ())), preferred_element_type=jnp.float32
    )


def matmul_right(former, latter):
    return lax.dot_general(
        former, latter, (((1,), (1,)), ((), ())), preferred_element_type=jnp.float32
    )


def col_swap(values, distance):
    count = lax.axis_size("col")
    return lax.ppermute(values, "col", [(i, i ^ distance) for i in range(count)])


def row_swap(values):
    return lax.ppermute(values, "row", [(0, 1), (1, 0)])


def together(*values):
    return lax.optimization_barrier(values)


def after(value, *earlier):
    return lax.optimization_barrier((value, earlier))[0]


def gather_start(block):
    return col_swap(block, 2), row_swap(block), col_swap(block, 1)


def gather_middle(block, first):
    along_x, along_y, _ = first
    half = block.shape[0] // 2
    return col_swap(along_y[:half], 2), row_swap(along_x[half:]), col_swap(along_x, 1), col_swap(along_y, 1)


def gather_end(block, first, middle):
    along_x, along_y, core = first
    top, low, core_x, core_y = middle
    own = [block, along_x, core, core_x]
    other = [along_y, (top, low), core_y, (col_swap(top, 1), col_swap(low, 1))]
    return own, other


def gather_slow_second(first):
    along_x, along_y, _ = first
    return row_swap(along_x), col_swap(along_x, 1), col_swap(along_y, 1)


def gather_slow_end(block, first, second):
    along_x, along_y, core = first
    diagonal, core_x, core_y = second
    return [block, along_x, core, core_x], [along_y, diagonal, core_y, col_swap(diagonal, 1)]


def add_low(former, latter):
    return (former.astype(jnp.float32) + latter.astype(jnp.float32)).astype(jnp.bfloat16)


def other_first(near, far_core):
    other = add_low(near, far_core)
    half = other.shape[1] // 2
    return other, row_swap(other[:, half:]), col_swap(other[1, :half], 2)


def other_second(other, other_got):
    half = other.shape[1] // 2
    return row_swap(add_low(other[0, :half], other_got))


def own_second(near, far_core, low_got):
    own = add_low(near, far_core)
    half = own.shape[1] // 2
    return own, col_swap(own[1, :half], 2), col_swap(add_low(own[1, half:], low_got[1]), 2)


def own_sum(own, low_got, own_got, top_last, low_last):
    half = own.shape[1] // 2
    wide = jnp.float32
    top = own[0, :half].astype(wide) + own_got.astype(wide) + top_last.astype(wide)
    low = own[0, half:].astype(wide) + low_got[0].astype(wide) + low_last.astype(wide)
    return jnp.concatenate([top, low], axis=0)


def scatter_sum_slow(shares):
    (own, own_far), (other, other_far) = shares
    wide = jnp.float32
    other = add_low(other, col_swap(other_far, 1))
    got, near = lax.optimization_barrier((row_swap(other), col_swap(own_far, 1)))
    total = own.astype(wide) + near.astype(wide) + got.astype(wide)
    last = col_swap(total[1].astype(jnp.bfloat16), 2)
    return total[0] + last.astype(wide)


def token_total(own, other):
    total = own + row_swap(other)
    total = total + col_swap(total, 1)
    return total + col_swap(total, 2)


def line_update_kernel(flags_ref, now_ref, got_ref, pair_ref, crossed_ref, later_ref, out_ref, sent_ref):
    @pl.when(flags_ref[1] == 1)
    def _():
        wide = jnp.float32
        out_ref[...] = (now_ref[...].astype(wide) + got_ref[...].astype(wide)).astype(out_ref.dtype)
        sent_ref[...] = (pair_ref[...].astype(wide) + crossed_ref[...].astype(wide)).astype(sent_ref.dtype)

    @pl.when(flags_ref[1] == 0)
    def _():
        sent_ref[...] = later_ref[...]


def line_update(flags, now, got, pair, crossed, later):
    rows, columns = now.shape[1:]

    def middle_block(i, f):
        return (i * f[1], 0, 0)

    def end_block(i, f):
        return (i * (1 - f[1]), 0, 0)

    def every_block(i, f):
        return (i, 0, 0)

    block = (None, rows, columns)
    return pl.pallas_call(
        line_update_kernel,
        grid_spec=pltpu.PrefetchScalarGridSpec(
            num_scalar_prefetch=1,
            grid=(4,),
            in_specs=[pl.BlockSpec(block, middle_block)] * 4 + [pl.BlockSpec(block, end_block)],
            out_specs=[pl.BlockSpec(block, middle_block), pl.BlockSpec(block, every_block)],
        ),
        out_shape=[jax.ShapeDtypeStruct(now.shape, now.dtype)] * 2,
        compiler_params=limits(32),
        cost_estimate=BRIEF,
        name="line_update",
    )(flags, now, got, pair, crossed, later)


class LineSums:
    def __init__(self, flags):
        self.flags = flags
        self.step = 0
        self.now = self.sent = self.pair = None
        self.outward = False
        self.flying = ()
        self.done = []

    def advance(self, later=None):
        if lax.axis_size("dp") != 4:
            if later is not None:
                total = lax.psum(later, "dp")
                self.sent = later
                self.done.append((total, total))
            return
        if self.outward:
            self.done.append((self.sent, self.flying[0]))
        self.outward = self.pair is not None
        sent = self.now if later is None else later
        if self.step == 0:
            self.sent = later
        elif self.now is None:
            self.sent = add_low(self.pair, self.flying[1])
            self.pair = None
            if later is not None:
                self.sent = jnp.where(self.flags[1] == 1, self.sent, later)
        elif self.pair is None:
            self.pair = add_low(self.now, self.flying[0])
            self.sent = sent
        else:
            self.pair, self.sent = line_update(
                self.flags, self.now, self.flying[0], self.pair, self.flying[1], sent
            )
        self.now = later
        self.step += 1
        self._start()

    def finish(self):
        if lax.axis_size("dp") == 4:
            self.done.append((self.sent, self.flying[0]))

    def _start(self):
        move = lax.ppermute(self.sent, "dp", [(0, 1), (3, 2), (1, 0), (2, 3)])
        if self.pair is None:
            self.flying = (move,)
        else:
            self.flying = (move, lax.ppermute(self.pair, "dp", [(1, 2), (2, 1)]))


def chosen(flags, pair):
    return jnp.where(flags[1] == 1, pair[0], pair[1])


def dp_total(values):
    count = lax.axis_size("dp")
    if count & (count - 1):
        return lax.psum(values, "dp")
    distance = 1
    while distance < count:
        values = values + lax.ppermute(values, "dp", [(i, i ^ distance) for i in range(count)])
        distance *= 2
    return values


def far_pair(blocks):
    return col_swap(jnp.stack([blocks[1], blocks[3]]), 2)


def near_pair(blocks, fetched):
    return col_swap(jnp.stack([blocks[2], fetched[1]]), 1)


def block_specs(size, count):
    return [
        pl.BlockSpec((None, size, count), lambda i, *_, at=at: (at, i, 0)) for at in (0, 0, 0, 1)
    ]


def block_values(blocks, fetched, passed):
    return blocks, fetched, passed, passed


def own_first(values, row_index):
    return jnp.where(row_index == 0, values, jnp.flip(values, 0))


def tile_blocks(refs, split):
    tile = pl.program_id(0)
    tiles = pl.num_programs(0)
    refs = list(refs)
    blocks = []
    for halves in split:
        if halves:
            top, low = refs.pop(0), refs.pop(0)
            blocks.append(jnp.where(tile < tiles // 2, top[...], low[...]))
        else:
            blocks.append(refs.pop(0)[...])
    return blocks, refs


def write_normed(blocks, gain_ref, out_ref, factor_ref):
    width = blocks[0].shape[1]
    total = jnp.zeros((blocks[0].shape[0], 1), jnp.float32)
    for block in blocks:
        values = block.astype(jnp.float32)
        total = total + jnp.sum(values * values, axis=1, keepdims=True)
    factor = lax.rsqrt(total * (1.0 / (width * len(blocks))) + EPS)
    for at, block in enumerate(blocks):
        span = slice(at * width, (at + 1) * width)
        out_ref[:, span] = (block.astype(jnp.float32) * factor * gain_ref[:, span]).astype(jnp.bfloat16)
    factor_ref[...] = jnp.broadcast_to(factor, factor_ref.shape)


def project_kernel(*refs, split):
    blocks, refs = tile_blocks(refs, split)
    gain_ref, weight_ref, normed_ref, factor_ref, raw_ref, step_ref = refs
    write_normed(blocks, gain_ref, normed_ref, factor_ref)
    raw = nn(normed_ref[...], weight_ref[...])
    main = raw_ref.shape[1]
    raw_ref[...] = raw[:, :main].astype(jnp.bfloat16)
    step_ref[...] = raw[:, main:]


def ffn_kernel(*refs, split):
    blocks, refs = tile_blocks(refs, split)
    gain_ref, weight_ref, grad_hidden_ref, normed_ref, factor_ref, hidden_ref, grad_ref, inner_ref = refs
    write_normed(blocks, gain_ref, normed_ref, factor_ref)
    low, wide = jnp.bfloat16, jnp.float32
    units = hidden_ref.shape[1]
    gate_up = nn(normed_ref[...], weight_ref[...])
    gate, up = gate_up[:, :units], gate_up[:, units:]
    sig = sigmoid_of(gate)
    silu = gate * sig
    hidden_ref[...] = (silu * up).astype(low)
    grad_hidden = grad_hidden_ref[...]
    grad_gate = (grad_hidden * up * sig * (1.0 + gate * (1.0 - sig))).astype(low)
    grad_up = (grad_hidden * silu).astype(low)
    grad_ref[:, :units] = grad_gate
    grad_ref[:, units:] = grad_up
    products = grad_gate.astype(wide) * gate + grad_up.astype(wide) * up
    inner = products[:, :LANES]
    for at in range(LANES, units, LANES):
        inner = inner + products[:, at : at + LANES]
    inner_ref[...] = inner


def meet_kernel(*refs, split):
    blocks, refs = tile_blocks(refs, split)
    weight_ref, out_ref, product_ref = refs
    width = blocks[0].shape[1]
    for at, block in enumerate(blocks):
        out_ref[:, at * width : (at + 1) * width] = block
    product_ref[...] = nt(out_ref[...], weight_ref[...]).astype(product_ref.dtype)


def tiled_call(kernel, name, pieces, operands, outs, tiles=4):
    tokens, width = pieces[0].shape
    size = tokens // tiles
    split = [isinstance(piece, tuple) for piece in pieces]
    specs, values = [], []
    for piece, halves in zip(pieces, split):
        if halves:
            specs.append(pl.BlockSpec((size, width), lambda i: (jnp.minimum(i, tiles // 2 - 1), 0)))
            specs.append(pl.BlockSpec((size, width), lambda i: (jnp.maximum(i - tiles // 2, 0), 0)))
            values.extend(piece)
        else:
            specs.append(pl.BlockSpec((size, width), lambda i: (i, 0)))
            values.append(piece)
    for value, is_whole in operands:
        specs.append(whole(value.shape) if is_whole else pl.BlockSpec((size, value.shape[1]), lambda i: (i, 0)))
        values.append(value)
    return pl.pallas_call(
        partial(kernel, split=split),
        grid=(tiles,),
        in_specs=specs,
        out_specs=[pl.BlockSpec((size, columns), lambda i: (i, 0)) for columns, _ in outs],
        out_shape=[jax.ShapeDtypeStruct((tokens, columns), dtype) for columns, dtype in outs],
        compiler_params=limits(56),
        cost_estimate=BRIEF,
        name=name,
    )(*values)


def weight_grad_kernel(former_0, former_1, latter_0, latter_1, out_ref):
    total = tn(former_0[...], latter_0[...]) + tn(former_1[...], latter_1[...])
    out_ref[...] = total.astype(out_ref.dtype)


def weight_grad(former, latter, width, at=0, count=None):
    length, depth = former[0].shape
    if count is None:
        left = pl.BlockSpec((length, depth), lambda i: (0, 0))
        right = pl.BlockSpec((length, width), lambda i: (0, i))
        shape = (4, depth, width)
    else:
        left = pl.BlockSpec((length, width), lambda i: (0, i))
        right = pl.BlockSpec((length, count), lambda i: (0, at))
        shape = (4, width, count)
    return pl.pallas_call(
        weight_grad_kernel,
        grid=(4,),
        in_specs=[left, left, right, right],
        out_specs=pl.BlockSpec((None, *shape[1:]), lambda i: (i, 0, 0)),
        out_shape=jax.ShapeDtypeStruct(shape, jnp.bfloat16),
        compiler_params=limits(56),
        cost_estimate=BRIEF,
        name="weight_grad",
    )(*former, *latter)


def spread_kernel(*refs, transposed):
    values, (weight_ref, far_ref, near_ref) = refs[:-3], refs[-3:]
    step = pl.program_id(0)
    total = None
    at = 0
    for ref in values:
        if transposed:
            part = nt(ref[...], weight_ref[:, at : at + ref.shape[1]])
            at += ref.shape[1]
        else:
            part = nn(ref[...], weight_ref[...])
        total = part if total is None else total + part
    total = total.astype(far_ref.dtype)

    @pl.when(step < 2)
    def _():
        far_ref[...] = total

    @pl.when(step >= 2)
    def _():
        near_ref[...] = total


def spread(values, weight, width, transposed):
    tokens = values[0].shape[0]

    def block_of(i):
        return (i + 2) % 4

    if transposed:
        weight_spec = pl.BlockSpec((width, weight.shape[1]), lambda i: (block_of(i), 0))
    else:
        weight_spec = pl.BlockSpec((weight.shape[0], width), lambda i: (0, block_of(i)))
    shape = jax.ShapeDtypeStruct((2, tokens, width), jnp.bfloat16)
    far, near = pl.pallas_call(
        partial(spread_kernel, transposed=transposed),
        grid=(4,),
        in_specs=[whole(v.shape) for v in values] + [weight_spec],
        out_specs=[
            pl.BlockSpec((None, tokens, width), lambda i: (jnp.minimum(i, 1), 0, 0)),
            pl.BlockSpec((None, tokens, width), lambda i: (jnp.maximum(i - 2, 0), 0, 0)),
        ],
        out_shape=[shape, shape],
        compiler_params=limits(56),
        cost_estimate=BRIEF,
        name="spread",
    )(*values, weight)
    return near, far


def cut_first_kernel(flags_ref, query_ref, gate_ref, conv_ref, step_ref, out_ref, *, distances, steps):
    at = 0
    for ref in (query_ref, gate_ref, conv_ref):
        out_ref[:, at : at + ref.shape[1]] = ref[...]
        at += ref.shape[1]
    place = jnp.bitwise_xor(flags_ref[0], distance_at(pl.program_id(0), distances))
    step = pltpu.roll(step_ref[...].astype(jnp.float32), (LANES - place * steps) % LANES, 1)
    lane = lax.broadcasted_iota(jnp.int32, step.shape, 1)
    out_ref[:, at:] = jnp.where(lane < steps, step, 0.0).astype(out_ref.dtype)


def distance_at(i, distances):
    value = distances[0]
    for at, distance in enumerate(distances[1:], 1):
        value = jnp.where(i == at, distance, value)
    return value


def cut_first(flags, query, gate, conv, step, distances, size, at_share):
    depth = gate.shape[0]
    widths = [array.shape[1] // 4 for array in (query, gate, conv)]
    steps = step.shape[1] // 4
    total = sum(widths) + LANES
    step = jnp.pad(step, ((0, 0), (0, LANES - step.shape[1])))

    def row(f):
        return f[3] if at_share else 0

    def column_index(i, f):
        return (row(f), jnp.bitwise_xor(f[0], distance_at(i, distances)))

    return pl.pallas_call(
        partial(cut_first_kernel, distances=distances, steps=steps),
        grid_spec=pltpu.PrefetchScalarGridSpec(
            num_scalar_prefetch=1,
            grid=(len(distances),),
            in_specs=[pl.BlockSpec((size, w), column_index) for w in widths]
            + [pl.BlockSpec((size, LANES), lambda i, f: (row(f), 0))],
            out_specs=pl.BlockSpec((None, size, total), lambda i, f: (i, 0, 0)),
        ),
        out_shape=jax.ShapeDtypeStruct((len(distances), size, total), gate.dtype),
        compiler_params=limits(32),
        cost_estimate=BRIEF,
        name="cut_first",
    )(flags, query, gate, conv, step)


def cut_rest_kernel(flags_ref, gate_ref, up_ref, down_ref, out_ref):
    at = 0
    for ref in (gate_ref, up_ref, down_ref):
        out_ref[:, at : at + ref.shape[1]] = ref[...]
        at += ref.shape[1]


def cut_rest(flags, gate, up, down, distances, size, at_share):
    units = gate.shape[1] // 4
    width = down.shape[1]
    total = 2 * units + width
    parts = units // size

    def column_index(i, f):
        return (f[3] if at_share else 0, jnp.bitwise_xor(f[0], distance_at(i, distances)))

    def row_index(i, f):
        place = jnp.bitwise_xor(f[0], distance_at(i, distances))
        return (place * parts + (f[3] if at_share else 0), 0)

    return pl.pallas_call(
        cut_rest_kernel,
        grid_spec=pltpu.PrefetchScalarGridSpec(
            num_scalar_prefetch=1,
            grid=(len(distances),),
            in_specs=[
                pl.BlockSpec((size, units), column_index),
                pl.BlockSpec((size, units), column_index),
                pl.BlockSpec((size, width), row_index),
            ],
            out_specs=pl.BlockSpec((None, size, total), lambda i, f: (i, 0, 0)),
        ),
        out_shape=jax.ShapeDtypeStruct((len(distances), size, total), gate.dtype),
        compiler_params=limits(32),
        cost_estimate=BRIEF,
        name="cut_rest",
    )(flags, gate, up, down)


def cut_out_kernel(flags_ref, mamba_ref, attn_ref, out_ref):
    out_ref[: mamba_ref.shape[0], :] = mamba_ref[...]
    out_ref[mamba_ref.shape[0] :, :] = attn_ref[...]


def cut_out(flags, mamba, attn):
    channels, query = mamba.shape[0] // 4, attn.shape[0] // 4
    width = mamba.shape[1]

    def row_index(i, f):
        return (jnp.bitwise_xor(f[0], distance_at(i, DISTANCES)), 0)

    return pl.pallas_call(
        cut_out_kernel,
        grid_spec=pltpu.PrefetchScalarGridSpec(
            num_scalar_prefetch=1,
            grid=(4,),
            in_specs=[pl.BlockSpec((channels, width), row_index), pl.BlockSpec((query, width), row_index)],
            out_specs=pl.BlockSpec((None, channels + query, width), lambda i, f: (i, 0, 0)),
        ),
        out_shape=jax.ShapeDtypeStruct((4, channels + query, width), mamba.dtype),
        compiler_params=limits(32),
        cost_estimate=BRIEF,
        name="cut_out",
    )(flags, mamba, attn)


def pack_first_kernel(*refs, places):
    pieces, out_ref = refs[:-1], refs[-1]
    query = places.key - places.query
    channels = places.value - places.gate
    head = places.gate - places.key
    total = out_ref.shape[2]

    def place(at, ref, begin, count, to):
        out_ref[at, :, to : to + count] = ref[:, begin : begin + count]

    for at in range(4):
        alone, common = pieces[2 * at], pieces[2 * at + 1]
        place(at, alone, 0, query, places.query)
        place(at, alone, query, channels, places.gate)
        place(at, alone, query + channels, channels, places.conv)
        place(at, alone, query + 2 * channels, total - places.step, places.step)
        place(at, common, 0, head, places.key)
        place(at, common, head, head, places.value)
        place(at, common, 2 * head, places.conv - places.shared, places.shared)


def pack_first(sources, places, total):
    depth, dtype = sources[0][0].shape[1], sources[0][0].dtype
    tiles = 4
    size = depth // tiles
    out = pl.pallas_call(
        partial(pack_first_kernel, places=places),
        grid=(tiles,),
        in_specs=[
            pl.BlockSpec((None, size, v.shape[2]), lambda i, at=at: (at, i, 0)) for v, at in sources
        ],
        out_specs=pl.BlockSpec((4, size, total), lambda i: (0, i, 0)),
        out_shape=jax.ShapeDtypeStruct((4, depth, total), dtype),
        compiler_params=limits(32),
        cost_estimate=BRIEF,
        name="pack_first",
    )(*[v for v, _ in sources])
    return out.reshape(4 * depth, total)


def pack_rest_kernel(mine_ref, far_ref, near_ref, both_ref, in_ref, down_ref):
    width = down_ref.shape[1] // 4
    inner = in_ref.shape[2]
    for at, ref in enumerate((mine_ref, far_ref, near_ref, both_ref)):
        in_ref[at] = ref[:, :inner]
        down_ref[:, at * width : (at + 1) * width] = ref[:, inner : inner + width]


def pack_rest(sources, width):
    _, depth, total = sources[0][0].shape
    dtype = sources[0][0].dtype
    inner = total - width
    tiles = 4
    size = depth // tiles
    into, down = pl.pallas_call(
        pack_rest_kernel,
        grid=(tiles,),
        in_specs=[
            pl.BlockSpec((None, size, total), lambda i, at=at: (at, i, 0)) for _, at in sources
        ],
        out_specs=[
            pl.BlockSpec((4, size, inner), lambda i: (0, i, 0)),
            pl.BlockSpec((size, 4 * width), lambda i: (i, 0)),
        ],
        out_shape=[
            jax.ShapeDtypeStruct((4, depth, inner), dtype),
            jax.ShapeDtypeStruct((depth, 4 * width), dtype),
        ],
        compiler_params=limits(32),
        cost_estimate=BRIEF,
        name="pack_rest",
    )(*[v for v, _ in sources])
    return into.reshape(4 * depth, inner), down


def collect_early_kernel(*refs, places):
    pieces, (out_ref, common_ref) = refs[:4], refs[4:]
    query = places.key - places.query
    key = jnp.zeros((out_ref.shape[1], places.gate - places.key), jnp.float32)
    value = jnp.zeros((out_ref.shape[1], places.shared - places.value), jnp.float32)
    for at, piece in enumerate(pieces):
        out_ref[at, :, :query] = piece[:, : places.key]
        out_ref[at, :, query:] = piece[:, places.gate : places.value]
        key = key + piece[:, places.key : places.gate].astype(jnp.float32)
        value = value + piece[:, places.value :].astype(jnp.float32)
    common_ref[:, : key.shape[1]] = key.astype(common_ref.dtype)
    common_ref[:, key.shape[1] :] = value.astype(common_ref.dtype)


def collect_early(blocks, fetched, passed, places):
    _, depth, count = blocks.shape
    alone = places.key - places.query + places.value - places.gate
    tiles = 2
    size = depth // tiles
    return pl.pallas_call(
        partial(collect_early_kernel, places=places),
        grid=(tiles,),
        in_specs=block_specs(size, count),
        out_specs=[
            pl.BlockSpec((4, size, alone), lambda i: (0, i, 0)),
            pl.BlockSpec((size, count - alone), lambda i: (i, 0)),
        ],
        out_shape=[
            jax.ShapeDtypeStruct((4, depth, alone), blocks.dtype),
            jax.ShapeDtypeStruct((depth, count - alone), blocks.dtype),
        ],
        compiler_params=limits(32),
        cost_estimate=BRIEF,
        name="collect_early",
    )(*block_values(blocks, fetched, passed))


def collect_late_kernel(*refs, shared, channels):
    pieces, (out_ref, step_ref) = refs[:4], refs[4:]
    quarter = shared // 4
    steps = jnp.zeros(step_ref.shape, jnp.float32)
    for at, piece in enumerate(pieces):
        out_ref[at, :, :channels] = piece[:, shared : shared + channels]
        span = slice(at * quarter, (at + 1) * quarter)
        total = jnp.zeros((out_ref.shape[1], quarter), jnp.float32)
        for other in pieces:
            total = total + other[:, span].astype(jnp.float32)
        out_ref[at, :, channels:] = total.astype(out_ref.dtype)
        step = piece[:, shared + channels :].astype(jnp.float32)
        steps = steps + (pltpu.roll(step, at * 8, 1) if at else step)
    step_ref[...] = steps


def collect_late(blocks, fetched, passed, shared, channels):
    _, depth, count = blocks.shape
    tiles = 2
    size = depth // tiles
    return pl.pallas_call(
        partial(collect_late_kernel, shared=shared, channels=channels),
        grid=(tiles,),
        in_specs=block_specs(size, count),
        out_specs=[
            pl.BlockSpec((4, size, channels + shared // 4), lambda i: (0, i, 0)),
            pl.BlockSpec((size, LANES), lambda i: (i, 0)),
        ],
        out_shape=[
            jax.ShapeDtypeStruct((4, depth, channels + shared // 4), blocks.dtype),
            jax.ShapeDtypeStruct((depth, LANES), jnp.float32),
        ],
        compiler_params=limits(32),
        cost_estimate=BRIEF,
        name="collect_late",
    )(*block_values(blocks, fetched, passed))


def slot_of(flags, place):
    distance = jnp.bitwise_xor(flags[0], place)
    return 2 * jnp.bitwise_and(distance, 1) + distance // 2


def finalize_kernel(flags_ref, total_ref, last_ref, *out_refs, cuts):
    values = jnp.where(flags_ref[1] == 1, total_ref[...], last_ref[...])
    for (span, columns), out_ref in zip(cuts, out_refs):
        out_ref[...] = values[span, columns].astype(jnp.float32)


def finalize(flags, total, last, block, index, outs):
    return pl.pallas_call(
        partial(finalize_kernel, cuts=[(rows, columns) for _, _, _, rows, columns in outs]),
        grid_spec=pltpu.PrefetchScalarGridSpec(
            num_scalar_prefetch=1,
            grid=(4,),
            in_specs=[pl.BlockSpec(block, index)] * 2,
            out_specs=[pl.BlockSpec(out_block, out_index) for _, out_block, out_index, _, _ in outs],
        ),
        out_shape=[jax.ShapeDtypeStruct(shape, jnp.float32) for shape, _, _, _, _ in outs],
        compiler_params=limits(32),
        cost_estimate=BRIEF,
        name="finalize",
    )(flags, total, last)


def finalize_blocks_kernel(flags_ref, *refs, cuts):
    pieces, out_refs = refs[:4], refs[4:]
    slot = slot_of(flags_ref, pl.program_id(0))
    for at, piece in enumerate(pieces):

        @pl.when(slot == at)
        def _():
            for (rows, columns), out_ref in zip(cuts, out_refs):
                out_ref[...] = piece[rows, columns].astype(jnp.float32)


def finalize_blocks(flags, blocks, fetched, passed, outs):
    _, rows, columns = blocks.shape
    return pl.pallas_call(
        partial(finalize_blocks_kernel, cuts=[(rows, columns) for _, _, _, rows, columns in outs]),
        grid_spec=pltpu.PrefetchScalarGridSpec(
            num_scalar_prefetch=1,
            grid=(4,),
            in_specs=[
                pl.BlockSpec((None, rows, columns), lambda i, f, at=at: (at, 0, 0)) for at in (0, 0, 0, 1)
            ],
            out_specs=[pl.BlockSpec(out_block, out_index) for _, out_block, out_index, _, _ in outs],
        ),
        out_shape=[jax.ShapeDtypeStruct(shape, jnp.float32) for shape, _, _, _, _ in outs],
        compiler_params=limits(32),
        cost_estimate=BRIEF,
        name="finalize_blocks",
    )(flags, *block_values(blocks, fetched, passed))


def meet_gathered_kernel(flags_ref, *refs):
    meet_kernel(*refs, split=[False] * 4)


def meet_gathered(flags, gathered, weight, other, tiles=4):
    _, tokens, width = gathered.shape
    size = tokens // tiles

    def block_at(distance):
        def index(i, f):
            row = jnp.bitwise_xor(f[2], other)
            return (4 * row + jnp.bitwise_xor(f[0], distance), i, 0)

        return pl.BlockSpec((None, size, width), index)

    model, units = weight.shape[1], weight.shape[0]
    return pl.pallas_call(
        meet_gathered_kernel,
        grid_spec=pltpu.PrefetchScalarGridSpec(
            num_scalar_prefetch=1,
            grid=(tiles,),
            in_specs=[block_at(d) for d in DISTANCES] + [pl.BlockSpec(weight.shape, lambda i, f: (0, 0))],
            out_specs=[
                pl.BlockSpec((size, model), lambda i, f: (i, 0)),
                pl.BlockSpec((size, units), lambda i, f: (i, 0)),
            ],
        ),
        out_shape=[
            jax.ShapeDtypeStruct((tokens, model), jnp.bfloat16),
            jax.ShapeDtypeStruct((tokens, units), jnp.float32),
        ],
        compiler_params=limits(56),
        cost_estimate=BRIEF,
        name="meet_gathered",
    )(flags, *[gathered] * 4, weight)


def on_device(
    tokens,
    cotangent,
    segment_ids,
    norm1_gain,
    proj_gate,
    proj_conv,
    proj_step,
    proj_shared,
    proj_query,
    proj_key,
    proj_value,
    conv_weight,
    conv_bias,
    shared_conv,
    shared_bias,
    step_bias,
    decay_log,
    skip_gain,
    mamba_out_proj,
    attn_out_proj,
    norm2_gain,
    ffn_gate,
    ffn_up,
    ffn_down,
):
    low = jnp.bfloat16
    wide = jnp.float32
    me = lax.axis_index("col")
    row_index = lax.axis_index("row")
    length = segment_ids.shape[1]
    width = tokens.shape[1]
    model = width * len(DISTANCES)
    head_dim = proj_key.shape[1]
    channels = proj_gate.shape[1] // 4
    steps = proj_step.shape[1] // 4
    head_width = channels // steps
    units = ffn_gate.shape[1] // 4
    query_width = proj_query.shape[1] // 4
    part = proj_shared.shape[1]
    at_gate = query_width + head_dim
    at_value = at_gate + channels
    at_shared = at_value + head_dim
    at_conv = at_shared + 2 * part
    at_step = at_conv + channels
    places = Places(0, query_width, at_gate, at_value, at_shared, at_conv, at_step)
    line_place = lax.axis_index("dp")
    share = width // lax.axis_size("dp")
    flags = jnp.stack(
        [me, ((line_place == 1) | (line_place == 2)).astype(me.dtype), row_index, line_place]
    ).astype(jnp.int32)
    firsts = (proj_query, proj_gate, proj_conv, proj_step)
    rests = (ffn_gate, ffn_up, ffn_down)

    def along_line(values):
        return lax.all_gather(values, "dp", axis=1, tiled=True)

    shared_twin = row_swap(proj_shared)
    fetched = col_swap(cut_first(flags, *firsts, DISTANCES[1::2], share, True), 2)
    gains = jnp.stack([norm1_gain, norm2_gain])
    gains_far = col_swap(gains, 2)
    block, shared_twin, fetched, gains_far = together(tokens, shared_twin, fetched, gains_far)
    first = gather_start(block)
    far = along_line(fetched)
    common = jnp.concatenate(
        [
            proj_key, proj_value,
            jnp.where(row_index == 0, proj_shared, shared_twin),
            jnp.where(row_index == 0, shared_twin, proj_shared),
        ],
        axis=1,
    )[None]
    common_far = col_swap(common, 2)
    alone = cut_first(flags, *firsts, DISTANCES[::2], width, False)
    segments = own_first(segment_ids, row_index)
    indices = jnp.arange(length, dtype=jnp.int32)
    same = segments[:, :, None] == segments[:, None, :]
    position = jnp.sum(same & (indices[:, None] > indices[None, :]), axis=2).astype(wide)
    remaining = jnp.sum(same & (indices[:, None] < indices[None, :]), axis=2).astype(wide)
    lane = jnp.arange(LANES)
    info = jnp.where(
        lane == 0,
        segments.astype(wide)[..., None],
        jnp.where(lane == 1, position[..., None], remaining[..., None]),
    )
    row_info = jnp.broadcast_to(segments.astype(wide)[:, None, :], (2, 8, length))
    half_dim = head_dim // 2
    frequency = ROPE_BASE ** (-2.0 * jnp.arange(half_dim, dtype=wide) / head_dim)
    angles = position[..., None] * frequency
    cosine, sine = jnp.cos(angles), jnp.sin(angles)
    cosine = jnp.concatenate([cosine, cosine], axis=2)
    sine = jnp.concatenate([-sine, sine], axis=2)
    head_rows = jnp.pad(
        jnp.stack([step_bias, jnp.exp(decay_log)]), ((0, 6), (0, LANES - steps))
    )
    gain1, gain2 = gains[0:1], gains[1:2]
    params = (
        conv_weight, conv_bias[None], shared_conv, shared_bias[None], head_rows,
        jnp.repeat(skip_gain, head_width)[None],
    )

    both = (0, 1)


    first, common_far, alone, info, row_info, cosine, sine, params = together(
        first, common_far, alone, info, row_info, cosine, sine, params
    )
    middle = gather_middle(block, first)
    gains = jnp.concatenate([gains, gains_far], axis=1)
    gains = jnp.concatenate([gains, col_swap(gains, 1)], axis=1)
    out_blocks = cut_out(flags, mamba_out_proj, attn_out_proj)
    middle, gains, out_blocks = together(middle, gains, out_blocks)
    gain1, gain2 = gains[0:1], gains[1:2]
    out_fetched = far_pair(out_blocks)
    near_common = col_swap(jnp.concatenate([common, common_far], axis=0), 1)
    near = col_swap(alone[1:], 1)
    cot_gathered = lax.all_gather(after(cotangent, middle), ("row", "col"), axis=0)
    token_own, token_other = gather_end(block, first, middle)
    rest_sent = cut_rest(flags, *rests, DISTANCES[1::2], share, True)
    rest_kept = cut_rest(flags, *rests, DISTANCES[::2], width, False)
    far, out_fetched, near_common, near, token_other, rest_sent, rest_kept = together(
        far, out_fetched, near_common, near, token_other, rest_sent, rest_kept
    )
    both_far = col_swap(far[1:], 1)
    out_passed = near_pair(out_blocks, out_fetched)
    both_far, out_passed = together(both_far, out_passed)
    weight_first = pack_first(
        [
            (alone, 0), (common, 0), (far, 0), (common_far, 0),
            (near, 0), (near_common, 0), (both_far, 0), (near_common, 1),
        ],
        places, at_step + LANES,
    )
    rest_sent, rest_kept = after((rest_sent, rest_kept), both_far)
    fetched = col_swap(rest_sent, 2)
    rest_near = col_swap(rest_kept[1:], 1)
    weight_out = jnp.concatenate(
        [out_blocks[0], out_fetched[0], out_passed[0], out_passed[1]], axis=1
    )

    both = (0, 1)
    normed1, factor1, raw, step_raw, mixed, combined, states = [[None, None] for _ in range(7)]

    def project(s, pieces):
        normed1[s], factor1[s], raw[s], step_raw[s] = tiled_call(
            project_kernel, "project", pieces, [(gain1, True), (weight_first, True)],
            [(model, low), (LANES, wide), (at_step, low), (LANES, wide)],
        )
        return attention_forward(raw[s], places, cosine[s], sine[s], info[s], row_info[s])

    def mamba(s, attended):
        mixed[s], combined[s], states[s] = mamba_forward(
            raw[s], places, step_raw[s], info[s], row_info[s], params, attended, head_width
        )

    attended = project(1, token_other)
    attended, fetched, rest_near = together(attended, fetched, rest_near)
    rest_far = along_line(fetched)
    mamba(1, attended)
    near, far = spread([mixed[1]], weight_out, width, False)
    far = col_swap(far, 1)
    near, far, token_own = together(near, far, token_own)
    other, low_got, other_got = other_first(near, far)
    attended = project(0, after(token_own, other))
    attended, low_got, other_got = together(attended, low_got, other_got)
    top_last = other_second(other, other_got)
    mamba(0, attended)
    near, far = spread([mixed[0]], weight_out, width, False)
    far = col_swap(far, 1)
    near, far, top_last = together(near, far, top_last)
    own, own_got, low_last = own_second(near, far, low_got)
    own_got, low_last, rest_far = together(own_got, low_last, rest_far)
    hidden1 = tokens.astype(wide) + own_sum(own, low_got, own_got, top_last, low_last)
    block, hidden1, rest_far = together(hidden1.astype(low), hidden1, rest_far)
    first = gather_start(block)
    rest_both = col_swap(rest_far[1:], 1)
    weight_in, weight_down = pack_rest(
        [(rest_kept, 0), (rest_far, 0), (rest_near, 0), (rest_both, 0)], width
    )
    first, weight_in, weight_down, cot_gathered = together(first, weight_in, weight_down, cot_gathered)
    middle = gather_middle(block, first)
    cot, grad_hidden = [None, None], [None, None]
    for s in both:
        cot[s], grad_hidden[s] = meet_gathered(flags, cot_gathered, weight_down, s)
    middle, cot, grad_hidden = together(middle, cot, grad_hidden)
    pieces = gather_end(block, first, middle)
    normed2, factor2, hidden, grad_in, inner = [[None, None] for _ in range(5)]

    def feed_forward(s, pieces):
        normed2[s], factor2[s], hidden[s], grad_in[s], products = tiled_call(
            ffn_kernel, "ffn", pieces, [(gain2, True), (weight_in, True), (grad_hidden[s], False)],
            [(model, low), (LANES, wide), (units, low), (2 * units, low), (LANES, wide)],
        )
        inner[s] = jnp.sum(products, axis=1).reshape(length // LANES, LANES)

    def piece_index(i, f):
        return (slot_of(f, i), 0, 0)

    def row_index_map(i, f):
        return (i, 0)

    def column_index_map(i, f):
        return (0, i)

    every = slice(None)
    line = LineSums(flags)
    feed_forward(1, pieces[1])
    near, far = spread([grad_in[1]], weight_in, width, True)
    far = col_swap(far, 1)
    feed_forward(0, after(pieces[0], near))
    near, far, hidden, inner, grad_in = together(near, far, hidden, inner, grad_in)
    other, low_got, other_got = other_first(near, far)
    inner_row = row_swap(inner[1])
    near, far = spread([after(grad_in[0], other)], weight_in, width, True)
    far = col_swap(far, 1)
    near, far = together(near, far)
    own = add_low(near, far)
    own_got = col_swap(own[1, : length // 2], 2)
    down = weight_grad(after(hidden, own), cot, width)
    line.advance(down)
    gate = weight_grad(after(normed2, down), grad_in, width, 0, units)
    low_got, other_got, own_got, inner_row, gate = together(low_got, other_got, own_got, inner_row, gate)
    top_last = other_second(other, other_got)
    low_last = col_swap(add_low(own[1, length // 2 :], low_got[1]), 2)
    inner = inner[0] + inner_row
    inner = inner + col_swap(inner, 1)
    up = weight_grad(after(normed2, own_got), grad_in, width, 1, units)
    top_last, low_last, inner, up, line.flying = together(top_last, low_last, inner, up, line.flying)
    line.advance(gate)
    inner = inner + col_swap(inner, 2)
    inner2 = inner.reshape(length, 1)
    grad_normed2 = own_sum(own, low_got, own_got, top_last, low_last)
    own_factor = factor2[0][:, :1]
    back2 = (
        own_factor * norm2_gain * grad_normed2
        - hidden1 * (own_factor * own_factor * inner2 / model)
    )
    grad_gain2 = jnp.sum(grad_normed2 * hidden1 * own_factor, axis=0)
    grad_hidden1 = cotangent.astype(wide) + back2
    block, grad_hidden1, grad_gain2 = together(grad_hidden1.astype(low), grad_hidden1, grad_gain2)
    first = together(*gather_start(block))
    middle = gather_middle(block, first)
    middle, line.flying = together(middle, line.flying)
    line.advance(up)
    pieces = gather_end(block, first, middle)
    mix_grad, grad_mixed = [None, None], [None, None]
    for s in both:
        mix_grad[s], grad_mixed[s] = tiled_call(
            meet_kernel, "meet_mixed", pieces[s], [(weight_out, True)],
            [(model, low), (channels + query_width, low)],
        )
    mix_grad, grad_mixed = together(mix_grad, grad_mixed)
    early, late, sums, products = [[None, None] for _ in range(4)]
    for s in both:
        early[s], products[s] = attention_backward(
            raw[s], places, cosine[s], sine[s], info[s], row_info[s], combined[s], grad_mixed[s]
        )
    first = weight_grad(normed1, after(early, line.sent), width, 0, at_shared)
    out = weight_grad(mixed, after(mix_grad, first), width)
    out, first, early, mix_grad, grad_mixed, line.flying = together(
        out, first, early, mix_grad, grad_mixed, line.flying
    )
    line.advance(out)
    first_far = far_pair(first)

    def mamba_step(s, *earlier):
        late[s], more, sums[s] = mamba_backward(
            raw[s], places, step_raw[s], info[s], row_info[s], params, states[s],
            after(grad_mixed[s], *earlier), head_width,
        )
        inner[s] = jnp.sum(products[s] + more, axis=1).reshape(length // LANES, LANES)

    inner = [None, None]
    mamba_step(1, line.sent)
    late[1], inner[1], first_far, line.flying = together(late[1], inner[1], first_far, line.flying)
    first_near = together(near_pair(first, first_far))[0]
    first, common_sum = collect_early(first, first_far, first_near, places)
    line.advance(first)
    down = chosen(flags, line.done[0])
    down_far = far_pair(down)
    mamba_step(0, late[1], line.sent)
    last = weight_grad(normed1, late, width, 0, late[0].shape[1])
    sums = sums[0] + sums[1]
    sums = jnp.concatenate([sums[:13], grad_gain2[None], jnp.zeros((2, width), wide)], axis=0)
    late, last, inner, sums, down_far, common_sum, line.flying = together(
        late, last, inner, sums, down_far, common_sum, line.flying
    )
    last_far = far_pair(last)
    line.advance()
    rank = jnp.arange(16)[:, None]
    taps = conv_weight.shape[0]
    is_shared = (rank > taps) & (rank < 2 * taps + 2)
    near, far = spread([early[1], after(late[1], line.sent)], weight_first, width, True)
    own_near, own_far = spread([early[0], after(late[0], near)], weight_first, width, True)
    near, far, own_near, own_far, last_far, line.flying = together(
        near, far, own_near, own_far, last_far, line.flying
    )
    last_near, far, own_far = together(near_pair(last, last_far), col_swap(far, 1), col_swap(own_far, 1))
    last, step_sum = collect_late(last, last_far, last_near, 2 * part, channels)
    line.advance(last)
    other, low_got, other_got = other_first(near, far)
    own = add_low(own_near, own_far)
    own_got = col_swap(own[1, : length // 2], 2)
    inner_row, sums_row = row_swap(inner[1]), row_swap(sums)
    low_got, other_got, own_got, inner_row, sums_row = together(low_got, other_got, own_got, inner_row, sums_row)
    top_last = other_second(other, other_got)
    low_last = col_swap(add_low(own[1, length // 2 :], low_got[1]), 2)
    inner = inner[0] + inner_row
    sums = sums + jnp.where(is_shared | (rank >= 13), sums_row, 0.0)
    inner_core, sums_core = col_swap(inner, 1), col_swap(sums, 1)
    output_shares = [spread([after(hidden[s], low_got)], weight_down, width, False) for s in both]
    top_last, low_last, inner_core, sums_core, line.flying, output_shares = together(
        top_last, low_last, inner_core, sums_core, line.flying, output_shares
    )
    line.advance()
    inner = inner + inner_core
    sums = sums + jnp.where(is_shared, sums_core, 0.0)
    inner_far, sums_far = col_swap(inner, 2), col_swap(sums, 2)
    down_near = near_pair(down, down_far)
    gate = chosen(flags, line.done[1])
    gate_far = far_pair(gate)
    inner_far, sums_far, down_near, gate_far = together(inner_far, sums_far, down_near, gate_far)
    inner1 = (inner + inner_far).reshape(length, 1)
    sums = sums + jnp.where(is_shared, sums_far, 0.0)
    grad_normed1 = own_sum(own, low_got, own_got, top_last, low_last)
    own_factor = factor1[0][:, :1]
    own_tokens = tokens.astype(wide)
    back1 = (
        own_factor * norm1_gain * grad_normed1
        - own_tokens * (own_factor * own_factor * inner1 / model)
    )
    grad_gain1 = jnp.sum(grad_normed1 * own_tokens * own_factor, axis=0)
    tokens_grad = (grad_hidden1 + back1).astype(low)
    gate_near = near_pair(gate, gate_far)
    up = chosen(flags, line.done[2])
    up_far = far_pair(up)
    gain_row = row_swap(grad_gain1[None])
    (d_ffn_down,) = finalize_blocks(
        flags, down, down_far, down_near, [(ffn_down.shape, (units, width), row_index_map, every, every)]
    )
    tokens_grad, gate_near, up_far, gain_row, d_ffn_down, line.flying = together(
        tokens_grad, gate_near, up_far, gain_row, d_ffn_down, line.flying
    )
    line.advance()
    up_near = near_pair(up, up_far)
    out = chosen(flags, line.done[3])
    out_far = far_pair(out)
    sums = jnp.concatenate(
        [
            jnp.where(rank == 14, grad_gain1[None] + gain_row, sums),
            jnp.transpose(step_sum)[: 4 * 8],
        ],
        axis=0,
    )
    (d_ffn_gate,) = finalize_blocks(
        flags, gate, gate_far, gate_near,
        [(ffn_gate.shape, (width, units), column_index_map, every, every)],
    )
    total, final = line.done[4]
    alone = query_width + channels
    d_query, d_gate = finalize(
        flags, total, final, (None, width, alone), piece_index,
        [
            (proj_query.shape, (width, query_width), column_index_map, every, slice(0, query_width)),
            (proj_gate.shape, (width, channels), column_index_map, every, slice(query_width, None)),
        ],
    )
    sums = dp_total(sums)
    common_sum = dp_total(common_sum)
    up_near, out_far, sums, common_sum, d_ffn_gate, d_query, d_gate = together(
        up_near, out_far, sums, common_sum, d_ffn_gate, d_query, d_gate
    )
    out_near = near_pair(out, out_far)
    (d_ffn_up,) = finalize_blocks(
        flags, up, up_far, up_near,
        [(ffn_up.shape, (width, units), column_index_map, every, every)],
    )
    d_mamba_out, d_attn_out = finalize_blocks(
        flags, out, out_far, out_near,
        [
            (mamba_out_proj.shape, (channels, width), row_index_map, slice(0, channels), every),
            (attn_out_proj.shape, (query_width, width), row_index_map, slice(channels, None), every),
        ],
    )
    output = (hidden1 + scatter_sum_slow(output_shares)).astype(low)
    line.finish()
    total, final = line.done[5]
    (d_conv,) = finalize(
        flags, total, final, (None, width, channels + part // 2), piece_index,
        [(proj_conv.shape, (width, channels), column_index_map, every, slice(0, channels))],
    )
    shared_sum = jnp.where(flags[1] == 1, total[:, :, channels:], final[:, :, channels:])
    halves = [jnp.concatenate([shared_sum[p], shared_sum[p + 1]], axis=1) for p in (0, 2)]
    kept = jnp.where(row_index == 0, halves[0], halves[1]).astype(wide)
    d_shared = kept + row_swap(jnp.where(row_index == 0, halves[1], halves[0])).astype(wide)
    step_sum = jnp.stack([sums[16 + p * 8 : 16 + p * 8 + steps] for p in (0, 2, 1, 3)])
    d_step = jnp.transpose(
        jnp.concatenate([lax.dynamic_index_in_dim(step_sum, me ^ d, 0, keepdims=False) for d in range(4)])
    )
    d_key = common_sum[:, :head_dim].astype(wide)
    d_value = common_sum[:, head_dim:].astype(wide)
    return (
        output, tokens_grad, sums[14], d_gate, d_conv, d_step, d_shared, d_query, d_key, d_value,
        sums[:taps, :channels], sums[taps, :channels], sums[taps + 1 : 2 * taps + 1],
        sums[2 * taps + 1],
        sums[11, :steps], sums[12, :steps],
        jnp.sum(sums[10, :channels].reshape(steps, head_width), axis=1),
        d_mamba_out, d_attn_out, sums[13], d_ffn_gate, d_ffn_up, d_ffn_down,
    )


def solution(mesh):
    return jax.shard_map(
        on_device,
        mesh=mesh,
        in_specs=(
            P(("dp", "row"), "col"),
            P(("dp", "row"), "col"),
            P("dp", None),
            P("col"),
            P("col", "row"),
            P("col", "row"),
            P("col", "row"),
            P("col", "row"),
            P("col", "row"),
            P("col", "row"),
            P("col", "row"),
            P(None, ("row", "col")),
            P(("row", "col")),
            P(),
            P(),
            P(("row", "col")),
            P(("row", "col")),
            P(("row", "col")),
            P("row", "col"),
            P("row", "col"),
            P("col"),
            P("col", "row"),
            P("col", "row"),
            P("row", "col"),
        ),
        out_specs=(
            P(("dp", "row"), "col"),
            P(("dp", "row"), "col"),
            P("col"),
            P("col", "row"),
            P("col", "row"),
            P("col", "row"),
            P("col", "row"),
            P("col", "row"),
            P("col", "row"),
            P("col", "row"),
            P(None, ("row", "col")),
            P(("row", "col")),
            P(),
            P(),
            P(("row", "col")),
            P(("row", "col")),
            P(("row", "col")),
            P("row", "col"),
            P("row", "col"),
            P("col"),
            P("col", "row"),
            P("col", "row"),
            P("row", "col"),
        ),
        check_vma=False,
    )
```

```python
from functools import partial
import math
from typing import NamedTuple

import jax
import jax.numpy as jnp
from jax import lax
from jax.experimental import pallas as pl
from jax.experimental.pallas import tpu as pltpu
from jax.sharding import PartitionSpec as P

EPS = 1e-05
ROPE_BASE = 100000000000.0
MASKED = -1e30
HIGHEST = lax.Precision.HIGHEST
DISTANCES = (0, 2, 1, 3)
LANES = 128
CHUNK = 128
TAIL = 8


class Places(NamedTuple):
    query: int
    key: int
    gate: int
    value: int
    shared: int
    conv: int
    step: int


def dot_any(former, latter, dims, precision=None):
    return lax.dot_general(
        former, latter, (dims, ((), ())), precision=precision, preferred_element_type=jnp.float32
    )


def nn(former, latter):
    return dot_any(former, latter, ((1,), (0,)))


def nt(former, latter):
    return dot_any(former, latter, ((1,), (1,)))


def tn(former, latter):
    return dot_any(former, latter, ((0,), (0,)))


def exact(former, latter):
    return dot_any(former, latter, ((1,), (0,)), HIGHEST)


def sigmoid_of(values):
    return 1.0 / (1.0 + jnp.exp(-values))


def softplus_of(values):
    return jnp.maximum(values, 0.0) + jnp.log1p(jnp.exp(-jnp.abs(values)))


def head_spread(head_width, width):
    heads = lax.broadcasted_iota(jnp.int32, (LANES, width), 0)
    columns = lax.broadcasted_iota(jnp.int32, (LANES, width), 1)
    return (columns // head_width == heads).astype(jnp.float32)


def head_gather(head_width, width):
    columns = lax.broadcasted_iota(jnp.int32, (width, LANES), 0)
    heads = lax.broadcasted_iota(jnp.int32, (width, LANES), 1)
    return (columns // head_width == heads).astype(jnp.float32)


def causal_conv(ext_ref, columns, weight_ref, bias_ref, position, taps):
    length = ext_ref.shape[0] - TAIL
    running = bias_ref[...] + weight_ref[taps - 1 : taps, :] * ext_ref[TAIL:, columns]
    for offset in range(1, taps):
        earlier = ext_ref[TAIL - offset : TAIL - offset + length, columns]
        running = running + weight_ref[taps - 1 - offset : taps - offset, :] * jnp.where(
            position >= offset, earlier, 0.0
        )
    return running


def chunk_decay(step_in, position, decay_rate):
    length = step_in.shape[0]
    step_size = softplus_of(step_in)
    log_decay = jnp.where(position == 0.0, 0.0, -step_size * decay_rate)
    rows = lax.broadcasted_iota(jnp.int32, (length, length), 0)
    columns = lax.broadcasted_iota(jnp.int32, (length, length), 1)
    causal = rows >= columns
    running = exact(causal.astype(jnp.float32), log_decay)
    return step_size, log_decay, running, jnp.transpose(running), causal


def split_pair(values, head_width):
    lane = lax.broadcasted_iota(jnp.int32, values.shape, 1)
    zero = jnp.zeros_like(values)
    return jnp.concatenate(
        [jnp.where(lane < head_width, values, zero), jnp.where(lane < head_width, zero, values)],
        axis=0,
    )


def mamba_forward_kernel(
    raw_ref, step_ref, info_ref, row_ref, weight_ref, bias_ref,
    shared_weight_ref, shared_bias_ref, head_ref, skip_ref, attended_ref,
    mixed_ref, combined_ref, states_ref,
    state, ext, *, head_width, places
):
    chunk = pl.program_id(0)
    length, width = combined_ref.shape
    gate_columns = slice(places.gate, places.value)
    conv_columns = slice(places.conv, places.step)
    shared_columns = slice(places.shared, places.conv)
    states = (places.conv - places.shared) // 2
    taps = weight_ref.shape[0]
    low = jnp.bfloat16

    @pl.when(chunk == 0)
    def _():
        state[...] = jnp.zeros_like(state)
        ext[...] = jnp.zeros_like(ext)

    ext[:TAIL, :] = ext[length : length + TAIL, :]
    ext[TAIL:, :width] = raw_ref[:, conv_columns].astype(jnp.float32)
    ext[TAIL:, width:] = raw_ref[:, shared_columns].astype(jnp.float32)
    segment = info_ref[:, 0:1]
    position = info_ref[:, 1:2]
    pre = causal_conv(ext, slice(0, width), weight_ref, bias_ref, position, taps)
    conv_out = pre * sigmoid_of(pre)
    pre = causal_conv(
        ext, slice(width, None), shared_weight_ref, shared_bias_ref, position, taps
    )
    shared = (pre * sigmoid_of(pre)).astype(low)
    b_map = shared[:, :states]
    c_map = shared[:, states:]
    step_size, _, running, running_t, causal = chunk_decay(
        step_ref[...] + head_ref[0:1, :], position, head_ref[1:2, :]
    )
    segment_row = row_ref[0:1, :]
    allowed = causal & (segment == segment_row)
    local = lax.broadcasted_iota(jnp.int32, (length, 1), 0).astype(jnp.float32)
    enters = jnp.where(position > local, jnp.exp(running), 0.0)
    last = running[length - 1 : length, :]
    leaves = jnp.where(segment == segment_row[:, length - 1 :], jnp.exp(last - running), 0.0)
    spread = head_spread(head_width, width)
    wide = exact(jnp.concatenate([step_size, enters, leaves], axis=0), spread)
    weighted = conv_out * wide[:length]
    gram = nt(c_map, b_map)
    weighted_low = weighted.astype(low)
    parts = []
    for pair in range(width // (2 * head_width)):
        weights = []
        for head in (2 * pair, 2 * pair + 1):
            gap = jnp.where(allowed, running[:, head : head + 1] - running_t[head : head + 1, :], MASKED)
            weights.append((gram * jnp.exp(gap)).astype(low))
        columns = slice(2 * pair * head_width, 2 * (pair + 1) * head_width)
        parts.append(
            nn(jnp.concatenate(weights, axis=1), split_pair(weighted_low[:, columns], head_width))
        )
    held = state[...]
    held_low = held.astype(low)
    states_ref[...] = held_low
    scanned = jnp.concatenate(parts, axis=1) + nn(c_map, held_low) * wide[length : 2 * length]
    fade = wide[2 * length - 1 : 2 * length]
    state[...] = held * fade + tn(b_map, (weighted * wide[2 * length :]).astype(low))
    combined = scanned + skip_ref[...] * conv_out
    combined_ref[...] = combined.astype(low)
    gate = raw_ref[:, gate_columns].astype(jnp.float32)
    mixed_ref[:, :width] = (combined * (gate * sigmoid_of(gate))).astype(low)
    mixed_ref[:, width:] = attended_ref[...]


def mamba_backward_kernel(
    raw_ref, tail_ref, step_ref, info_ref, row_ref, weight_ref, bias_ref,
    shared_weight_ref, shared_bias_ref, head_ref, skip_ref, states_ref, grad_ref,
    out_ref, inner_ref, sums_ref,
    grad_state, ext, ext_grad, *, head_width, places
):
    count = pl.num_programs(0)
    step = pl.program_id(0)
    length = grad_ref.shape[0]
    width = places.step - places.conv
    states = (places.conv - places.shared) // 2
    taps = weight_ref.shape[0]
    low = jnp.bfloat16
    f32 = jnp.float32
    gate_columns = slice(places.gate, places.value)
    conv_columns = slice(places.conv, places.step)
    shared_columns = slice(places.shared, places.conv)

    @pl.when(step == 0)
    def _():
        grad_state[...] = jnp.zeros_like(grad_state)
        ext_grad[...] = jnp.zeros_like(ext_grad)
        sums_ref[...] = jnp.zeros_like(sums_ref)

    tail_at = tail_ref.shape[0] - TAIL
    ext[:TAIL, :width] = tail_ref[:, conv_columns].astype(f32)[tail_at:]
    ext[:TAIL, width:] = tail_ref[:, shared_columns].astype(f32)[tail_at:]
    ext[TAIL:, :width] = raw_ref[:, conv_columns].astype(f32)
    ext[TAIL:, width:] = raw_ref[:, shared_columns].astype(f32)
    segment = info_ref[:, 0:1]
    position = info_ref[:, 1:2]
    remaining = info_ref[:, 2:3]
    pre = causal_conv(ext, slice(0, width), weight_ref, bias_ref, position, taps)
    sig = sigmoid_of(pre)
    conv_out = pre * sig
    conv_slope = sig * (1.0 + pre * (1.0 - sig))
    pre = causal_conv(
        ext, slice(width, None), shared_weight_ref, shared_bias_ref, position, taps
    )
    sig = sigmoid_of(pre)
    shared = (pre * sig).astype(low)
    shared_slope = sig * (1.0 + pre * (1.0 - sig))
    b_map = shared[:, :states]
    c_map = shared[:, states:]
    step_in = step_ref[...] + head_ref[0:1, :]
    rate = head_ref[1:2, :]
    step_size, log_decay, running, running_t, causal = chunk_decay(step_in, position, rate)
    segment_row = row_ref[0:1, :]
    allowed = causal & (segment == segment_row)
    local = lax.broadcasted_iota(jnp.int32, (length, 1), 0).astype(f32)
    enters = jnp.where(position > local, jnp.exp(running), 0.0)
    last = running[length - 1 : length, :]
    leaves = jnp.where(segment == segment_row[:, length - 1 :], jnp.exp(last - running), 0.0)
    spread = head_spread(head_width, width)
    wide = exact(jnp.concatenate([step_size, enters, leaves], axis=0), spread)
    step_wide = wide[:length]
    enters_wide = wide[length : 2 * length]
    leaves_wide = wide[2 * length :]
    fade = wide[2 * length - 1 : 2 * length]
    weighted = conv_out * step_wide

    gate = raw_ref[:, gate_columns].astype(f32)
    sig = sigmoid_of(gate)
    grad_scan = grad_ref[:, :width].astype(f32) * (gate * sig)

    gram = nt(c_map, b_map)
    weighted_low = weighted.astype(low)
    grad_low = grad_scan.astype(low)
    lane = lax.broadcasted_iota(jnp.int32, (length, LANES), 1)
    sub = lax.broadcasted_iota(jnp.int32, (LANES, length), 0)
    grad_gram = jnp.zeros((length, length), f32)
    by_row = jnp.zeros((length, LANES), f32)
    by_column = jnp.zeros((LANES, length), f32)
    parts = []
    for pair in range(width // (2 * head_width)):
        columns = slice(2 * pair * head_width, 2 * (pair + 1) * head_width)
        split_grad = split_pair(grad_low[:, columns], head_width)
        products = nt(split_grad, weighted_low[:, columns])
        weights = []
        for place, head in enumerate((2 * pair, 2 * pair + 1)):
            gap = jnp.where(allowed, running[:, head : head + 1] - running_t[head : head + 1, :], MASKED)
            fading = jnp.exp(gap)
            weight = gram * fading
            product = products[place * length : (place + 1) * length]
            grad_gram = grad_gram + fading * product
            meeting = weight * product
            by_row = jnp.where(lane == head, jnp.sum(meeting, axis=1, keepdims=True), by_row)
            by_column = jnp.where(sub == head, jnp.sum(meeting, axis=0, keepdims=True), by_column)
            weights.append(weight.astype(low))
        parts.append(tn(jnp.concatenate(weights, axis=0), split_grad))
    held = states_ref[...]
    entering = (grad_scan * enters_wide).astype(low)
    leaving = (weighted * leaves_wide).astype(low)
    grad_held = grad_state[...]
    grad_held_low = grad_held.astype(low)
    from_state = nn(b_map, grad_held_low) * leaves_wide
    grad_weighted = jnp.concatenate(parts, axis=1) + from_state
    grad_gram_low = grad_gram.astype(low)
    grad_c = nn(grad_gram_low, b_map) + nt(entering, held)
    grad_b = tn(grad_gram_low, c_map) + nt(leaving, grad_held_low)
    met_in = grad_scan * enters_wide * nn(c_map, held)
    met_out = weighted * from_state
    met_state = fade * jnp.sum(held.astype(f32) * grad_held, axis=0, keepdims=True)
    grad_state[...] = grad_held * fade + tn(c_map, entering)
    grad_conv_out = grad_weighted * step_wide + skip_ref[...] * grad_scan
    gathered = exact(
        jnp.concatenate(
            [met_in, met_out, conv_out * grad_weighted, jnp.broadcast_to(met_state, (TAIL, width))],
            axis=0,
        ),
        head_gather(head_width, width),
    )
    out_rows = gathered[length : 2 * length]
    at_last = jnp.sum(out_rows, axis=0, keepdims=True) + gathered[3 * length : 3 * length + 1]
    grad_running = by_row - jnp.transpose(by_column) + gathered[:length] - out_rows
    grad_running = grad_running + jnp.where(local == length - 1.0, at_last, 0.0)
    rows = lax.broadcasted_iota(jnp.int32, (length, length), 0)
    later = lax.broadcasted_iota(jnp.int32, (length, length), 1) >= rows
    grad_decay = jnp.where(position == 0.0, 0.0, exact(later.astype(f32), grad_running))
    grad_step = (gathered[2 * length : 3 * length] - grad_decay * rate) * sigmoid_of(step_in)

    ext_grad[length : length + TAIL, :] = ext_grad[:TAIL, :]
    ext_grad[:length, :width] = grad_conv_out * conv_slope
    ext_grad[:length, width : width + states] = grad_b * shared_slope[:, :states]
    ext_grad[:length, width + states :] = grad_c * shared_slope[:, states:]

    def conv_back(columns, weights, row_at):
        now = ext_grad[:length, columns]
        running = weights[taps - 1 : taps, :] * now
        wide_columns = slice(0, now.shape[1])
        sums_ref[row_at + taps : row_at + taps + 1, wide_columns] += jnp.sum(now, axis=0, keepdims=True)
        sums_ref[row_at + taps - 1 : row_at + taps, wide_columns] += jnp.sum(
            now * ext[TAIL:, columns], axis=0, keepdims=True
        )
        for offset in range(1, taps):
            at = taps - 1 - offset
            running = running + weights[at : at + 1, :] * jnp.where(
                remaining >= offset, ext_grad[offset : offset + length, columns], 0.0
            )
            earlier = jnp.where(
                position >= offset, ext[TAIL - offset : TAIL - offset + length, columns], 0.0
            )
            sums_ref[row_at + at : row_at + at + 1, wide_columns] += jnp.sum(
                now * earlier, axis=0, keepdims=True
            )
        return running

    grad_conv = conv_back(slice(0, width), weight_ref, 0).astype(low)
    grad_shared = conv_back(slice(width, None), shared_weight_ref, taps + 1).astype(low)
    row_at = 2 * (taps + 1)
    sums_ref[row_at : row_at + 1, :width] += jnp.sum(grad_scan * conv_out, axis=0, keepdims=True)
    sums_ref[row_at + 1 : row_at + 2, :LANES] += jnp.sum(grad_step, axis=0, keepdims=True)
    sums_ref[row_at + 2 : row_at + 3, :LANES] += jnp.sum(
        grad_decay * log_decay, axis=0, keepdims=True
    )
    grad_step = grad_step.astype(low)
    out_ref[:, : 2 * states] = grad_shared
    out_ref[:, 2 * states : 2 * states + width] = grad_conv
    out_ref[:, 2 * states + width :] = grad_step
    inner = grad_step.astype(f32) * step_ref[...]
    for at in range(0, places.step - places.shared, LANES):
        raw = raw_ref[:, places.shared + at : places.shared + at + LANES]
        inner = inner + out_ref[:, at : at + LANES].astype(f32) * raw.astype(f32)
    inner_ref[...] = inner


def rope(values, cosine, sine):
    return values * cosine + pltpu.roll(values, values.shape[1] // 2, 1) * sine


def attention_rows(query, key, begin, size, info_ref, row_ref, factor):
    seen = begin + size
    scores = nt(query, key) * factor
    rows = begin + lax.broadcasted_iota(jnp.int32, (size, seen), 0)
    columns = lax.broadcasted_iota(jnp.int32, (size, seen), 1)
    allowed = (rows >= columns) & (info_ref[begin:seen, 0:1] == row_ref[0:1, :seen])
    scores = jnp.where(allowed, scores, MASKED)
    raised = jnp.exp(scores - jnp.max(scores, axis=1, keepdims=True))
    return raised * (1.0 / jnp.sum(raised, axis=1, keepdims=True))


def attention_forward_kernel(
    query_ref, key_ref, value_ref, cosine_ref, sine_ref, info_ref, row_ref, out_ref, *, block
):
    low = jnp.bfloat16
    length, head_dim = query_ref.shape
    factor = 1.0 / math.sqrt(head_dim)
    cosine, sine = cosine_ref[...], sine_ref[...]
    query = rope(query_ref[...].astype(jnp.float32), cosine, sine).astype(low)
    key = rope(key_ref[...].astype(jnp.float32), cosine, sine).astype(low)
    value = value_ref[...]
    for begin in range(0, length, block):
        seen = begin + block
        probs = attention_rows(
            query[begin:seen], key[:seen], begin, block, info_ref, row_ref, factor
        )
        out_ref[begin:seen, :] = nn(probs.astype(low), value[:seen]).astype(low)


def attention_backward_kernel(
    raw_ref, cosine_ref, sine_ref, info_ref, row_ref, combined_ref, grad_ref,
    out_ref, inner_ref, key_total, value_total, *, block, places
):
    low = jnp.bfloat16
    length, head_dim = cosine_ref.shape
    channels = combined_ref.shape[1]
    factor = 1.0 / math.sqrt(head_dim)
    cosine, sine = cosine_ref[...], sine_ref[...]
    query = rope(raw_ref[:, : places.key].astype(jnp.float32), cosine, sine).astype(low)
    key = rope(raw_ref[:, places.key : places.gate].astype(jnp.float32), cosine, sine).astype(low)
    value = raw_ref[:, places.value : places.shared]
    key_total[...] = jnp.zeros_like(key_total)
    value_total[...] = jnp.zeros_like(value_total)
    for begin in range(0, length, block):
        seen = begin + block
        probs = attention_rows(
            query[begin:seen], key[:seen], begin, block, info_ref, row_ref, factor
        )
        grad_out = grad_ref[begin:seen, channels:]
        gate = raw_ref[begin:seen, places.gate : places.value].astype(jnp.float32)
        sig = sigmoid_of(gate)
        out_ref[begin:seen, places.gate : places.value] = (
            grad_ref[begin:seen, :channels].astype(jnp.float32)
            * combined_ref[begin:seen, :].astype(jnp.float32)
            * (sig * (1.0 + gate * (1.0 - sig)))
        ).astype(low)
        grad_probs = nt(grad_out, value[:seen])
        inner = jnp.sum(probs * grad_probs, axis=1, keepdims=True)
        grad_scores = (probs * (grad_probs - inner)).astype(low)
        grad_query = nn(grad_scores, key[:seen]) * factor
        out_ref[begin:seen, : places.key] = rope(
            grad_query, cosine[begin:seen], -sine[begin:seen]
        ).astype(low)
        key_total[:seen, :] += tn(grad_scores, query[begin:seen])
        value_total[:seen, :] += tn(probs.astype(low), grad_out)
    out_ref[:, places.key : places.gate] = rope(key_total[...] * factor, cosine, -sine).astype(low)
    out_ref[:, places.value :] = value_total[...].astype(low)
    inner = jnp.zeros(inner_ref.shape, jnp.float32)
    for at in range(0, places.shared, LANES):
        span = slice(at, at + LANES)
        inner = inner + out_ref[:, span].astype(jnp.float32) * raw_ref[:, span].astype(jnp.float32)
    inner_ref[...] = inner


BRIEF = pl.CostEstimate(flops=1, bytes_accessed=1, transcendentals=0)


def whole(shape):
    return pl.BlockSpec(shape, lambda i: (0,) * len(shape))


def limits(megabytes):
    return pltpu.CompilerParams(vmem_limit_bytes=megabytes * 1024 * 1024)


def column_block(rows, width, at):
    return pl.BlockSpec((rows, width), lambda i: (0, at // width))


def attention_forward(raw, places, cosine, sine, info, row):
    length, width = cosine.shape
    return pl.pallas_call(
        partial(attention_forward_kernel, block=256),
        grid=(1,),
        in_specs=[
            column_block(length, width, places.query),
            column_block(length, width, places.key),
            column_block(length, width, places.value),
            whole(cosine.shape), whole(sine.shape), whole(info.shape), whole(row.shape),
        ],
        out_specs=whole((length, width)),
        out_shape=jax.ShapeDtypeStruct((length, width), jnp.bfloat16),
        compiler_params=limits(48),
        cost_estimate=BRIEF,
        name="attention_forward",
    )(raw, raw, raw, cosine, sine, info, row)


def attention_backward(raw, places, cosine, sine, info, row, combined, grad_mixed):
    length, width = cosine.shape
    return pl.pallas_call(
        partial(attention_backward_kernel, block=256, places=places),
        grid=(1,),
        in_specs=[
            column_block(length, places.shared, 0),
            whole(cosine.shape), whole(sine.shape), whole(info.shape), whole(row.shape),
            whole(combined.shape), whole(grad_mixed.shape),
        ],
        out_specs=[whole((length, places.shared)), whole((length, LANES))],
        out_shape=[
            jax.ShapeDtypeStruct((length, places.shared), jnp.bfloat16),
            jax.ShapeDtypeStruct((length, LANES), jnp.float32),
        ],
        scratch_shapes=[pltpu.VMEM((length, width), jnp.float32)] * 2,
        compiler_params=limits(48),
        cost_estimate=BRIEF,
        name="attention_backward",
    )(raw, cosine, sine, info, row, combined, grad_mixed)


def mamba_forward(raw, places, step_raw, info, row, params, attended, head_width):
    length = raw.shape[0]
    width = places.step - places.conv
    states = (places.conv - places.shared) // 2
    head_dim = attended.shape[1]
    chunks = length // CHUNK

    def block(columns):
        return pl.BlockSpec((CHUNK, columns), lambda i: (i, 0))

    return pl.pallas_call(
        partial(mamba_forward_kernel, head_width=head_width, places=places),
        grid=(chunks,),
        in_specs=[
            block(places.step),
            block(LANES), block(LANES), pl.BlockSpec((8, CHUNK), lambda i: (0, i)),
            *[whole(p.shape) for p in params],
            block(head_dim),
        ],
        out_specs=[
            block(width + head_dim), block(width),
            pl.BlockSpec((None, states, width), lambda i: (i, 0, 0)),
        ],
        out_shape=[
            jax.ShapeDtypeStruct((length, width + head_dim), jnp.bfloat16),
            jax.ShapeDtypeStruct((length, width), jnp.bfloat16),
            jax.ShapeDtypeStruct((chunks, states, width), jnp.bfloat16),
        ],
        scratch_shapes=[
            pltpu.VMEM((states, width), jnp.float32),
            pltpu.VMEM((TAIL + CHUNK, width + 2 * states), jnp.float32),
        ],
        compiler_params=limits(48),
        cost_estimate=BRIEF,
        name="mamba_forward",
    )(raw, step_raw, info, row, *params, attended)


def mamba_backward(raw, places, step_raw, info, row, params, states, grad_mixed, head_width):
    length = raw.shape[0]
    width = places.step - places.conv
    shared = places.conv - places.shared
    chunks = length // CHUNK
    total = places.step + LANES - places.shared
    tail = 16

    def block(columns):
        return pl.BlockSpec((CHUNK, columns), lambda i: (chunks - 1 - i, 0))

    return pl.pallas_call(
        partial(mamba_backward_kernel, head_width=head_width, places=places),
        grid=(chunks,),
        in_specs=[
            block(places.step),
            pl.BlockSpec(
                (tail, places.step),
                lambda i: (jnp.maximum((chunks - 1 - i) * (CHUNK // tail) - 1, 0), 0),
            ),
            block(LANES), block(LANES),
            pl.BlockSpec((8, CHUNK), lambda i: (0, chunks - 1 - i)),
            *[whole(p.shape) for p in params],
            pl.BlockSpec((None, shared // 2, width), lambda i: (chunks - 1 - i, 0, 0)),
            block(grad_mixed.shape[1]),
        ],
        out_specs=[block(total), block(LANES), whole((16, shared))],
        out_shape=[
            jax.ShapeDtypeStruct((length, total), jnp.bfloat16),
            jax.ShapeDtypeStruct((length, LANES), jnp.float32),
            jax.ShapeDtypeStruct((16, shared), jnp.float32),
        ],
        scratch_shapes=[
            pltpu.VMEM((shared // 2, width), jnp.float32),
            pltpu.VMEM((TAIL + CHUNK, width + shared), jnp.float32),
            pltpu.VMEM((TAIL + CHUNK, width + shared), jnp.float32),
        ],
        compiler_params=limits(48),
        cost_estimate=BRIEF,
        name="mamba_backward",
    )(raw, raw, step_raw, info, row, *params, states, grad_mixed)


def matmul(former, latter):
    return jnp.dot(former, latter, preferred_element_type=jnp.float32)


def matmul_left(former, latter):
    return lax.dot_general(
        former, latter, (((0,), (0,)), ((), ())), preferred_element_type=jnp.float32
    )


def matmul_right(former, latter):
    return lax.dot_general(
        former, latter, (((1,), (1,)), ((), ())), preferred_element_type=jnp.float32
    )


def col_swap(values, distance):
    count = lax.axis_size("col")
    return lax.ppermute(values, "col", [(i, i ^ distance) for i in range(count)])


def row_swap(values):
    return lax.ppermute(values, "row", [(0, 1), (1, 0)])


def together(*values):
    return lax.optimization_barrier(values)


def after(value, *earlier):
    return lax.optimization_barrier((value, earlier))[0]


def gather_start(block):
    return col_swap(block, 2), row_swap(block), col_swap(block, 1)


def gather_middle(block, first):
    along_x, along_y, _ = first
    half = block.shape[0] // 2
    return col_swap(along_y[:half], 2), row_swap(along_x[half:]), col_swap(along_x, 1), col_swap(along_y, 1)


def gather_end(block, first, middle):
    along_x, along_y, core = first
    top, low, core_x, core_y = middle
    own = [block, along_x, core, core_x]
    other = [along_y, (top, low), core_y, (col_swap(top, 1), col_swap(low, 1))]
    return own, other


def gather_slow_second(first):
    along_x, along_y, _ = first
    return row_swap(along_x), col_swap(along_x, 1), col_swap(along_y, 1)


def gather_slow_end(block, first, second):
    along_x, along_y, core = first
    diagonal, core_x, core_y = second
    return [block, along_x, core, core_x], [along_y, diagonal, core_y, col_swap(diagonal, 1)]


def add_kernel(former_ref, latter_ref, out_ref):
    total = former_ref[...].astype(jnp.float32) + latter_ref[...].astype(jnp.float32)
    out_ref[...] = total.astype(out_ref.dtype)


def add_low(former, latter):
    shape = former.shape
    tiles = shape[0] if len(shape) == 3 else 2
    block = (1, *shape[1:]) if len(shape) == 3 else (shape[0] // tiles, shape[1])
    spec = pl.BlockSpec(block, lambda i: (i,) + (0,) * (len(shape) - 1))
    return pl.pallas_call(
        add_kernel,
        grid=(tiles,),
        in_specs=[spec, spec],
        out_specs=spec,
        out_shape=jax.ShapeDtypeStruct(shape, jnp.bfloat16),
        compiler_params=limits(32),
        cost_estimate=BRIEF,
        name="add",
    )(former, latter)


def add_three_kernel(first_ref, second_ref, third_ref, out_ref):
    wide = jnp.float32
    total = first_ref[...].astype(wide) + second_ref[...].astype(wide) + third_ref[...].astype(wide)
    out_ref[...] = total.astype(out_ref.dtype)


def add_three(first, second, third, at):
    _, rows, columns = first.shape
    tiles = 2
    spec = pl.BlockSpec((None, rows // tiles, columns), lambda i: (at, i, 0))
    return pl.pallas_call(
        add_three_kernel,
        grid=(tiles,),
        in_specs=[spec] * 3,
        out_specs=pl.BlockSpec((rows // tiles, columns), lambda i: (i, 0)),
        out_shape=jax.ShapeDtypeStruct((rows, columns), jnp.bfloat16),
        compiler_params=limits(32),
        cost_estimate=BRIEF,
        name="add_three",
    )(first, second, third)


def sum_quarters_kernel(base_ref, *refs):
    (*parts, out_ref, low_ref) = refs
    tops, lows = parts[:3], parts[3:]
    wide = jnp.float32

    def write(pieces):
        total = base_ref[...].astype(wide)
        for piece in pieces:
            total = total + piece[...].astype(wide)
        out_ref[...] = total
        low_ref[...] = total.astype(low_ref.dtype)

    @pl.when(pl.program_id(0) == 0)
    def _():
        write(tops)

    @pl.when(pl.program_id(0) == 1)
    def _():
        write(lows)


def sum_quarters(base, own, low_got, own_got, top_last, low_last):
    tokens, width = base.shape
    half = tokens // 2
    row = pl.BlockSpec((half, width), lambda i: (i, 0))
    part = pl.BlockSpec((half, width), lambda i: (0, 0))
    first = pl.BlockSpec((None, half, width), lambda i: (0, 0, 0))
    return pl.pallas_call(
        sum_quarters_kernel,
        grid=(2,),
        in_specs=[row, part, part, part, part, first, part],
        out_specs=[row, row],
        out_shape=[
            jax.ShapeDtypeStruct((tokens, width), jnp.float32),
            jax.ShapeDtypeStruct((tokens, width), jnp.bfloat16),
        ],
        compiler_params=limits(32),
        cost_estimate=BRIEF,
        name="sum_quarters",
    )(base, own[0], own_got, top_last, own[2], low_got, low_last)


def fold_other_kernel(near_ref, far_ref, top_near_ref, top_far_ref, low_ref):
    half = low_ref.shape[0]
    total = (near_ref[...].astype(jnp.float32) + far_ref[...].astype(jnp.float32)).astype(low_ref.dtype)
    low_ref[...] = total[half:]

    @pl.when(pl.program_id(0) == 0)
    def _():
        top_near_ref[...] = total[:half]

    @pl.when(pl.program_id(0) == 1)
    def _():
        top_far_ref[...] = total[:half]


def fold_own_kernel(near_ref, far_ref, top_near_ref, top_far_ref, low_near_ref, low_far_ref):
    half = top_near_ref.shape[0]
    total = (near_ref[...].astype(jnp.float32) + far_ref[...].astype(jnp.float32)).astype(top_near_ref.dtype)

    @pl.when(pl.program_id(0) == 0)
    def _():
        top_near_ref[...] = total[:half]
        low_near_ref[...] = total[half:]

    @pl.when(pl.program_id(0) == 1)
    def _():
        top_far_ref[...] = total[:half]
        low_far_ref[...] = total[half:]


def fold(near, far, is_own):
    _, tokens, width = near.shape
    half = tokens // 2
    share = pl.BlockSpec((None, tokens, width), lambda i: (i, 0, 0))
    quarter = pl.BlockSpec((half, width), lambda i: (0, 0))
    shape = jax.ShapeDtypeStruct((half, width), near.dtype)
    if is_own:
        specs, shapes = [quarter] * 4, [shape] * 4
    else:
        specs = [quarter, quarter, pl.BlockSpec((None, half, width), lambda i: (i, 0, 0))]
        shapes = [shape, shape, jax.ShapeDtypeStruct((2, half, width), near.dtype)]
    return pl.pallas_call(
        fold_own_kernel if is_own else fold_other_kernel,
        grid=(2,),
        in_specs=[share, share],
        out_specs=specs,
        out_shape=shapes,
        compiler_params=limits(32),
        cost_estimate=BRIEF,
        name="fold",
    )(near, far)


def own_sum(own, low_got, own_got, top_last, low_last):
    top_near, _, low_near, _ = own
    wide = jnp.float32
    top = top_near.astype(wide) + own_got.astype(wide) + top_last.astype(wide)
    low = low_near.astype(wide) + low_got[0].astype(wide) + low_last.astype(wide)
    return jnp.concatenate([top, low], axis=0)


def token_total(own, other):
    total = own + row_swap(other)
    total = total + col_swap(total, 1)
    return total + col_swap(total, 2)


def line_update_kernel(flags_ref, now_ref, got_ref, pair_ref, crossed_ref, later_ref, out_ref, sent_ref):
    @pl.when(flags_ref[1] == 1)
    def _():
        wide = jnp.float32
        out_ref[...] = (now_ref[...].astype(wide) + got_ref[...].astype(wide)).astype(out_ref.dtype)
        sent_ref[...] = (pair_ref[...].astype(wide) + crossed_ref[...].astype(wide)).astype(sent_ref.dtype)

    @pl.when(flags_ref[1] == 0)
    def _():
        sent_ref[...] = later_ref[...]


def line_update(flags, now, got, pair, crossed, later):
    rows, columns = now.shape[1:]

    def middle_block(i, f):
        return (i * f[1], 0, 0)

    def end_block(i, f):
        return (i * (1 - f[1]), 0, 0)

    def every_block(i, f):
        return (i, 0, 0)

    block = (None, rows, columns)
    return pl.pallas_call(
        line_update_kernel,
        grid_spec=pltpu.PrefetchScalarGridSpec(
            num_scalar_prefetch=1,
            grid=(4,),
            in_specs=[pl.BlockSpec(block, middle_block)] * 4 + [pl.BlockSpec(block, end_block)],
            out_specs=[pl.BlockSpec(block, middle_block), pl.BlockSpec(block, every_block)],
        ),
        out_shape=[jax.ShapeDtypeStruct(now.shape, now.dtype)] * 2,
        compiler_params=limits(32),
        cost_estimate=BRIEF,
        name="line_update",
    )(flags, now, got, pair, crossed, later)


class LineSums:
    def __init__(self, flags):
        self.flags = flags
        self.step = 0
        self.now = self.sent = self.pair = None
        self.outward = False
        self.flying = ()
        self.done = []

    def advance(self, later=None):
        if lax.axis_size("dp") != 4:
            if later is not None:
                total = lax.psum(later, "dp")
                self.sent = later
                self.done.append((total, total))
            return
        if self.outward:
            self.done.append((self.sent, self.flying[0]))
        self.outward = self.pair is not None
        sent = self.now if later is None else later
        if self.step == 0:
            self.sent = later
        elif self.now is None:
            self.sent = add_low(self.pair, self.flying[1])
            self.pair = None
            if later is not None:
                self.sent = jnp.where(self.flags[1] == 1, self.sent, later)
        elif self.pair is None:
            self.pair = add_low(self.now, self.flying[0])
            self.sent = sent
        else:
            self.pair, self.sent = line_update(
                self.flags, self.now, self.flying[0], self.pair, self.flying[1], sent
            )
        self.now = later
        self.step += 1
        self._start()

    def finish(self):
        if lax.axis_size("dp") == 4:
            self.done.append((self.sent, self.flying[0]))

    def _start(self):
        move = lax.ppermute(self.sent, "dp", [(0, 1), (3, 2), (1, 0), (2, 3)])
        if self.pair is None:
            self.flying = (move,)
        else:
            self.flying = (move, lax.ppermute(self.pair, "dp", [(1, 2), (2, 1)]))


def dp_part(values, distance):
    count = lax.axis_size("dp")
    return lax.ppermute(values, "dp", [(i, i ^ distance) for i in range(count)])


def dp_rest(values):
    distance = 2
    while distance < lax.axis_size("dp"):
        values = values + dp_part(values, distance)
        distance *= 2
    return values


def pick_kernel(*refs, count):
    out_ref = refs[-1]
    for at in range(count):

        @pl.when(pl.program_id(0) == at)
        def _():
            out_ref[...] = refs[at][...]


def pick(sources):
    rows, columns = sources[0][0].shape[1:]
    return pl.pallas_call(
        partial(pick_kernel, count=len(sources)),
        grid=(len(sources),),
        in_specs=[pl.BlockSpec((None, rows, columns), lambda i, at=at: (at, 0, 0)) for _, at in sources],
        out_specs=pl.BlockSpec((None, rows, columns), lambda i: (i, 0, 0)),
        out_shape=jax.ShapeDtypeStruct((len(sources), rows, columns), sources[0][0].dtype),
        compiler_params=limits(32),
        cost_estimate=BRIEF,
        name="pick",
    )(*[array for array, _ in sources])


def pick_at_kernel(flags_ref, in_ref, out_ref):
    out_ref[...] = in_ref[...]


def pick_at(flags, values, distance, tiles=2):
    _, rows, columns = values.shape
    size = rows // tiles
    return pl.pallas_call(
        pick_at_kernel,
        grid_spec=pltpu.PrefetchScalarGridSpec(
            num_scalar_prefetch=1,
            grid=(tiles,),
            in_specs=[
                pl.BlockSpec((None, size, columns), lambda i, f: (jnp.bitwise_xor(f[0], distance), i, 0))
            ],
            out_specs=pl.BlockSpec((size, columns), lambda i, f: (i, 0)),
        ),
        out_shape=jax.ShapeDtypeStruct((rows, columns), values.dtype),
        compiler_params=limits(32),
        cost_estimate=BRIEF,
        name="pick_at",
    )(flags, values)


def choose_kernel(flags_ref, middle_ref, end_ref, out_ref):
    @pl.when(flags_ref[1] == 1)
    def _():
        out_ref[...] = middle_ref[...]

    @pl.when(flags_ref[1] == 0)
    def _():
        out_ref[...] = end_ref[...]


def chosen(flags, pair):
    middle, end = pair
    block = (None, *middle.shape[1:])
    return pl.pallas_call(
        choose_kernel,
        grid_spec=pltpu.PrefetchScalarGridSpec(
            num_scalar_prefetch=1,
            grid=(middle.shape[0],),
            in_specs=[
                pl.BlockSpec(block, lambda i, f: (i * f[1], 0, 0)),
                pl.BlockSpec(block, lambda i, f: (i * (1 - f[1]), 0, 0)),
            ],
            out_specs=pl.BlockSpec(block, lambda i, f: (i, 0, 0)),
        ),
        out_shape=jax.ShapeDtypeStruct(middle.shape, middle.dtype),
        compiler_params=limits(32),
        cost_estimate=BRIEF,
        name="choose",
    )(flags, middle, end)


def pick_chosen_kernel(flags_ref, middle_ref, end_ref, out_ref):
    choose_kernel(flags_ref, middle_ref, end_ref, out_ref)


def pick_chosen(flags, pair, places):
    middle, end = pair
    block = (None, *middle.shape[1:])
    return pl.pallas_call(
        pick_chosen_kernel,
        grid_spec=pltpu.PrefetchScalarGridSpec(
            num_scalar_prefetch=1,
            grid=(len(places),),
            in_specs=[
                pl.BlockSpec(block, lambda i, f: (distance_at(i, places) * f[1], 0, 0)),
                pl.BlockSpec(block, lambda i, f: (distance_at(i, places) * (1 - f[1]), 0, 0)),
            ],
            out_specs=pl.BlockSpec(block, lambda i, f: (i, 0, 0)),
        ),
        out_shape=jax.ShapeDtypeStruct((len(places), *middle.shape[1:]), middle.dtype),
        compiler_params=limits(32),
        cost_estimate=BRIEF,
        name="pick_chosen",
    )(flags, middle, end)


def near_of_sum(flags, pair, fetched):
    kept = pick_chosen(flags, pair, (2,))
    return col_swap(pick([(kept, 0), (fetched, 1)]), 1)


def far_pair(blocks):
    return col_swap(pick([(blocks, 1), (blocks, 3)]), 2)


def near_pair(blocks, fetched):
    return col_swap(pick([(blocks, 2), (fetched, 1)]), 1)


def halves_kernel(flags_ref, in_ref, keep_ref, send_ref):
    part = keep_ref.shape[1]

    @pl.when(flags_ref[2] == 0)
    def _():
        keep_ref[...] = in_ref[:, :part]
        send_ref[...] = in_ref[:, part:]

    @pl.when(flags_ref[2] == 1)
    def _():
        keep_ref[...] = in_ref[:, part:]
        send_ref[...] = in_ref[:, :part]


def row_halves(flags, blocks):
    count, rows, columns = blocks.shape
    half = pl.BlockSpec((None, rows, columns // 2), lambda i, f: (i, 0, 0))
    return pl.pallas_call(
        halves_kernel,
        grid_spec=pltpu.PrefetchScalarGridSpec(
            num_scalar_prefetch=1,
            grid=(count,),
            in_specs=[pl.BlockSpec((None, rows, columns), lambda i, f: (i, 0, 0))],
            out_specs=[half, half],
        ),
        out_shape=[jax.ShapeDtypeStruct((count, rows, columns // 2), blocks.dtype)] * 2,
        compiler_params=limits(32),
        cost_estimate=BRIEF,
        name="row_halves",
    )(flags, blocks)


def pack_out_kernel(mine_ref, far_ref, near_ref, both_ref, out_ref):
    width = mine_ref.shape[1]
    for at, ref in enumerate((mine_ref, far_ref, near_ref, both_ref)):
        out_ref[:, at * width : (at + 1) * width] = ref[...]


def pack_out(blocks, fetched, passed):
    _, depth, width = blocks.shape
    tiles = 2
    return pl.pallas_call(
        pack_out_kernel,
        grid=(tiles,),
        in_specs=block_specs(depth // tiles, width),
        out_specs=pl.BlockSpec((depth // tiles, 4 * width), lambda i: (i, 0)),
        out_shape=jax.ShapeDtypeStruct((depth, 4 * width), blocks.dtype),
        compiler_params=limits(32),
        cost_estimate=BRIEF,
        name="pack_out",
    )(*block_values(blocks, fetched, passed))


def block_specs(size, count):
    return [
        pl.BlockSpec((None, size, count), lambda i, *_, at=at: (at, i, 0)) for at in (0, 0, 0, 1)
    ]


def block_values(blocks, fetched, passed):
    return blocks, fetched, passed, passed


def own_first(values, row_index):
    return jnp.where(row_index == 0, values, jnp.flip(values, 0))


def tile_blocks(refs, split):
    tile = pl.program_id(0)
    tiles = pl.num_programs(0)
    refs = list(refs)
    blocks = []
    for halves in split:
        if halves:
            top, low = refs.pop(0), refs.pop(0)
            blocks.append(jnp.where(tile < tiles // 2, top[...], low[...]))
        else:
            blocks.append(refs.pop(0)[...])
    return blocks, refs


def write_normed(blocks, gain_ref, out_ref, factor_ref):
    width = blocks[0].shape[1]
    total = jnp.zeros((blocks[0].shape[0], 1), jnp.float32)
    for block in blocks:
        values = block.astype(jnp.float32)
        total = total + jnp.sum(values * values, axis=1, keepdims=True)
    factor = lax.rsqrt(total * (1.0 / (width * len(blocks))) + EPS)
    for at, block in enumerate(blocks):
        span = slice(at * width, (at + 1) * width)
        out_ref[:, span] = (block.astype(jnp.float32) * factor * gain_ref[:, span]).astype(jnp.bfloat16)
    factor_ref[...] = jnp.broadcast_to(factor, factor_ref.shape)


def project_kernel(*refs, split):
    blocks, refs = tile_blocks(refs, split)
    gain_ref, weight_ref, normed_ref, factor_ref, raw_ref, step_ref = refs
    write_normed(blocks, gain_ref, normed_ref, factor_ref)
    raw = nn(normed_ref[...], weight_ref[...])
    main = raw_ref.shape[1]
    raw_ref[...] = raw[:, :main].astype(jnp.bfloat16)
    step_ref[...] = raw[:, main:]


def ffn_kernel(*refs, split):
    blocks, refs = tile_blocks(refs, split)
    gain_ref, weight_ref, grad_hidden_ref, normed_ref, factor_ref, hidden_ref, grad_ref, inner_ref = refs
    write_normed(blocks, gain_ref, normed_ref, factor_ref)
    low, wide = jnp.bfloat16, jnp.float32
    units = hidden_ref.shape[1]
    gate_up = nn(normed_ref[...], weight_ref[...])
    gate, up = gate_up[:, :units], gate_up[:, units:]
    sig = sigmoid_of(gate)
    silu = gate * sig
    hidden_ref[...] = (silu * up).astype(low)
    grad_hidden = grad_hidden_ref[...]
    grad_gate = (grad_hidden * up * sig * (1.0 + gate * (1.0 - sig))).astype(low)
    grad_up = (grad_hidden * silu).astype(low)
    grad_ref[:, :units] = grad_gate
    grad_ref[:, units:] = grad_up
    products = grad_gate.astype(wide) * gate + grad_up.astype(wide) * up
    inner = products[:, :LANES]
    for at in range(LANES, units, LANES):
        inner = inner + products[:, at : at + LANES]
    inner_ref[...] = inner


def meet_kernel(*refs, split):
    blocks, refs = tile_blocks(refs, split)
    weight_ref, out_ref, product_ref = refs
    width = blocks[0].shape[1]
    for at, block in enumerate(blocks):
        out_ref[:, at * width : (at + 1) * width] = block
    product_ref[...] = nt(out_ref[...], weight_ref[...]).astype(product_ref.dtype)


def tiled_call(kernel, name, pieces, operands, outs, tiles=4):
    tokens, width = pieces[0].shape
    size = tokens // tiles
    split = [isinstance(piece, tuple) for piece in pieces]
    specs, values = [], []
    for piece, halves in zip(pieces, split):
        if halves:
            specs.append(pl.BlockSpec((size, width), lambda i: (jnp.minimum(i, tiles // 2 - 1), 0)))
            specs.append(pl.BlockSpec((size, width), lambda i: (jnp.maximum(i - tiles // 2, 0), 0)))
            values.extend(piece)
        else:
            specs.append(pl.BlockSpec((size, width), lambda i: (i, 0)))
            values.append(piece)
    for value, is_whole in operands:
        specs.append(whole(value.shape) if is_whole else pl.BlockSpec((size, value.shape[1]), lambda i: (i, 0)))
        values.append(value)
    return pl.pallas_call(
        partial(kernel, split=split),
        grid=(tiles,),
        in_specs=specs,
        out_specs=[pl.BlockSpec((size, columns), lambda i: (i, 0)) for columns, _ in outs],
        out_shape=[jax.ShapeDtypeStruct((tokens, columns), dtype) for columns, dtype in outs],
        compiler_params=limits(56),
        cost_estimate=BRIEF,
        name=name,
    )(*values)


def weight_grad_kernel(former_0, former_1, latter_0, latter_1, *out_refs):
    total = tn(former_0[...], latter_0[...]) + tn(former_1[...], latter_1[...])
    at = 0
    for out_ref in out_refs:
        out_ref[...] = total[:, at : at + out_ref.shape[1]].astype(out_ref.dtype)
        at += out_ref.shape[1]


def weight_grad(former, latter, width, at=0, counts=None):
    length, depth = former[0].shape
    if counts is None:
        left = pl.BlockSpec((length, depth), lambda i: (0, 0))
        right = pl.BlockSpec((length, width), lambda i: (0, i))
        shapes = [(4, depth, width)]
    else:
        left = pl.BlockSpec((length, width), lambda i: (0, i))
        right = pl.BlockSpec((length, sum(counts)), lambda i: (0, at))
        shapes = [(4, width, count) for count in counts]
    out = pl.pallas_call(
        weight_grad_kernel,
        grid=(4,),
        in_specs=[left, left, right, right],
        out_specs=[pl.BlockSpec((None, *shape[1:]), lambda i: (i, 0, 0)) for shape in shapes],
        out_shape=[jax.ShapeDtypeStruct(shape, jnp.bfloat16) for shape in shapes],
        compiler_params=limits(56),
        cost_estimate=BRIEF,
        name="weight_grad",
    )(*former, *latter)
    return out[0] if len(out) == 1 else out


def spread_kernel(*refs, transposed):
    values, (weight_ref, far_ref, near_ref) = refs[:-3], refs[-3:]
    step = pl.program_id(0)
    total = None
    at = 0
    for ref in values:
        if transposed:
            part = nt(ref[...], weight_ref[:, at : at + ref.shape[1]])
            at += ref.shape[1]
        else:
            part = nn(ref[...], weight_ref[...])
        total = part if total is None else total + part
    total = total.astype(far_ref.dtype)

    @pl.when(step < 2)
    def _():
        far_ref[...] = total

    @pl.when(step >= 2)
    def _():
        near_ref[...] = total


def spread(values, weight, width, transposed):
    tokens = values[0].shape[0]

    def block_of(i):
        return (i + 2) % 4

    if transposed:
        weight_spec = pl.BlockSpec((width, weight.shape[1]), lambda i: (block_of(i), 0))
    else:
        weight_spec = pl.BlockSpec((weight.shape[0], width), lambda i: (0, block_of(i)))
    shape = jax.ShapeDtypeStruct((2, tokens, width), jnp.bfloat16)
    far, near = pl.pallas_call(
        partial(spread_kernel, transposed=transposed),
        grid=(4,),
        in_specs=[whole(v.shape) for v in values] + [weight_spec],
        out_specs=[
            pl.BlockSpec((None, tokens, width), lambda i: (jnp.minimum(i, 1), 0, 0)),
            pl.BlockSpec((None, tokens, width), lambda i: (jnp.maximum(i - 2, 0), 0, 0)),
        ],
        out_shape=[shape, shape],
        compiler_params=limits(56),
        cost_estimate=BRIEF,
        name="spread",
    )(*values, weight)
    return near, far


def cut_first_kernel(flags_ref, query_ref, gate_ref, conv_ref, step_ref, out_ref, *, distances, steps):
    at = 0
    for ref in (query_ref, gate_ref, conv_ref):
        out_ref[:, at : at + ref.shape[1]] = ref[...]
        at += ref.shape[1]
    place = jnp.bitwise_xor(flags_ref[0], distance_at(pl.program_id(0), distances))
    step = pltpu.roll(step_ref[...].astype(jnp.float32), (LANES - place * steps) % LANES, 1)
    lane = lax.broadcasted_iota(jnp.int32, step.shape, 1)
    out_ref[:, at:] = jnp.where(lane < steps, step, 0.0).astype(out_ref.dtype)


def distance_at(i, distances):
    value = distances[0]
    for at, distance in enumerate(distances[1:], 1):
        value = jnp.where(i == at, distance, value)
    return value


def cut_first(flags, query, gate, conv, step, distances, size, at_share):
    depth = gate.shape[0]
    widths = [array.shape[1] // 4 for array in (query, gate, conv)]
    steps = step.shape[1] // 4
    total = sum(widths) + LANES
    step = jnp.pad(step, ((0, 0), (0, LANES - step.shape[1])))

    def row(f):
        return f[3] if at_share else 0

    def column_index(i, f):
        return (row(f), jnp.bitwise_xor(f[0], distance_at(i, distances)))

    return pl.pallas_call(
        partial(cut_first_kernel, distances=distances, steps=steps),
        grid_spec=pltpu.PrefetchScalarGridSpec(
            num_scalar_prefetch=1,
            grid=(len(distances),),
            in_specs=[pl.BlockSpec((size, w), column_index) for w in widths]
            + [pl.BlockSpec((size, LANES), lambda i, f: (row(f), 0))],
            out_specs=pl.BlockSpec((None, size, total), lambda i, f: (i, 0, 0)),
        ),
        out_shape=jax.ShapeDtypeStruct((len(distances), size, total), gate.dtype),
        compiler_params=limits(32),
        cost_estimate=BRIEF,
        name="cut_first",
    )(flags, query, gate, conv, step)


def cut_rest_kernel(flags_ref, gate_ref, up_ref, down_ref, out_ref):
    at = 0
    for ref in (gate_ref, up_ref, down_ref):
        out_ref[:, at : at + ref.shape[1]] = ref[...]
        at += ref.shape[1]


def cut_rest(flags, gate, up, down, distances, size, at_share):
    units = gate.shape[1] // 4
    width = down.shape[1]
    total = 2 * units + width
    parts = units // size

    def column_index(i, f):
        return (f[3] if at_share else 0, jnp.bitwise_xor(f[0], distance_at(i, distances)))

    def row_index(i, f):
        place = jnp.bitwise_xor(f[0], distance_at(i, distances))
        return (place * parts + (f[3] if at_share else 0), 0)

    return pl.pallas_call(
        cut_rest_kernel,
        grid_spec=pltpu.PrefetchScalarGridSpec(
            num_scalar_prefetch=1,
            grid=(len(distances),),
            in_specs=[
                pl.BlockSpec((size, units), column_index),
                pl.BlockSpec((size, units), column_index),
                pl.BlockSpec((size, width), row_index),
            ],
            out_specs=pl.BlockSpec((None, size, total), lambda i, f: (i, 0, 0)),
        ),
        out_shape=jax.ShapeDtypeStruct((len(distances), size, total), gate.dtype),
        compiler_params=limits(32),
        cost_estimate=BRIEF,
        name="cut_rest",
    )(flags, gate, up, down)


def cut_out_kernel(flags_ref, mamba_ref, attn_ref, out_ref):
    out_ref[: mamba_ref.shape[0], :] = mamba_ref[...]
    out_ref[mamba_ref.shape[0] :, :] = attn_ref[...]


def cut_out(flags, mamba, attn):
    channels, query = mamba.shape[0] // 4, attn.shape[0] // 4
    width = mamba.shape[1]

    def row_index(i, f):
        return (jnp.bitwise_xor(f[0], distance_at(i, DISTANCES)), 0)

    return pl.pallas_call(
        cut_out_kernel,
        grid_spec=pltpu.PrefetchScalarGridSpec(
            num_scalar_prefetch=1,
            grid=(4,),
            in_specs=[pl.BlockSpec((channels, width), row_index), pl.BlockSpec((query, width), row_index)],
            out_specs=pl.BlockSpec((None, channels + query, width), lambda i, f: (i, 0, 0)),
        ),
        out_shape=jax.ShapeDtypeStruct((4, channels + query, width), mamba.dtype),
        compiler_params=limits(32),
        cost_estimate=BRIEF,
        name="cut_out",
    )(flags, mamba, attn)


def pack_first_kernel(*refs, places, begins):
    pieces, out_ref = refs[:-1], refs[-1]
    query = places.key - places.query
    channels = places.value - places.gate
    head = places.gate - places.key
    total = out_ref.shape[2]

    def place(at, ref, begin, count, to):
        out_ref[at, :, to : to + count] = ref[:, begin : begin + count]

    for at in range(4):
        alone, common = pieces[2 * at], pieces[2 * at + 1]
        begin = begins[2 * at + 1]
        place(at, alone, 0, query, places.query)
        place(at, alone, query, channels, places.gate)
        place(at, alone, query + channels, channels, places.conv)
        place(at, alone, query + 2 * channels, total - places.step, places.step)
        place(at, common, begin, head, places.key)
        place(at, common, begin + head, head, places.value)
        place(at, common, begin + 2 * head, places.conv - places.shared, places.shared)


def pack_first(sources, places, total):
    depth, dtype = sources[0][0].shape[1], sources[0][0].dtype
    tiles = 4
    size = depth // tiles
    out = pl.pallas_call(
        partial(pack_first_kernel, places=places, begins=[begin for _, _, begin in sources]),
        grid=(tiles,),
        in_specs=[
            pl.BlockSpec((None, size, v.shape[2]), lambda i, at=at: (at, i, 0)) for v, at, _ in sources
        ],
        out_specs=pl.BlockSpec((4, size, total), lambda i: (0, i, 0)),
        out_shape=jax.ShapeDtypeStruct((4, depth, total), dtype),
        compiler_params=limits(48),
        cost_estimate=BRIEF,
        name="pack_first",
    )(*[v for v, _, _ in sources])
    return out.reshape(4 * depth, total)


def pack_rest_kernel(mine_ref, far_ref, near_ref, both_ref, in_ref, down_ref):
    width = down_ref.shape[1] // 4
    inner = in_ref.shape[2]
    for at, ref in enumerate((mine_ref, far_ref, near_ref, both_ref)):
        in_ref[at] = ref[:, :inner]
        down_ref[:, at * width : (at + 1) * width] = ref[:, inner : inner + width]


def pack_rest(sources, width):
    _, depth, total = sources[0][0].shape
    dtype = sources[0][0].dtype
    inner = total - width
    tiles = 4
    size = depth // tiles
    into, down = pl.pallas_call(
        pack_rest_kernel,
        grid=(tiles,),
        in_specs=[
            pl.BlockSpec((None, size, total), lambda i, at=at: (at, i, 0)) for _, at in sources
        ],
        out_specs=[
            pl.BlockSpec((4, size, inner), lambda i: (0, i, 0)),
            pl.BlockSpec((size, 4 * width), lambda i: (i, 0)),
        ],
        out_shape=[
            jax.ShapeDtypeStruct((4, depth, inner), dtype),
            jax.ShapeDtypeStruct((depth, 4 * width), dtype),
        ],
        compiler_params=limits(32),
        cost_estimate=BRIEF,
        name="pack_rest",
    )(*[v for v, _ in sources])
    return into.reshape(4 * depth, inner), down


def collect_early_kernel(*refs, places):
    pieces, (out_ref, common_ref) = refs[:4], refs[4:]
    query = places.key - places.query
    key = jnp.zeros((out_ref.shape[1], places.gate - places.key), jnp.float32)
    value = jnp.zeros((out_ref.shape[1], places.shared - places.value), jnp.float32)
    for at, piece in enumerate(pieces):
        out_ref[at, :, :query] = piece[:, : places.key]
        out_ref[at, :, query:] = piece[:, places.gate : places.value]
        key = key + piece[:, places.key : places.gate].astype(jnp.float32)
        value = value + piece[:, places.value :].astype(jnp.float32)
    common_ref[:, : key.shape[1]] = key.astype(common_ref.dtype)
    common_ref[:, key.shape[1] :] = value.astype(common_ref.dtype)


def collect_early(blocks, fetched, passed, places):
    _, depth, count = blocks.shape
    alone = places.key - places.query + places.value - places.gate
    tiles = 2
    size = depth // tiles
    return pl.pallas_call(
        partial(collect_early_kernel, places=places),
        grid=(tiles,),
        in_specs=block_specs(size, count),
        out_specs=[
            pl.BlockSpec((4, size, alone), lambda i: (0, i, 0)),
            pl.BlockSpec((size, count - alone), lambda i: (i, 0)),
        ],
        out_shape=[
            jax.ShapeDtypeStruct((4, depth, alone), blocks.dtype),
            jax.ShapeDtypeStruct((depth, count - alone), blocks.dtype),
        ],
        compiler_params=limits(32),
        cost_estimate=BRIEF,
        name="collect_early",
    )(*block_values(blocks, fetched, passed))


def collect_late_kernel(*refs, channels):
    alone, shared, (common_ref, out_ref, step_ref) = refs[:4], refs[4:8], refs[8:]
    quarter = out_ref.shape[2] - channels
    wide = jnp.float32
    steps = jnp.zeros(step_ref.shape, wide)
    total = jnp.zeros((out_ref.shape[1], shared[0].shape[1]), wide)
    for at, piece in enumerate(alone):
        out_ref[at, :, :channels] = piece[:, :channels]
        step = piece[:, channels:].astype(wide)
        steps = steps + (pltpu.roll(step, at * 8, 1) if at else step)
        total = total + shared[at][...].astype(wide)
    step_ref[...] = steps
    for at in range(2):
        span = slice(at * quarter, (at + 1) * quarter)
        out_ref[at, :, channels:] = total[:, span].astype(out_ref.dtype)
        out_ref[at + 2, :, channels:] = common_ref[:, span]


def collect_late(alone, shared, common, channels):
    _, depth, count = alone[0].shape
    part = shared[0].shape[2]
    tiles = 2
    size = depth // tiles
    return pl.pallas_call(
        partial(collect_late_kernel, channels=channels),
        grid=(tiles,),
        in_specs=[
            *block_specs(size, count), *block_specs(size, part),
            pl.BlockSpec((size, common.shape[1]), lambda i: (i, 0)),
        ],
        out_specs=[
            pl.BlockSpec((4, size, channels + part // 2), lambda i: (0, i, 0)),
            pl.BlockSpec((size, LANES), lambda i: (i, 0)),
        ],
        out_shape=[
            jax.ShapeDtypeStruct((4, depth, channels + part // 2), alone[0].dtype),
            jax.ShapeDtypeStruct((depth, LANES), jnp.float32),
        ],
        compiler_params=limits(32),
        cost_estimate=BRIEF,
        name="collect_late",
    )(*block_values(*alone), *block_values(*shared), common)


def slot_of(flags, place):
    distance = jnp.bitwise_xor(flags[0], place)
    return 2 * jnp.bitwise_and(distance, 1) + distance // 2


def finalize_kernel(flags_ref, total_ref, last_ref, *out_refs, cuts):
    values = jnp.where(flags_ref[1] == 1, total_ref[...], last_ref[...])
    for (span, columns), out_ref in zip(cuts, out_refs):
        out_ref[...] = values[span, columns].astype(jnp.float32)


def finalize(flags, total, last, block, index, outs):
    return pl.pallas_call(
        partial(finalize_kernel, cuts=[(rows, columns) for _, _, _, rows, columns in outs]),
        grid_spec=pltpu.PrefetchScalarGridSpec(
            num_scalar_prefetch=1,
            grid=(4,),
            in_specs=[pl.BlockSpec(block, index)] * 2,
            out_specs=[pl.BlockSpec(out_block, out_index) for _, out_block, out_index, _, _ in outs],
        ),
        out_shape=[jax.ShapeDtypeStruct(shape, jnp.float32) for shape, _, _, _, _ in outs],
        compiler_params=limits(32),
        cost_estimate=BRIEF,
        name="finalize",
    )(flags, total, last)


def finalize_blocks_kernel(flags_ref, *refs, cuts):
    pieces, out_refs = refs[:4], refs[4:]
    slot = slot_of(flags_ref, pl.program_id(0))
    for at, piece in enumerate(pieces):

        @pl.when(slot == at)
        def _():
            for (rows, columns), out_ref in zip(cuts, out_refs):
                out_ref[...] = piece[rows, columns].astype(jnp.float32)


def finalize_blocks(flags, blocks, fetched, passed, outs):
    _, rows, columns = blocks.shape
    return pl.pallas_call(
        partial(finalize_blocks_kernel, cuts=[(rows, columns) for _, _, _, rows, columns in outs]),
        grid_spec=pltpu.PrefetchScalarGridSpec(
            num_scalar_prefetch=1,
            grid=(4,),
            in_specs=[
                pl.BlockSpec((None, rows, columns), lambda i, f, at=at: (at, 0, 0)) for at in (0, 0, 0, 1)
            ],
            out_specs=[pl.BlockSpec(out_block, out_index) for _, out_block, out_index, _, _ in outs],
        ),
        out_shape=[jax.ShapeDtypeStruct(shape, jnp.float32) for shape, _, _, _, _ in outs],
        compiler_params=limits(32),
        cost_estimate=BRIEF,
        name="finalize_blocks",
    )(flags, *block_values(blocks, fetched, passed))


def meet_gathered_kernel(flags_ref, *refs):
    meet_kernel(*refs, split=[False] * 4)


def meet_gathered(flags, gathered, weight, tiles=4):
    _, tokens, width = gathered.shape
    size = tokens // tiles

    def block_at(distance):
        return pl.BlockSpec((None, size, width), lambda i, f: (jnp.bitwise_xor(f[0], distance), i, 0))

    model, units = weight.shape[1], weight.shape[0]
    return pl.pallas_call(
        meet_gathered_kernel,
        grid_spec=pltpu.PrefetchScalarGridSpec(
            num_scalar_prefetch=1,
            grid=(tiles,),
            in_specs=[block_at(d) for d in DISTANCES] + [pl.BlockSpec(weight.shape, lambda i, f: (0, 0))],
            out_specs=[
                pl.BlockSpec((size, model), lambda i, f: (i, 0)),
                pl.BlockSpec((size, units), lambda i, f: (i, 0)),
            ],
        ),
        out_shape=[
            jax.ShapeDtypeStruct((tokens, model), jnp.bfloat16),
            jax.ShapeDtypeStruct((tokens, units), jnp.float32),
        ],
        compiler_params=limits(56),
        cost_estimate=BRIEF,
        name="meet_gathered",
    )(flags, *[gathered] * 4, weight)


def on_device(
    tokens,
    cotangent,
    segment_ids,
    norm1_gain,
    proj_gate,
    proj_conv,
    proj_step,
    proj_shared,
    proj_query,
    proj_key,
    proj_value,
    conv_weight,
    conv_bias,
    shared_conv,
    shared_bias,
    step_bias,
    decay_log,
    skip_gain,
    mamba_out_proj,
    attn_out_proj,
    norm2_gain,
    ffn_gate,
    ffn_up,
    ffn_down,
):
    low = jnp.bfloat16
    wide = jnp.float32
    me = lax.axis_index("col")
    row_index = lax.axis_index("row")
    length = segment_ids.shape[1]
    width = tokens.shape[1]
    model = width * len(DISTANCES)
    head_dim = proj_key.shape[1]
    channels = proj_gate.shape[1] // 4
    steps = proj_step.shape[1] // 4
    head_width = channels // steps
    units = ffn_gate.shape[1] // 4
    query_width = proj_query.shape[1] // 4
    part = proj_shared.shape[1]
    at_gate = query_width + head_dim
    at_value = at_gate + channels
    at_shared = at_value + head_dim
    at_conv = at_shared + 2 * part
    at_step = at_conv + channels
    places = Places(0, query_width, at_gate, at_value, at_shared, at_conv, at_step)
    line_place = lax.axis_index("dp")
    share = width // lax.axis_size("dp")
    flags = jnp.stack(
        [me, ((line_place == 1) | (line_place == 2)).astype(me.dtype), row_index, line_place]
    ).astype(jnp.int32)
    firsts = (proj_query, proj_gate, proj_conv, proj_step)
    rests = (ffn_gate, ffn_up, ffn_down)

    def along_line(values):
        return lax.all_gather(values, "dp", axis=1, tiled=True)

    shared_twin = row_swap(proj_shared)
    fetched = col_swap(cut_first(flags, *firsts, DISTANCES[1::2], share, True), 2)
    gains = jnp.stack([norm1_gain, norm2_gain])
    gains_far = col_swap(gains, 2)
    block, shared_twin, fetched, gains_far = together(tokens, shared_twin, fetched, gains_far)
    first = gather_start(block)
    far = along_line(fetched)
    common = jnp.concatenate(
        [
            proj_key, proj_value,
            jnp.where(row_index == 0, proj_shared, shared_twin),
            jnp.where(row_index == 0, shared_twin, proj_shared),
        ],
        axis=1,
    )[None]
    alone = cut_first(flags, *firsts, DISTANCES[::2], width, False)
    lone = alone.shape[2]
    near = col_swap(jnp.concatenate([alone[1:], common], axis=2), 1)
    common_far = col_swap(common, 2)
    segments = own_first(segment_ids, row_index)
    indices = jnp.arange(length, dtype=jnp.int32)
    same = segments[:, :, None] == segments[:, None, :]
    position = jnp.sum(same & (indices[:, None] > indices[None, :]), axis=2).astype(wide)
    remaining = jnp.sum(same & (indices[:, None] < indices[None, :]), axis=2).astype(wide)
    lane = jnp.arange(LANES)
    info = jnp.where(
        lane == 0,
        segments.astype(wide)[..., None],
        jnp.where(lane == 1, position[..., None], remaining[..., None]),
    )
    row_info = jnp.broadcast_to(segments.astype(wide)[:, None, :], (2, 8, length))
    half_dim = head_dim // 2
    frequency = ROPE_BASE ** (-2.0 * jnp.arange(half_dim, dtype=wide) / head_dim)
    angles = position[..., None] * frequency
    cosine, sine = jnp.cos(angles), jnp.sin(angles)
    cosine = jnp.concatenate([cosine, cosine], axis=2)
    sine = jnp.concatenate([-sine, sine], axis=2)
    head_rows = jnp.pad(
        jnp.stack([step_bias, jnp.exp(decay_log)]), ((0, 6), (0, LANES - steps))
    )
    gain1, gain2 = gains[0:1], gains[1:2]
    params = (
        conv_weight, conv_bias[None], shared_conv, shared_bias[None], head_rows,
        jnp.repeat(skip_gain, head_width)[None],
    )

    both = (0, 1)


    first, near, alone, info, row_info, cosine, sine, params = together(
        first, near, alone, info, row_info, cosine, sine, params
    )
    middle = gather_middle(block, first)
    gains = jnp.concatenate([gains, gains_far], axis=1)
    out_blocks = cut_out(flags, mamba_out_proj, attn_out_proj)
    rest_sent = cut_rest(flags, *rests, DISTANCES[1::2], share, True)
    rest_kept = cut_rest(flags, *rests, DISTANCES[::2], width, False)
    middle, far, common_far, out_blocks, rest_sent, rest_kept = together(
        middle, far, common_far, out_blocks, rest_sent, rest_kept
    )
    both_far = col_swap(jnp.concatenate([far[1:], common_far], axis=2), 1)
    out_fetched = far_pair(out_blocks)
    gains = jnp.concatenate([gains, col_swap(gains, 1)], axis=1)
    gain1, gain2 = gains[0:1], gains[1:2]
    token_own, token_other = gather_end(block, first, middle)
    both_far, gain1, gain2, token_other = together(both_far, gain1, gain2, token_other)
    weight_first = pack_first(
        [
            (alone, 0, 0), (common, 0, 0), (far, 0, 0), (common_far, 0, 0),
            (near, 0, 0), (near, 0, lone), (both_far, 0, 0), (both_far, 0, lone),
        ],
        places, at_step + LANES,
    )

    both = (0, 1)
    normed1, factor1, raw, step_raw, mixed, combined, states = [[None, None] for _ in range(7)]

    def project(s, pieces):
        normed1[s], factor1[s], raw[s], step_raw[s] = tiled_call(
            project_kernel, "project", pieces, [(gain1, True), (weight_first, True)],
            [(model, low), (LANES, wide), (at_step, low), (LANES, wide)],
        )
        return attention_forward(raw[s], places, cosine[s], sine[s], info[s], row_info[s])

    def mamba(s, attended):
        mixed[s], combined[s], states[s] = mamba_forward(
            raw[s], places, step_raw[s], info[s], row_info[s], params, attended, head_width
        )

    cot_y = row_swap(after(cotangent, weight_first))
    attended = project(1, token_other)
    attended, out_fetched, cot_y = together(attended, out_fetched, cot_y)
    out_passed = near_pair(out_blocks, out_fetched)
    fetched = col_swap(after(rest_sent, out_fetched), 2)
    mamba(1, attended)
    mixed[1], out_passed, fetched = together(mixed[1], out_passed, fetched)
    cot_col = lax.all_gather(after(cotangent, fetched), "col", axis=0)
    rest_far = along_line(fetched)
    weight_out = pack_out(out_blocks, out_fetched, out_passed)
    near, far = spread([mixed[1]], weight_out, width, False)
    far = col_swap(far, 1)
    near, far, token_own = together(near, far, token_own)
    rest_near = col_swap(rest_kept[1:], 1)
    top_near, top_far, low_send = fold(near, far, False)
    low_got, other_got = row_swap(low_send), col_swap(top_far, 2)
    attended = project(0, after(token_own, low_send))
    attended, low_got, other_got, rest_near = together(attended, low_got, other_got, rest_near)
    top_last = row_swap(add_low(top_near, other_got))
    mamba(0, attended)
    mixed[0], top_last = together(mixed[0], top_last)
    near, far = spread([mixed[0]], weight_out, width, False)
    far = col_swap(far, 1)
    near, far, cot_col = together(near, far, cot_col)
    own = fold(near, far, True)
    low_sent = add_low(own[3], low_got[1])
    own_got, low_last = col_swap(own[1], 2), col_swap(low_sent, 2)
    cot_xy = row_swap(pick_at(flags, after(cot_col, low_sent), 2))
    own_got, low_last, cot_xy = together(own_got, low_last, cot_xy)
    hidden1, block = sum_quarters(tokens, own, low_got, own_got, top_last, low_last)
    block, hidden1, rest_far = together(block, hidden1, rest_far)
    first = gather_start(block)
    rest_both = col_swap(rest_far[1:], 1)
    cot_cores = [col_swap(cot_y, 1), col_swap(cot_xy, 1)]
    weight_in, weight_down = pack_rest(
        [(rest_kept, 0), (rest_far, 0), (rest_near, 0), (rest_both, 0)], width
    )
    first, weight_in, weight_down, cot_cores = together(first, weight_in, weight_down, cot_cores)
    middle = gather_middle(block, first)
    cot, grad_hidden = [None, None], [None, None]
    cot[0], grad_hidden[0] = meet_gathered(flags, cot_col, weight_down)
    cot[1], grad_hidden[1] = tiled_call(
        meet_kernel, "meet_cotangent", [cot_y, cot_xy, *cot_cores], [(weight_down, True)],
        [(model, low), (units, wide)],
    )
    middle, cot, grad_hidden = together(middle, cot, grad_hidden)
    pieces = gather_end(block, first, middle)
    normed2, factor2, hidden, grad_in, inner = [[None, None] for _ in range(5)]

    def feed_forward(s, pieces):
        normed2[s], factor2[s], hidden[s], grad_in[s], products = tiled_call(
            ffn_kernel, "ffn", pieces, [(gain2, True), (weight_in, True), (grad_hidden[s], False)],
            [(model, low), (LANES, wide), (units, low), (2 * units, low), (LANES, wide)],
        )
        inner[s] = jnp.sum(products, axis=1).reshape(length // LANES, LANES)

    def piece_index(i, f):
        return (slot_of(f, i), 0, 0)

    def row_index_map(i, f):
        return (i, 0)

    def column_index_map(i, f):
        return (0, i)

    every = slice(None)
    line = LineSums(flags)
    feed_forward(1, pieces[1])
    near, far = spread([grad_in[1]], weight_in, width, True)
    far = col_swap(far, 1)
    feed_forward(0, after(pieces[0], near))
    near, far, hidden, inner, grad_in = together(near, far, hidden, inner, grad_in)
    top_near, top_far, low_send = fold(near, far, False)
    low_got, other_got = row_swap(low_send), col_swap(top_far, 2)
    inner_row = row_swap(inner[1])
    near, far = spread([after(grad_in[0], low_send)], weight_in, width, True)
    far = col_swap(far, 1)
    near, far = together(near, far)
    own = fold(near, far, True)
    own_got = col_swap(own[1], 2)
    down = weight_grad(after(hidden, own), cot, width)
    low_got, other_got, inner_row, down, own = together(low_got, other_got, inner_row, down, own)
    top_last = row_swap(add_low(top_near, other_got))
    low_last = col_swap(add_low(own[3], low_got[1]), 2)
    inner = inner[0] + inner_row
    inner_core = col_swap(inner, 1)
    line.advance(down)
    gate = weight_grad(after(normed2, line.sent), grad_in, width, 0, [units])
    up = weight_grad(after(normed2, gate), grad_in, width, 1, [units])
    top_last, low_last, own_got, inner_core, up, gate = together(
        top_last, low_last, own_got, inner_core, up, gate
    )
    inner = inner + inner_core
    inner = inner + col_swap(inner, 2)
    inner2 = inner.reshape(length, 1)
    grad_normed2 = own_sum(own, low_got, own_got, top_last, low_last)
    own_factor = factor2[0][:, :1]
    back2 = (
        own_factor * norm2_gain * grad_normed2
        - hidden1 * (own_factor * own_factor * inner2 / model)
    )
    grad_gain2 = jnp.sum(grad_normed2 * hidden1 * own_factor, axis=0)
    grad_hidden1 = cotangent.astype(wide) + back2
    block, grad_hidden1, grad_gain2 = together(grad_hidden1.astype(low), grad_hidden1, grad_gain2)
    first = gather_start(block)
    output_shares = [spread([after(hidden[s], block)], weight_down, width, False) for s in both]
    first, output_shares, line.flying = together(first, output_shares, line.flying)
    line.advance(gate)
    middle = together(*gather_middle(block, first))
    pieces = gather_end(block, first, middle)
    output_far = [col_swap(output_shares[s][1], 1) for s in both]
    mix_grad, grad_mixed = [None, None], [None, None]
    for s in both:
        mix_grad[s], grad_mixed[s] = tiled_call(
            meet_kernel, "meet_mixed", pieces[s], [(weight_out, True)],
            [(model, low), (channels + query_width, low)],
        )
    out = weight_grad(mixed, mix_grad, width)
    early, late, sums, products, inner = [[None, None] for _ in range(5)]

    def mamba_step(s, *earlier):
        late[s], inner[s], sums[s] = mamba_backward(
            raw[s], places, step_raw[s], info[s], row_info[s], params, states[s],
            after(grad_mixed[s], *earlier), head_width,
        )

    for s in both:
        early[s], products[s] = attention_backward(
            raw[s], places, cosine[s], sine[s], info[s], row_info[s], combined[s],
            after(grad_mixed[s], out),
        )
    out, grad_mixed, early, output_far, line.flying = together(out, grad_mixed, early, output_far, line.flying)
    line.advance(up)
    output_other = add_low(output_shares[1][0], output_far[1])
    output_got = row_swap(output_other)
    early = after(early, line.sent, output_other)
    first = weight_grad(normed1, early, width, 0, [at_shared])
    first_far = far_pair(first)
    mamba_step(1, first)
    late[1], output_got, output_near, first_far, line.flying = together(
        late[1], output_got, output_far[0], first_far, line.flying
    )
    line.advance(out)
    first_near = near_pair(first, first_far)
    output_sent = add_three(output_shares[0][0], output_near, output_got, 1)
    output_last = col_swap(output_sent, 2)
    down = line.done[0]
    down_sent = pick_chosen(flags, down, (1, 3))
    down_far = col_swap(down_sent, 2)
    mamba_step(0, line.sent, output_sent, down_sent)
    shared, last = weight_grad(normed1, late, width, 0, [2 * part, channels + LANES])
    shared, last, late, sums, inner, output_last, down_far, first_near, line.flying = together(
        shared, last, late, sums, inner, output_last, down_far, first_near, line.flying
    )
    shared_keep, shared_send = row_halves(flags, shared)
    shared_got = row_swap(shared_send)
    last_far = far_pair(last)
    down_near = near_of_sum(flags, down, down_far)
    first, common_sum = collect_early(first, first_far, first_near, places)
    line.advance(first)
    small_rows = length // width
    inner = [
        jnp.sum(inner[s] + products[s], axis=1).reshape(small_rows, width) for s in both
    ]
    small = jnp.concatenate(
        [(sums[0] + sums[1])[:13], grad_gain2[None], inner[0], inner[1], jnp.zeros((14, width), wide)],
        axis=0,
    )[:24]
    rank = jnp.arange(24)[:, None]
    taps = conv_weight.shape[0]
    is_shared = (rank > taps) & (rank < 2 * taps + 2)
    is_inner = (rank >= 14) & (rank < 14 + small_rows)
    is_gain = rank == 13
    last_far, shared_got, small, down_near = together(last_far, shared_got, small, down_near)
    shared = add_low(shared_keep, shared_got)
    shared_far = far_pair(shared)
    small_got = row_swap(small)
    last_near = near_pair(last, last_far)
    shared_far, last_near, small_got, line.flying = together(shared_far, last_near, small_got, line.flying)
    shared_near = together(near_pair(shared, shared_far))[0]
    last, step_sum = collect_late(
        (last, last_far, last_near), (shared, shared_far, shared_near), common_sum, channels
    )
    line.advance(last)
    small_other = jnp.concatenate(
        [small_got[:14], small_got[14 + small_rows : 14 + 2 * small_rows], small_got[14 + small_rows :]], axis=0
    )[:24]
    late, small, small_other = after((late, small, small_other), line.sent)
    gate, up = line.done[1], line.done[2]
    gate_far = col_swap(pick_chosen(flags, gate, (1, 3)), 2)
    up_far = col_swap(pick_chosen(flags, up, (1, 3)), 2)
    near, far = spread([early[1], late[1]], weight_first, width, True)
    own_near, own_far = spread([early[0], after(late[0], near)], weight_first, width, True)
    small = small + jnp.where(is_shared | is_gain | is_inner, small_other, 0.0)
    near, far, own_near, own_far, small, gate_far, up_far, line.flying = together(
        near, far, own_near, own_far, small, gate_far, up_far, line.flying
    )
    line.advance()
    far, own_far, small = after((far, own_far, small), line.sent)
    far, own_far, small_got = together(col_swap(far, 1), col_swap(own_far, 1), col_swap(small, 1))
    top_near, top_far, low_send = fold(near, far, False)
    low_got, other_got = row_swap(low_send), col_swap(top_far, 2)
    own = fold(own_near, own_far, True)
    own_got = col_swap(own[1], 2)
    small = small + jnp.where(is_shared | is_inner, small_got, 0.0)
    small_got = col_swap(small, 2)
    gate_near = near_of_sum(flags, gate, gate_far)
    up_near = near_of_sum(flags, up, up_far)
    low_got, other_got, own_got, small_got, gate_near, up_near, line.flying = together(
        low_got, other_got, own_got, small_got, gate_near, up_near, line.flying
    )
    line.advance()
    low_got, other_got, small, small_got = after((low_got, other_got, small, small_got), line.sent)
    top_last = row_swap(add_low(top_near, other_got))
    low_last = col_swap(add_low(own[3], low_got[1]), 2)
    out = line.done[3]
    out_far = col_swap(pick_chosen(flags, out, (1, 3)), 2)
    small = small + jnp.where(is_shared | is_inner, small_got, 0.0)
    total, final = line.done[4]
    alone = query_width + channels
    d_query, d_gate = finalize(
        flags, total, final, (None, width, alone), piece_index,
        [
            (proj_query.shape, (width, query_width), column_index_map, every, slice(0, query_width)),
            (proj_gate.shape, (width, channels), column_index_map, every, slice(query_width, None)),
        ],
    )
    (d_ffn_down,) = finalize_blocks(
        flags, pick_chosen(flags, down, (0,)), down_far, down_near,
        [(ffn_down.shape, (units, width), row_index_map, every, every)],
    )
    (d_ffn_gate,) = finalize_blocks(
        flags, pick_chosen(flags, gate, (0,)), gate_far, gate_near,
        [(ffn_gate.shape, (width, units), column_index_map, every, every)],
    )
    (d_ffn_up,) = finalize_blocks(
        flags, pick_chosen(flags, up, (0,)), up_far, up_near,
        [(ffn_up.shape, (width, units), column_index_map, every, every)],
    )
    output = (
        hidden1 + output_shares[0][0][0].astype(wide) + output_near[0].astype(wide)
        + output_got[0].astype(wide) + output_last.astype(wide)
    ).astype(low)
    top_last, low_last, out_far, d_query, d_gate, d_ffn_down, d_ffn_gate, d_ffn_up, output = together(
        top_last, low_last, out_far, d_query, d_gate, d_ffn_down, d_ffn_gate, d_ffn_up, output
    )
    out_near = near_of_sum(flags, out, out_far)
    inner1 = small[14 : 14 + small_rows].reshape(length, 1)
    grad_normed1 = own_sum(own, low_got, own_got, top_last, low_last)
    own_factor = factor1[0][:, :1]
    own_tokens = tokens.astype(wide)
    back1 = (
        own_factor * norm1_gain * grad_normed1
        - own_tokens * (own_factor * own_factor * inner1 / model)
    )
    grad_gain1 = jnp.sum(grad_normed1 * own_tokens * own_factor, axis=0)
    tokens_grad = (grad_hidden1 + back1).astype(low)
    gain_got = row_swap(grad_gain1[None])
    tokens_grad, gain_got, out_near, line.flying = together(tokens_grad, gain_got, out_near, line.flying)
    small = jnp.concatenate(
        [
            small[:14], grad_gain1[None] + gain_got, jnp.zeros((1, width), wide),
            jnp.transpose(step_sum)[: 4 * 8],
        ],
        axis=0,
    )
    small_got = dp_part(small, 1)
    line.finish()
    total, final = line.done[5]
    (d_conv,) = finalize(
        flags, total, final, (None, width, channels + part // 2), piece_index,
        [(proj_conv.shape, (width, channels), column_index_map, every, slice(0, channels))],
    )
    small_got, d_conv = together(small_got, d_conv)
    sums = dp_rest(small + small_got)
    d_mamba_out, d_attn_out = finalize_blocks(
        flags, pick_chosen(flags, out, (0,)), out_far, out_near,
        [
            (mamba_out_proj.shape, (channels, width), row_index_map, slice(0, channels), every),
            (attn_out_proj.shape, (query_width, width), row_index_map, slice(channels, None), every),
        ],
    )
    extra = jnp.where(flags[1] == 1, total[:, :, channels:], final[:, :, channels:]).astype(wide)
    d_shared = jnp.concatenate([extra[0], extra[1]], axis=1)
    d_key, d_value = extra[2], extra[3]
    step_sum = jnp.stack([sums[16 + p * 8 : 16 + p * 8 + steps] for p in (0, 2, 1, 3)])
    d_step = jnp.transpose(
        jnp.concatenate([lax.dynamic_index_in_dim(step_sum, me ^ d, 0, keepdims=False) for d in range(4)])
    )
    return (
        output, tokens_grad, sums[14], d_gate, d_conv, d_step, d_shared, d_query, d_key, d_value,
        sums[:taps, :channels], sums[taps, :channels], sums[taps + 1 : 2 * taps + 1],
        sums[2 * taps + 1],
        sums[11, :steps], sums[12, :steps],
        jnp.sum(sums[10, :channels].reshape(steps, head_width), axis=1),
        d_mamba_out, d_attn_out, sums[13], d_ffn_gate, d_ffn_up, d_ffn_down,
    )


def solution(mesh):
    return jax.shard_map(
        on_device,
        mesh=mesh,
        in_specs=(
            P(("dp", "row"), "col"),
            P(("dp", "row"), "col"),
            P("dp", None),
            P("col"),
            P("col", "row"),
            P("col", "row"),
            P("col", "row"),
            P("col", "row"),
            P("col", "row"),
            P("col", "row"),
            P("col", "row"),
            P(None, ("row", "col")),
            P(("row", "col")),
            P(),
            P(),
            P(("row", "col")),
            P(("row", "col")),
            P(("row", "col")),
            P("row", "col"),
            P("row", "col"),
            P("col"),
            P("col", "row"),
            P("col", "row"),
            P("row", "col"),
        ),
        out_specs=(
            P(("dp", "row"), "col"),
            P(("dp", "row"), "col"),
            P("col"),
            P("col", "row"),
            P("col", "row"),
            P("col", "row"),
            P("col", "row"),
            P("col", "row"),
            P("col", "row"),
            P("col", "row"),
            P(None, ("row", "col")),
            P(("row", "col")),
            P(),
            P(),
            P(("row", "col")),
            P(("row", "col")),
            P(("row", "col")),
            P("row", "col"),
            P("row", "col"),
            P("col"),
            P("col", "row"),
            P("col", "row"),
            P("row", "col"),
        ),
        check_vma=False,
    )
```

```python
from functools import partial
import math
from typing import NamedTuple

import jax
import jax.numpy as jnp
from jax import lax
from jax.experimental import pallas as pl
from jax.experimental.pallas import tpu as pltpu
from jax.sharding import PartitionSpec as P

EPS = 1e-05
ROPE_BASE = 100000000000.0
MASKED = -1e30
HIGHEST = lax.Precision.HIGHEST
DISTANCES = (0, 2, 1, 3)
LANES = 128
CHUNK = 128
TAIL = 8


class Places(NamedTuple):
    query: int
    key: int
    gate: int
    value: int
    shared: int
    conv: int
    step: int


def dot_any(former, latter, dims, precision=None):
    return lax.dot_general(
        former, latter, (dims, ((), ())), precision=precision, preferred_element_type=jnp.float32
    )


def nn(former, latter):
    return dot_any(former, latter, ((1,), (0,)))


def nt(former, latter):
    return dot_any(former, latter, ((1,), (1,)))


def tn(former, latter):
    return dot_any(former, latter, ((0,), (0,)))


def low_terms(values, count):
    terms = []
    for _ in range(count):
        term = values.astype(jnp.bfloat16)
        values = values - term.astype(jnp.float32)
        terms.append(term)
    return terms


def times_marks(values, marks, count):
    return sum(nn(term, marks) for term in low_terms(values, count))


def marks_times(marks, values, count):
    return sum(nn(marks, term) for term in low_terms(values, count))


def sigmoid_of(values):
    return 1.0 / (1.0 + jnp.exp(-values))


def softplus_of(values):
    return jnp.maximum(values, 0.0) + jnp.log1p(jnp.exp(-jnp.abs(values)))


def head_spread(head_width, width):
    heads = lax.broadcasted_iota(jnp.int32, (LANES, width), 0)
    columns = lax.broadcasted_iota(jnp.int32, (LANES, width), 1)
    return (columns // head_width == heads).astype(jnp.bfloat16)


def head_gather(head_width, width):
    columns = lax.broadcasted_iota(jnp.int32, (width, LANES), 0)
    heads = lax.broadcasted_iota(jnp.int32, (width, LANES), 1)
    return (columns // head_width == heads).astype(jnp.bfloat16)


def causal_conv(ext_ref, columns, weight_ref, bias_ref, position, taps):
    length = ext_ref.shape[0] - TAIL
    running = bias_ref[...] + weight_ref[taps - 1 : taps, :] * ext_ref[TAIL:, columns]
    for offset in range(1, taps):
        earlier = ext_ref[TAIL - offset : TAIL - offset + length, columns]
        running = running + weight_ref[taps - 1 - offset : taps - offset, :] * jnp.where(
            position >= offset, earlier, 0.0
        )
    return running


def chunk_decay(step_in, position, decay_rate):
    length = step_in.shape[0]
    step_size = softplus_of(step_in)
    log_decay = jnp.where(position == 0.0, 0.0, -step_size * decay_rate)
    rows = lax.broadcasted_iota(jnp.int32, (length, length), 0)
    columns = lax.broadcasted_iota(jnp.int32, (length, length), 1)
    causal = rows >= columns
    running = marks_times(causal.astype(jnp.bfloat16), log_decay, 3)
    return step_size, log_decay, running, jnp.transpose(running), causal


def split_pair(values, head_width):
    lane = lax.broadcasted_iota(jnp.int32, values.shape, 1)
    zero = jnp.zeros_like(values)
    return jnp.concatenate(
        [jnp.where(lane < head_width, values, zero), jnp.where(lane < head_width, zero, values)],
        axis=0,
    )


def mamba_forward_kernel(
    raw_ref, step_ref, info_ref, row_ref, weight_ref, bias_ref,
    shared_weight_ref, shared_bias_ref, head_ref, skip_ref, attended_ref,
    mixed_ref, combined_ref, states_ref,
    state, ext, *, head_width, places
):
    chunk = pl.program_id(0)
    length, width = combined_ref.shape
    gate_columns = slice(places.gate, places.value)
    conv_columns = slice(places.conv, places.step)
    shared_columns = slice(places.shared, places.conv)
    states = (places.conv - places.shared) // 2
    taps = weight_ref.shape[0]
    low = jnp.bfloat16

    @pl.when(chunk == 0)
    def _():
        state[...] = jnp.zeros_like(state)
        ext[...] = jnp.zeros_like(ext)

    ext[:TAIL, :] = ext[length : length + TAIL, :]
    ext[TAIL:, :width] = raw_ref[:, conv_columns].astype(jnp.float32)
    ext[TAIL:, width:] = raw_ref[:, shared_columns].astype(jnp.float32)
    segment = info_ref[:, 0:1]
    position = info_ref[:, 1:2]
    pre = causal_conv(ext, slice(0, width), weight_ref, bias_ref, position, taps)
    conv_out = pre * sigmoid_of(pre)
    pre = causal_conv(
        ext, slice(width, None), shared_weight_ref, shared_bias_ref, position, taps
    )
    shared = (pre * sigmoid_of(pre)).astype(low)
    b_map = shared[:, :states]
    c_map = shared[:, states:]
    step_size, _, running, running_t, causal = chunk_decay(
        step_ref[...] + head_ref[0:1, :], position, head_ref[1:2, :]
    )
    segment_row = row_ref[0:1, :]
    allowed = causal & (segment == segment_row)
    local = lax.broadcasted_iota(jnp.int32, (length, 1), 0).astype(jnp.float32)
    enters = jnp.where(position > local, jnp.exp(running), 0.0)
    last = running[length - 1 : length, :]
    leaves = jnp.where(segment == segment_row[:, length - 1 :], jnp.exp(last - running), 0.0)
    spread = head_spread(head_width, width)
    wide = times_marks(jnp.concatenate([step_size, enters, leaves], axis=0), spread, 2)
    weighted = conv_out * wide[:length]
    gram = nt(c_map, b_map)
    weighted_low = weighted.astype(low)
    parts = []
    for pair in range(width // (2 * head_width)):
        weights = []
        for head in (2 * pair, 2 * pair + 1):
            gap = jnp.where(allowed, running[:, head : head + 1] - running_t[head : head + 1, :], MASKED)
            weights.append((gram * jnp.exp(gap)).astype(low))
        columns = slice(2 * pair * head_width, 2 * (pair + 1) * head_width)
        parts.append(
            nn(jnp.concatenate(weights, axis=1), split_pair(weighted_low[:, columns], head_width))
        )
    held = state[...]
    held_low = held.astype(low)
    states_ref[...] = held_low
    scanned = jnp.concatenate(parts, axis=1) + nn(c_map, held_low) * wide[length : 2 * length]
    fade = wide[2 * length - 1 : 2 * length]
    state[...] = held * fade + tn(b_map, (weighted * wide[2 * length :]).astype(low))
    combined = scanned + skip_ref[...] * conv_out
    combined_ref[...] = combined.astype(low)
    gate = raw_ref[:, gate_columns].astype(jnp.float32)
    mixed_ref[:, :width] = (combined * (gate * sigmoid_of(gate))).astype(low)
    mixed_ref[:, width:] = attended_ref[...]


def mamba_backward_kernel(
    raw_ref, tail_ref, step_ref, info_ref, row_ref, weight_ref, bias_ref,
    shared_weight_ref, shared_bias_ref, head_ref, skip_ref, states_ref, grad_ref,
    out_ref, inner_ref, sums_ref,
    grad_state, ext, ext_grad, *, head_width, places
):
    count = pl.num_programs(0)
    step = pl.program_id(0)
    length = grad_ref.shape[0]
    width = places.step - places.conv
    states = (places.conv - places.shared) // 2
    taps = weight_ref.shape[0]
    low = jnp.bfloat16
    f32 = jnp.float32
    gate_columns = slice(places.gate, places.value)
    conv_columns = slice(places.conv, places.step)
    shared_columns = slice(places.shared, places.conv)

    @pl.when(step == 0)
    def _():
        grad_state[...] = jnp.zeros_like(grad_state)
        ext_grad[...] = jnp.zeros_like(ext_grad)
        sums_ref[...] = jnp.zeros_like(sums_ref)

    tail_at = tail_ref.shape[0] - TAIL
    ext[:TAIL, :width] = tail_ref[:, conv_columns].astype(f32)[tail_at:]
    ext[:TAIL, width:] = tail_ref[:, shared_columns].astype(f32)[tail_at:]
    ext[TAIL:, :width] = raw_ref[:, conv_columns].astype(f32)
    ext[TAIL:, width:] = raw_ref[:, shared_columns].astype(f32)
    segment = info_ref[:, 0:1]
    position = info_ref[:, 1:2]
    remaining = info_ref[:, 2:3]
    pre = causal_conv(ext, slice(0, width), weight_ref, bias_ref, position, taps)
    sig = sigmoid_of(pre)
    conv_out = pre * sig
    conv_slope = sig * (1.0 + pre * (1.0 - sig))
    pre = causal_conv(
        ext, slice(width, None), shared_weight_ref, shared_bias_ref, position, taps
    )
    sig = sigmoid_of(pre)
    shared = (pre * sig).astype(low)
    shared_slope = sig * (1.0 + pre * (1.0 - sig))
    b_map = shared[:, :states]
    c_map = shared[:, states:]
    step_in = step_ref[...] + head_ref[0:1, :]
    rate = head_ref[1:2, :]
    step_size, log_decay, running, running_t, causal = chunk_decay(step_in, position, rate)
    segment_row = row_ref[0:1, :]
    allowed = causal & (segment == segment_row)
    local = lax.broadcasted_iota(jnp.int32, (length, 1), 0).astype(f32)
    enters = jnp.where(position > local, jnp.exp(running), 0.0)
    last = running[length - 1 : length, :]
    leaves = jnp.where(segment == segment_row[:, length - 1 :], jnp.exp(last - running), 0.0)
    spread = head_spread(head_width, width)
    wide = times_marks(jnp.concatenate([step_size, enters, leaves], axis=0), spread, 2)
    step_wide = wide[:length]
    enters_wide = wide[length : 2 * length]
    leaves_wide = wide[2 * length :]
    fade = wide[2 * length - 1 : 2 * length]
    weighted = conv_out * step_wide

    gate = raw_ref[:, gate_columns].astype(f32)
    sig = sigmoid_of(gate)
    grad_scan = grad_ref[:, :width].astype(f32) * (gate * sig)

    gram = nt(c_map, b_map)
    weighted_low = weighted.astype(low)
    grad_low = grad_scan.astype(low)
    lane = lax.broadcasted_iota(jnp.int32, (length, LANES), 1)
    sub = lax.broadcasted_iota(jnp.int32, (LANES, length), 0)
    grad_gram = jnp.zeros((length, length), f32)
    by_row = jnp.zeros((length, LANES), f32)
    by_column = jnp.zeros((LANES, length), f32)
    parts = []
    for pair in range(width // (2 * head_width)):
        columns = slice(2 * pair * head_width, 2 * (pair + 1) * head_width)
        split_grad = split_pair(grad_low[:, columns], head_width)
        products = nt(split_grad, weighted_low[:, columns])
        weights = []
        for place, head in enumerate((2 * pair, 2 * pair + 1)):
            gap = jnp.where(allowed, running[:, head : head + 1] - running_t[head : head + 1, :], MASKED)
            fading = jnp.exp(gap)
            weight = gram * fading
            product = products[place * length : (place + 1) * length]
            grad_gram = grad_gram + fading * product
            meeting = weight * product
            by_row = jnp.where(lane == head, jnp.sum(meeting, axis=1, keepdims=True), by_row)
            by_column = jnp.where(sub == head, jnp.sum(meeting, axis=0, keepdims=True), by_column)
            weights.append(weight.astype(low))
        parts.append(tn(jnp.concatenate(weights, axis=0), split_grad))
    held = states_ref[...]
    entering = (grad_scan * enters_wide).astype(low)
    leaving = (weighted * leaves_wide).astype(low)
    grad_held = grad_state[...]
    grad_held_low = grad_held.astype(low)
    from_state = nn(b_map, grad_held_low) * leaves_wide
    grad_weighted = jnp.concatenate(parts, axis=1) + from_state
    grad_gram_low = grad_gram.astype(low)
    grad_c = nn(grad_gram_low, b_map) + nt(entering, held)
    grad_b = tn(grad_gram_low, c_map) + nt(leaving, grad_held_low)
    met_in = grad_scan * enters_wide * nn(c_map, held)
    met_out = weighted * from_state
    met_state = fade * jnp.sum(held.astype(f32) * grad_held, axis=0, keepdims=True)
    grad_state[...] = grad_held * fade + tn(c_map, entering)
    grad_conv_out = grad_weighted * step_wide + skip_ref[...] * grad_scan
    gathered = times_marks(
        jnp.concatenate(
            [met_in, met_out, conv_out * grad_weighted, jnp.broadcast_to(met_state, (TAIL, width))],
            axis=0,
        ),
        head_gather(head_width, width),
        2,
    )
    out_rows = gathered[length : 2 * length]
    at_last = jnp.sum(out_rows, axis=0, keepdims=True) + gathered[3 * length : 3 * length + 1]
    grad_running = by_row - jnp.transpose(by_column) + gathered[:length] - out_rows
    grad_running = grad_running + jnp.where(local == length - 1.0, at_last, 0.0)
    rows = lax.broadcasted_iota(jnp.int32, (length, length), 0)
    later = lax.broadcasted_iota(jnp.int32, (length, length), 1) >= rows
    grad_decay = jnp.where(position == 0.0, 0.0, marks_times(later.astype(low), grad_running, 3))
    grad_step = (gathered[2 * length : 3 * length] - grad_decay * rate) * sigmoid_of(step_in)

    ext_grad[length : length + TAIL, :] = ext_grad[:TAIL, :]
    ext_grad[:length, :width] = grad_conv_out * conv_slope
    ext_grad[:length, width : width + states] = grad_b * shared_slope[:, :states]
    ext_grad[:length, width + states :] = grad_c * shared_slope[:, states:]

    def conv_back(columns, weights, row_at):
        now = ext_grad[:length, columns]
        running = weights[taps - 1 : taps, :] * now
        wide_columns = slice(0, now.shape[1])
        sums_ref[row_at + taps : row_at + taps + 1, wide_columns] += jnp.sum(now, axis=0, keepdims=True)
        sums_ref[row_at + taps - 1 : row_at + taps, wide_columns] += jnp.sum(
            now * ext[TAIL:, columns], axis=0, keepdims=True
        )
        for offset in range(1, taps):
            at = taps - 1 - offset
            running = running + weights[at : at + 1, :] * jnp.where(
                remaining >= offset, ext_grad[offset : offset + length, columns], 0.0
            )
            earlier = jnp.where(
                position >= offset, ext[TAIL - offset : TAIL - offset + length, columns], 0.0
            )
            sums_ref[row_at + at : row_at + at + 1, wide_columns] += jnp.sum(
                now * earlier, axis=0, keepdims=True
            )
        return running

    grad_conv = conv_back(slice(0, width), weight_ref, 0).astype(low)
    grad_shared = conv_back(slice(width, None), shared_weight_ref, taps + 1).astype(low)
    row_at = 2 * (taps + 1)
    sums_ref[row_at : row_at + 1, :width] += jnp.sum(grad_scan * conv_out, axis=0, keepdims=True)
    sums_ref[row_at + 1 : row_at + 2, :LANES] += jnp.sum(grad_step, axis=0, keepdims=True)
    sums_ref[row_at + 2 : row_at + 3, :LANES] += jnp.sum(
        grad_decay * log_decay, axis=0, keepdims=True
    )
    grad_step = grad_step.astype(low)
    out_ref[:, : 2 * states] = grad_shared
    out_ref[:, 2 * states : 2 * states + width] = grad_conv
    out_ref[:, 2 * states + width :] = grad_step
    inner = grad_step.astype(f32) * step_ref[...]
    for at in range(0, places.step - places.shared, LANES):
        raw = raw_ref[:, places.shared + at : places.shared + at + LANES]
        inner = inner + out_ref[:, at : at + LANES].astype(f32) * raw.astype(f32)
    inner_ref[...] = inner


def rope(values, cosine, sine):
    return values * cosine + pltpu.roll(values, values.shape[1] // 2, 1) * sine


def attention_rows(query, key, begin, size, info_ref, row_ref, factor):
    seen = begin + size
    scores = nt(query, key) * factor
    rows = begin + lax.broadcasted_iota(jnp.int32, (size, seen), 0)
    columns = lax.broadcasted_iota(jnp.int32, (size, seen), 1)
    allowed = (rows >= columns) & (info_ref[begin:seen, 0:1] == row_ref[0:1, :seen])
    scores = jnp.where(allowed, scores, MASKED)
    raised = jnp.exp(scores - jnp.max(scores, axis=1, keepdims=True))
    return raised * (1.0 / jnp.sum(raised, axis=1, keepdims=True))


def attention_forward_kernel(
    query_ref, key_ref, value_ref, cosine_ref, sine_ref, info_ref, row_ref, out_ref, *, block
):
    low = jnp.bfloat16
    length, head_dim = query_ref.shape
    factor = 1.0 / math.sqrt(head_dim)
    cosine, sine = cosine_ref[...], sine_ref[...]
    query = rope(query_ref[...].astype(jnp.float32), cosine, sine).astype(low)
    key = rope(key_ref[...].astype(jnp.float32), cosine, sine).astype(low)
    value = value_ref[...]
    for begin in range(0, length, block):
        seen = begin + block
        probs = attention_rows(
            query[begin:seen], key[:seen], begin, block, info_ref, row_ref, factor
        )
        out_ref[begin:seen, :] = nn(probs.astype(low), value[:seen]).astype(low)


def attention_backward_kernel(
    raw_ref, cosine_ref, sine_ref, info_ref, row_ref, combined_ref, grad_ref,
    out_ref, inner_ref, key_total, value_total, *, block, places
):
    low = jnp.bfloat16
    length, head_dim = cosine_ref.shape
    channels = combined_ref.shape[1]
    factor = 1.0 / math.sqrt(head_dim)
    cosine, sine = cosine_ref[...], sine_ref[...]
    query = rope(raw_ref[:, : places.key].astype(jnp.float32), cosine, sine).astype(low)
    key = rope(raw_ref[:, places.key : places.gate].astype(jnp.float32), cosine, sine).astype(low)
    value = raw_ref[:, places.value : places.shared]
    key_total[...] = jnp.zeros_like(key_total)
    value_total[...] = jnp.zeros_like(value_total)
    for begin in range(0, length, block):
        seen = begin + block
        probs = attention_rows(
            query[begin:seen], key[:seen], begin, block, info_ref, row_ref, factor
        )
        grad_out = grad_ref[begin:seen, channels:]
        gate = raw_ref[begin:seen, places.gate : places.value].astype(jnp.float32)
        sig = sigmoid_of(gate)
        out_ref[begin:seen, places.gate : places.value] = (
            grad_ref[begin:seen, :channels].astype(jnp.float32)
            * combined_ref[begin:seen, :].astype(jnp.float32)
            * (sig * (1.0 + gate * (1.0 - sig)))
        ).astype(low)
        grad_probs = nt(grad_out, value[:seen])
        inner = jnp.sum(probs * grad_probs, axis=1, keepdims=True)
        grad_scores = (probs * (grad_probs - inner)).astype(low)
        grad_query = nn(grad_scores, key[:seen]) * factor
        out_ref[begin:seen, : places.key] = rope(
            grad_query, cosine[begin:seen], -sine[begin:seen]
        ).astype(low)
        key_total[:seen, :] += tn(grad_scores, query[begin:seen])
        value_total[:seen, :] += tn(probs.astype(low), grad_out)
    out_ref[:, places.key : places.gate] = rope(key_total[...] * factor, cosine, -sine).astype(low)
    out_ref[:, places.value :] = value_total[...].astype(low)
    inner = jnp.zeros(inner_ref.shape, jnp.float32)
    for at in range(0, places.shared, LANES):
        span = slice(at, at + LANES)
        inner = inner + out_ref[:, span].astype(jnp.float32) * raw_ref[:, span].astype(jnp.float32)
    inner_ref[...] = inner


BRIEF = pl.CostEstimate(flops=1, bytes_accessed=1, transcendentals=0)


def whole(shape):
    return pl.BlockSpec(shape, lambda i: (0,) * len(shape))


def limits(megabytes):
    return pltpu.CompilerParams(vmem_limit_bytes=megabytes * 1024 * 1024)


def column_block(rows, width, at):
    return pl.BlockSpec((rows, width), lambda i: (0, at // width))


def attention_forward(raw, places, cosine, sine, info, row):
    length, width = cosine.shape
    return pl.pallas_call(
        partial(attention_forward_kernel, block=256),
        grid=(1,),
        in_specs=[
            column_block(length, width, places.query),
            column_block(length, width, places.key),
            column_block(length, width, places.value),
            whole(cosine.shape), whole(sine.shape), whole(info.shape), whole(row.shape),
        ],
        out_specs=whole((length, width)),
        out_shape=jax.ShapeDtypeStruct((length, width), jnp.bfloat16),
        compiler_params=limits(48),
        cost_estimate=BRIEF,
        name="attention_forward",
    )(raw, raw, raw, cosine, sine, info, row)


def attention_backward(raw, places, cosine, sine, info, row, combined, grad_mixed):
    length, width = cosine.shape
    return pl.pallas_call(
        partial(attention_backward_kernel, block=256, places=places),
        grid=(1,),
        in_specs=[
            column_block(length, places.shared, 0),
            whole(cosine.shape), whole(sine.shape), whole(info.shape), whole(row.shape),
            whole(combined.shape), whole(grad_mixed.shape),
        ],
        out_specs=[whole((length, places.shared)), whole((length, LANES))],
        out_shape=[
            jax.ShapeDtypeStruct((length, places.shared), jnp.bfloat16),
            jax.ShapeDtypeStruct((length, LANES), jnp.float32),
        ],
        scratch_shapes=[pltpu.VMEM((length, width), jnp.float32)] * 2,
        compiler_params=limits(48),
        cost_estimate=BRIEF,
        name="attention_backward",
    )(raw, cosine, sine, info, row, combined, grad_mixed)


def mamba_forward(raw, places, step_raw, info, row, params, attended, head_width):
    length = raw.shape[0]
    width = places.step - places.conv
    states = (places.conv - places.shared) // 2
    head_dim = attended.shape[1]
    chunks = length // CHUNK

    def block(columns):
        return pl.BlockSpec((CHUNK, columns), lambda i: (i, 0))

    return pl.pallas_call(
        partial(mamba_forward_kernel, head_width=head_width, places=places),
        grid=(chunks,),
        in_specs=[
            block(places.step),
            block(LANES), block(LANES), pl.BlockSpec((8, CHUNK), lambda i: (0, i)),
            *[whole(p.shape) for p in params],
            block(head_dim),
        ],
        out_specs=[
            block(width + head_dim), block(width),
            pl.BlockSpec((None, states, width), lambda i: (i, 0, 0)),
        ],
        out_shape=[
            jax.ShapeDtypeStruct((length, width + head_dim), jnp.bfloat16),
            jax.ShapeDtypeStruct((length, width), jnp.bfloat16),
            jax.ShapeDtypeStruct((chunks, states, width), jnp.bfloat16),
        ],
        scratch_shapes=[
            pltpu.VMEM((states, width), jnp.float32),
            pltpu.VMEM((TAIL + CHUNK, width + 2 * states), jnp.float32),
        ],
        compiler_params=limits(48),
        cost_estimate=BRIEF,
        name="mamba_forward",
    )(raw, step_raw, info, row, *params, attended)


def mamba_backward(raw, places, step_raw, info, row, params, states, grad_mixed, head_width):
    length = raw.shape[0]
    width = places.step - places.conv
    shared = places.conv - places.shared
    chunks = length // CHUNK
    total = places.step + LANES - places.shared
    tail = 16

    def block(columns):
        return pl.BlockSpec((CHUNK, columns), lambda i: (chunks - 1 - i, 0))

    return pl.pallas_call(
        partial(mamba_backward_kernel, head_width=head_width, places=places),
        grid=(chunks,),
        in_specs=[
            block(places.step),
            pl.BlockSpec(
                (tail, places.step),
                lambda i: (jnp.maximum((chunks - 1 - i) * (CHUNK // tail) - 1, 0), 0),
            ),
            block(LANES), block(LANES),
            pl.BlockSpec((8, CHUNK), lambda i: (0, chunks - 1 - i)),
            *[whole(p.shape) for p in params],
            pl.BlockSpec((None, shared // 2, width), lambda i: (chunks - 1 - i, 0, 0)),
            block(grad_mixed.shape[1]),
        ],
        out_specs=[block(total), block(LANES), whole((16, shared))],
        out_shape=[
            jax.ShapeDtypeStruct((length, total), jnp.bfloat16),
            jax.ShapeDtypeStruct((length, LANES), jnp.float32),
            jax.ShapeDtypeStruct((16, shared), jnp.float32),
        ],
        scratch_shapes=[
            pltpu.VMEM((shared // 2, width), jnp.float32),
            pltpu.VMEM((TAIL + CHUNK, width + shared), jnp.float32),
            pltpu.VMEM((TAIL + CHUNK, width + shared), jnp.float32),
        ],
        compiler_params=limits(48),
        cost_estimate=BRIEF,
        name="mamba_backward",
    )(raw, raw, step_raw, info, row, *params, states, grad_mixed)


def matmul(former, latter):
    return jnp.dot(former, latter, preferred_element_type=jnp.float32)


def matmul_left(former, latter):
    return lax.dot_general(
        former, latter, (((0,), (0,)), ((), ())), preferred_element_type=jnp.float32
    )


def matmul_right(former, latter):
    return lax.dot_general(
        former, latter, (((1,), (1,)), ((), ())), preferred_element_type=jnp.float32
    )


def col_swap(values, distance):
    count = lax.axis_size("col")
    return lax.ppermute(values, "col", [(i, i ^ distance) for i in range(count)])


def row_swap(values):
    return lax.ppermute(values, "row", [(0, 1), (1, 0)])


def together(*values):
    return lax.optimization_barrier(values)


def after(value, *earlier):
    return lax.optimization_barrier((value, earlier))[0]


def gather_start(block):
    return col_swap(block, 2), row_swap(block), col_swap(block, 1)


def gather_middle(block, first):
    along_x, along_y, _ = first
    half = block.shape[0] // 2
    return col_swap(along_y[:half], 2), row_swap(along_x[half:]), col_swap(along_x, 1), col_swap(along_y, 1)


def gather_end(block, first, middle):
    along_x, along_y, core = first
    top, low, core_x, core_y = middle
    own = [block, along_x, core, core_x]
    other = [along_y, (top, low), core_y, (col_swap(top, 1), col_swap(low, 1))]
    return own, other


def gather_slow_second(first):
    along_x, along_y, _ = first
    return row_swap(along_x), col_swap(along_x, 1), col_swap(along_y, 1)


def gather_slow_end(block, first, second):
    along_x, along_y, core = first
    diagonal, core_x, core_y = second
    return [block, along_x, core, core_x], [along_y, diagonal, core_y, col_swap(diagonal, 1)]


def add_kernel(former_ref, latter_ref, out_ref):
    total = former_ref[...].astype(jnp.float32) + latter_ref[...].astype(jnp.float32)
    out_ref[...] = total.astype(out_ref.dtype)


def add_low(former, latter):
    shape = former.shape
    tiles = shape[0] if len(shape) == 3 else 2
    block = (1, *shape[1:]) if len(shape) == 3 else (shape[0] // tiles, shape[1])
    spec = pl.BlockSpec(block, lambda i: (i,) + (0,) * (len(shape) - 1))
    return pl.pallas_call(
        add_kernel,
        grid=(tiles,),
        in_specs=[spec, spec],
        out_specs=spec,
        out_shape=jax.ShapeDtypeStruct(shape, jnp.bfloat16),
        compiler_params=limits(32),
        cost_estimate=BRIEF,
        name="add",
    )(former, latter)


def add_three_kernel(first_ref, second_ref, third_ref, out_ref):
    wide = jnp.float32
    total = first_ref[...].astype(wide) + second_ref[...].astype(wide) + third_ref[...].astype(wide)
    out_ref[...] = total.astype(out_ref.dtype)


def add_three(first, second, third, at):
    _, rows, columns = first.shape
    tiles = 2
    spec = pl.BlockSpec((None, rows // tiles, columns), lambda i: (at, i, 0))
    return pl.pallas_call(
        add_three_kernel,
        grid=(tiles,),
        in_specs=[spec] * 3,
        out_specs=pl.BlockSpec((rows // tiles, columns), lambda i: (i, 0)),
        out_shape=jax.ShapeDtypeStruct((rows, columns), jnp.bfloat16),
        compiler_params=limits(32),
        cost_estimate=BRIEF,
        name="add_three",
    )(first, second, third)


def sum_quarters_kernel(base_ref, *refs):
    (*parts, out_ref, low_ref) = refs
    tops, lows = parts[:3], parts[3:]
    wide = jnp.float32

    def write(pieces):
        total = base_ref[...].astype(wide)
        for piece in pieces:
            total = total + piece[...].astype(wide)
        out_ref[...] = total
        low_ref[...] = total.astype(low_ref.dtype)

    @pl.when(pl.program_id(0) == 0)
    def _():
        write(tops)

    @pl.when(pl.program_id(0) == 1)
    def _():
        write(lows)


def sum_quarters(base, own, low_got, own_got, top_last, low_last):
    tokens, width = base.shape
    half = tokens // 2
    row = pl.BlockSpec((half, width), lambda i: (i, 0))
    part = pl.BlockSpec((half, width), lambda i: (0, 0))
    first = pl.BlockSpec((None, half, width), lambda i: (0, 0, 0))
    return pl.pallas_call(
        sum_quarters_kernel,
        grid=(2,),
        in_specs=[row, part, part, part, part, first, part],
        out_specs=[row, row],
        out_shape=[
            jax.ShapeDtypeStruct((tokens, width), jnp.float32),
            jax.ShapeDtypeStruct((tokens, width), jnp.bfloat16),
        ],
        compiler_params=limits(32),
        cost_estimate=BRIEF,
        name="sum_quarters",
    )(base, own[0], own_got, top_last, own[2], low_got, low_last)


def fold_other_kernel(near_ref, far_ref, top_near_ref, top_far_ref, low_ref):
    half = low_ref.shape[0]
    total = (near_ref[...].astype(jnp.float32) + far_ref[...].astype(jnp.float32)).astype(low_ref.dtype)
    low_ref[...] = total[half:]

    @pl.when(pl.program_id(0) == 0)
    def _():
        top_near_ref[...] = total[:half]

    @pl.when(pl.program_id(0) == 1)
    def _():
        top_far_ref[...] = total[:half]


def fold_own_kernel(near_ref, far_ref, top_near_ref, top_far_ref, low_near_ref, low_far_ref):
    half = top_near_ref.shape[0]
    total = (near_ref[...].astype(jnp.float32) + far_ref[...].astype(jnp.float32)).astype(top_near_ref.dtype)

    @pl.when(pl.program_id(0) == 0)
    def _():
        top_near_ref[...] = total[:half]
        low_near_ref[...] = total[half:]

    @pl.when(pl.program_id(0) == 1)
    def _():
        top_far_ref[...] = total[:half]
        low_far_ref[...] = total[half:]


def fold(near, far, is_own):
    _, tokens, width = near.shape
    half = tokens // 2
    share = pl.BlockSpec((None, tokens, width), lambda i: (i, 0, 0))
    quarter = pl.BlockSpec((half, width), lambda i: (0, 0))
    shape = jax.ShapeDtypeStruct((half, width), near.dtype)
    if is_own:
        specs, shapes = [quarter] * 4, [shape] * 4
    else:
        specs = [quarter, quarter, pl.BlockSpec((None, half, width), lambda i: (i, 0, 0))]
        shapes = [shape, shape, jax.ShapeDtypeStruct((2, half, width), near.dtype)]
    return pl.pallas_call(
        fold_own_kernel if is_own else fold_other_kernel,
        grid=(2,),
        in_specs=[share, share],
        out_specs=specs,
        out_shape=shapes,
        compiler_params=limits(32),
        cost_estimate=BRIEF,
        name="fold",
    )(near, far)


def own_sum(own, low_got, own_got, top_last, low_last):
    top_near, _, low_near, _ = own
    wide = jnp.float32
    top = top_near.astype(wide) + own_got.astype(wide) + top_last.astype(wide)
    low = low_near.astype(wide) + low_got[0].astype(wide) + low_last.astype(wide)
    return jnp.concatenate([top, low], axis=0)


def token_total(own, other):
    total = own + row_swap(other)
    total = total + col_swap(total, 1)
    return total + col_swap(total, 2)


def line_update_kernel(flags_ref, now_ref, got_ref, pair_ref, crossed_ref, later_ref, out_ref, sent_ref):
    @pl.when(flags_ref[1] == 1)
    def _():
        wide = jnp.float32
        out_ref[...] = (now_ref[...].astype(wide) + got_ref[...].astype(wide)).astype(out_ref.dtype)
        sent_ref[...] = (pair_ref[...].astype(wide) + crossed_ref[...].astype(wide)).astype(sent_ref.dtype)

    @pl.when(flags_ref[1] == 0)
    def _():
        sent_ref[...] = later_ref[...]


def line_update(flags, now, got, pair, crossed, later):
    rows, columns = now.shape[1:]

    def middle_block(i, f):
        return (i * f[1], 0, 0)

    def end_block(i, f):
        return (i * (1 - f[1]), 0, 0)

    def every_block(i, f):
        return (i, 0, 0)

    block = (None, rows, columns)
    return pl.pallas_call(
        line_update_kernel,
        grid_spec=pltpu.PrefetchScalarGridSpec(
            num_scalar_prefetch=1,
            grid=(4,),
            in_specs=[pl.BlockSpec(block, middle_block)] * 4 + [pl.BlockSpec(block, end_block)],
            out_specs=[pl.BlockSpec(block, middle_block), pl.BlockSpec(block, every_block)],
        ),
        out_shape=[jax.ShapeDtypeStruct(now.shape, now.dtype)] * 2,
        compiler_params=limits(32),
        cost_estimate=BRIEF,
        name="line_update",
    )(flags, now, got, pair, crossed, later)


class LineSums:
    def __init__(self, flags):
        self.flags = flags
        self.step = 0
        self.now = self.sent = self.pair = None
        self.outward = False
        self.flying = ()
        self.done = []

    def advance(self, later=None):
        if lax.axis_size("dp") != 4:
            if later is not None:
                total = lax.psum(later, "dp")
                self.sent = later
                self.done.append((total, total))
            return
        if self.outward:
            self.done.append((self.sent, self.flying[0]))
        self.outward = self.pair is not None
        sent = self.now if later is None else later
        if self.step == 0:
            self.sent = later
        elif self.now is None:
            self.sent = add_low(self.pair, self.flying[1])
            self.pair = None
            if later is not None:
                self.sent = jnp.where(self.flags[1] == 1, self.sent, later)
        elif self.pair is None:
            self.pair = add_low(self.now, self.flying[0])
            self.sent = sent
        else:
            self.pair, self.sent = line_update(
                self.flags, self.now, self.flying[0], self.pair, self.flying[1], sent
            )
        self.now = later
        self.step += 1
        self._start()

    def finish(self):
        if lax.axis_size("dp") == 4:
            self.done.append((self.sent, self.flying[0]))

    def _start(self):
        move = lax.ppermute(self.sent, "dp", [(0, 1), (3, 2), (1, 0), (2, 3)])
        if self.pair is None:
            self.flying = (move,)
        else:
            self.flying = (move, lax.ppermute(self.pair, "dp", [(1, 2), (2, 1)]))


def dp_part(values, distance):
    count = lax.axis_size("dp")
    return lax.ppermute(values, "dp", [(i, i ^ distance) for i in range(count)])


def dp_rest(values):
    distance = 2
    while distance < lax.axis_size("dp"):
        values = values + dp_part(values, distance)
        distance *= 2
    return values


def pick_kernel(*refs, count):
    out_ref = refs[-1]
    for at in range(count):

        @pl.when(pl.program_id(0) == at)
        def _():
            out_ref[...] = refs[at][...]


def pick(sources):
    rows, columns = sources[0][0].shape[1:]
    return pl.pallas_call(
        partial(pick_kernel, count=len(sources)),
        grid=(len(sources),),
        in_specs=[pl.BlockSpec((None, rows, columns), lambda i, at=at: (at, 0, 0)) for _, at in sources],
        out_specs=pl.BlockSpec((None, rows, columns), lambda i: (i, 0, 0)),
        out_shape=jax.ShapeDtypeStruct((len(sources), rows, columns), sources[0][0].dtype),
        compiler_params=limits(32),
        cost_estimate=BRIEF,
        name="pick",
    )(*[array for array, _ in sources])


def pick_at_kernel(flags_ref, in_ref, out_ref):
    out_ref[...] = in_ref[...]


def pick_at(flags, values, distance, tiles=2):
    _, rows, columns = values.shape
    size = rows // tiles
    return pl.pallas_call(
        pick_at_kernel,
        grid_spec=pltpu.PrefetchScalarGridSpec(
            num_scalar_prefetch=1,
            grid=(tiles,),
            in_specs=[
                pl.BlockSpec((None, size, columns), lambda i, f: (jnp.bitwise_xor(f[0], distance), i, 0))
            ],
            out_specs=pl.BlockSpec((size, columns), lambda i, f: (i, 0)),
        ),
        out_shape=jax.ShapeDtypeStruct((rows, columns), values.dtype),
        compiler_params=limits(32),
        cost_estimate=BRIEF,
        name="pick_at",
    )(flags, values)


def choose_kernel(flags_ref, middle_ref, end_ref, out_ref):
    @pl.when(flags_ref[1] == 1)
    def _():
        out_ref[...] = middle_ref[...]

    @pl.when(flags_ref[1] == 0)
    def _():
        out_ref[...] = end_ref[...]


def chosen(flags, pair):
    middle, end = pair
    block = (None, *middle.shape[1:])
    return pl.pallas_call(
        choose_kernel,
        grid_spec=pltpu.PrefetchScalarGridSpec(
            num_scalar_prefetch=1,
            grid=(middle.shape[0],),
            in_specs=[
                pl.BlockSpec(block, lambda i, f: (i * f[1], 0, 0)),
                pl.BlockSpec(block, lambda i, f: (i * (1 - f[1]), 0, 0)),
            ],
            out_specs=pl.BlockSpec(block, lambda i, f: (i, 0, 0)),
        ),
        out_shape=jax.ShapeDtypeStruct(middle.shape, middle.dtype),
        compiler_params=limits(32),
        cost_estimate=BRIEF,
        name="choose",
    )(flags, middle, end)


def pick_chosen_kernel(flags_ref, middle_ref, end_ref, out_ref):
    choose_kernel(flags_ref, middle_ref, end_ref, out_ref)


def pick_chosen(flags, pair, places):
    middle, end = pair
    block = (None, *middle.shape[1:])
    return pl.pallas_call(
        pick_chosen_kernel,
        grid_spec=pltpu.PrefetchScalarGridSpec(
            num_scalar_prefetch=1,
            grid=(len(places),),
            in_specs=[
                pl.BlockSpec(block, lambda i, f: (distance_at(i, places) * f[1], 0, 0)),
                pl.BlockSpec(block, lambda i, f: (distance_at(i, places) * (1 - f[1]), 0, 0)),
            ],
            out_specs=pl.BlockSpec(block, lambda i, f: (i, 0, 0)),
        ),
        out_shape=jax.ShapeDtypeStruct((len(places), *middle.shape[1:]), middle.dtype),
        compiler_params=limits(32),
        cost_estimate=BRIEF,
        name="pick_chosen",
    )(flags, middle, end)


def near_of_sum(flags, pair, fetched):
    kept = pick_chosen(flags, pair, (2,))
    return col_swap(pick([(kept, 0), (fetched, 1)]), 1)


def far_pair(blocks):
    return col_swap(pick([(blocks, 1), (blocks, 3)]), 2)


def near_pair(blocks, fetched):
    return col_swap(pick([(blocks, 2), (fetched, 1)]), 1)


def halves_kernel(flags_ref, in_ref, keep_ref, send_ref):
    part = keep_ref.shape[1]

    @pl.when(flags_ref[2] == 0)
    def _():
        keep_ref[...] = in_ref[:, :part]
        send_ref[...] = in_ref[:, part:]

    @pl.when(flags_ref[2] == 1)
    def _():
        keep_ref[...] = in_ref[:, part:]
        send_ref[...] = in_ref[:, :part]


def row_halves(flags, blocks):
    count, rows, columns = blocks.shape
    half = pl.BlockSpec((None, rows, columns // 2), lambda i, f: (i, 0, 0))
    return pl.pallas_call(
        halves_kernel,
        grid_spec=pltpu.PrefetchScalarGridSpec(
            num_scalar_prefetch=1,
            grid=(count,),
            in_specs=[pl.BlockSpec((None, rows, columns), lambda i, f: (i, 0, 0))],
            out_specs=[half, half],
        ),
        out_shape=[jax.ShapeDtypeStruct((count, rows, columns // 2), blocks.dtype)] * 2,
        compiler_params=limits(32),
        cost_estimate=BRIEF,
        name="row_halves",
    )(flags, blocks)


def pack_out_kernel(mine_ref, far_ref, near_ref, both_ref, out_ref):
    width = mine_ref.shape[1]
    for at, ref in enumerate((mine_ref, far_ref, near_ref, both_ref)):
        out_ref[:, at * width : (at + 1) * width] = ref[...]


def pack_out(blocks, fetched, passed):
    _, depth, width = blocks.shape
    tiles = 2
    return pl.pallas_call(
        pack_out_kernel,
        grid=(tiles,),
        in_specs=block_specs(depth // tiles, width),
        out_specs=pl.BlockSpec((depth // tiles, 4 * width), lambda i: (i, 0)),
        out_shape=jax.ShapeDtypeStruct((depth, 4 * width), blocks.dtype),
        compiler_params=limits(32),
        cost_estimate=BRIEF,
        name="pack_out",
    )(*block_values(blocks, fetched, passed))


def block_specs(size, count):
    return [
        pl.BlockSpec((None, size, count), lambda i, *_, at=at: (at, i, 0)) for at in (0, 0, 0, 1)
    ]


def block_values(blocks, fetched, passed):
    return blocks, fetched, passed, passed


def own_first(values, row_index):
    return jnp.where(row_index == 0, values, jnp.flip(values, 0))


def tile_blocks(refs, split):
    tile = pl.program_id(0)
    tiles = pl.num_programs(0)
    refs = list(refs)
    blocks = []
    for halves in split:
        if halves:
            top, low = refs.pop(0), refs.pop(0)
            blocks.append(jnp.where(tile < tiles // 2, top[...], low[...]))
        else:
            blocks.append(refs.pop(0)[...])
    return blocks, refs


def write_normed(blocks, gain_ref, out_ref, factor_ref):
    width = blocks[0].shape[1]
    total = jnp.zeros((blocks[0].shape[0], 1), jnp.float32)
    for block in blocks:
        values = block.astype(jnp.float32)
        total = total + jnp.sum(values * values, axis=1, keepdims=True)
    factor = lax.rsqrt(total * (1.0 / (width * len(blocks))) + EPS)
    for at, block in enumerate(blocks):
        span = slice(at * width, (at + 1) * width)
        out_ref[:, span] = (block.astype(jnp.float32) * factor * gain_ref[:, span]).astype(jnp.bfloat16)
    factor_ref[...] = jnp.broadcast_to(factor, factor_ref.shape)


def project_kernel(*refs, split):
    blocks, refs = tile_blocks(refs, split)
    gain_ref, weight_ref, normed_ref, factor_ref, raw_ref, step_ref = refs
    write_normed(blocks, gain_ref, normed_ref, factor_ref)
    raw = nn(normed_ref[...], weight_ref[...])
    main = raw_ref.shape[1]
    raw_ref[...] = raw[:, :main].astype(jnp.bfloat16)
    step_ref[...] = raw[:, main:]


def ffn_kernel(*refs, split):
    blocks, refs = tile_blocks(refs, split)
    gain_ref, weight_ref, grad_hidden_ref, normed_ref, factor_ref, hidden_ref, grad_ref, inner_ref = refs
    write_normed(blocks, gain_ref, normed_ref, factor_ref)
    low, wide = jnp.bfloat16, jnp.float32
    units = hidden_ref.shape[1]
    gate_up = nn(normed_ref[...], weight_ref[...])
    gate, up = gate_up[:, :units], gate_up[:, units:]
    sig = sigmoid_of(gate)
    silu = gate * sig
    hidden_ref[...] = (silu * up).astype(low)
    grad_hidden = grad_hidden_ref[...]
    grad_gate = (grad_hidden * up * sig * (1.0 + gate * (1.0 - sig))).astype(low)
    grad_up = (grad_hidden * silu).astype(low)
    grad_ref[:, :units] = grad_gate
    grad_ref[:, units:] = grad_up
    products = grad_gate.astype(wide) * gate + grad_up.astype(wide) * up
    inner = products[:, :LANES]
    for at in range(LANES, units, LANES):
        inner = inner + products[:, at : at + LANES]
    inner_ref[...] = inner


def meet_kernel(*refs, split):
    blocks, refs = tile_blocks(refs, split)
    weight_ref, out_ref, product_ref = refs
    width = blocks[0].shape[1]
    for at, block in enumerate(blocks):
        out_ref[:, at * width : (at + 1) * width] = block
    product_ref[...] = nt(out_ref[...], weight_ref[...]).astype(product_ref.dtype)


def tiled_call(kernel, name, pieces, operands, outs, tiles=4):
    tokens, width = pieces[0].shape
    size = tokens // tiles
    split = [isinstance(piece, tuple) for piece in pieces]
    specs, values = [], []
    for piece, halves in zip(pieces, split):
        if halves:
            specs.append(pl.BlockSpec((size, width), lambda i: (jnp.minimum(i, tiles // 2 - 1), 0)))
            specs.append(pl.BlockSpec((size, width), lambda i: (jnp.maximum(i - tiles // 2, 0), 0)))
            values.extend(piece)
        else:
            specs.append(pl.BlockSpec((size, width), lambda i: (i, 0)))
            values.append(piece)
    for value, is_whole in operands:
        specs.append(whole(value.shape) if is_whole else pl.BlockSpec((size, value.shape[1]), lambda i: (i, 0)))
        values.append(value)
    return pl.pallas_call(
        partial(kernel, split=split),
        grid=(tiles,),
        in_specs=specs,
        out_specs=[pl.BlockSpec((size, columns), lambda i: (i, 0)) for columns, _ in outs],
        out_shape=[jax.ShapeDtypeStruct((tokens, columns), dtype) for columns, dtype in outs],
        compiler_params=limits(56),
        cost_estimate=BRIEF,
        name=name,
    )(*values)


def weight_grad_kernel(former_0, former_1, latter_0, latter_1, *out_refs):
    total = tn(former_0[...], latter_0[...]) + tn(former_1[...], latter_1[...])
    at = 0
    for out_ref in out_refs:
        out_ref[...] = total[:, at : at + out_ref.shape[1]].astype(out_ref.dtype)
        at += out_ref.shape[1]


def weight_grad(former, latter, width, at=0, counts=None):
    length, depth = former[0].shape
    if counts is None:
        left = pl.BlockSpec((length, depth), lambda i: (0, 0))
        right = pl.BlockSpec((length, width), lambda i: (0, i))
        shapes = [(4, depth, width)]
    else:
        left = pl.BlockSpec((length, width), lambda i: (0, i))
        right = pl.BlockSpec((length, sum(counts)), lambda i: (0, at))
        shapes = [(4, width, count) for count in counts]
    out = pl.pallas_call(
        weight_grad_kernel,
        grid=(4,),
        in_specs=[left, left, right, right],
        out_specs=[pl.BlockSpec((None, *shape[1:]), lambda i: (i, 0, 0)) for shape in shapes],
        out_shape=[jax.ShapeDtypeStruct(shape, jnp.bfloat16) for shape in shapes],
        compiler_params=limits(56),
        cost_estimate=BRIEF,
        name="weight_grad",
    )(*former, *latter)
    return out[0] if len(out) == 1 else out


def spread_kernel(*refs, transposed):
    values, (weight_ref, far_ref, near_ref) = refs[:-3], refs[-3:]
    step = pl.program_id(0)
    total = None
    at = 0
    for ref in values:
        if transposed:
            part = nt(ref[...], weight_ref[:, at : at + ref.shape[1]])
            at += ref.shape[1]
        else:
            part = nn(ref[...], weight_ref[...])
        total = part if total is None else total + part
    total = total.astype(far_ref.dtype)

    @pl.when(step < 2)
    def _():
        far_ref[...] = total

    @pl.when(step >= 2)
    def _():
        near_ref[...] = total


def spread(values, weight, width, transposed):
    tokens = values[0].shape[0]

    def block_of(i):
        return (i + 2) % 4

    if transposed:
        weight_spec = pl.BlockSpec((width, weight.shape[1]), lambda i: (block_of(i), 0))
    else:
        weight_spec = pl.BlockSpec((weight.shape[0], width), lambda i: (0, block_of(i)))
    shape = jax.ShapeDtypeStruct((2, tokens, width), jnp.bfloat16)
    far, near = pl.pallas_call(
        partial(spread_kernel, transposed=transposed),
        grid=(4,),
        in_specs=[whole(v.shape) for v in values] + [weight_spec],
        out_specs=[
            pl.BlockSpec((None, tokens, width), lambda i: (jnp.minimum(i, 1), 0, 0)),
            pl.BlockSpec((None, tokens, width), lambda i: (jnp.maximum(i - 2, 0), 0, 0)),
        ],
        out_shape=[shape, shape],
        compiler_params=limits(56),
        cost_estimate=BRIEF,
        name="spread",
    )(*values, weight)
    return near, far


def cut_first_kernel(flags_ref, query_ref, gate_ref, conv_ref, step_ref, out_ref, *, distances, steps):
    at = 0
    for ref in (query_ref, gate_ref, conv_ref):
        out_ref[:, at : at + ref.shape[1]] = ref[...]
        at += ref.shape[1]
    place = jnp.bitwise_xor(flags_ref[0], distance_at(pl.program_id(0), distances))
    step = pltpu.roll(step_ref[...].astype(jnp.float32), (LANES - place * steps) % LANES, 1)
    lane = lax.broadcasted_iota(jnp.int32, step.shape, 1)
    out_ref[:, at:] = jnp.where(lane < steps, step, 0.0).astype(out_ref.dtype)


def distance_at(i, distances):
    value = distances[0]
    for at, distance in enumerate(distances[1:], 1):
        value = jnp.where(i == at, distance, value)
    return value


def cut_first(flags, query, gate, conv, step, distances, size, at_share):
    depth = gate.shape[0]
    widths = [array.shape[1] // 4 for array in (query, gate, conv)]
    steps = step.shape[1] // 4
    total = sum(widths) + LANES
    step = jnp.pad(step, ((0, 0), (0, LANES - step.shape[1])))

    def row(f):
        return f[3] if at_share else 0

    def column_index(i, f):
        return (row(f), jnp.bitwise_xor(f[0], distance_at(i, distances)))

    return pl.pallas_call(
        partial(cut_first_kernel, distances=distances, steps=steps),
        grid_spec=pltpu.PrefetchScalarGridSpec(
            num_scalar_prefetch=1,
            grid=(len(distances),),
            in_specs=[pl.BlockSpec((size, w), column_index) for w in widths]
            + [pl.BlockSpec((size, LANES), lambda i, f: (row(f), 0))],
            out_specs=pl.BlockSpec((None, size, total), lambda i, f: (i, 0, 0)),
        ),
        out_shape=jax.ShapeDtypeStruct((len(distances), size, total), gate.dtype),
        compiler_params=limits(32),
        cost_estimate=BRIEF,
        name="cut_first",
    )(flags, query, gate, conv, step)


def cut_rest_kernel(flags_ref, gate_ref, up_ref, down_ref, out_ref):
    at = 0
    for ref in (gate_ref, up_ref, down_ref):
        out_ref[:, at : at + ref.shape[1]] = ref[...]
        at += ref.shape[1]


def cut_rest(flags, gate, up, down, distances, size, at_share):
    units = gate.shape[1] // 4
    width = down.shape[1]
    total = 2 * units + width
    parts = units // size

    def column_index(i, f):
        return (f[3] if at_share else 0, jnp.bitwise_xor(f[0], distance_at(i, distances)))

    def row_index(i, f):
        place = jnp.bitwise_xor(f[0], distance_at(i, distances))
        return (place * parts + (f[3] if at_share else 0), 0)

    return pl.pallas_call(
        cut_rest_kernel,
        grid_spec=pltpu.PrefetchScalarGridSpec(
            num_scalar_prefetch=1,
            grid=(len(distances),),
            in_specs=[
                pl.BlockSpec((size, units), column_index),
                pl.BlockSpec((size, units), column_index),
                pl.BlockSpec((size, width), row_index),
            ],
            out_specs=pl.BlockSpec((None, size, total), lambda i, f: (i, 0, 0)),
        ),
        out_shape=jax.ShapeDtypeStruct((len(distances), size, total), gate.dtype),
        compiler_params=limits(32),
        cost_estimate=BRIEF,
        name="cut_rest",
    )(flags, gate, up, down)


def cut_out_kernel(flags_ref, mamba_ref, attn_ref, out_ref):
    out_ref[: mamba_ref.shape[0], :] = mamba_ref[...]
    out_ref[mamba_ref.shape[0] :, :] = attn_ref[...]


def cut_out(flags, mamba, attn):
    channels, query = mamba.shape[0] // 4, attn.shape[0] // 4
    width = mamba.shape[1]

    def row_index(i, f):
        return (jnp.bitwise_xor(f[0], distance_at(i, DISTANCES)), 0)

    return pl.pallas_call(
        cut_out_kernel,
        grid_spec=pltpu.PrefetchScalarGridSpec(
            num_scalar_prefetch=1,
            grid=(4,),
            in_specs=[pl.BlockSpec((channels, width), row_index), pl.BlockSpec((query, width), row_index)],
            out_specs=pl.BlockSpec((None, channels + query, width), lambda i, f: (i, 0, 0)),
        ),
        out_shape=jax.ShapeDtypeStruct((4, channels + query, width), mamba.dtype),
        compiler_params=limits(32),
        cost_estimate=BRIEF,
        name="cut_out",
    )(flags, mamba, attn)


def pack_first_kernel(*refs, places, begins):
    pieces, out_ref = refs[:-1], refs[-1]
    query = places.key - places.query
    channels = places.value - places.gate
    head = places.gate - places.key
    total = out_ref.shape[2]

    def place(at, ref, begin, count, to):
        out_ref[at, :, to : to + count] = ref[:, begin : begin + count]

    for at in range(4):
        alone, common = pieces[2 * at], pieces[2 * at + 1]
        begin = begins[2 * at + 1]
        place(at, alone, 0, query, places.query)
        place(at, alone, query, channels, places.gate)
        place(at, alone, query + channels, channels, places.conv)
        place(at, alone, query + 2 * channels, total - places.step, places.step)
        place(at, common, begin, head, places.key)
        place(at, common, begin + head, head, places.value)
        place(at, common, begin + 2 * head, places.conv - places.shared, places.shared)


def pack_first(sources, places, total):
    depth, dtype = sources[0][0].shape[1], sources[0][0].dtype
    tiles = 4
    size = depth // tiles
    out = pl.pallas_call(
        partial(pack_first_kernel, places=places, begins=[begin for _, _, begin in sources]),
        grid=(tiles,),
        in_specs=[
            pl.BlockSpec((None, size, v.shape[2]), lambda i, at=at: (at, i, 0)) for v, at, _ in sources
        ],
        out_specs=pl.BlockSpec((4, size, total), lambda i: (0, i, 0)),
        out_shape=jax.ShapeDtypeStruct((4, depth, total), dtype),
        compiler_params=limits(48),
        cost_estimate=BRIEF,
        name="pack_first",
    )(*[v for v, _, _ in sources])
    return out.reshape(4 * depth, total)


def pack_rest_kernel(mine_ref, far_ref, near_ref, both_ref, in_ref, down_ref):
    width = down_ref.shape[1] // 4
    inner = in_ref.shape[2]
    for at, ref in enumerate((mine_ref, far_ref, near_ref, both_ref)):
        in_ref[at] = ref[:, :inner]
        down_ref[:, at * width : (at + 1) * width] = ref[:, inner : inner + width]


def pack_rest(sources, width):
    _, depth, total = sources[0][0].shape
    dtype = sources[0][0].dtype
    inner = total - width
    tiles = 4
    size = depth // tiles
    into, down = pl.pallas_call(
        pack_rest_kernel,
        grid=(tiles,),
        in_specs=[
            pl.BlockSpec((None, size, total), lambda i, at=at: (at, i, 0)) for _, at in sources
        ],
        out_specs=[
            pl.BlockSpec((4, size, inner), lambda i: (0, i, 0)),
            pl.BlockSpec((size, 4 * width), lambda i: (i, 0)),
        ],
        out_shape=[
            jax.ShapeDtypeStruct((4, depth, inner), dtype),
            jax.ShapeDtypeStruct((depth, 4 * width), dtype),
        ],
        compiler_params=limits(32),
        cost_estimate=BRIEF,
        name="pack_rest",
    )(*[v for v, _ in sources])
    return into.reshape(4 * depth, inner), down


def collect_early_kernel(*refs, places):
    pieces, (out_ref, common_ref) = refs[:4], refs[4:]
    query = places.key - places.query
    key = jnp.zeros((out_ref.shape[1], places.gate - places.key), jnp.float32)
    value = jnp.zeros((out_ref.shape[1], places.shared - places.value), jnp.float32)
    for at, piece in enumerate(pieces):
        out_ref[at, :, :query] = piece[:, : places.key]
        out_ref[at, :, query:] = piece[:, places.gate : places.value]
        key = key + piece[:, places.key : places.gate].astype(jnp.float32)
        value = value + piece[:, places.value :].astype(jnp.float32)
    common_ref[:, : key.shape[1]] = key.astype(common_ref.dtype)
    common_ref[:, key.shape[1] :] = value.astype(common_ref.dtype)


def collect_early(blocks, fetched, passed, places):
    _, depth, count = blocks.shape
    alone = places.key - places.query + places.value - places.gate
    tiles = 2
    size = depth // tiles
    return pl.pallas_call(
        partial(collect_early_kernel, places=places),
        grid=(tiles,),
        in_specs=block_specs(size, count),
        out_specs=[
            pl.BlockSpec((4, size, alone), lambda i: (0, i, 0)),
            pl.BlockSpec((size, count - alone), lambda i: (i, 0)),
        ],
        out_shape=[
            jax.ShapeDtypeStruct((4, depth, alone), blocks.dtype),
            jax.ShapeDtypeStruct((depth, count - alone), blocks.dtype),
        ],
        compiler_params=limits(32),
        cost_estimate=BRIEF,
        name="collect_early",
    )(*block_values(blocks, fetched, passed))


def collect_late_kernel(*refs, channels):
    alone, shared, (common_ref, out_ref, step_ref) = refs[:4], refs[4:8], refs[8:]
    quarter = out_ref.shape[2] - channels
    wide = jnp.float32
    steps = jnp.zeros(step_ref.shape, wide)
    total = jnp.zeros((out_ref.shape[1], shared[0].shape[1]), wide)
    for at, piece in enumerate(alone):
        out_ref[at, :, :channels] = piece[:, :channels]
        step = piece[:, channels:].astype(wide)
        steps = steps + (pltpu.roll(step, at * 8, 1) if at else step)
        total = total + shared[at][...].astype(wide)
    step_ref[...] = steps
    for at in range(2):
        span = slice(at * quarter, (at + 1) * quarter)
        out_ref[at, :, channels:] = total[:, span].astype(out_ref.dtype)
        out_ref[at + 2, :, channels:] = common_ref[:, span]


def collect_late(alone, shared, common, channels):
    _, depth, count = alone[0].shape
    part = shared[0].shape[2]
    tiles = 2
    size = depth // tiles
    return pl.pallas_call(
        partial(collect_late_kernel, channels=channels),
        grid=(tiles,),
        in_specs=[
            *block_specs(size, count), *block_specs(size, part),
            pl.BlockSpec((size, common.shape[1]), lambda i: (i, 0)),
        ],
        out_specs=[
            pl.BlockSpec((4, size, channels + part // 2), lambda i: (0, i, 0)),
            pl.BlockSpec((size, LANES), lambda i: (i, 0)),
        ],
        out_shape=[
            jax.ShapeDtypeStruct((4, depth, channels + part // 2), alone[0].dtype),
            jax.ShapeDtypeStruct((depth, LANES), jnp.float32),
        ],
        compiler_params=limits(32),
        cost_estimate=BRIEF,
        name="collect_late",
    )(*block_values(*alone), *block_values(*shared), common)


def slot_of(flags, place):
    distance = jnp.bitwise_xor(flags[0], place)
    return 2 * jnp.bitwise_and(distance, 1) + distance // 2


def finalize_kernel(flags_ref, total_ref, last_ref, *out_refs, cuts):
    values = jnp.where(flags_ref[1] == 1, total_ref[...], last_ref[...])
    for (span, columns), out_ref in zip(cuts, out_refs):
        out_ref[...] = values[span, columns].astype(jnp.float32)


def finalize(flags, total, last, block, index, outs):
    return pl.pallas_call(
        partial(finalize_kernel, cuts=[(rows, columns) for _, _, _, rows, columns in outs]),
        grid_spec=pltpu.PrefetchScalarGridSpec(
            num_scalar_prefetch=1,
            grid=(4,),
            in_specs=[pl.BlockSpec(block, index)] * 2,
            out_specs=[pl.BlockSpec(out_block, out_index) for _, out_block, out_index, _, _ in outs],
        ),
        out_shape=[jax.ShapeDtypeStruct(shape, jnp.float32) for shape, _, _, _, _ in outs],
        compiler_params=limits(32),
        cost_estimate=BRIEF,
        name="finalize",
    )(flags, total, last)


def finalize_blocks_kernel(flags_ref, *refs, cuts):
    pieces, out_refs = refs[:4], refs[4:]
    slot = slot_of(flags_ref, pl.program_id(0))
    for at, piece in enumerate(pieces):

        @pl.when(slot == at)
        def _():
            for (rows, columns), out_ref in zip(cuts, out_refs):
                out_ref[...] = piece[rows, columns].astype(jnp.float32)


def finalize_blocks(flags, blocks, fetched, passed, outs):
    _, rows, columns = blocks.shape
    return pl.pallas_call(
        partial(finalize_blocks_kernel, cuts=[(rows, columns) for _, _, _, rows, columns in outs]),
        grid_spec=pltpu.PrefetchScalarGridSpec(
            num_scalar_prefetch=1,
            grid=(4,),
            in_specs=[
                pl.BlockSpec((None, rows, columns), lambda i, f, at=at: (at, 0, 0)) for at in (0, 0, 0, 1)
            ],
            out_specs=[pl.BlockSpec(out_block, out_index) for _, out_block, out_index, _, _ in outs],
        ),
        out_shape=[jax.ShapeDtypeStruct(shape, jnp.float32) for shape, _, _, _, _ in outs],
        compiler_params=limits(32),
        cost_estimate=BRIEF,
        name="finalize_blocks",
    )(flags, *block_values(blocks, fetched, passed))


def meet_gathered_kernel(flags_ref, *refs):
    meet_kernel(*refs, split=[False] * 4)


def meet_gathered(flags, gathered, weight, tiles=4):
    _, tokens, width = gathered.shape
    size = tokens // tiles

    def block_at(distance):
        return pl.BlockSpec((None, size, width), lambda i, f: (jnp.bitwise_xor(f[0], distance), i, 0))

    model, units = weight.shape[1], weight.shape[0]
    return pl.pallas_call(
        meet_gathered_kernel,
        grid_spec=pltpu.PrefetchScalarGridSpec(
            num_scalar_prefetch=1,
            grid=(tiles,),
            in_specs=[block_at(d) for d in DISTANCES] + [pl.BlockSpec(weight.shape, lambda i, f: (0, 0))],
            out_specs=[
                pl.BlockSpec((size, model), lambda i, f: (i, 0)),
                pl.BlockSpec((size, units), lambda i, f: (i, 0)),
            ],
        ),
        out_shape=[
            jax.ShapeDtypeStruct((tokens, model), jnp.bfloat16),
            jax.ShapeDtypeStruct((tokens, units), jnp.float32),
        ],
        compiler_params=limits(56),
        cost_estimate=BRIEF,
        name="meet_gathered",
    )(flags, *[gathered] * 4, weight)


def on_device(
    tokens,
    cotangent,
    segment_ids,
    norm1_gain,
    proj_gate,
    proj_conv,
    proj_step,
    proj_shared,
    proj_query,
    proj_key,
    proj_value,
    conv_weight,
    conv_bias,
    shared_conv,
    shared_bias,
    step_bias,
    decay_log,
    skip_gain,
    mamba_out_proj,
    attn_out_proj,
    norm2_gain,
    ffn_gate,
    ffn_up,
    ffn_down,
):
    low = jnp.bfloat16
    wide = jnp.float32
    me = lax.axis_index("col")
    row_index = lax.axis_index("row")
    length = segment_ids.shape[1]
    width = tokens.shape[1]
    model = width * len(DISTANCES)
    head_dim = proj_key.shape[1]
    channels = proj_gate.shape[1] // 4
    steps = proj_step.shape[1] // 4
    head_width = channels // steps
    units = ffn_gate.shape[1] // 4
    query_width = proj_query.shape[1] // 4
    part = proj_shared.shape[1]
    at_gate = query_width + head_dim
    at_value = at_gate + channels
    at_shared = at_value + head_dim
    at_conv = at_shared + 2 * part
    at_step = at_conv + channels
    places = Places(0, query_width, at_gate, at_value, at_shared, at_conv, at_step)
    line_place = lax.axis_index("dp")
    share = width // lax.axis_size("dp")
    flags = jnp.stack(
        [me, ((line_place == 1) | (line_place == 2)).astype(me.dtype), row_index, line_place]
    ).astype(jnp.int32)
    firsts = (proj_query, proj_gate, proj_conv, proj_step)
    rests = (ffn_gate, ffn_up, ffn_down)

    def along_line(values):
        return lax.all_gather(values, "dp", axis=1, tiled=True)

    shared_twin = row_swap(proj_shared)
    fetched = col_swap(cut_first(flags, *firsts, DISTANCES[1::2], share, True), 2)
    gains = jnp.stack([norm1_gain, norm2_gain])
    gains_far = col_swap(gains, 2)
    block, shared_twin, fetched, gains_far = together(tokens, shared_twin, fetched, gains_far)
    first = gather_start(block)
    far = along_line(fetched)
    common = jnp.concatenate(
        [
            proj_key, proj_value,
            jnp.where(row_index == 0, proj_shared, shared_twin),
            jnp.where(row_index == 0, shared_twin, proj_shared),
        ],
        axis=1,
    )[None]
    alone = cut_first(flags, *firsts, DISTANCES[::2], width, False)
    lone = alone.shape[2]
    near = col_swap(jnp.concatenate([alone[1:], common], axis=2), 1)
    common_far = col_swap(common, 2)
    segments = own_first(segment_ids, row_index)
    indices = jnp.arange(length, dtype=jnp.int32)
    same = segments[:, :, None] == segments[:, None, :]
    position = jnp.sum(same & (indices[:, None] > indices[None, :]), axis=2).astype(wide)
    remaining = jnp.sum(same & (indices[:, None] < indices[None, :]), axis=2).astype(wide)
    lane = jnp.arange(LANES)
    info = jnp.where(
        lane == 0,
        segments.astype(wide)[..., None],
        jnp.where(lane == 1, position[..., None], remaining[..., None]),
    )
    row_info = jnp.broadcast_to(segments.astype(wide)[:, None, :], (2, 8, length))
    half_dim = head_dim // 2
    frequency = ROPE_BASE ** (-2.0 * jnp.arange(half_dim, dtype=wide) / head_dim)
    angles = position[..., None] * frequency
    cosine, sine = jnp.cos(angles), jnp.sin(angles)
    cosine = jnp.concatenate([cosine, cosine], axis=2)
    sine = jnp.concatenate([-sine, sine], axis=2)
    head_rows = jnp.pad(
        jnp.stack([step_bias, jnp.exp(decay_log)]), ((0, 6), (0, LANES - steps))
    )
    gain1, gain2 = gains[0:1], gains[1:2]
    params = (
        conv_weight, conv_bias[None], shared_conv, shared_bias[None], head_rows,
        jnp.repeat(skip_gain, head_width)[None],
    )

    both = (0, 1)


    first, near, alone, info, row_info, cosine, sine, params = together(
        first, near, alone, info, row_info, cosine, sine, params
    )
    middle = gather_middle(block, first)
    gains = jnp.concatenate([gains, gains_far], axis=1)
    out_blocks = cut_out(flags, mamba_out_proj, attn_out_proj)
    rest_sent = cut_rest(flags, *rests, DISTANCES[1::2], share, True)
    rest_kept = cut_rest(flags, *rests, DISTANCES[::2], width, False)
    middle, far, common_far, out_blocks, rest_sent, rest_kept = together(
        middle, far, common_far, out_blocks, rest_sent, rest_kept
    )
    both_far = col_swap(jnp.concatenate([far[1:], common_far], axis=2), 1)
    out_fetched = far_pair(out_blocks)
    gains = jnp.concatenate([gains, col_swap(gains, 1)], axis=1)
    gain1, gain2 = gains[0:1], gains[1:2]
    token_own, token_other = gather_end(block, first, middle)
    both_far, gain1, gain2, token_other = together(both_far, gain1, gain2, token_other)
    weight_first = pack_first(
        [
            (alone, 0, 0), (common, 0, 0), (far, 0, 0), (common_far, 0, 0),
            (near, 0, 0), (near, 0, lone), (both_far, 0, 0), (both_far, 0, lone),
        ],
        places, at_step + LANES,
    )

    both = (0, 1)
    normed1, factor1, raw, step_raw, mixed, combined, states = [[None, None] for _ in range(7)]

    def project(s, pieces):
        normed1[s], factor1[s], raw[s], step_raw[s] = tiled_call(
            project_kernel, "project", pieces, [(gain1, True), (weight_first, True)],
            [(model, low), (LANES, wide), (at_step, low), (LANES, wide)],
        )
        return attention_forward(raw[s], places, cosine[s], sine[s], info[s], row_info[s])

    def mamba(s, attended):
        mixed[s], combined[s], states[s] = mamba_forward(
            raw[s], places, step_raw[s], info[s], row_info[s], params, attended, head_width
        )

    cot_y = row_swap(after(cotangent, weight_first))
    attended = project(1, token_other)
    attended, out_fetched, cot_y = together(attended, out_fetched, cot_y)
    out_passed = near_pair(out_blocks, out_fetched)
    fetched = col_swap(after(rest_sent, out_fetched), 2)
    mamba(1, attended)
    mixed[1], out_passed, fetched = together(mixed[1], out_passed, fetched)
    cot_col = lax.all_gather(after(cotangent, fetched), "col", axis=0)
    rest_far = along_line(fetched)
    weight_out = pack_out(out_blocks, out_fetched, out_passed)
    near, far = spread([mixed[1]], weight_out, width, False)
    far = col_swap(far, 1)
    near, far, token_own = together(near, far, token_own)
    rest_near = col_swap(rest_kept[1:], 1)
    top_near, top_far, low_send = fold(near, far, False)
    low_got, other_got = row_swap(low_send), col_swap(top_far, 2)
    attended = project(0, after(token_own, low_send))
    attended, low_got, other_got, rest_near = together(attended, low_got, other_got, rest_near)
    top_last = row_swap(add_low(top_near, other_got))
    mamba(0, attended)
    mixed[0], top_last = together(mixed[0], top_last)
    near, far = spread([mixed[0]], weight_out, width, False)
    far = col_swap(far, 1)
    near, far, cot_col = together(near, far, cot_col)
    own = fold(near, far, True)
    low_sent = add_low(own[3], low_got[1])
    own_got, low_last = col_swap(own[1], 2), col_swap(low_sent, 2)
    cot_xy = row_swap(pick_at(flags, after(cot_col, low_sent), 2))
    own_got, low_last, cot_xy = together(own_got, low_last, cot_xy)
    hidden1, block = sum_quarters(tokens, own, low_got, own_got, top_last, low_last)
    block, hidden1, rest_far = together(block, hidden1, rest_far)
    first = gather_start(block)
    rest_both = col_swap(rest_far[1:], 1)
    cot_cores = [col_swap(cot_y, 1), col_swap(cot_xy, 1)]
    weight_in, weight_down = pack_rest(
        [(rest_kept, 0), (rest_far, 0), (rest_near, 0), (rest_both, 0)], width
    )
    cot, grad_hidden = [None, None], [None, None]
    cot[0], grad_hidden[0] = meet_gathered(flags, cot_col, weight_down)
    first, weight_in, weight_down, cot_cores, cot[0], grad_hidden[0] = together(
        first, weight_in, weight_down, cot_cores, cot[0], grad_hidden[0]
    )
    middle = gather_middle(block, first)
    cot[1], grad_hidden[1] = tiled_call(
        meet_kernel, "meet_cotangent", [cot_y, cot_xy, *cot_cores], [(weight_down, True)],
        [(model, low), (units, wide)],
    )
    middle, cot, grad_hidden = together(middle, cot, grad_hidden)
    pieces = gather_end(block, first, middle)
    normed2, factor2, hidden, grad_in, inner = [[None, None] for _ in range(5)]

    def feed_forward(s, pieces):
        normed2[s], factor2[s], hidden[s], grad_in[s], products = tiled_call(
            ffn_kernel, "ffn", pieces, [(gain2, True), (weight_in, True), (grad_hidden[s], False)],
            [(model, low), (LANES, wide), (units, low), (2 * units, low), (LANES, wide)],
        )
        inner[s] = jnp.sum(products, axis=1).reshape(length // LANES, LANES)

    def piece_index(i, f):
        return (slot_of(f, i), 0, 0)

    def row_index_map(i, f):
        return (i, 0)

    def column_index_map(i, f):
        return (0, i)

    every = slice(None)
    line = LineSums(flags)
    feed_forward(1, pieces[1])
    near, far = spread([grad_in[1]], weight_in, width, True)
    far = col_swap(far, 1)
    feed_forward(0, after(pieces[0], near))
    near, far, hidden, inner, grad_in = together(near, far, hidden, inner, grad_in)
    top_near, top_far, low_send = fold(near, far, False)
    low_got, other_got = row_swap(low_send), col_swap(top_far, 2)
    inner_row = row_swap(inner[1])
    near, far = spread([after(grad_in[0], low_send)], weight_in, width, True)
    far = col_swap(far, 1)
    near, far = together(near, far)
    own = fold(near, far, True)
    own_got = col_swap(own[1], 2)
    down = weight_grad(after(hidden, own), cot, width)
    low_got, other_got, inner_row, down, own = together(low_got, other_got, inner_row, down, own)
    top_last = row_swap(add_low(top_near, other_got))
    low_last = col_swap(add_low(own[3], low_got[1]), 2)
    inner = inner[0] + inner_row
    inner_core = col_swap(inner, 1)
    line.advance(down)
    gate = weight_grad(after(normed2, line.sent), grad_in, width, 0, [units])
    up = weight_grad(after(normed2, gate), grad_in, width, 1, [units])
    top_last, low_last, own_got, inner_core, up, gate = together(
        top_last, low_last, own_got, inner_core, up, gate
    )
    inner = inner + inner_core
    inner = inner + col_swap(inner, 2)
    inner2 = inner.reshape(length, 1)
    grad_normed2 = own_sum(own, low_got, own_got, top_last, low_last)
    own_factor = factor2[0][:, :1]
    back2 = (
        own_factor * norm2_gain * grad_normed2
        - hidden1 * (own_factor * own_factor * inner2 / model)
    )
    grad_gain2 = jnp.sum(grad_normed2 * hidden1 * own_factor, axis=0)
    grad_hidden1 = cotangent.astype(wide) + back2
    block, grad_hidden1, grad_gain2 = together(grad_hidden1.astype(low), grad_hidden1, grad_gain2)
    first = gather_start(block)
    output_shares = [spread([after(hidden[s], block)], weight_down, width, False) for s in both]
    first, output_shares, line.flying = together(first, output_shares, line.flying)
    line.advance(gate)
    middle = together(*gather_middle(block, first))
    pieces = gather_end(block, first, middle)
    output_far = [col_swap(output_shares[s][1], 1) for s in both]
    mix_grad, grad_mixed = [None, None], [None, None]
    for s in both:
        mix_grad[s], grad_mixed[s] = tiled_call(
            meet_kernel, "meet_mixed", pieces[s], [(weight_out, True)],
            [(model, low), (channels + query_width, low)],
        )
    out = weight_grad(mixed, mix_grad, width)
    early, late, sums, products, inner = [[None, None] for _ in range(5)]

    def mamba_step(s, *earlier):
        late[s], inner[s], sums[s] = mamba_backward(
            raw[s], places, step_raw[s], info[s], row_info[s], params, states[s],
            after(grad_mixed[s], *earlier), head_width,
        )

    for s in both:
        early[s], products[s] = attention_backward(
            raw[s], places, cosine[s], sine[s], info[s], row_info[s], combined[s],
            after(grad_mixed[s], out),
        )
    out, grad_mixed, early, output_far, line.flying = together(out, grad_mixed, early, output_far, line.flying)
    line.advance(up)
    output_other = add_low(output_shares[1][0], output_far[1])
    output_got = row_swap(output_other)
    early = after(early, line.sent, output_other)
    first = weight_grad(normed1, early, width, 0, [at_shared])
    first_far = far_pair(first)
    mamba_step(1, first)
    late[1], output_got, output_near, first_far, line.flying = together(
        late[1], output_got, output_far[0], first_far, line.flying
    )
    line.advance(out)
    first_near = near_pair(first, first_far)
    output_sent = add_three(output_shares[0][0], output_near, output_got, 1)
    output_last = col_swap(output_sent, 2)
    down = line.done[0]
    down_sent = pick_chosen(flags, down, (1, 3))
    down_far = col_swap(down_sent, 2)
    mamba_step(0, line.sent, output_sent, down_sent)
    shared, last = weight_grad(normed1, late, width, 0, [2 * part, channels + LANES])
    shared, last, late, sums, inner, output_last, down_far, first_near, line.flying = together(
        shared, last, late, sums, inner, output_last, down_far, first_near, line.flying
    )
    shared_keep, shared_send = row_halves(flags, shared)
    shared_got = row_swap(shared_send)
    last_far = far_pair(last)
    down_near = near_of_sum(flags, down, down_far)
    first, common_sum = collect_early(first, first_far, first_near, places)
    line.advance(first)
    small_rows = length // width
    inner = [
        jnp.sum(inner[s] + products[s], axis=1).reshape(small_rows, width) for s in both
    ]
    small = jnp.concatenate(
        [(sums[0] + sums[1])[:13], grad_gain2[None], inner[0], inner[1], jnp.zeros((14, width), wide)],
        axis=0,
    )[:24]
    rank = jnp.arange(24)[:, None]
    taps = conv_weight.shape[0]
    is_shared = (rank > taps) & (rank < 2 * taps + 2)
    is_inner = (rank >= 14) & (rank < 14 + small_rows)
    is_gain = rank == 13
    last_far, shared_got, small, down_near = together(last_far, shared_got, small, down_near)
    shared = add_low(shared_keep, shared_got)
    shared_far = far_pair(shared)
    small_got = row_swap(small)
    last_near = near_pair(last, last_far)
    shared_far, last_near, small_got, line.flying = together(shared_far, last_near, small_got, line.flying)
    shared_near = together(near_pair(shared, shared_far))[0]
    last, step_sum = collect_late(
        (last, last_far, last_near), (shared, shared_far, shared_near), common_sum, channels
    )
    line.advance(last)
    small_other = jnp.concatenate(
        [small_got[:14], small_got[14 + small_rows : 14 + 2 * small_rows], small_got[14 + small_rows :]], axis=0
    )[:24]
    late, small, small_other = after((late, small, small_other), line.sent)
    gate, up = line.done[1], line.done[2]
    gate_far = col_swap(pick_chosen(flags, gate, (1, 3)), 2)
    up_far = col_swap(pick_chosen(flags, up, (1, 3)), 2)
    near, far = spread([early[1], late[1]], weight_first, width, True)
    own_near, own_far = spread([early[0], after(late[0], near)], weight_first, width, True)
    small = small + jnp.where(is_shared | is_gain | is_inner, small_other, 0.0)
    near, far, own_near, own_far, small, gate_far, up_far, line.flying = together(
        near, far, own_near, own_far, small, gate_far, up_far, line.flying
    )
    line.advance()
    far, own_far, small = after((far, own_far, small), line.sent)
    far, own_far, small_got = together(col_swap(far, 1), col_swap(own_far, 1), col_swap(small, 1))
    top_near, top_far, low_send = fold(near, far, False)
    low_got, other_got = row_swap(low_send), col_swap(top_far, 2)
    own = fold(own_near, own_far, True)
    own_got = col_swap(own[1], 2)
    small = small + jnp.where(is_shared | is_inner, small_got, 0.0)
    small_got = col_swap(small, 2)
    gate_near = near_of_sum(flags, gate, gate_far)
    up_near = near_of_sum(flags, up, up_far)
    low_got, other_got, own_got, small_got, gate_near, up_near, line.flying = together(
        low_got, other_got, own_got, small_got, gate_near, up_near, line.flying
    )
    line.advance()
    low_got, other_got, small, small_got = after((low_got, other_got, small, small_got), line.sent)
    top_last = row_swap(add_low(top_near, other_got))
    low_last = col_swap(add_low(own[3], low_got[1]), 2)
    out = line.done[3]
    out_far = col_swap(pick_chosen(flags, out, (1, 3)), 2)
    small = small + jnp.where(is_shared | is_inner, small_got, 0.0)
    total, final = line.done[4]
    alone = query_width + channels
    d_query, d_gate = finalize(
        flags, total, final, (None, width, alone), piece_index,
        [
            (proj_query.shape, (width, query_width), column_index_map, every, slice(0, query_width)),
            (proj_gate.shape, (width, channels), column_index_map, every, slice(query_width, None)),
        ],
    )
    (d_ffn_down,) = finalize_blocks(
        flags, pick_chosen(flags, down, (0,)), down_far, down_near,
        [(ffn_down.shape, (units, width), row_index_map, every, every)],
    )
    (d_ffn_gate,) = finalize_blocks(
        flags, pick_chosen(flags, gate, (0,)), gate_far, gate_near,
        [(ffn_gate.shape, (width, units), column_index_map, every, every)],
    )
    (d_ffn_up,) = finalize_blocks(
        flags, pick_chosen(flags, up, (0,)), up_far, up_near,
        [(ffn_up.shape, (width, units), column_index_map, every, every)],
    )
    output = (
        hidden1 + output_shares[0][0][0].astype(wide) + output_near[0].astype(wide)
        + output_got[0].astype(wide) + output_last.astype(wide)
    ).astype(low)
    top_last, low_last, out_far, d_query, d_gate, d_ffn_down, d_ffn_gate, d_ffn_up, output = together(
        top_last, low_last, out_far, d_query, d_gate, d_ffn_down, d_ffn_gate, d_ffn_up, output
    )
    out_near = near_of_sum(flags, out, out_far)
    inner1 = small[14 : 14 + small_rows].reshape(length, 1)
    grad_normed1 = own_sum(own, low_got, own_got, top_last, low_last)
    own_factor = factor1[0][:, :1]
    own_tokens = tokens.astype(wide)
    back1 = (
        own_factor * norm1_gain * grad_normed1
        - own_tokens * (own_factor * own_factor * inner1 / model)
    )
    grad_gain1 = jnp.sum(grad_normed1 * own_tokens * own_factor, axis=0)
    tokens_grad = (grad_hidden1 + back1).astype(low)
    gain_got = row_swap(grad_gain1[None])
    out_near, tokens_grad = together(out_near, tokens_grad)
    d_mamba_out, d_attn_out = finalize_blocks(
        flags, pick_chosen(flags, out, (0,)), out_far, out_near,
        [
            (mamba_out_proj.shape, (channels, width), row_index_map, slice(0, channels), every),
            (attn_out_proj.shape, (query_width, width), row_index_map, slice(channels, None), every),
        ],
    )
    tokens_grad, gain_got, d_mamba_out, d_attn_out, line.flying = together(
        tokens_grad, gain_got, d_mamba_out, d_attn_out, line.flying
    )
    small = jnp.concatenate(
        [
            small[:14], grad_gain1[None] + gain_got, jnp.zeros((1, width), wide),
            jnp.transpose(step_sum)[: 4 * 8],
        ],
        axis=0,
    )
    small_got = dp_part(small, 1)
    line.finish()
    total, final = line.done[5]
    (d_conv,) = finalize(
        flags, total, final, (None, width, channels + part // 2), piece_index,
        [(proj_conv.shape, (width, channels), column_index_map, every, slice(0, channels))],
    )
    small_got, d_conv = together(small_got, d_conv)
    sums = dp_rest(small + small_got)
    extra = jnp.where(flags[1] == 1, total[:, :, channels:], final[:, :, channels:]).astype(wide)
    d_shared = jnp.concatenate([extra[0], extra[1]], axis=1)
    d_key, d_value = extra[2], extra[3]
    step_sum = jnp.stack([sums[16 + p * 8 : 16 + p * 8 + steps] for p in (0, 2, 1, 3)])
    d_step = jnp.transpose(
        jnp.concatenate([lax.dynamic_index_in_dim(step_sum, me ^ d, 0, keepdims=False) for d in range(4)])
    )
    return (
        output, tokens_grad, sums[14], d_gate, d_conv, d_step, d_shared, d_query, d_key, d_value,
        sums[:taps, :channels], sums[taps, :channels], sums[taps + 1 : 2 * taps + 1],
        sums[2 * taps + 1],
        sums[11, :steps], sums[12, :steps],
        jnp.sum(sums[10, :channels].reshape(steps, head_width), axis=1),
        d_mamba_out, d_attn_out, sums[13], d_ffn_gate, d_ffn_up, d_ffn_down,
    )


def solution(mesh):
    return jax.shard_map(
        on_device,
        mesh=mesh,
        in_specs=(
            P(("dp", "row"), "col"),
            P(("dp", "row"), "col"),
            P("dp", None),
            P("col"),
            P("col", "row"),
            P("col", "row"),
            P("col", "row"),
            P("col", "row"),
            P("col", "row"),
            P("col", "row"),
            P("col", "row"),
            P(None, ("row", "col")),
            P(("row", "col")),
            P(),
            P(),
            P(("row", "col")),
            P(("row", "col")),
            P(("row", "col")),
            P("row", "col"),
            P("row", "col"),
            P("col"),
            P("col", "row"),
            P("col", "row"),
            P("row", "col"),
        ),
        out_specs=(
            P(("dp", "row"), "col"),
            P(("dp", "row"), "col"),
            P("col"),
            P("col", "row"),
            P("col", "row"),
            P("col", "row"),
            P("col", "row"),
            P("col", "row"),
            P("col", "row"),
            P("col", "row"),
            P(None, ("row", "col")),
            P(("row", "col")),
            P(),
            P(),
            P(("row", "col")),
            P(("row", "col")),
            P(("row", "col")),
            P("row", "col"),
            P("row", "col"),
            P("col"),
            P("col", "row"),
            P("col", "row"),
            P("row", "col"),
        ),
        check_vma=False,
    )
```

```python
from functools import partial
import math
from typing import NamedTuple

import jax
import jax.numpy as jnp
from jax import lax
from jax.experimental import pallas as pl
from jax.experimental.pallas import tpu as pltpu
from jax.sharding import PartitionSpec as P

EPS = 1e-05
ROPE_BASE = 100000000000.0
MASKED = -1e30
HIGHEST = lax.Precision.HIGHEST
DISTANCES = (0, 2, 1, 3)
LANES = 128
CHUNK = 128
TAIL = 8


class Places(NamedTuple):
    query: int
    key: int
    gate: int
    value: int
    shared: int
    conv: int
    step: int


def dot_any(former, latter, dims, precision=None):
    return lax.dot_general(
        former, latter, (dims, ((), ())), precision=precision, preferred_element_type=jnp.float32
    )


def nn(former, latter):
    return dot_any(former, latter, ((1,), (0,)))


def nt(former, latter):
    return dot_any(former, latter, ((1,), (1,)))


def tn(former, latter):
    return dot_any(former, latter, ((0,), (0,)))


def low_terms(values, count):
    terms = []
    for _ in range(count):
        term = values.astype(jnp.bfloat16)
        values = values - term.astype(jnp.float32)
        terms.append(term)
    return terms


def times_marks(values, marks, count):
    return sum(nn(term, marks) for term in low_terms(values, count))


def marks_times(marks, values, count):
    return sum(nn(marks, term) for term in low_terms(values, count))


def sigmoid_of(values):
    return 1.0 / (1.0 + jnp.exp(-values))


def softplus_of(values):
    return jnp.maximum(values, 0.0) + jnp.log1p(jnp.exp(-jnp.abs(values)))


def head_spread(head_width, width):
    heads = lax.broadcasted_iota(jnp.int32, (LANES, width), 0)
    columns = lax.broadcasted_iota(jnp.int32, (LANES, width), 1)
    return (columns // head_width == heads).astype(jnp.bfloat16)


def head_gather(head_width, width):
    columns = lax.broadcasted_iota(jnp.int32, (width, LANES), 0)
    heads = lax.broadcasted_iota(jnp.int32, (width, LANES), 1)
    return (columns // head_width == heads).astype(jnp.bfloat16)


def causal_conv(ext_ref, columns, weight_ref, bias_ref, position, taps):
    length = ext_ref.shape[0] - TAIL
    running = bias_ref[...] + weight_ref[taps - 1 : taps, :] * ext_ref[TAIL:, columns]
    for offset in range(1, taps):
        earlier = ext_ref[TAIL - offset : TAIL - offset + length, columns]
        running = running + weight_ref[taps - 1 - offset : taps - offset, :] * jnp.where(
            position >= offset, earlier, 0.0
        )
    return running


def chunk_decay(step_in, position, decay_rate):
    length = step_in.shape[0]
    step_size = softplus_of(step_in)
    log_decay = jnp.where(position == 0.0, 0.0, -step_size * decay_rate)
    rows = lax.broadcasted_iota(jnp.int32, (length, length), 0)
    columns = lax.broadcasted_iota(jnp.int32, (length, length), 1)
    causal = rows >= columns
    running = marks_times(causal.astype(jnp.bfloat16), log_decay, 3)
    return step_size, log_decay, running, jnp.transpose(running), causal


def split_pair(values, head_width):
    lane = lax.broadcasted_iota(jnp.int32, values.shape, 1)
    zero = jnp.zeros_like(values)
    return jnp.concatenate(
        [jnp.where(lane < head_width, values, zero), jnp.where(lane < head_width, zero, values)],
        axis=0,
    )


def mamba_forward_kernel(
    raw_ref, step_ref, info_ref, row_ref, weight_ref, bias_ref,
    shared_weight_ref, shared_bias_ref, head_ref, skip_ref, attended_ref,
    mixed_ref, combined_ref, states_ref,
    state, ext, *, head_width, places
):
    chunk = pl.program_id(0)
    length, width = combined_ref.shape
    gate_columns = slice(places.gate, places.value)
    conv_columns = slice(places.conv, places.step)
    shared_columns = slice(places.shared, places.conv)
    states = (places.conv - places.shared) // 2
    taps = weight_ref.shape[0]
    low = jnp.bfloat16

    @pl.when(chunk == 0)
    def _():
        state[...] = jnp.zeros_like(state)
        ext[...] = jnp.zeros_like(ext)

    ext[:TAIL, :] = ext[length : length + TAIL, :]
    ext[TAIL:, :width] = raw_ref[:, conv_columns].astype(jnp.float32)
    ext[TAIL:, width:] = raw_ref[:, shared_columns].astype(jnp.float32)
    segment = info_ref[:, 0:1]
    position = info_ref[:, 1:2]
    pre = causal_conv(ext, slice(0, width), weight_ref, bias_ref, position, taps)
    conv_out = pre * sigmoid_of(pre)
    pre = causal_conv(
        ext, slice(width, None), shared_weight_ref, shared_bias_ref, position, taps
    )
    shared = (pre * sigmoid_of(pre)).astype(low)
    b_map = shared[:, :states]
    c_map = shared[:, states:]
    step_size, _, running, running_t, causal = chunk_decay(
        step_ref[...] + head_ref[0:1, :], position, head_ref[1:2, :]
    )
    segment_row = row_ref[0:1, :]
    allowed = causal & (segment == segment_row)
    local = lax.broadcasted_iota(jnp.int32, (length, 1), 0).astype(jnp.float32)
    enters = jnp.where(position > local, jnp.exp(running), 0.0)
    last = running[length - 1 : length, :]
    leaves = jnp.where(segment == segment_row[:, length - 1 :], jnp.exp(last - running), 0.0)
    spread = head_spread(head_width, width)
    wide = times_marks(jnp.concatenate([step_size, enters, leaves], axis=0), spread, 2)
    weighted = conv_out * wide[:length]
    gram = nt(c_map, b_map)
    weighted_low = weighted.astype(low)
    parts = []
    for pair in range(width // (2 * head_width)):
        weights = []
        for head in (2 * pair, 2 * pair + 1):
            gap = jnp.where(allowed, running[:, head : head + 1] - running_t[head : head + 1, :], MASKED)
            weights.append((gram * jnp.exp(gap)).astype(low))
        columns = slice(2 * pair * head_width, 2 * (pair + 1) * head_width)
        parts.append(
            nn(jnp.concatenate(weights, axis=1), split_pair(weighted_low[:, columns], head_width))
        )
    held = state[...]
    held_low = held.astype(low)
    states_ref[...] = held_low
    scanned = jnp.concatenate(parts, axis=1) + nn(c_map, held_low) * wide[length : 2 * length]
    fade = wide[2 * length - 1 : 2 * length]
    state[...] = held * fade + tn(b_map, (weighted * wide[2 * length :]).astype(low))
    combined = scanned + skip_ref[...] * conv_out
    combined_ref[...] = combined.astype(low)
    gate = raw_ref[:, gate_columns].astype(jnp.float32)
    mixed_ref[:, :width] = (combined * (gate * sigmoid_of(gate))).astype(low)
    mixed_ref[:, width:] = attended_ref[...]


def mamba_backward_kernel(
    raw_ref, tail_ref, step_ref, info_ref, row_ref, weight_ref, bias_ref,
    shared_weight_ref, shared_bias_ref, head_ref, skip_ref, states_ref, grad_ref,
    out_ref, inner_ref, sums_ref,
    grad_state, ext, ext_grad, *, head_width, places
):
    count = pl.num_programs(0)
    step = pl.program_id(0)
    length = grad_ref.shape[0]
    width = places.step - places.conv
    states = (places.conv - places.shared) // 2
    taps = weight_ref.shape[0]
    low = jnp.bfloat16
    f32 = jnp.float32
    gate_columns = slice(places.gate, places.value)
    conv_columns = slice(places.conv, places.step)
    shared_columns = slice(places.shared, places.conv)

    @pl.when(step == 0)
    def _():
        grad_state[...] = jnp.zeros_like(grad_state)
        ext_grad[...] = jnp.zeros_like(ext_grad)
        sums_ref[...] = jnp.zeros_like(sums_ref)

    tail_at = tail_ref.shape[0] - TAIL
    ext[:TAIL, :width] = tail_ref[:, conv_columns].astype(f32)[tail_at:]
    ext[:TAIL, width:] = tail_ref[:, shared_columns].astype(f32)[tail_at:]
    ext[TAIL:, :width] = raw_ref[:, conv_columns].astype(f32)
    ext[TAIL:, width:] = raw_ref[:, shared_columns].astype(f32)
    segment = info_ref[:, 0:1]
    position = info_ref[:, 1:2]
    remaining = info_ref[:, 2:3]
    pre = causal_conv(ext, slice(0, width), weight_ref, bias_ref, position, taps)
    sig = sigmoid_of(pre)
    conv_out = pre * sig
    conv_slope = sig * (1.0 + pre * (1.0 - sig))
    pre = causal_conv(
        ext, slice(width, None), shared_weight_ref, shared_bias_ref, position, taps
    )
    sig = sigmoid_of(pre)
    shared = (pre * sig).astype(low)
    shared_slope = sig * (1.0 + pre * (1.0 - sig))
    b_map = shared[:, :states]
    c_map = shared[:, states:]
    step_in = step_ref[...] + head_ref[0:1, :]
    rate = head_ref[1:2, :]
    step_size, log_decay, running, running_t, causal = chunk_decay(step_in, position, rate)
    segment_row = row_ref[0:1, :]
    allowed = causal & (segment == segment_row)
    local = lax.broadcasted_iota(jnp.int32, (length, 1), 0).astype(f32)
    enters = jnp.where(position > local, jnp.exp(running), 0.0)
    last = running[length - 1 : length, :]
    leaves = jnp.where(segment == segment_row[:, length - 1 :], jnp.exp(last - running), 0.0)
    spread = head_spread(head_width, width)
    wide = times_marks(jnp.concatenate([step_size, enters, leaves], axis=0), spread, 2)
    step_wide = wide[:length]
    enters_wide = wide[length : 2 * length]
    leaves_wide = wide[2 * length :]
    fade = wide[2 * length - 1 : 2 * length]
    weighted = conv_out * step_wide

    gate = raw_ref[:, gate_columns].astype(f32)
    sig = sigmoid_of(gate)
    grad_scan = grad_ref[:, :width].astype(f32) * (gate * sig)

    gram = nt(c_map, b_map)
    weighted_low = weighted.astype(low)
    grad_low = grad_scan.astype(low)
    lane = lax.broadcasted_iota(jnp.int32, (length, LANES), 1)
    sub = lax.broadcasted_iota(jnp.int32, (LANES, length), 0)
    grad_gram = jnp.zeros((length, length), f32)
    by_row = jnp.zeros((length, LANES), f32)
    by_column = jnp.zeros((LANES, length), f32)
    parts = []
    for pair in range(width // (2 * head_width)):
        columns = slice(2 * pair * head_width, 2 * (pair + 1) * head_width)
        split_grad = split_pair(grad_low[:, columns], head_width)
        products = nt(split_grad, weighted_low[:, columns])
        weights = []
        for place, head in enumerate((2 * pair, 2 * pair + 1)):
            gap = jnp.where(allowed, running[:, head : head + 1] - running_t[head : head + 1, :], MASKED)
            fading = jnp.exp(gap)
            weight = gram * fading
            product = products[place * length : (place + 1) * length]
            grad_gram = grad_gram + fading * product
            meeting = weight * product
            by_row = jnp.where(lane == head, jnp.sum(meeting, axis=1, keepdims=True), by_row)
            by_column = jnp.where(sub == head, jnp.sum(meeting, axis=0, keepdims=True), by_column)
            weights.append(weight.astype(low))
        parts.append(tn(jnp.concatenate(weights, axis=0), split_grad))
    held = states_ref[...]
    entering = (grad_scan * enters_wide).astype(low)
    leaving = (weighted * leaves_wide).astype(low)
    grad_held = grad_state[...]
    grad_held_low = grad_held.astype(low)
    from_state = nn(b_map, grad_held_low) * leaves_wide
    grad_weighted = jnp.concatenate(parts, axis=1) + from_state
    grad_gram_low = grad_gram.astype(low)
    grad_c = nn(grad_gram_low, b_map) + nt(entering, held)
    grad_b = tn(grad_gram_low, c_map) + nt(leaving, grad_held_low)
    met_in = grad_scan * enters_wide * nn(c_map, held)
    met_out = weighted * from_state
    met_state = fade * jnp.sum(held.astype(f32) * grad_held, axis=0, keepdims=True)
    grad_state[...] = grad_held * fade + tn(c_map, entering)
    grad_conv_out = grad_weighted * step_wide + skip_ref[...] * grad_scan
    gathered = times_marks(
        jnp.concatenate(
            [met_in, met_out, conv_out * grad_weighted, jnp.broadcast_to(met_state, (TAIL, width))],
            axis=0,
        ),
        head_gather(head_width, width),
        2,
    )
    out_rows = gathered[length : 2 * length]
    at_last = jnp.sum(out_rows, axis=0, keepdims=True) + gathered[3 * length : 3 * length + 1]
    grad_running = by_row - jnp.transpose(by_column) + gathered[:length] - out_rows
    grad_running = grad_running + jnp.where(local == length - 1.0, at_last, 0.0)
    rows = lax.broadcasted_iota(jnp.int32, (length, length), 0)
    later = lax.broadcasted_iota(jnp.int32, (length, length), 1) >= rows
    grad_decay = jnp.where(position == 0.0, 0.0, marks_times(later.astype(low), grad_running, 3))
    grad_step = (gathered[2 * length : 3 * length] - grad_decay * rate) * sigmoid_of(step_in)

    ext_grad[length : length + TAIL, :] = ext_grad[:TAIL, :]
    ext_grad[:length, :width] = grad_conv_out * conv_slope
    ext_grad[:length, width : width + states] = grad_b * shared_slope[:, :states]
    ext_grad[:length, width + states :] = grad_c * shared_slope[:, states:]

    def conv_back(columns, weights, row_at):
        now = ext_grad[:length, columns]
        running = weights[taps - 1 : taps, :] * now
        wide_columns = slice(0, now.shape[1])
        sums_ref[row_at + taps : row_at + taps + 1, wide_columns] += jnp.sum(now, axis=0, keepdims=True)
        sums_ref[row_at + taps - 1 : row_at + taps, wide_columns] += jnp.sum(
            now * ext[TAIL:, columns], axis=0, keepdims=True
        )
        for offset in range(1, taps):
            at = taps - 1 - offset
            running = running + weights[at : at + 1, :] * jnp.where(
                remaining >= offset, ext_grad[offset : offset + length, columns], 0.0
            )
            earlier = jnp.where(
                position >= offset, ext[TAIL - offset : TAIL - offset + length, columns], 0.0
            )
            sums_ref[row_at + at : row_at + at + 1, wide_columns] += jnp.sum(
                now * earlier, axis=0, keepdims=True
            )
        return running

    grad_conv = conv_back(slice(0, width), weight_ref, 0).astype(low)
    grad_shared = conv_back(slice(width, None), shared_weight_ref, taps + 1).astype(low)
    row_at = 2 * (taps + 1)
    sums_ref[row_at : row_at + 1, :width] += jnp.sum(grad_scan * conv_out, axis=0, keepdims=True)
    sums_ref[row_at + 1 : row_at + 2, :LANES] += jnp.sum(grad_step, axis=0, keepdims=True)
    sums_ref[row_at + 2 : row_at + 3, :LANES] += jnp.sum(
        grad_decay * log_decay, axis=0, keepdims=True
    )
    grad_step = grad_step.astype(low)
    out_ref[:, : 2 * states] = grad_shared
    out_ref[:, 2 * states : 2 * states + width] = grad_conv
    out_ref[:, 2 * states + width :] = grad_step
    inner = grad_step.astype(f32) * step_ref[...]
    for at in range(0, places.step - places.shared, LANES):
        raw = raw_ref[:, places.shared + at : places.shared + at + LANES]
        inner = inner + out_ref[:, at : at + LANES].astype(f32) * raw.astype(f32)
    inner_ref[...] = inner


def rope(values, cosine, sine):
    return values * cosine + pltpu.roll(values, values.shape[1] // 2, 1) * sine


def attention_rows(query, key, begin, size, info_ref, row_ref, factor):
    seen = begin + size
    scores = nt(query, key) * factor
    rows = begin + lax.broadcasted_iota(jnp.int32, (size, seen), 0)
    columns = lax.broadcasted_iota(jnp.int32, (size, seen), 1)
    allowed = (rows >= columns) & (info_ref[begin:seen, 0:1] == row_ref[0:1, :seen])
    scores = jnp.where(allowed, scores, MASKED)
    raised = jnp.exp(scores - jnp.max(scores, axis=1, keepdims=True))
    return raised * (1.0 / jnp.sum(raised, axis=1, keepdims=True))


def attention_forward_kernel(
    query_ref, key_ref, value_ref, cosine_ref, sine_ref, info_ref, row_ref, out_ref, *, block
):
    low = jnp.bfloat16
    length, head_dim = query_ref.shape
    factor = 1.0 / math.sqrt(head_dim)
    cosine, sine = cosine_ref[...], sine_ref[...]
    query = rope(query_ref[...].astype(jnp.float32), cosine, sine).astype(low)
    key = rope(key_ref[...].astype(jnp.float32), cosine, sine).astype(low)
    value = value_ref[...]
    for begin in range(0, length, block):
        seen = begin + block
        probs = attention_rows(
            query[begin:seen], key[:seen], begin, block, info_ref, row_ref, factor
        )
        out_ref[begin:seen, :] = nn(probs.astype(low), value[:seen]).astype(low)


def attention_backward_kernel(
    raw_ref, cosine_ref, sine_ref, info_ref, row_ref, combined_ref, grad_ref,
    out_ref, inner_ref, key_total, value_total, *, block, places
):
    low = jnp.bfloat16
    length, head_dim = cosine_ref.shape
    channels = combined_ref.shape[1]
    factor = 1.0 / math.sqrt(head_dim)
    cosine, sine = cosine_ref[...], sine_ref[...]
    query = rope(raw_ref[:, : places.key].astype(jnp.float32), cosine, sine).astype(low)
    key = rope(raw_ref[:, places.key : places.gate].astype(jnp.float32), cosine, sine).astype(low)
    value = raw_ref[:, places.value : places.shared]
    key_total[...] = jnp.zeros_like(key_total)
    value_total[...] = jnp.zeros_like(value_total)
    for begin in range(0, length, block):
        seen = begin + block
        probs = attention_rows(
            query[begin:seen], key[:seen], begin, block, info_ref, row_ref, factor
        )
        grad_out = grad_ref[begin:seen, channels:]
        gate = raw_ref[begin:seen, places.gate : places.value].astype(jnp.float32)
        sig = sigmoid_of(gate)
        out_ref[begin:seen, places.gate : places.value] = (
            grad_ref[begin:seen, :channels].astype(jnp.float32)
            * combined_ref[begin:seen, :].astype(jnp.float32)
            * (sig * (1.0 + gate * (1.0 - sig)))
        ).astype(low)
        grad_probs = nt(grad_out, value[:seen])
        inner = jnp.sum(probs * grad_probs, axis=1, keepdims=True)
        grad_scores = (probs * (grad_probs - inner)).astype(low)
        grad_query = nn(grad_scores, key[:seen]) * factor
        out_ref[begin:seen, : places.key] = rope(
            grad_query, cosine[begin:seen], -sine[begin:seen]
        ).astype(low)
        key_total[:seen, :] += tn(grad_scores, query[begin:seen])
        value_total[:seen, :] += tn(probs.astype(low), grad_out)
    out_ref[:, places.key : places.gate] = rope(key_total[...] * factor, cosine, -sine).astype(low)
    out_ref[:, places.value :] = value_total[...].astype(low)
    inner = jnp.zeros(inner_ref.shape, jnp.float32)
    for at in range(0, places.shared, LANES):
        span = slice(at, at + LANES)
        inner = inner + out_ref[:, span].astype(jnp.float32) * raw_ref[:, span].astype(jnp.float32)
    inner_ref[...] = inner


BRIEF = pl.CostEstimate(flops=1, bytes_accessed=1, transcendentals=0)


def whole(shape):
    return pl.BlockSpec(shape, lambda i: (0,) * len(shape))


def limits(megabytes):
    return pltpu.CompilerParams(vmem_limit_bytes=megabytes * 1024 * 1024)


def column_block(rows, width, at):
    return pl.BlockSpec((rows, width), lambda i: (0, at // width))


def attention_forward(raw, places, cosine, sine, info, row):
    length, width = cosine.shape
    return pl.pallas_call(
        partial(attention_forward_kernel, block=256),
        grid=(1,),
        in_specs=[
            column_block(length, width, places.query),
            column_block(length, width, places.key),
            column_block(length, width, places.value),
            whole(cosine.shape), whole(sine.shape), whole(info.shape), whole(row.shape),
        ],
        out_specs=whole((length, width)),
        out_shape=jax.ShapeDtypeStruct((length, width), jnp.bfloat16),
        compiler_params=limits(48),
        cost_estimate=BRIEF,
        name="attention_forward",
    )(raw, raw, raw, cosine, sine, info, row)


def attention_backward(raw, places, cosine, sine, info, row, combined, grad_mixed):
    length, width = cosine.shape
    return pl.pallas_call(
        partial(attention_backward_kernel, block=256, places=places),
        grid=(1,),
        in_specs=[
            column_block(length, places.shared, 0),
            whole(cosine.shape), whole(sine.shape), whole(info.shape), whole(row.shape),
            whole(combined.shape), whole(grad_mixed.shape),
        ],
        out_specs=[whole((length, places.shared)), whole((length, LANES))],
        out_shape=[
            jax.ShapeDtypeStruct((length, places.shared), jnp.bfloat16),
            jax.ShapeDtypeStruct((length, LANES), jnp.float32),
        ],
        scratch_shapes=[pltpu.VMEM((length, width), jnp.float32)] * 2,
        compiler_params=limits(48),
        cost_estimate=BRIEF,
        name="attention_backward",
    )(raw, cosine, sine, info, row, combined, grad_mixed)


def mamba_forward(raw, places, step_raw, info, row, params, attended, head_width):
    length = raw.shape[0]
    width = places.step - places.conv
    states = (places.conv - places.shared) // 2
    head_dim = attended.shape[1]
    chunks = length // CHUNK

    def block(columns):
        return pl.BlockSpec((CHUNK, columns), lambda i: (i, 0))

    return pl.pallas_call(
        partial(mamba_forward_kernel, head_width=head_width, places=places),
        grid=(chunks,),
        in_specs=[
            block(places.step),
            block(LANES), block(LANES), pl.BlockSpec((8, CHUNK), lambda i: (0, i)),
            *[whole(p.shape) for p in params],
            block(head_dim),
        ],
        out_specs=[
            block(width + head_dim), block(width),
            pl.BlockSpec((None, states, width), lambda i: (i, 0, 0)),
        ],
        out_shape=[
            jax.ShapeDtypeStruct((length, width + head_dim), jnp.bfloat16),
            jax.ShapeDtypeStruct((length, width), jnp.bfloat16),
            jax.ShapeDtypeStruct((chunks, states, width), jnp.bfloat16),
        ],
        scratch_shapes=[
            pltpu.VMEM((states, width), jnp.float32),
            pltpu.VMEM((TAIL + CHUNK, width + 2 * states), jnp.float32),
        ],
        compiler_params=limits(48),
        cost_estimate=BRIEF,
        name="mamba_forward",
    )(raw, step_raw, info, row, *params, attended)


def mamba_backward(raw, places, step_raw, info, row, params, states, grad_mixed, head_width):
    length = raw.shape[0]
    width = places.step - places.conv
    shared = places.conv - places.shared
    chunks = length // CHUNK
    total = places.step + LANES - places.shared
    tail = 16

    def block(columns):
        return pl.BlockSpec((CHUNK, columns), lambda i: (chunks - 1 - i, 0))

    return pl.pallas_call(
        partial(mamba_backward_kernel, head_width=head_width, places=places),
        grid=(chunks,),
        in_specs=[
            block(places.step),
            pl.BlockSpec(
                (tail, places.step),
                lambda i: (jnp.maximum((chunks - 1 - i) * (CHUNK // tail) - 1, 0), 0),
            ),
            block(LANES), block(LANES),
            pl.BlockSpec((8, CHUNK), lambda i: (0, chunks - 1 - i)),
            *[whole(p.shape) for p in params],
            pl.BlockSpec((None, shared // 2, width), lambda i: (chunks - 1 - i, 0, 0)),
            block(grad_mixed.shape[1]),
        ],
        out_specs=[block(total), block(LANES), whole((16, shared))],
        out_shape=[
            jax.ShapeDtypeStruct((length, total), jnp.bfloat16),
            jax.ShapeDtypeStruct((length, LANES), jnp.float32),
            jax.ShapeDtypeStruct((16, shared), jnp.float32),
        ],
        scratch_shapes=[
            pltpu.VMEM((shared // 2, width), jnp.float32),
            pltpu.VMEM((TAIL + CHUNK, width + shared), jnp.float32),
            pltpu.VMEM((TAIL + CHUNK, width + shared), jnp.float32),
        ],
        compiler_params=limits(48),
        cost_estimate=BRIEF,
        name="mamba_backward",
    )(raw, raw, step_raw, info, row, *params, states, grad_mixed)


def matmul(former, latter):
    return jnp.dot(former, latter, preferred_element_type=jnp.float32)


def matmul_left(former, latter):
    return lax.dot_general(
        former, latter, (((0,), (0,)), ((), ())), preferred_element_type=jnp.float32
    )


def matmul_right(former, latter):
    return lax.dot_general(
        former, latter, (((1,), (1,)), ((), ())), preferred_element_type=jnp.float32
    )


def col_swap(values, distance):
    count = lax.axis_size("col")
    return lax.ppermute(values, "col", [(i, i ^ distance) for i in range(count)])


def row_swap(values):
    return lax.ppermute(values, "row", [(0, 1), (1, 0)])


def together(*values):
    return lax.optimization_barrier(values)


def after(value, *earlier):
    return lax.optimization_barrier((value, earlier))[0]


def gather_start(block):
    return col_swap(block, 2), row_swap(block), col_swap(block, 1)


def gather_middle(block, first):
    along_x, along_y, _ = first
    half = block.shape[0] // 2
    return col_swap(along_y[:half], 2), row_swap(along_x[half:]), col_swap(along_x, 1), col_swap(along_y, 1)


def gather_end(block, first, middle):
    along_x, along_y, core = first
    top, low, core_x, core_y = middle
    own = [block, along_x, core, core_x]
    other = [along_y, (top, low), core_y, (col_swap(top, 1), col_swap(low, 1))]
    return own, other


def gather_slow_second(first):
    along_x, along_y, _ = first
    return row_swap(along_x), col_swap(along_x, 1), col_swap(along_y, 1)


def gather_slow_end(block, first, second):
    along_x, along_y, core = first
    diagonal, core_x, core_y = second
    return [block, along_x, core, core_x], [along_y, diagonal, core_y, col_swap(diagonal, 1)]


def add_kernel(former_ref, latter_ref, out_ref):
    total = former_ref[...].astype(jnp.float32) + latter_ref[...].astype(jnp.float32)
    out_ref[...] = total.astype(out_ref.dtype)


def add_low(former, latter):
    shape = former.shape
    tiles = shape[0] if len(shape) == 3 else 2
    block = (1, *shape[1:]) if len(shape) == 3 else (shape[0] // tiles, shape[1])
    spec = pl.BlockSpec(block, lambda i: (i,) + (0,) * (len(shape) - 1))
    return pl.pallas_call(
        add_kernel,
        grid=(tiles,),
        in_specs=[spec, spec],
        out_specs=spec,
        out_shape=jax.ShapeDtypeStruct(shape, jnp.bfloat16),
        compiler_params=limits(32),
        cost_estimate=BRIEF,
        name="add",
    )(former, latter)


def add_three_kernel(first_ref, second_ref, third_ref, out_ref):
    wide = jnp.float32
    total = first_ref[...].astype(wide) + second_ref[...].astype(wide) + third_ref[...].astype(wide)
    out_ref[...] = total.astype(out_ref.dtype)


def add_three(first, second, third, at):
    _, rows, columns = first.shape
    tiles = 2
    spec = pl.BlockSpec((None, rows // tiles, columns), lambda i: (at, i, 0))
    return pl.pallas_call(
        add_three_kernel,
        grid=(tiles,),
        in_specs=[spec] * 3,
        out_specs=pl.BlockSpec((rows // tiles, columns), lambda i: (i, 0)),
        out_shape=jax.ShapeDtypeStruct((rows, columns), jnp.bfloat16),
        compiler_params=limits(32),
        cost_estimate=BRIEF,
        name="add_three",
    )(first, second, third)


def sum_quarters_kernel(base_ref, *refs):
    (*parts, out_ref, low_ref) = refs
    tops, lows = parts[:3], parts[3:]
    wide = jnp.float32

    def write(pieces):
        total = base_ref[...].astype(wide)
        for piece in pieces:
            total = total + piece[...].astype(wide)
        out_ref[...] = total
        low_ref[...] = total.astype(low_ref.dtype)

    @pl.when(pl.program_id(0) == 0)
    def _():
        write(tops)

    @pl.when(pl.program_id(0) == 1)
    def _():
        write(lows)


def sum_quarters(base, own, low_got, own_got, top_last, low_last):
    tokens, width = base.shape
    half = tokens // 2
    row = pl.BlockSpec((half, width), lambda i: (i, 0))
    part = pl.BlockSpec((half, width), lambda i: (0, 0))
    first = pl.BlockSpec((None, half, width), lambda i: (0, 0, 0))
    return pl.pallas_call(
        sum_quarters_kernel,
        grid=(2,),
        in_specs=[row, part, part, part, part, first, part],
        out_specs=[row, row],
        out_shape=[
            jax.ShapeDtypeStruct((tokens, width), jnp.float32),
            jax.ShapeDtypeStruct((tokens, width), jnp.bfloat16),
        ],
        compiler_params=limits(32),
        cost_estimate=BRIEF,
        name="sum_quarters",
    )(base, own[0], own_got, top_last, own[2], low_got, low_last)


def fold_other_kernel(near_ref, far_ref, top_near_ref, top_far_ref, low_ref):
    half = low_ref.shape[0]
    total = (near_ref[...].astype(jnp.float32) + far_ref[...].astype(jnp.float32)).astype(low_ref.dtype)
    low_ref[...] = total[half:]

    @pl.when(pl.program_id(0) == 0)
    def _():
        top_near_ref[...] = total[:half]

    @pl.when(pl.program_id(0) == 1)
    def _():
        top_far_ref[...] = total[:half]


def fold_own_kernel(near_ref, far_ref, top_near_ref, top_far_ref, low_near_ref, low_far_ref):
    half = top_near_ref.shape[0]
    total = (near_ref[...].astype(jnp.float32) + far_ref[...].astype(jnp.float32)).astype(top_near_ref.dtype)

    @pl.when(pl.program_id(0) == 0)
    def _():
        top_near_ref[...] = total[:half]
        low_near_ref[...] = total[half:]

    @pl.when(pl.program_id(0) == 1)
    def _():
        top_far_ref[...] = total[:half]
        low_far_ref[...] = total[half:]


def fold(near, far, is_own):
    _, tokens, width = near.shape
    half = tokens // 2
    share = pl.BlockSpec((None, tokens, width), lambda i: (i, 0, 0))
    quarter = pl.BlockSpec((half, width), lambda i: (0, 0))
    shape = jax.ShapeDtypeStruct((half, width), near.dtype)
    if is_own:
        specs, shapes = [quarter] * 4, [shape] * 4
    else:
        specs = [quarter, quarter, pl.BlockSpec((None, half, width), lambda i: (i, 0, 0))]
        shapes = [shape, shape, jax.ShapeDtypeStruct((2, half, width), near.dtype)]
    return pl.pallas_call(
        fold_own_kernel if is_own else fold_other_kernel,
        grid=(2,),
        in_specs=[share, share],
        out_specs=specs,
        out_shape=shapes,
        compiler_params=limits(32),
        cost_estimate=BRIEF,
        name="fold",
    )(near, far)


def own_sum(own, low_got, own_got, top_last, low_last):
    top_near, _, low_near, _ = own
    wide = jnp.float32
    top = top_near.astype(wide) + own_got.astype(wide) + top_last.astype(wide)
    low = low_near.astype(wide) + low_got[0].astype(wide) + low_last.astype(wide)
    return jnp.concatenate([top, low], axis=0)


def token_total(own, other):
    total = own + row_swap(other)
    total = total + col_swap(total, 1)
    return total + col_swap(total, 2)


def line_update_kernel(flags_ref, now_ref, got_ref, pair_ref, crossed_ref, later_ref, out_ref, sent_ref):
    @pl.when(flags_ref[1] == 1)
    def _():
        wide = jnp.float32
        out_ref[...] = (now_ref[...].astype(wide) + got_ref[...].astype(wide)).astype(out_ref.dtype)
        sent_ref[...] = (pair_ref[...].astype(wide) + crossed_ref[...].astype(wide)).astype(sent_ref.dtype)

    @pl.when(flags_ref[1] == 0)
    def _():
        sent_ref[...] = later_ref[...]


def line_update(flags, now, got, pair, crossed, later):
    rows, columns = now.shape[1:]

    def middle_block(i, f):
        return (i * f[1], 0, 0)

    def end_block(i, f):
        return (i * (1 - f[1]), 0, 0)

    def every_block(i, f):
        return (i, 0, 0)

    block = (None, rows, columns)
    return pl.pallas_call(
        line_update_kernel,
        grid_spec=pltpu.PrefetchScalarGridSpec(
            num_scalar_prefetch=1,
            grid=(4,),
            in_specs=[pl.BlockSpec(block, middle_block)] * 4 + [pl.BlockSpec(block, end_block)],
            out_specs=[pl.BlockSpec(block, middle_block), pl.BlockSpec(block, every_block)],
        ),
        out_shape=[jax.ShapeDtypeStruct(now.shape, now.dtype)] * 2,
        compiler_params=limits(32),
        cost_estimate=BRIEF,
        name="line_update",
    )(flags, now, got, pair, crossed, later)


class LineSums:
    def __init__(self, flags):
        self.flags = flags
        self.step = 0
        self.now = self.sent = self.pair = None
        self.outward = False
        self.flying = ()
        self.done = []

    def advance(self, later=None):
        if lax.axis_size("dp") != 4:
            if later is not None:
                total = lax.psum(later, "dp")
                self.sent = later
                self.done.append((total, total))
            return
        if self.outward:
            self.done.append((self.sent, self.flying[0]))
        self.outward = self.pair is not None
        sent = self.now if later is None else later
        if self.step == 0:
            self.sent = later
        elif self.now is None:
            self.sent = add_low(self.pair, self.flying[1])
            self.pair = None
            if later is not None:
                self.sent = jnp.where(self.flags[1] == 1, self.sent, later)
        elif self.pair is None:
            self.pair = add_low(self.now, self.flying[0])
            self.sent = sent
        else:
            self.pair, self.sent = line_update(
                self.flags, self.now, self.flying[0], self.pair, self.flying[1], sent
            )
        self.now = later
        self.step += 1
        self._start()

    def finish(self):
        if lax.axis_size("dp") == 4:
            self.done.append((self.sent, self.flying[0]))

    def _start(self):
        move = lax.ppermute(self.sent, "dp", [(0, 1), (3, 2), (1, 0), (2, 3)])
        if self.pair is None:
            self.flying = (move,)
        else:
            self.flying = (move, lax.ppermute(self.pair, "dp", [(1, 2), (2, 1)]))


def dp_part(values, distance):
    count = lax.axis_size("dp")
    return lax.ppermute(values, "dp", [(i, i ^ distance) for i in range(count)])


def dp_rest(values):
    distance = 2
    while distance < lax.axis_size("dp"):
        values = values + dp_part(values, distance)
        distance *= 2
    return values


def pick_kernel(*refs, count):
    out_ref = refs[-1]
    for at in range(count):

        @pl.when(pl.program_id(0) == at)
        def _():
            out_ref[...] = refs[at][...]


def pick(sources):
    rows, columns = sources[0][0].shape[1:]
    return pl.pallas_call(
        partial(pick_kernel, count=len(sources)),
        grid=(len(sources),),
        in_specs=[pl.BlockSpec((None, rows, columns), lambda i, at=at: (at, 0, 0)) for _, at in sources],
        out_specs=pl.BlockSpec((None, rows, columns), lambda i: (i, 0, 0)),
        out_shape=jax.ShapeDtypeStruct((len(sources), rows, columns), sources[0][0].dtype),
        compiler_params=limits(32),
        cost_estimate=BRIEF,
        name="pick",
    )(*[array for array, _ in sources])


def pick_at_kernel(flags_ref, in_ref, out_ref):
    out_ref[...] = in_ref[...]


def pick_at(flags, values, distance, tiles=2):
    _, rows, columns = values.shape
    size = rows // tiles
    return pl.pallas_call(
        pick_at_kernel,
        grid_spec=pltpu.PrefetchScalarGridSpec(
            num_scalar_prefetch=1,
            grid=(tiles,),
            in_specs=[
                pl.BlockSpec((None, size, columns), lambda i, f: (jnp.bitwise_xor(f[0], distance), i, 0))
            ],
            out_specs=pl.BlockSpec((size, columns), lambda i, f: (i, 0)),
        ),
        out_shape=jax.ShapeDtypeStruct((rows, columns), values.dtype),
        compiler_params=limits(32),
        cost_estimate=BRIEF,
        name="pick_at",
    )(flags, values)


def choose_kernel(flags_ref, middle_ref, end_ref, out_ref):
    @pl.when(flags_ref[1] == 1)
    def _():
        out_ref[...] = middle_ref[...]

    @pl.when(flags_ref[1] == 0)
    def _():
        out_ref[...] = end_ref[...]


def chosen(flags, pair):
    middle, end = pair
    block = (None, *middle.shape[1:])
    return pl.pallas_call(
        choose_kernel,
        grid_spec=pltpu.PrefetchScalarGridSpec(
            num_scalar_prefetch=1,
            grid=(middle.shape[0],),
            in_specs=[
                pl.BlockSpec(block, lambda i, f: (i * f[1], 0, 0)),
                pl.BlockSpec(block, lambda i, f: (i * (1 - f[1]), 0, 0)),
            ],
            out_specs=pl.BlockSpec(block, lambda i, f: (i, 0, 0)),
        ),
        out_shape=jax.ShapeDtypeStruct(middle.shape, middle.dtype),
        compiler_params=limits(32),
        cost_estimate=BRIEF,
        name="choose",
    )(flags, middle, end)


def pick_chosen_kernel(flags_ref, middle_ref, end_ref, out_ref):
    choose_kernel(flags_ref, middle_ref, end_ref, out_ref)


def pick_chosen(flags, pair, places):
    middle, end = pair
    block = (None, *middle.shape[1:])
    return pl.pallas_call(
        pick_chosen_kernel,
        grid_spec=pltpu.PrefetchScalarGridSpec(
            num_scalar_prefetch=1,
            grid=(len(places),),
            in_specs=[
                pl.BlockSpec(block, lambda i, f: (distance_at(i, places) * f[1], 0, 0)),
                pl.BlockSpec(block, lambda i, f: (distance_at(i, places) * (1 - f[1]), 0, 0)),
            ],
            out_specs=pl.BlockSpec(block, lambda i, f: (i, 0, 0)),
        ),
        out_shape=jax.ShapeDtypeStruct((len(places), *middle.shape[1:]), middle.dtype),
        compiler_params=limits(32),
        cost_estimate=BRIEF,
        name="pick_chosen",
    )(flags, middle, end)


def near_of_sum(flags, pair, fetched):
    kept = pick_chosen(flags, pair, (2,))
    return col_swap(pick([(kept, 0), (fetched, 1)]), 1)


def far_pair(blocks):
    return col_swap(pick([(blocks, 1), (blocks, 3)]), 2)


def near_pair(blocks, fetched):
    return col_swap(pick([(blocks, 2), (fetched, 1)]), 1)


def halves_kernel(flags_ref, in_ref, keep_ref, send_ref):
    part = keep_ref.shape[1]

    @pl.when(flags_ref[2] == 0)
    def _():
        keep_ref[...] = in_ref[:, :part]
        send_ref[...] = in_ref[:, part:]

    @pl.when(flags_ref[2] == 1)
    def _():
        keep_ref[...] = in_ref[:, part:]
        send_ref[...] = in_ref[:, :part]


def row_halves(flags, blocks):
    count, rows, columns = blocks.shape
    half = pl.BlockSpec((None, rows, columns // 2), lambda i, f: (i, 0, 0))
    return pl.pallas_call(
        halves_kernel,
        grid_spec=pltpu.PrefetchScalarGridSpec(
            num_scalar_prefetch=1,
            grid=(count,),
            in_specs=[pl.BlockSpec((None, rows, columns), lambda i, f: (i, 0, 0))],
            out_specs=[half, half],
        ),
        out_shape=[jax.ShapeDtypeStruct((count, rows, columns // 2), blocks.dtype)] * 2,
        compiler_params=limits(32),
        cost_estimate=BRIEF,
        name="row_halves",
    )(flags, blocks)


def pack_out_kernel(mine_ref, far_ref, near_ref, both_ref, out_ref):
    width = mine_ref.shape[1]
    for at, ref in enumerate((mine_ref, far_ref, near_ref, both_ref)):
        out_ref[:, at * width : (at + 1) * width] = ref[...]


def pack_out(blocks, fetched, passed):
    _, depth, width = blocks.shape
    tiles = 2
    return pl.pallas_call(
        pack_out_kernel,
        grid=(tiles,),
        in_specs=block_specs(depth // tiles, width),
        out_specs=pl.BlockSpec((depth // tiles, 4 * width), lambda i: (i, 0)),
        out_shape=jax.ShapeDtypeStruct((depth, 4 * width), blocks.dtype),
        compiler_params=limits(32),
        cost_estimate=BRIEF,
        name="pack_out",
    )(*block_values(blocks, fetched, passed))


def block_specs(size, count):
    return [
        pl.BlockSpec((None, size, count), lambda i, *_, at=at: (at, i, 0)) for at in (0, 0, 0, 1)
    ]


def block_values(blocks, fetched, passed):
    return blocks, fetched, passed, passed


def own_first(values, row_index):
    return jnp.where(row_index == 0, values, jnp.flip(values, 0))


def tile_blocks(refs, split):
    tile = pl.program_id(0)
    tiles = pl.num_programs(0)
    refs = list(refs)
    blocks = []
    for halves in split:
        if halves:
            top, low = refs.pop(0), refs.pop(0)
            blocks.append(jnp.where(tile < tiles // 2, top[...], low[...]))
        else:
            blocks.append(refs.pop(0)[...])
    return blocks, refs


def write_normed(blocks, gain_ref, out_ref, factor_ref):
    width = blocks[0].shape[1]
    total = jnp.zeros((blocks[0].shape[0], 1), jnp.float32)
    for block in blocks:
        values = block.astype(jnp.float32)
        total = total + jnp.sum(values * values, axis=1, keepdims=True)
    factor = lax.rsqrt(total * (1.0 / (width * len(blocks))) + EPS)
    for at, block in enumerate(blocks):
        span = slice(at * width, (at + 1) * width)
        out_ref[:, span] = (block.astype(jnp.float32) * factor * gain_ref[:, span]).astype(jnp.bfloat16)
    factor_ref[...] = jnp.broadcast_to(factor, factor_ref.shape)


def project_kernel(*refs, split):
    blocks, refs = tile_blocks(refs, split)
    gain_ref, weight_ref, normed_ref, factor_ref, raw_ref, step_ref = refs
    write_normed(blocks, gain_ref, normed_ref, factor_ref)
    raw = nn(normed_ref[...], weight_ref[...])
    main = raw_ref.shape[1]
    raw_ref[...] = raw[:, :main].astype(jnp.bfloat16)
    step_ref[...] = raw[:, main:]


def ffn_kernel(*refs, split):
    blocks, refs = tile_blocks(refs, split)
    gain_ref, weight_ref, grad_hidden_ref, normed_ref, factor_ref, hidden_ref, grad_ref, inner_ref = refs
    write_normed(blocks, gain_ref, normed_ref, factor_ref)
    low, wide = jnp.bfloat16, jnp.float32
    units = hidden_ref.shape[1]
    gate_up = nn(normed_ref[...], weight_ref[...])
    gate, up = gate_up[:, :units], gate_up[:, units:]
    sig = sigmoid_of(gate)
    silu = gate * sig
    hidden_ref[...] = (silu * up).astype(low)
    grad_hidden = grad_hidden_ref[...]
    grad_gate = (grad_hidden * up * sig * (1.0 + gate * (1.0 - sig))).astype(low)
    grad_up = (grad_hidden * silu).astype(low)
    grad_ref[:, :units] = grad_gate
    grad_ref[:, units:] = grad_up
    products = grad_gate.astype(wide) * gate + grad_up.astype(wide) * up
    inner = products[:, :LANES]
    for at in range(LANES, units, LANES):
        inner = inner + products[:, at : at + LANES]
    inner_ref[...] = inner


def meet_kernel(*refs, split):
    blocks, refs = tile_blocks(refs, split)
    weight_ref, out_ref, product_ref = refs
    width = blocks[0].shape[1]
    for at, block in enumerate(blocks):
        out_ref[:, at * width : (at + 1) * width] = block
    product_ref[...] = nt(out_ref[...], weight_ref[...]).astype(product_ref.dtype)


def tiled_call(kernel, name, pieces, operands, outs, tiles=4):
    tokens, width = pieces[0].shape
    size = tokens // tiles
    split = [isinstance(piece, tuple) for piece in pieces]
    specs, values = [], []
    for piece, halves in zip(pieces, split):
        if halves:
            specs.append(pl.BlockSpec((size, width), lambda i: (jnp.minimum(i, tiles // 2 - 1), 0)))
            specs.append(pl.BlockSpec((size, width), lambda i: (jnp.maximum(i - tiles // 2, 0), 0)))
            values.extend(piece)
        else:
            specs.append(pl.BlockSpec((size, width), lambda i: (i, 0)))
            values.append(piece)
    for value, is_whole in operands:
        specs.append(whole(value.shape) if is_whole else pl.BlockSpec((size, value.shape[1]), lambda i: (i, 0)))
        values.append(value)
    return pl.pallas_call(
        partial(kernel, split=split),
        grid=(tiles,),
        in_specs=specs,
        out_specs=[pl.BlockSpec((size, columns), lambda i: (i, 0)) for columns, _ in outs],
        out_shape=[jax.ShapeDtypeStruct((tokens, columns), dtype) for columns, dtype in outs],
        compiler_params=limits(56),
        cost_estimate=BRIEF,
        name=name,
    )(*values)


def weight_grad_kernel(former_0, former_1, latter_0, latter_1, *out_refs):
    total = tn(former_0[...], latter_0[...]) + tn(former_1[...], latter_1[...])
    at = 0
    for out_ref in out_refs:
        out_ref[...] = total[:, at : at + out_ref.shape[1]].astype(out_ref.dtype)
        at += out_ref.shape[1]


def weight_grad(former, latter, width, at=0, counts=None):
    length, depth = former[0].shape
    if counts is None:
        left = pl.BlockSpec((length, depth), lambda i: (0, 0))
        right = pl.BlockSpec((length, width), lambda i: (0, i))
        shapes = [(4, depth, width)]
    else:
        left = pl.BlockSpec((length, width), lambda i: (0, i))
        right = pl.BlockSpec((length, sum(counts)), lambda i: (0, at))
        shapes = [(4, width, count) for count in counts]
    out = pl.pallas_call(
        weight_grad_kernel,
        grid=(4,),
        in_specs=[left, left, right, right],
        out_specs=[pl.BlockSpec((None, *shape[1:]), lambda i: (i, 0, 0)) for shape in shapes],
        out_shape=[jax.ShapeDtypeStruct(shape, jnp.bfloat16) for shape in shapes],
        compiler_params=limits(56),
        cost_estimate=BRIEF,
        name="weight_grad",
    )(*former, *latter)
    return out[0] if len(out) == 1 else out


def spread_kernel(*refs, transposed):
    values, (weight_ref, far_ref, near_ref) = refs[:-3], refs[-3:]
    step = pl.program_id(0)
    total = None
    at = 0
    for ref in values:
        if transposed:
            part = nt(ref[...], weight_ref[:, at : at + ref.shape[1]])
            at += ref.shape[1]
        else:
            part = nn(ref[...], weight_ref[...])
        total = part if total is None else total + part
    total = total.astype(far_ref.dtype)

    @pl.when(step < 2)
    def _():
        far_ref[...] = total

    @pl.when(step >= 2)
    def _():
        near_ref[...] = total


def spread(values, weight, width, transposed):
    tokens = values[0].shape[0]

    def block_of(i):
        return (i + 2) % 4

    if transposed:
        weight_spec = pl.BlockSpec((width, weight.shape[1]), lambda i: (block_of(i), 0))
    else:
        weight_spec = pl.BlockSpec((weight.shape[0], width), lambda i: (0, block_of(i)))
    shape = jax.ShapeDtypeStruct((2, tokens, width), jnp.bfloat16)
    far, near = pl.pallas_call(
        partial(spread_kernel, transposed=transposed),
        grid=(4,),
        in_specs=[whole(v.shape) for v in values] + [weight_spec],
        out_specs=[
            pl.BlockSpec((None, tokens, width), lambda i: (jnp.minimum(i, 1), 0, 0)),
            pl.BlockSpec((None, tokens, width), lambda i: (jnp.maximum(i - 2, 0), 0, 0)),
        ],
        out_shape=[shape, shape],
        compiler_params=limits(56),
        cost_estimate=BRIEF,
        name="spread",
    )(*values, weight)
    return near, far


def cut_first_kernel(flags_ref, query_ref, gate_ref, conv_ref, step_ref, out_ref, *, distances, steps):
    at = 0
    for ref in (query_ref, gate_ref, conv_ref):
        out_ref[:, at : at + ref.shape[1]] = ref[...]
        at += ref.shape[1]
    place = jnp.bitwise_xor(flags_ref[0], distance_at(pl.program_id(0), distances))
    step = pltpu.roll(step_ref[...].astype(jnp.float32), (LANES - place * steps) % LANES, 1)
    lane = lax.broadcasted_iota(jnp.int32, step.shape, 1)
    out_ref[:, at:] = jnp.where(lane < steps, step, 0.0).astype(out_ref.dtype)


def distance_at(i, distances):
    value = distances[0]
    for at, distance in enumerate(distances[1:], 1):
        value = jnp.where(i == at, distance, value)
    return value


def cut_first(flags, query, gate, conv, step, distances, size, at_share):
    depth = gate.shape[0]
    widths = [array.shape[1] // 4 for array in (query, gate, conv)]
    steps = step.shape[1] // 4
    total = sum(widths) + LANES
    step = jnp.pad(step, ((0, 0), (0, LANES - step.shape[1])))

    def row(f):
        return f[3] if at_share else 0

    def column_index(i, f):
        return (row(f), jnp.bitwise_xor(f[0], distance_at(i, distances)))

    return pl.pallas_call(
        partial(cut_first_kernel, distances=distances, steps=steps),
        grid_spec=pltpu.PrefetchScalarGridSpec(
            num_scalar_prefetch=1,
            grid=(len(distances),),
            in_specs=[pl.BlockSpec((size, w), column_index) for w in widths]
            + [pl.BlockSpec((size, LANES), lambda i, f: (row(f), 0))],
            out_specs=pl.BlockSpec((None, size, total), lambda i, f: (i, 0, 0)),
        ),
        out_shape=jax.ShapeDtypeStruct((len(distances), size, total), gate.dtype),
        compiler_params=limits(32),
        cost_estimate=BRIEF,
        name="cut_first",
    )(flags, query, gate, conv, step)


def cut_rest_kernel(flags_ref, gate_ref, up_ref, down_ref, out_ref):
    at = 0
    for ref in (gate_ref, up_ref, down_ref):
        out_ref[:, at : at + ref.shape[1]] = ref[...]
        at += ref.shape[1]


def cut_rest(flags, gate, up, down, distances, size, at_share):
    units = gate.shape[1] // 4
    width = down.shape[1]
    total = 2 * units + width
    parts = units // size

    def column_index(i, f):
        return (f[3] if at_share else 0, jnp.bitwise_xor(f[0], distance_at(i, distances)))

    def row_index(i, f):
        place = jnp.bitwise_xor(f[0], distance_at(i, distances))
        return (place * parts + (f[3] if at_share else 0), 0)

    return pl.pallas_call(
        cut_rest_kernel,
        grid_spec=pltpu.PrefetchScalarGridSpec(
            num_scalar_prefetch=1,
            grid=(len(distances),),
            in_specs=[
                pl.BlockSpec((size, units), column_index),
                pl.BlockSpec((size, units), column_index),
                pl.BlockSpec((size, width), row_index),
            ],
            out_specs=pl.BlockSpec((None, size, total), lambda i, f: (i, 0, 0)),
        ),
        out_shape=jax.ShapeDtypeStruct((len(distances), size, total), gate.dtype),
        compiler_params=limits(32),
        cost_estimate=BRIEF,
        name="cut_rest",
    )(flags, gate, up, down)


def cut_out_kernel(flags_ref, mamba_ref, attn_ref, out_ref):
    out_ref[: mamba_ref.shape[0], :] = mamba_ref[...]
    out_ref[mamba_ref.shape[0] :, :] = attn_ref[...]


def cut_out(flags, mamba, attn):
    channels, query = mamba.shape[0] // 4, attn.shape[0] // 4
    width = mamba.shape[1]

    def row_index(i, f):
        return (jnp.bitwise_xor(f[0], distance_at(i, DISTANCES)), 0)

    return pl.pallas_call(
        cut_out_kernel,
        grid_spec=pltpu.PrefetchScalarGridSpec(
            num_scalar_prefetch=1,
            grid=(4,),
            in_specs=[pl.BlockSpec((channels, width), row_index), pl.BlockSpec((query, width), row_index)],
            out_specs=pl.BlockSpec((None, channels + query, width), lambda i, f: (i, 0, 0)),
        ),
        out_shape=jax.ShapeDtypeStruct((4, channels + query, width), mamba.dtype),
        compiler_params=limits(32),
        cost_estimate=BRIEF,
        name="cut_out",
    )(flags, mamba, attn)


def pack_first_kernel(*refs, places, begins):
    pieces, out_ref = refs[:-1], refs[-1]
    query = places.key - places.query
    channels = places.value - places.gate
    head = places.gate - places.key
    total = out_ref.shape[2]

    def place(at, ref, begin, count, to):
        out_ref[at, :, to : to + count] = ref[:, begin : begin + count]

    for at in range(4):
        alone, common = pieces[2 * at], pieces[2 * at + 1]
        begin = begins[2 * at + 1]
        place(at, alone, 0, query, places.query)
        place(at, alone, query, channels, places.gate)
        place(at, alone, query + channels, channels, places.conv)
        place(at, alone, query + 2 * channels, total - places.step, places.step)
        place(at, common, begin, head, places.key)
        place(at, common, begin + head, head, places.value)
        place(at, common, begin + 2 * head, places.conv - places.shared, places.shared)


def pack_first(sources, places, total):
    depth, dtype = sources[0][0].shape[1], sources[0][0].dtype
    tiles = 4
    size = depth // tiles
    out = pl.pallas_call(
        partial(pack_first_kernel, places=places, begins=[begin for _, _, begin in sources]),
        grid=(tiles,),
        in_specs=[
            pl.BlockSpec((None, size, v.shape[2]), lambda i, at=at: (at, i, 0)) for v, at, _ in sources
        ],
        out_specs=pl.BlockSpec((4, size, total), lambda i: (0, i, 0)),
        out_shape=jax.ShapeDtypeStruct((4, depth, total), dtype),
        compiler_params=limits(48),
        cost_estimate=BRIEF,
        name="pack_first",
    )(*[v for v, _, _ in sources])
    return out.reshape(4 * depth, total)


def pack_rest_kernel(mine_ref, far_ref, near_ref, both_ref, in_ref, down_ref):
    width = down_ref.shape[1] // 4
    inner = in_ref.shape[2]
    for at, ref in enumerate((mine_ref, far_ref, near_ref, both_ref)):
        in_ref[at] = ref[:, :inner]
        down_ref[:, at * width : (at + 1) * width] = ref[:, inner : inner + width]


def pack_rest(sources, width):
    _, depth, total = sources[0][0].shape
    dtype = sources[0][0].dtype
    inner = total - width
    tiles = 4
    size = depth // tiles
    into, down = pl.pallas_call(
        pack_rest_kernel,
        grid=(tiles,),
        in_specs=[
            pl.BlockSpec((None, size, total), lambda i, at=at: (at, i, 0)) for _, at in sources
        ],
        out_specs=[
            pl.BlockSpec((4, size, inner), lambda i: (0, i, 0)),
            pl.BlockSpec((size, 4 * width), lambda i: (i, 0)),
        ],
        out_shape=[
            jax.ShapeDtypeStruct((4, depth, inner), dtype),
            jax.ShapeDtypeStruct((depth, 4 * width), dtype),
        ],
        compiler_params=limits(32),
        cost_estimate=BRIEF,
        name="pack_rest",
    )(*[v for v, _ in sources])
    return into.reshape(4 * depth, inner), down


def collect_early_kernel(*refs, places):
    pieces, (out_ref, common_ref) = refs[:4], refs[4:]
    query = places.key - places.query
    key = jnp.zeros((out_ref.shape[1], places.gate - places.key), jnp.float32)
    value = jnp.zeros((out_ref.shape[1], places.shared - places.value), jnp.float32)
    for at, piece in enumerate(pieces):
        out_ref[at, :, :query] = piece[:, : places.key]
        out_ref[at, :, query:] = piece[:, places.gate : places.value]
        key = key + piece[:, places.key : places.gate].astype(jnp.float32)
        value = value + piece[:, places.value :].astype(jnp.float32)
    common_ref[:, : key.shape[1]] = key.astype(common_ref.dtype)
    common_ref[:, key.shape[1] :] = value.astype(common_ref.dtype)


def collect_early(blocks, fetched, passed, places):
    _, depth, count = blocks.shape
    alone = places.key - places.query + places.value - places.gate
    tiles = 2
    size = depth // tiles
    return pl.pallas_call(
        partial(collect_early_kernel, places=places),
        grid=(tiles,),
        in_specs=block_specs(size, count),
        out_specs=[
            pl.BlockSpec((4, size, alone), lambda i: (0, i, 0)),
            pl.BlockSpec((size, count - alone), lambda i: (i, 0)),
        ],
        out_shape=[
            jax.ShapeDtypeStruct((4, depth, alone), blocks.dtype),
            jax.ShapeDtypeStruct((depth, count - alone), blocks.dtype),
        ],
        compiler_params=limits(32),
        cost_estimate=BRIEF,
        name="collect_early",
    )(*block_values(blocks, fetched, passed))


def collect_late_kernel(*refs, channels):
    alone, shared, (common_ref, out_ref, step_ref) = refs[:4], refs[4:8], refs[8:]
    quarter = out_ref.shape[2] - channels
    wide = jnp.float32
    steps = jnp.zeros(step_ref.shape, wide)
    total = jnp.zeros((out_ref.shape[1], shared[0].shape[1]), wide)
    for at, piece in enumerate(alone):
        out_ref[at, :, :channels] = piece[:, :channels]
        step = piece[:, channels:].astype(wide)
        steps = steps + (pltpu.roll(step, at * 8, 1) if at else step)
        total = total + shared[at][...].astype(wide)
    step_ref[...] = steps
    for at in range(2):
        span = slice(at * quarter, (at + 1) * quarter)
        out_ref[at, :, channels:] = total[:, span].astype(out_ref.dtype)
        out_ref[at + 2, :, channels:] = common_ref[:, span]


def collect_late(alone, shared, common, channels):
    _, depth, count = alone[0].shape
    part = shared[0].shape[2]
    tiles = 2
    size = depth // tiles
    return pl.pallas_call(
        partial(collect_late_kernel, channels=channels),
        grid=(tiles,),
        in_specs=[
            *block_specs(size, count), *block_specs(size, part),
            pl.BlockSpec((size, common.shape[1]), lambda i: (i, 0)),
        ],
        out_specs=[
            pl.BlockSpec((4, size, channels + part // 2), lambda i: (0, i, 0)),
            pl.BlockSpec((size, LANES), lambda i: (i, 0)),
        ],
        out_shape=[
            jax.ShapeDtypeStruct((4, depth, channels + part // 2), alone[0].dtype),
            jax.ShapeDtypeStruct((depth, LANES), jnp.float32),
        ],
        compiler_params=limits(32),
        cost_estimate=BRIEF,
        name="collect_late",
    )(*block_values(*alone), *block_values(*shared), common)


def slot_of(flags, place):
    distance = jnp.bitwise_xor(flags[0], place)
    return 2 * jnp.bitwise_and(distance, 1) + distance // 2


def finalize_kernel(flags_ref, total_ref, last_ref, *out_refs, cuts):
    values = jnp.where(flags_ref[1] == 1, total_ref[...], last_ref[...])
    for (span, columns), out_ref in zip(cuts, out_refs):
        out_ref[...] = values[span, columns].astype(jnp.float32)


def finalize(flags, total, last, block, index, outs):
    return pl.pallas_call(
        partial(finalize_kernel, cuts=[(rows, columns) for _, _, _, rows, columns in outs]),
        grid_spec=pltpu.PrefetchScalarGridSpec(
            num_scalar_prefetch=1,
            grid=(4,),
            in_specs=[pl.BlockSpec(block, index)] * 2,
            out_specs=[pl.BlockSpec(out_block, out_index) for _, out_block, out_index, _, _ in outs],
        ),
        out_shape=[jax.ShapeDtypeStruct(shape, jnp.float32) for shape, _, _, _, _ in outs],
        compiler_params=limits(32),
        cost_estimate=BRIEF,
        name="finalize",
    )(flags, total, last)


def finalize_blocks_kernel(flags_ref, *refs, cuts):
    pieces, out_refs = refs[:4], refs[4:]
    slot = slot_of(flags_ref, pl.program_id(0))
    for at, piece in enumerate(pieces):

        @pl.when(slot == at)
        def _():
            for (rows, columns), out_ref in zip(cuts, out_refs):
                out_ref[...] = piece[rows, columns].astype(jnp.float32)


def finalize_blocks(flags, blocks, fetched, passed, outs):
    _, rows, columns = blocks.shape
    return pl.pallas_call(
        partial(finalize_blocks_kernel, cuts=[(rows, columns) for _, _, _, rows, columns in outs]),
        grid_spec=pltpu.PrefetchScalarGridSpec(
            num_scalar_prefetch=1,
            grid=(4,),
            in_specs=[
                pl.BlockSpec((None, rows, columns), lambda i, f, at=at: (at, 0, 0)) for at in (0, 0, 0, 1)
            ],
            out_specs=[pl.BlockSpec(out_block, out_index) for _, out_block, out_index, _, _ in outs],
        ),
        out_shape=[jax.ShapeDtypeStruct(shape, jnp.float32) for shape, _, _, _, _ in outs],
        compiler_params=limits(32),
        cost_estimate=BRIEF,
        name="finalize_blocks",
    )(flags, *block_values(blocks, fetched, passed))


def meet_gathered_kernel(flags_ref, *refs):
    meet_kernel(*refs, split=[False] * 4)


def meet_gathered(flags, gathered, weight, tiles=4):
    _, tokens, width = gathered.shape
    size = tokens // tiles

    def block_at(distance):
        return pl.BlockSpec((None, size, width), lambda i, f: (jnp.bitwise_xor(f[0], distance), i, 0))

    model, units = weight.shape[1], weight.shape[0]
    return pl.pallas_call(
        meet_gathered_kernel,
        grid_spec=pltpu.PrefetchScalarGridSpec(
            num_scalar_prefetch=1,
            grid=(tiles,),
            in_specs=[block_at(d) for d in DISTANCES] + [pl.BlockSpec(weight.shape, lambda i, f: (0, 0))],
            out_specs=[
                pl.BlockSpec((size, model), lambda i, f: (i, 0)),
                pl.BlockSpec((size, units), lambda i, f: (i, 0)),
            ],
        ),
        out_shape=[
            jax.ShapeDtypeStruct((tokens, model), jnp.bfloat16),
            jax.ShapeDtypeStruct((tokens, units), jnp.float32),
        ],
        compiler_params=limits(56),
        cost_estimate=BRIEF,
        name="meet_gathered",
    )(flags, *[gathered] * 4, weight)


def on_device(
    tokens,
    cotangent,
    segment_ids,
    norm1_gain,
    proj_gate,
    proj_conv,
    proj_step,
    proj_shared,
    proj_query,
    proj_key,
    proj_value,
    conv_weight,
    conv_bias,
    shared_conv,
    shared_bias,
    step_bias,
    decay_log,
    skip_gain,
    mamba_out_proj,
    attn_out_proj,
    norm2_gain,
    ffn_gate,
    ffn_up,
    ffn_down,
):
    low = jnp.bfloat16
    wide = jnp.float32
    me = lax.axis_index("col")
    row_index = lax.axis_index("row")
    length = segment_ids.shape[1]
    width = tokens.shape[1]
    model = width * len(DISTANCES)
    head_dim = proj_key.shape[1]
    channels = proj_gate.shape[1] // 4
    steps = proj_step.shape[1] // 4
    head_width = channels // steps
    units = ffn_gate.shape[1] // 4
    query_width = proj_query.shape[1] // 4
    part = proj_shared.shape[1]
    at_gate = query_width + head_dim
    at_value = at_gate + channels
    at_shared = at_value + head_dim
    at_conv = at_shared + 2 * part
    at_step = at_conv + channels
    places = Places(0, query_width, at_gate, at_value, at_shared, at_conv, at_step)
    line_place = lax.axis_index("dp")
    share = width // lax.axis_size("dp")
    flags = jnp.stack(
        [me, ((line_place == 1) | (line_place == 2)).astype(me.dtype), row_index, line_place]
    ).astype(jnp.int32)
    firsts = (proj_query, proj_gate, proj_conv, proj_step)
    rests = (ffn_gate, ffn_up, ffn_down)

    def along_line(values):
        return lax.all_gather(values, "dp", axis=1, tiled=True)

    shared_twin = row_swap(proj_shared)
    fetched = col_swap(cut_first(flags, *firsts, DISTANCES[1::2], share, True), 2)
    gains = jnp.stack([norm1_gain, norm2_gain])
    gains_far = col_swap(gains, 2)
    block, shared_twin, fetched, gains_far = together(tokens, shared_twin, fetched, gains_far)
    first = gather_start(block)
    far = along_line(fetched)
    common = jnp.concatenate(
        [
            proj_key, proj_value,
            jnp.where(row_index == 0, proj_shared, shared_twin),
            jnp.where(row_index == 0, shared_twin, proj_shared),
        ],
        axis=1,
    )[None]
    alone = cut_first(flags, *firsts, DISTANCES[::2], width, False)
    lone = alone.shape[2]
    near = col_swap(jnp.concatenate([alone[1:], common], axis=2), 1)
    common_far = col_swap(common, 2)
    segments = own_first(segment_ids, row_index)
    indices = jnp.arange(length, dtype=jnp.int32)
    same = segments[:, :, None] == segments[:, None, :]
    position = jnp.sum(same & (indices[:, None] > indices[None, :]), axis=2).astype(wide)
    remaining = jnp.sum(same & (indices[:, None] < indices[None, :]), axis=2).astype(wide)
    lane = jnp.arange(LANES)
    info = jnp.where(
        lane == 0,
        segments.astype(wide)[..., None],
        jnp.where(lane == 1, position[..., None], remaining[..., None]),
    )
    row_info = jnp.broadcast_to(segments.astype(wide)[:, None, :], (2, 8, length))
    half_dim = head_dim // 2
    frequency = ROPE_BASE ** (-2.0 * jnp.arange(half_dim, dtype=wide) / head_dim)
    angles = position[..., None] * frequency
    cosine, sine = jnp.cos(angles), jnp.sin(angles)
    cosine = jnp.concatenate([cosine, cosine], axis=2)
    sine = jnp.concatenate([-sine, sine], axis=2)
    head_rows = jnp.pad(
        jnp.stack([step_bias, jnp.exp(decay_log)]), ((0, 6), (0, LANES - steps))
    )
    gain1, gain2 = gains[0:1], gains[1:2]
    params = (
        conv_weight, conv_bias[None], shared_conv, shared_bias[None], head_rows,
        jnp.repeat(skip_gain, head_width)[None],
    )

    both = (0, 1)


    first, near, alone, info, row_info, cosine, sine, params = together(
        first, near, alone, info, row_info, cosine, sine, params
    )
    middle = gather_middle(block, first)
    gains = jnp.concatenate([gains, gains_far], axis=1)
    out_blocks = cut_out(flags, mamba_out_proj, attn_out_proj)
    rest_sent = cut_rest(flags, *rests, DISTANCES[1::2], share, True)
    rest_kept = cut_rest(flags, *rests, DISTANCES[::2], width, False)
    middle, far, common_far, out_blocks, rest_sent, rest_kept = together(
        middle, far, common_far, out_blocks, rest_sent, rest_kept
    )
    both_far = col_swap(jnp.concatenate([far[1:], common_far], axis=2), 1)
    out_fetched = far_pair(out_blocks)
    gains = jnp.concatenate([gains, col_swap(gains, 1)], axis=1)
    gain1, gain2 = gains[0:1], gains[1:2]
    token_own, token_other = gather_end(block, first, middle)
    both_far, gain1, gain2, token_other = together(both_far, gain1, gain2, token_other)
    weight_first = pack_first(
        [
            (alone, 0, 0), (common, 0, 0), (far, 0, 0), (common_far, 0, 0),
            (near, 0, 0), (near, 0, lone), (both_far, 0, 0), (both_far, 0, lone),
        ],
        places, at_step + LANES,
    )

    both = (0, 1)
    normed1, factor1, raw, step_raw, mixed, combined, states = [[None, None] for _ in range(7)]

    def project(s, pieces):
        normed1[s], factor1[s], raw[s], step_raw[s] = tiled_call(
            project_kernel, "project", pieces, [(gain1, True), (weight_first, True)],
            [(model, low), (LANES, wide), (at_step, low), (LANES, wide)],
        )
        return attention_forward(raw[s], places, cosine[s], sine[s], info[s], row_info[s])

    def mamba(s, attended):
        mixed[s], combined[s], states[s] = mamba_forward(
            raw[s], places, step_raw[s], info[s], row_info[s], params, attended, head_width
        )

    cot_y = row_swap(after(cotangent, weight_first))
    attended = project(1, token_other)
    attended, out_fetched, cot_y = together(attended, out_fetched, cot_y)
    out_passed = near_pair(out_blocks, out_fetched)
    fetched = col_swap(after(rest_sent, out_fetched), 2)
    mamba(1, attended)
    mixed[1], out_passed, fetched = together(mixed[1], out_passed, fetched)
    cot_col = lax.all_gather(after(cotangent, fetched), "col", axis=0)
    rest_far = along_line(fetched)
    weight_out = pack_out(out_blocks, out_fetched, out_passed)
    near, far = spread([mixed[1]], weight_out, width, False)
    far = col_swap(far, 1)
    near, far, token_own = together(near, far, token_own)
    rest_near = col_swap(rest_kept[1:], 1)
    top_near, top_far, low_send = fold(near, far, False)
    low_got, other_got = row_swap(low_send), col_swap(top_far, 2)
    attended = project(0, after(token_own, low_send))
    attended, low_got, other_got, rest_near = together(attended, low_got, other_got, rest_near)
    top_last = row_swap(add_low(top_near, other_got))
    mamba(0, attended)
    mixed[0], top_last = together(mixed[0], top_last)
    near, far = spread([mixed[0]], weight_out, width, False)
    far = col_swap(far, 1)
    near, far, cot_col = together(near, far, cot_col)
    own = fold(near, far, True)
    low_sent = add_low(own[3], low_got[1])
    own_got, low_last = col_swap(own[1], 2), col_swap(low_sent, 2)
    cot_xy = row_swap(pick_at(flags, after(cot_col, low_sent), 2))
    own_got, low_last, cot_xy = together(own_got, low_last, cot_xy)
    hidden1, block = sum_quarters(tokens, own, low_got, own_got, top_last, low_last)
    block, hidden1, rest_far = together(block, hidden1, rest_far)
    first = gather_start(block)
    rest_both = col_swap(rest_far[1:], 1)
    cot_cores = [col_swap(cot_y, 1), col_swap(cot_xy, 1)]
    weight_in, weight_down = pack_rest(
        [(rest_kept, 0), (rest_far, 0), (rest_near, 0), (rest_both, 0)], width
    )
    cot, grad_hidden = [None, None], [None, None]
    cot[0], grad_hidden[0] = meet_gathered(flags, cot_col, weight_down)
    first, weight_in, weight_down, cot_cores, cot[0], grad_hidden[0] = together(
        first, weight_in, weight_down, cot_cores, cot[0], grad_hidden[0]
    )
    middle = gather_middle(block, first)
    cot[1], grad_hidden[1] = tiled_call(
        meet_kernel, "meet_cotangent", [cot_y, cot_xy, *cot_cores], [(weight_down, True)],
        [(model, low), (units, wide)],
    )
    middle, cot, grad_hidden = together(middle, cot, grad_hidden)
    pieces = gather_end(block, first, middle)
    normed2, factor2, hidden, grad_in, inner = [[None, None] for _ in range(5)]

    def feed_forward(s, pieces):
        normed2[s], factor2[s], hidden[s], grad_in[s], products = tiled_call(
            ffn_kernel, "ffn", pieces, [(gain2, True), (weight_in, True), (grad_hidden[s], False)],
            [(model, low), (LANES, wide), (units, low), (2 * units, low), (LANES, wide)],
        )
        inner[s] = jnp.sum(products, axis=1).reshape(length // LANES, LANES)

    def piece_index(i, f):
        return (slot_of(f, i), 0, 0)

    def row_index_map(i, f):
        return (i, 0)

    def column_index_map(i, f):
        return (0, i)

    every = slice(None)
    line = LineSums(flags)
    feed_forward(1, pieces[1])
    near, far = spread([grad_in[1]], weight_in, width, True)
    far = col_swap(far, 1)
    feed_forward(0, after(pieces[0], near))
    near, far, hidden, inner, grad_in = together(near, far, hidden, inner, grad_in)
    top_near, top_far, low_send = fold(near, far, False)
    low_got, other_got = row_swap(low_send), col_swap(top_far, 2)
    inner_row = row_swap(inner[1])
    near, far = spread([after(grad_in[0], low_send)], weight_in, width, True)
    far = col_swap(far, 1)
    near, far = together(near, far)
    own = fold(near, far, True)
    own_got = col_swap(own[1], 2)
    down = weight_grad(after(hidden, own), cot, width)
    low_got, other_got, inner_row, down, own = together(low_got, other_got, inner_row, down, own)
    top_last = row_swap(add_low(top_near, other_got))
    low_last = col_swap(add_low(own[3], low_got[1]), 2)
    inner = inner[0] + inner_row
    inner_core = col_swap(inner, 1)
    line.advance(down)
    gate = weight_grad(after(normed2, line.sent), grad_in, width, 0, [units])
    up = weight_grad(after(normed2, gate), grad_in, width, 1, [units])
    top_last, low_last, own_got, inner_core, up, gate = together(
        top_last, low_last, own_got, inner_core, up, gate
    )
    inner = inner + inner_core
    inner = inner + col_swap(inner, 2)
    inner2 = inner.reshape(length, 1)
    grad_normed2 = own_sum(own, low_got, own_got, top_last, low_last)
    own_factor = factor2[0][:, :1]
    back2 = (
        own_factor * norm2_gain * grad_normed2
        - hidden1 * (own_factor * own_factor * inner2 / model)
    )
    grad_gain2 = jnp.sum(grad_normed2 * hidden1 * own_factor, axis=0)
    grad_hidden1 = cotangent.astype(wide) + back2
    block, grad_hidden1, grad_gain2 = together(grad_hidden1.astype(low), grad_hidden1, grad_gain2)
    first = gather_start(block)
    output_shares = [spread([after(hidden[s], block)], weight_down, width, False) for s in both]
    first, output_shares, line.flying = together(first, output_shares, line.flying)
    line.advance(gate)
    middle = together(*gather_middle(block, first))
    pieces = gather_end(block, first, middle)
    output_far = [col_swap(output_shares[s][1], 1) for s in both]
    mix_grad, grad_mixed = [None, None], [None, None]
    for s in both:
        mix_grad[s], grad_mixed[s] = tiled_call(
            meet_kernel, "meet_mixed", pieces[s], [(weight_out, True)],
            [(model, low), (channels + query_width, low)],
        )
    out = weight_grad(mixed, mix_grad, width)
    early, late, sums, products, inner = [[None, None] for _ in range(5)]

    def mamba_step(s, *earlier):
        late[s], inner[s], sums[s] = mamba_backward(
            raw[s], places, step_raw[s], info[s], row_info[s], params, states[s],
            after(grad_mixed[s], *earlier), head_width,
        )

    for s in both:
        early[s], products[s] = attention_backward(
            raw[s], places, cosine[s], sine[s], info[s], row_info[s], combined[s],
            after(grad_mixed[s], out),
        )
    out, grad_mixed, early, output_far, line.flying = together(out, grad_mixed, early, output_far, line.flying)
    line.advance(up)
    output_other = add_low(output_shares[1][0], output_far[1])
    output_got = row_swap(output_other)
    early = after(early, line.sent, output_other)
    first = weight_grad(normed1, early, width, 0, [at_shared])
    first_far = far_pair(first)
    mamba_step(1, first)
    late[1], output_got, output_near, line.flying = together(
        late[1], output_got, output_far[0], line.flying
    )
    line.advance(out)
    first_far = after(first_far, line.sent)
    first_near = near_pair(first, first_far)
    output_sent = add_three(output_shares[0][0], output_near, output_got, 1)
    output_last = col_swap(output_sent, 2)
    down = line.done[0]
    down_sent = pick_chosen(flags, down, (1, 3))
    down_far = col_swap(down_sent, 2)
    mamba_step(0, line.sent, output_sent, down_sent)
    shared, last = weight_grad(normed1, late, width, 0, [2 * part, channels + LANES])
    shared, last, late, sums, inner, output_last, down_far, first_near, line.flying = together(
        shared, last, late, sums, inner, output_last, down_far, first_near, line.flying
    )
    shared_keep, shared_send = row_halves(flags, shared)
    shared_got = row_swap(shared_send)
    last_far = far_pair(last)
    down_near = near_of_sum(flags, down, down_far)
    first, common_sum = collect_early(first, first_far, first_near, places)
    line.advance(first)
    small_rows = length // width
    inner = [
        jnp.sum(inner[s] + products[s], axis=1).reshape(small_rows, width) for s in both
    ]
    small = jnp.concatenate(
        [(sums[0] + sums[1])[:13], grad_gain2[None], inner[0], inner[1], jnp.zeros((14, width), wide)],
        axis=0,
    )[:24]
    rank = jnp.arange(24)[:, None]
    taps = conv_weight.shape[0]
    is_shared = (rank > taps) & (rank < 2 * taps + 2)
    is_inner = (rank >= 14) & (rank < 14 + small_rows)
    is_gain = rank == 13
    last_far, shared_got, small, down_near = together(last_far, shared_got, small, down_near)
    shared = add_low(shared_keep, shared_got)
    shared_far = far_pair(shared)
    small_got = row_swap(small)
    last_near = near_pair(last, last_far)
    shared_far, last_near, small_got, line.flying = together(shared_far, last_near, small_got, line.flying)
    shared_near = together(near_pair(shared, shared_far))[0]
    last, step_sum = collect_late(
        (last, last_far, last_near), (shared, shared_far, shared_near), common_sum, channels
    )
    line.advance(last)
    small_other = jnp.concatenate(
        [small_got[:14], small_got[14 + small_rows : 14 + 2 * small_rows], small_got[14 + small_rows :]], axis=0
    )[:24]
    late, small, small_other = after((late, small, small_other), line.sent)
    gate, up = line.done[1], line.done[2]
    gate_far = col_swap(pick_chosen(flags, gate, (1, 3)), 2)
    up_far = col_swap(pick_chosen(flags, up, (1, 3)), 2)
    near, far = spread([early[1], late[1]], weight_first, width, True)
    own_near, own_far = spread([early[0], after(late[0], near)], weight_first, width, True)
    small = small + jnp.where(is_shared | is_gain | is_inner, small_other, 0.0)
    near, far, own_near, own_far, small, gate_far, up_far, line.flying = together(
        near, far, own_near, own_far, small, gate_far, up_far, line.flying
    )
    line.advance()
    far, own_far, small = after((far, own_far, small), line.sent)
    far, own_far, small_got = together(col_swap(far, 1), col_swap(own_far, 1), col_swap(small, 1))
    top_near, top_far, low_send = fold(near, far, False)
    low_got, other_got = row_swap(low_send), col_swap(top_far, 2)
    own = fold(own_near, own_far, True)
    own_got = col_swap(own[1], 2)
    small = small + jnp.where(is_shared | is_inner, small_got, 0.0)
    small_got = col_swap(small, 2)
    gate_near = near_of_sum(flags, gate, gate_far)
    up_near = near_of_sum(flags, up, up_far)
    low_got, other_got, own_got, small_got, gate_near, up_near, line.flying = together(
        low_got, other_got, own_got, small_got, gate_near, up_near, line.flying
    )
    line.advance()
    low_got, other_got, small, small_got = after((low_got, other_got, small, small_got), line.sent)
    top_last = row_swap(add_low(top_near, other_got))
    low_last = col_swap(add_low(own[3], low_got[1]), 2)
    out = line.done[3]
    out_far = col_swap(pick_chosen(flags, out, (1, 3)), 2)
    small = small + jnp.where(is_shared | is_inner, small_got, 0.0)
    total, final = line.done[4]
    alone = query_width + channels
    d_query, d_gate = finalize(
        flags, total, final, (None, width, alone), piece_index,
        [
            (proj_query.shape, (width, query_width), column_index_map, every, slice(0, query_width)),
            (proj_gate.shape, (width, channels), column_index_map, every, slice(query_width, None)),
        ],
    )
    (d_ffn_down,) = finalize_blocks(
        flags, pick_chosen(flags, down, (0,)), down_far, down_near,
        [(ffn_down.shape, (units, width), row_index_map, every, every)],
    )
    (d_ffn_gate,) = finalize_blocks(
        flags, pick_chosen(flags, gate, (0,)), gate_far, gate_near,
        [(ffn_gate.shape, (width, units), column_index_map, every, every)],
    )
    (d_ffn_up,) = finalize_blocks(
        flags, pick_chosen(flags, up, (0,)), up_far, up_near,
        [(ffn_up.shape, (width, units), column_index_map, every, every)],
    )
    output = (
        hidden1 + output_shares[0][0][0].astype(wide) + output_near[0].astype(wide)
        + output_got[0].astype(wide) + output_last.astype(wide)
    ).astype(low)
    top_last, low_last, out_far, d_query, d_gate, d_ffn_down, d_ffn_gate, d_ffn_up, output = together(
        top_last, low_last, out_far, d_query, d_gate, d_ffn_down, d_ffn_gate, d_ffn_up, output
    )
    out_near = near_of_sum(flags, out, out_far)
    inner1 = small[14 : 14 + small_rows].reshape(length, 1)
    grad_normed1 = own_sum(own, low_got, own_got, top_last, low_last)
    own_factor = factor1[0][:, :1]
    own_tokens = tokens.astype(wide)
    back1 = (
        own_factor * norm1_gain * grad_normed1
        - own_tokens * (own_factor * own_factor * inner1 / model)
    )
    grad_gain1 = jnp.sum(grad_normed1 * own_tokens * own_factor, axis=0)
    tokens_grad = (grad_hidden1 + back1).astype(low)
    gain_got = row_swap(grad_gain1[None])
    out_near, tokens_grad = together(out_near, tokens_grad)
    d_mamba_out, d_attn_out = finalize_blocks(
        flags, pick_chosen(flags, out, (0,)), out_far, out_near,
        [
            (mamba_out_proj.shape, (channels, width), row_index_map, slice(0, channels), every),
            (attn_out_proj.shape, (query_width, width), row_index_map, slice(channels, None), every),
        ],
    )
    gain_got, d_mamba_out, d_attn_out = together(gain_got, d_mamba_out, d_attn_out)
    small = jnp.concatenate(
        [
            small[:14], grad_gain1[None] + gain_got, jnp.zeros((1, width), wide),
            jnp.transpose(step_sum)[: 4 * 8],
        ],
        axis=0,
    )
    small_got = dp_part(small, 1)
    tokens_grad, small, small_got, line.flying = together(tokens_grad, small, small_got, line.flying)
    line.finish()
    total, final = line.done[5]
    (d_conv,) = finalize(
        flags, total, final, (None, width, channels + part // 2), piece_index,
        [(proj_conv.shape, (width, channels), column_index_map, every, slice(0, channels))],
    )
    sums = dp_rest(small + small_got)
    extra = jnp.where(flags[1] == 1, total[:, :, channels:], final[:, :, channels:]).astype(wide)
    d_shared = jnp.concatenate([extra[0], extra[1]], axis=1)
    d_key, d_value = extra[2], extra[3]
    step_sum = jnp.stack([sums[16 + p * 8 : 16 + p * 8 + steps] for p in (0, 2, 1, 3)])
    d_step = jnp.transpose(
        jnp.concatenate([lax.dynamic_index_in_dim(step_sum, me ^ d, 0, keepdims=False) for d in range(4)])
    )
    return (
        output, tokens_grad, sums[14], d_gate, d_conv, d_step, d_shared, d_query, d_key, d_value,
        sums[:taps, :channels], sums[taps, :channels], sums[taps + 1 : 2 * taps + 1],
        sums[2 * taps + 1],
        sums[11, :steps], sums[12, :steps],
        jnp.sum(sums[10, :channels].reshape(steps, head_width), axis=1),
        d_mamba_out, d_attn_out, sums[13], d_ffn_gate, d_ffn_up, d_ffn_down,
    )


def solution(mesh):
    return jax.shard_map(
        on_device,
        mesh=mesh,
        in_specs=(
            P(("dp", "row"), "col"),
            P(("dp", "row"), "col"),
            P("dp", None),
            P("col"),
            P("col", "row"),
            P("col", "row"),
            P("col", "row"),
            P("col", "row"),
            P("col", "row"),
            P("col", "row"),
            P("col", "row"),
            P(None, ("row", "col")),
            P(("row", "col")),
            P(),
            P(),
            P(("row", "col")),
            P(("row", "col")),
            P(("row", "col")),
            P("row", "col"),
            P("row", "col"),
            P("col"),
            P("col", "row"),
            P("col", "row"),
            P("row", "col"),
        ),
        out_specs=(
            P(("dp", "row"), "col"),
            P(("dp", "row"), "col"),
            P("col"),
            P("col", "row"),
            P("col", "row"),
            P("col", "row"),
            P("col", "row"),
            P("col", "row"),
            P("col", "row"),
            P("col", "row"),
            P(None, ("row", "col")),
            P(("row", "col")),
            P(),
            P(),
            P(("row", "col")),
            P(("row", "col")),
            P(("row", "col")),
            P("row", "col"),
            P("row", "col"),
            P("col"),
            P("col", "row"),
            P("col", "row"),
            P("row", "col"),
        ),
        check_vma=False,
    )
```

```python
from functools import partial
import math
from typing import NamedTuple

import jax
import jax.numpy as jnp
from jax import lax
from jax.experimental import pallas as pl
from jax.experimental.pallas import tpu as pltpu
from jax.sharding import PartitionSpec as P

EPS = 1e-05
ROPE_BASE = 100000000000.0
MASKED = -1e30
HIGHEST = lax.Precision.HIGHEST
DISTANCES = (0, 2, 1, 3)
LANES = 128
CHUNK = 128
TAIL = 8


class Places(NamedTuple):
    query: int
    key: int
    gate: int
    value: int
    shared: int
    conv: int
    step: int


def dot_any(former, latter, dims, precision=None):
    return lax.dot_general(
        former, latter, (dims, ((), ())), precision=precision, preferred_element_type=jnp.float32
    )


def nn(former, latter):
    return dot_any(former, latter, ((1,), (0,)))


def nt(former, latter):
    return dot_any(former, latter, ((1,), (1,)))


def tn(former, latter):
    return dot_any(former, latter, ((0,), (0,)))


def low_terms(values, count):
    terms = []
    for _ in range(count):
        term = values.astype(jnp.bfloat16)
        values = values - term.astype(jnp.float32)
        terms.append(term)
    return terms


def times_marks(values, marks, count):
    return sum(nn(term, marks) for term in low_terms(values, count))


def marks_times(marks, values, count):
    return sum(nn(marks, term) for term in low_terms(values, count))


def sigmoid_of(values):
    return 1.0 / (1.0 + jnp.exp(-values))


def softplus_of(values):
    return jnp.maximum(values, 0.0) + jnp.log1p(jnp.exp(-jnp.abs(values)))


def head_spread(head_width, width):
    heads = lax.broadcasted_iota(jnp.int32, (LANES, width), 0)
    columns = lax.broadcasted_iota(jnp.int32, (LANES, width), 1)
    return (columns // head_width == heads).astype(jnp.bfloat16)


def head_gather(head_width, width):
    columns = lax.broadcasted_iota(jnp.int32, (width, LANES), 0)
    heads = lax.broadcasted_iota(jnp.int32, (width, LANES), 1)
    return (columns // head_width == heads).astype(jnp.bfloat16)


def causal_conv(ext_ref, columns, weight_ref, bias_ref, position, taps):
    length = ext_ref.shape[0] - TAIL
    running = bias_ref[...] + weight_ref[taps - 1 : taps, :] * ext_ref[TAIL:, columns]
    for offset in range(1, taps):
        earlier = ext_ref[TAIL - offset : TAIL - offset + length, columns]
        running = running + weight_ref[taps - 1 - offset : taps - offset, :] * jnp.where(
            position >= offset, earlier, 0.0
        )
    return running


def chunk_decay(step_in, position, decay_rate):
    length = step_in.shape[0]
    step_size = softplus_of(step_in)
    log_decay = jnp.where(position == 0.0, 0.0, -step_size * decay_rate)
    rows = lax.broadcasted_iota(jnp.int32, (length, length), 0)
    columns = lax.broadcasted_iota(jnp.int32, (length, length), 1)
    causal = rows >= columns
    running = marks_times(causal.astype(jnp.bfloat16), log_decay, 3)
    return step_size, log_decay, running, jnp.transpose(running), causal


def split_pair(values, head_width):
    lane = lax.broadcasted_iota(jnp.int32, values.shape, 1)
    zero = jnp.zeros_like(values)
    return jnp.concatenate(
        [jnp.where(lane < head_width, values, zero), jnp.where(lane < head_width, zero, values)],
        axis=0,
    )


def mamba_forward_kernel(
    raw_ref, step_ref, info_ref, row_ref, weight_ref, bias_ref,
    shared_weight_ref, shared_bias_ref, head_ref, skip_ref, attended_ref,
    mixed_ref, combined_ref, states_ref,
    state, ext, *, head_width, places
):
    chunk = pl.program_id(0)
    length, width = combined_ref.shape
    gate_columns = slice(places.gate, places.value)
    conv_columns = slice(places.conv, places.step)
    shared_columns = slice(places.shared, places.conv)
    states = (places.conv - places.shared) // 2
    taps = weight_ref.shape[0]
    low = jnp.bfloat16

    @pl.when(chunk == 0)
    def _():
        state[...] = jnp.zeros_like(state)
        ext[...] = jnp.zeros_like(ext)

    ext[:TAIL, :] = ext[length : length + TAIL, :]
    ext[TAIL:, :width] = raw_ref[:, conv_columns].astype(jnp.float32)
    ext[TAIL:, width:] = raw_ref[:, shared_columns].astype(jnp.float32)
    segment = info_ref[:, 0:1]
    position = info_ref[:, 1:2]
    pre = causal_conv(ext, slice(0, width), weight_ref, bias_ref, position, taps)
    conv_out = pre * sigmoid_of(pre)
    pre = causal_conv(
        ext, slice(width, None), shared_weight_ref, shared_bias_ref, position, taps
    )
    shared = (pre * sigmoid_of(pre)).astype(low)
    b_map = shared[:, :states]
    c_map = shared[:, states:]
    step_size, _, running, running_t, causal = chunk_decay(
        step_ref[...] + head_ref[0:1, :], position, head_ref[1:2, :]
    )
    segment_row = row_ref[0:1, :]
    allowed = causal & (segment == segment_row)
    local = lax.broadcasted_iota(jnp.int32, (length, 1), 0).astype(jnp.float32)
    enters = jnp.where(position > local, jnp.exp(running), 0.0)
    last = running[length - 1 : length, :]
    leaves = jnp.where(segment == segment_row[:, length - 1 :], jnp.exp(last - running), 0.0)
    spread = head_spread(head_width, width)
    wide = times_marks(jnp.concatenate([step_size, enters, leaves], axis=0), spread, 2)
    weighted = conv_out * wide[:length]
    gram = nt(c_map, b_map)
    weighted_low = weighted.astype(low)
    parts = []
    for pair in range(width // (2 * head_width)):
        weights = []
        for head in (2 * pair, 2 * pair + 1):
            gap = jnp.where(allowed, running[:, head : head + 1] - running_t[head : head + 1, :], MASKED)
            weights.append((gram * jnp.exp(gap)).astype(low))
        columns = slice(2 * pair * head_width, 2 * (pair + 1) * head_width)
        parts.append(
            nn(jnp.concatenate(weights, axis=1), split_pair(weighted_low[:, columns], head_width))
        )
    held = state[...]
    held_low = held.astype(low)
    states_ref[...] = held_low
    scanned = jnp.concatenate(parts, axis=1) + nn(c_map, held_low) * wide[length : 2 * length]
    fade = wide[2 * length - 1 : 2 * length]
    state[...] = held * fade + tn(b_map, (weighted * wide[2 * length :]).astype(low))
    combined = scanned + skip_ref[...] * conv_out
    combined_ref[...] = combined.astype(low)
    gate = raw_ref[:, gate_columns].astype(jnp.float32)
    mixed_ref[:, :width] = (combined * (gate * sigmoid_of(gate))).astype(low)
    mixed_ref[:, width:] = attended_ref[...]


def mamba_backward_kernel(
    raw_ref, tail_ref, step_ref, info_ref, row_ref, weight_ref, bias_ref,
    shared_weight_ref, shared_bias_ref, head_ref, skip_ref, states_ref, grad_ref,
    out_ref, inner_ref, sums_ref,
    grad_state, ext, ext_grad, *, head_width, places
):
    count = pl.num_programs(0)
    step = pl.program_id(0)
    length = grad_ref.shape[0]
    width = places.step - places.conv
    states = (places.conv - places.shared) // 2
    taps = weight_ref.shape[0]
    low = jnp.bfloat16
    f32 = jnp.float32
    gate_columns = slice(places.gate, places.value)
    conv_columns = slice(places.conv, places.step)
    shared_columns = slice(places.shared, places.conv)

    @pl.when(step == 0)
    def _():
        grad_state[...] = jnp.zeros_like(grad_state)
        ext_grad[...] = jnp.zeros_like(ext_grad)
        sums_ref[...] = jnp.zeros_like(sums_ref)

    tail_at = tail_ref.shape[0] - TAIL
    ext[:TAIL, :width] = tail_ref[:, conv_columns].astype(f32)[tail_at:]
    ext[:TAIL, width:] = tail_ref[:, shared_columns].astype(f32)[tail_at:]
    ext[TAIL:, :width] = raw_ref[:, conv_columns].astype(f32)
    ext[TAIL:, width:] = raw_ref[:, shared_columns].astype(f32)
    segment = info_ref[:, 0:1]
    position = info_ref[:, 1:2]
    remaining = info_ref[:, 2:3]
    pre = causal_conv(ext, slice(0, width), weight_ref, bias_ref, position, taps)
    sig = sigmoid_of(pre)
    conv_out = pre * sig
    conv_slope = sig * (1.0 + pre * (1.0 - sig))
    pre = causal_conv(
        ext, slice(width, None), shared_weight_ref, shared_bias_ref, position, taps
    )
    sig = sigmoid_of(pre)
    shared = (pre * sig).astype(low)
    shared_slope = sig * (1.0 + pre * (1.0 - sig))
    b_map = shared[:, :states]
    c_map = shared[:, states:]
    step_in = step_ref[...] + head_ref[0:1, :]
    rate = head_ref[1:2, :]
    step_size, log_decay, running, running_t, causal = chunk_decay(step_in, position, rate)
    segment_row = row_ref[0:1, :]
    allowed = causal & (segment == segment_row)
    local = lax.broadcasted_iota(jnp.int32, (length, 1), 0).astype(f32)
    enters = jnp.where(position > local, jnp.exp(running), 0.0)
    last = running[length - 1 : length, :]
    leaves = jnp.where(segment == segment_row[:, length - 1 :], jnp.exp(last - running), 0.0)
    spread = head_spread(head_width, width)
    wide = times_marks(jnp.concatenate([step_size, enters, leaves], axis=0), spread, 2)
    step_wide = wide[:length]
    enters_wide = wide[length : 2 * length]
    leaves_wide = wide[2 * length :]
    fade = wide[2 * length - 1 : 2 * length]
    weighted = conv_out * step_wide

    gate = raw_ref[:, gate_columns].astype(f32)
    sig = sigmoid_of(gate)
    grad_scan = grad_ref[:, :width].astype(f32) * (gate * sig)

    gram = nt(c_map, b_map)
    weighted_low = weighted.astype(low)
    grad_low = grad_scan.astype(low)
    lane = lax.broadcasted_iota(jnp.int32, (length, LANES), 1)
    sub = lax.broadcasted_iota(jnp.int32, (LANES, length), 0)
    grad_gram = jnp.zeros((length, length), f32)
    by_row = jnp.zeros((length, LANES), f32)
    by_column = jnp.zeros((LANES, length), f32)
    parts = []
    for pair in range(width // (2 * head_width)):
        columns = slice(2 * pair * head_width, 2 * (pair + 1) * head_width)
        split_grad = split_pair(grad_low[:, columns], head_width)
        products = nt(split_grad, weighted_low[:, columns])
        weights = []
        for place, head in enumerate((2 * pair, 2 * pair + 1)):
            gap = jnp.where(allowed, running[:, head : head + 1] - running_t[head : head + 1, :], MASKED)
            fading = jnp.exp(gap)
            weight = gram * fading
            product = products[place * length : (place + 1) * length]
            grad_gram = grad_gram + fading * product
            meeting = weight * product
            by_row = jnp.where(lane == head, jnp.sum(meeting, axis=1, keepdims=True), by_row)
            by_column = jnp.where(sub == head, jnp.sum(meeting, axis=0, keepdims=True), by_column)
            weights.append(weight.astype(low))
        parts.append(tn(jnp.concatenate(weights, axis=0), split_grad))
    held = states_ref[...]
    entering = (grad_scan * enters_wide).astype(low)
    leaving = (weighted * leaves_wide).astype(low)
    grad_held = grad_state[...]
    grad_held_low = grad_held.astype(low)
    from_state = nn(b_map, grad_held_low) * leaves_wide
    grad_weighted = jnp.concatenate(parts, axis=1) + from_state
    grad_gram_low = grad_gram.astype(low)
    grad_c = nn(grad_gram_low, b_map) + nt(entering, held)
    grad_b = tn(grad_gram_low, c_map) + nt(leaving, grad_held_low)
    met_in = grad_scan * enters_wide * nn(c_map, held)
    met_out = weighted * from_state
    met_state = fade * jnp.sum(held.astype(f32) * grad_held, axis=0, keepdims=True)
    grad_state[...] = grad_held * fade + tn(c_map, entering)
    grad_conv_out = grad_weighted * step_wide + skip_ref[...] * grad_scan
    gathered = times_marks(
        jnp.concatenate(
            [met_in, met_out, conv_out * grad_weighted, jnp.broadcast_to(met_state, (TAIL, width))],
            axis=0,
        ),
        head_gather(head_width, width),
        2,
    )
    out_rows = gathered[length : 2 * length]
    at_last = jnp.sum(out_rows, axis=0, keepdims=True) + gathered[3 * length : 3 * length + 1]
    grad_running = by_row - jnp.transpose(by_column) + gathered[:length] - out_rows
    grad_running = grad_running + jnp.where(local == length - 1.0, at_last, 0.0)
    rows = lax.broadcasted_iota(jnp.int32, (length, length), 0)
    later = lax.broadcasted_iota(jnp.int32, (length, length), 1) >= rows
    grad_decay = jnp.where(position == 0.0, 0.0, marks_times(later.astype(low), grad_running, 3))
    grad_step = (gathered[2 * length : 3 * length] - grad_decay * rate) * sigmoid_of(step_in)

    ext_grad[length : length + TAIL, :] = ext_grad[:TAIL, :]
    ext_grad[:length, :width] = grad_conv_out * conv_slope
    ext_grad[:length, width : width + states] = grad_b * shared_slope[:, :states]
    ext_grad[:length, width + states :] = grad_c * shared_slope[:, states:]

    def conv_back(columns, weights, row_at):
        now = ext_grad[:length, columns]
        running = weights[taps - 1 : taps, :] * now
        wide_columns = slice(0, now.shape[1])
        sums_ref[row_at + taps : row_at + taps + 1, wide_columns] += jnp.sum(now, axis=0, keepdims=True)
        sums_ref[row_at + taps - 1 : row_at + taps, wide_columns] += jnp.sum(
            now * ext[TAIL:, columns], axis=0, keepdims=True
        )
        for offset in range(1, taps):
            at = taps - 1 - offset
            running = running + weights[at : at + 1, :] * jnp.where(
                remaining >= offset, ext_grad[offset : offset + length, columns], 0.0
            )
            earlier = jnp.where(
                position >= offset, ext[TAIL - offset : TAIL - offset + length, columns], 0.0
            )
            sums_ref[row_at + at : row_at + at + 1, wide_columns] += jnp.sum(
                now * earlier, axis=0, keepdims=True
            )
        return running

    grad_conv = conv_back(slice(0, width), weight_ref, 0).astype(low)
    grad_shared = conv_back(slice(width, None), shared_weight_ref, taps + 1).astype(low)
    row_at = 2 * (taps + 1)
    sums_ref[row_at : row_at + 1, :width] += jnp.sum(grad_scan * conv_out, axis=0, keepdims=True)
    sums_ref[row_at + 1 : row_at + 2, :LANES] += jnp.sum(grad_step, axis=0, keepdims=True)
    sums_ref[row_at + 2 : row_at + 3, :LANES] += jnp.sum(
        grad_decay * log_decay, axis=0, keepdims=True
    )
    grad_step = grad_step.astype(low)
    out_ref[:, : 2 * states] = grad_shared
    out_ref[:, 2 * states : 2 * states + width] = grad_conv
    out_ref[:, 2 * states + width :] = grad_step
    inner = grad_step.astype(f32) * step_ref[...]
    for at in range(0, places.step - places.shared, LANES):
        raw = raw_ref[:, places.shared + at : places.shared + at + LANES]
        inner = inner + out_ref[:, at : at + LANES].astype(f32) * raw.astype(f32)
    inner_ref[...] = inner


def rope(values, cosine, sine):
    return values * cosine + pltpu.roll(values, values.shape[1] // 2, 1) * sine


def attention_rows(query, key, begin, size, info_ref, row_ref, factor):
    seen = begin + size
    scores = nt(query, key) * factor
    rows = begin + lax.broadcasted_iota(jnp.int32, (size, seen), 0)
    columns = lax.broadcasted_iota(jnp.int32, (size, seen), 1)
    allowed = (rows >= columns) & (info_ref[begin:seen, 0:1] == row_ref[0:1, :seen])
    scores = jnp.where(allowed, scores, MASKED)
    raised = jnp.exp(scores - jnp.max(scores, axis=1, keepdims=True))
    return raised * (1.0 / jnp.sum(raised, axis=1, keepdims=True))


def attention_forward_kernel(
    query_ref, key_ref, value_ref, cosine_ref, sine_ref, info_ref, row_ref, out_ref, *, block
):
    low = jnp.bfloat16
    length, head_dim = query_ref.shape
    factor = 1.0 / math.sqrt(head_dim)
    cosine, sine = cosine_ref[...], sine_ref[...]
    query = rope(query_ref[...].astype(jnp.float32), cosine, sine).astype(low)
    key = rope(key_ref[...].astype(jnp.float32), cosine, sine).astype(low)
    value = value_ref[...]
    for begin in range(0, length, block):
        seen = begin + block
        probs = attention_rows(
            query[begin:seen], key[:seen], begin, block, info_ref, row_ref, factor
        )
        out_ref[begin:seen, :] = nn(probs.astype(low), value[:seen]).astype(low)


def attention_backward_kernel(
    raw_ref, cosine_ref, sine_ref, info_ref, row_ref, combined_ref, grad_ref,
    out_ref, inner_ref, key_total, value_total, *, block, places
):
    low = jnp.bfloat16
    length, head_dim = cosine_ref.shape
    channels = combined_ref.shape[1]
    factor = 1.0 / math.sqrt(head_dim)
    cosine, sine = cosine_ref[...], sine_ref[...]
    query = rope(raw_ref[:, : places.key].astype(jnp.float32), cosine, sine).astype(low)
    key = rope(raw_ref[:, places.key : places.gate].astype(jnp.float32), cosine, sine).astype(low)
    value = raw_ref[:, places.value : places.shared]
    key_total[...] = jnp.zeros_like(key_total)
    value_total[...] = jnp.zeros_like(value_total)
    for begin in range(0, length, block):
        seen = begin + block
        probs = attention_rows(
            query[begin:seen], key[:seen], begin, block, info_ref, row_ref, factor
        )
        grad_out = grad_ref[begin:seen, channels:]
        gate = raw_ref[begin:seen, places.gate : places.value].astype(jnp.float32)
        sig = sigmoid_of(gate)
        out_ref[begin:seen, places.gate : places.value] = (
            grad_ref[begin:seen, :channels].astype(jnp.float32)
            * combined_ref[begin:seen, :].astype(jnp.float32)
            * (sig * (1.0 + gate * (1.0 - sig)))
        ).astype(low)
        grad_probs = nt(grad_out, value[:seen])
        inner = jnp.sum(probs * grad_probs, axis=1, keepdims=True)
        grad_scores = (probs * (grad_probs - inner)).astype(low)
        grad_query = nn(grad_scores, key[:seen]) * factor
        out_ref[begin:seen, : places.key] = rope(
            grad_query, cosine[begin:seen], -sine[begin:seen]
        ).astype(low)
        key_total[:seen, :] += tn(grad_scores, query[begin:seen])
        value_total[:seen, :] += tn(probs.astype(low), grad_out)
    out_ref[:, places.key : places.gate] = rope(key_total[...] * factor, cosine, -sine).astype(low)
    out_ref[:, places.value :] = value_total[...].astype(low)
    inner = jnp.zeros(inner_ref.shape, jnp.float32)
    for at in range(0, places.shared, LANES):
        span = slice(at, at + LANES)
        inner = inner + out_ref[:, span].astype(jnp.float32) * raw_ref[:, span].astype(jnp.float32)
    inner_ref[...] = inner


BRIEF = pl.CostEstimate(flops=1, bytes_accessed=1, transcendentals=0)


def whole(shape):
    return pl.BlockSpec(shape, lambda i: (0,) * len(shape))


def limits(megabytes):
    return pltpu.CompilerParams(vmem_limit_bytes=megabytes * 1024 * 1024)


def column_block(rows, width, at):
    return pl.BlockSpec((rows, width), lambda i: (0, at // width))


def attention_forward(raw, places, cosine, sine, info, row):
    length, width = cosine.shape
    return pl.pallas_call(
        partial(attention_forward_kernel, block=256),
        grid=(1,),
        in_specs=[
            column_block(length, width, places.query),
            column_block(length, width, places.key),
            column_block(length, width, places.value),
            whole(cosine.shape), whole(sine.shape), whole(info.shape), whole(row.shape),
        ],
        out_specs=whole((length, width)),
        out_shape=jax.ShapeDtypeStruct((length, width), jnp.bfloat16),
        compiler_params=limits(48),
        cost_estimate=BRIEF,
        name="attention_forward",
    )(raw, raw, raw, cosine, sine, info, row)


def attention_backward(raw, places, cosine, sine, info, row, combined, grad_mixed):
    length, width = cosine.shape
    return pl.pallas_call(
        partial(attention_backward_kernel, block=256, places=places),
        grid=(1,),
        in_specs=[
            column_block(length, places.shared, 0),
            whole(cosine.shape), whole(sine.shape), whole(info.shape), whole(row.shape),
            whole(combined.shape), whole(grad_mixed.shape),
        ],
        out_specs=[whole((length, places.shared)), whole((length, LANES))],
        out_shape=[
            jax.ShapeDtypeStruct((length, places.shared), jnp.bfloat16),
            jax.ShapeDtypeStruct((length, LANES), jnp.float32),
        ],
        scratch_shapes=[pltpu.VMEM((length, width), jnp.float32)] * 2,
        compiler_params=limits(48),
        cost_estimate=BRIEF,
        name="attention_backward",
    )(raw, cosine, sine, info, row, combined, grad_mixed)


def mamba_forward(raw, places, step_raw, info, row, params, attended, head_width):
    length = raw.shape[0]
    width = places.step - places.conv
    states = (places.conv - places.shared) // 2
    head_dim = attended.shape[1]
    chunks = length // CHUNK

    def block(columns):
        return pl.BlockSpec((CHUNK, columns), lambda i: (i, 0))

    return pl.pallas_call(
        partial(mamba_forward_kernel, head_width=head_width, places=places),
        grid=(chunks,),
        in_specs=[
            block(places.step),
            block(LANES), block(LANES), pl.BlockSpec((8, CHUNK), lambda i: (0, i)),
            *[whole(p.shape) for p in params],
            block(head_dim),
        ],
        out_specs=[
            block(width + head_dim), block(width),
            pl.BlockSpec((None, states, width), lambda i: (i, 0, 0)),
        ],
        out_shape=[
            jax.ShapeDtypeStruct((length, width + head_dim), jnp.bfloat16),
            jax.ShapeDtypeStruct((length, width), jnp.bfloat16),
            jax.ShapeDtypeStruct((chunks, states, width), jnp.bfloat16),
        ],
        scratch_shapes=[
            pltpu.VMEM((states, width), jnp.float32),
            pltpu.VMEM((TAIL + CHUNK, width + 2 * states), jnp.float32),
        ],
        compiler_params=limits(48),
        cost_estimate=BRIEF,
        name="mamba_forward",
    )(raw, step_raw, info, row, *params, attended)


def mamba_backward(raw, places, step_raw, info, row, params, states, grad_mixed, head_width):
    length = raw.shape[0]
    width = places.step - places.conv
    shared = places.conv - places.shared
    chunks = length // CHUNK
    total = places.step + LANES - places.shared
    tail = 16

    def block(columns):
        return pl.BlockSpec((CHUNK, columns), lambda i: (chunks - 1 - i, 0))

    return pl.pallas_call(
        partial(mamba_backward_kernel, head_width=head_width, places=places),
        grid=(chunks,),
        in_specs=[
            block(places.step),
            pl.BlockSpec(
                (tail, places.step),
                lambda i: (jnp.maximum((chunks - 1 - i) * (CHUNK // tail) - 1, 0), 0),
            ),
            block(LANES), block(LANES),
            pl.BlockSpec((8, CHUNK), lambda i: (0, chunks - 1 - i)),
            *[whole(p.shape) for p in params],
            pl.BlockSpec((None, shared // 2, width), lambda i: (chunks - 1 - i, 0, 0)),
            block(grad_mixed.shape[1]),
        ],
        out_specs=[block(total), block(LANES), whole((16, shared))],
        out_shape=[
            jax.ShapeDtypeStruct((length, total), jnp.bfloat16),
            jax.ShapeDtypeStruct((length, LANES), jnp.float32),
            jax.ShapeDtypeStruct((16, shared), jnp.float32),
        ],
        scratch_shapes=[
            pltpu.VMEM((shared // 2, width), jnp.float32),
            pltpu.VMEM((TAIL + CHUNK, width + shared), jnp.float32),
            pltpu.VMEM((TAIL + CHUNK, width + shared), jnp.float32),
        ],
        compiler_params=limits(48),
        cost_estimate=BRIEF,
        name="mamba_backward",
    )(raw, raw, step_raw, info, row, *params, states, grad_mixed)


def matmul(former, latter):
    return jnp.dot(former, latter, preferred_element_type=jnp.float32)


def matmul_left(former, latter):
    return lax.dot_general(
        former, latter, (((0,), (0,)), ((), ())), preferred_element_type=jnp.float32
    )


def matmul_right(former, latter):
    return lax.dot_general(
        former, latter, (((1,), (1,)), ((), ())), preferred_element_type=jnp.float32
    )


def col_swap(values, distance):
    count = lax.axis_size("col")
    return lax.ppermute(values, "col", [(i, i ^ distance) for i in range(count)])


def row_swap(values):
    return lax.ppermute(values, "row", [(0, 1), (1, 0)])


def together(*values):
    return lax.optimization_barrier(values)


def after(value, *earlier):
    return lax.optimization_barrier((value, earlier))[0]


def gather_start(block):
    return col_swap(block, 2), row_swap(block), col_swap(block, 1)


def gather_middle(block, first):
    along_x, along_y, _ = first
    half = block.shape[0] // 2
    return col_swap(along_y[:half], 2), row_swap(along_x[half:]), col_swap(along_x, 1), col_swap(along_y, 1)


def gather_end(block, first, middle):
    along_x, along_y, core = first
    top, low, core_x, core_y = middle
    own = [block, along_x, core, core_x]
    other = [along_y, (top, low), core_y, (col_swap(top, 1), col_swap(low, 1))]
    return own, other


def gather_slow_second(first):
    along_x, along_y, _ = first
    return row_swap(along_x), col_swap(along_x, 1), col_swap(along_y, 1)


def gather_slow_end(block, first, second):
    along_x, along_y, core = first
    diagonal, core_x, core_y = second
    return [block, along_x, core, core_x], [along_y, diagonal, core_y, col_swap(diagonal, 1)]


def add_kernel(former_ref, latter_ref, out_ref):
    total = former_ref[...].astype(jnp.float32) + latter_ref[...].astype(jnp.float32)
    out_ref[...] = total.astype(out_ref.dtype)


def add_low(former, latter):
    shape = former.shape
    tiles = shape[0] if len(shape) == 3 else 2
    block = (1, *shape[1:]) if len(shape) == 3 else (shape[0] // tiles, shape[1])
    spec = pl.BlockSpec(block, lambda i: (i,) + (0,) * (len(shape) - 1))
    return pl.pallas_call(
        add_kernel,
        grid=(tiles,),
        in_specs=[spec, spec],
        out_specs=spec,
        out_shape=jax.ShapeDtypeStruct(shape, jnp.bfloat16),
        compiler_params=limits(32),
        cost_estimate=BRIEF,
        name="add",
    )(former, latter)


def add_three_kernel(first_ref, second_ref, third_ref, out_ref):
    wide = jnp.float32
    total = first_ref[...].astype(wide) + second_ref[...].astype(wide) + third_ref[...].astype(wide)
    out_ref[...] = total.astype(out_ref.dtype)


def add_three(first, second, third, at):
    _, rows, columns = first.shape
    tiles = 2
    spec = pl.BlockSpec((None, rows // tiles, columns), lambda i: (at, i, 0))
    return pl.pallas_call(
        add_three_kernel,
        grid=(tiles,),
        in_specs=[spec] * 3,
        out_specs=pl.BlockSpec((rows // tiles, columns), lambda i: (i, 0)),
        out_shape=jax.ShapeDtypeStruct((rows, columns), jnp.bfloat16),
        compiler_params=limits(32),
        cost_estimate=BRIEF,
        name="add_three",
    )(first, second, third)


def sum_quarters_kernel(base_ref, *refs):
    (*parts, out_ref, low_ref) = refs
    tops, lows = parts[:3], parts[3:]
    wide = jnp.float32

    def write(pieces):
        total = base_ref[...].astype(wide)
        for piece in pieces:
            total = total + piece[...].astype(wide)
        out_ref[...] = total
        low_ref[...] = total.astype(low_ref.dtype)

    @pl.when(pl.program_id(0) == 0)
    def _():
        write(tops)

    @pl.when(pl.program_id(0) == 1)
    def _():
        write(lows)


def sum_quarters(base, own, low_got, own_got, top_last, low_last):
    tokens, width = base.shape
    half = tokens // 2
    row = pl.BlockSpec((half, width), lambda i: (i, 0))
    part = pl.BlockSpec((half, width), lambda i: (0, 0))
    first = pl.BlockSpec((None, half, width), lambda i: (0, 0, 0))
    return pl.pallas_call(
        sum_quarters_kernel,
        grid=(2,),
        in_specs=[row, part, part, part, part, first, part],
        out_specs=[row, row],
        out_shape=[
            jax.ShapeDtypeStruct((tokens, width), jnp.float32),
            jax.ShapeDtypeStruct((tokens, width), jnp.bfloat16),
        ],
        compiler_params=limits(32),
        cost_estimate=BRIEF,
        name="sum_quarters",
    )(base, own[0], own_got, top_last, own[2], low_got, low_last)


def fold_other_kernel(near_ref, far_ref, top_near_ref, top_far_ref, low_ref):
    half = low_ref.shape[0]
    total = (near_ref[...].astype(jnp.float32) + far_ref[...].astype(jnp.float32)).astype(low_ref.dtype)
    low_ref[...] = total[half:]

    @pl.when(pl.program_id(0) == 0)
    def _():
        top_near_ref[...] = total[:half]

    @pl.when(pl.program_id(0) == 1)
    def _():
        top_far_ref[...] = total[:half]


def fold_own_kernel(near_ref, far_ref, top_near_ref, top_far_ref, low_near_ref, low_far_ref):
    half = top_near_ref.shape[0]
    total = (near_ref[...].astype(jnp.float32) + far_ref[...].astype(jnp.float32)).astype(top_near_ref.dtype)

    @pl.when(pl.program_id(0) == 0)
    def _():
        top_near_ref[...] = total[:half]
        low_near_ref[...] = total[half:]

    @pl.when(pl.program_id(0) == 1)
    def _():
        top_far_ref[...] = total[:half]
        low_far_ref[...] = total[half:]


def fold(near, far, is_own):
    _, tokens, width = near.shape
    half = tokens // 2
    share = pl.BlockSpec((None, tokens, width), lambda i: (i, 0, 0))
    quarter = pl.BlockSpec((half, width), lambda i: (0, 0))
    shape = jax.ShapeDtypeStruct((half, width), near.dtype)
    if is_own:
        specs, shapes = [quarter] * 4, [shape] * 4
    else:
        specs = [quarter, quarter, pl.BlockSpec((None, half, width), lambda i: (i, 0, 0))]
        shapes = [shape, shape, jax.ShapeDtypeStruct((2, half, width), near.dtype)]
    return pl.pallas_call(
        fold_own_kernel if is_own else fold_other_kernel,
        grid=(2,),
        in_specs=[share, share],
        out_specs=specs,
        out_shape=shapes,
        compiler_params=limits(32),
        cost_estimate=BRIEF,
        name="fold",
    )(near, far)


def own_sum(own, low_got, own_got, top_last, low_last):
    top_near, _, low_near, _ = own
    wide = jnp.float32
    top = top_near.astype(wide) + own_got.astype(wide) + top_last.astype(wide)
    low = low_near.astype(wide) + low_got[0].astype(wide) + low_last.astype(wide)
    return jnp.concatenate([top, low], axis=0)


def token_total(own, other):
    total = own + row_swap(other)
    total = total + col_swap(total, 1)
    return total + col_swap(total, 2)


def line_update_kernel(flags_ref, now_ref, got_ref, pair_ref, crossed_ref, later_ref, out_ref, sent_ref):
    @pl.when(flags_ref[1] == 1)
    def _():
        wide = jnp.float32
        out_ref[...] = (now_ref[...].astype(wide) + got_ref[...].astype(wide)).astype(out_ref.dtype)
        sent_ref[...] = (pair_ref[...].astype(wide) + crossed_ref[...].astype(wide)).astype(sent_ref.dtype)

    @pl.when(flags_ref[1] == 0)
    def _():
        sent_ref[...] = later_ref[...]


def line_update(flags, now, got, pair, crossed, later):
    rows, columns = now.shape[1:]

    def middle_block(i, f):
        return (i * f[1], 0, 0)

    def end_block(i, f):
        return (i * (1 - f[1]), 0, 0)

    def every_block(i, f):
        return (i, 0, 0)

    block = (None, rows, columns)
    return pl.pallas_call(
        line_update_kernel,
        grid_spec=pltpu.PrefetchScalarGridSpec(
            num_scalar_prefetch=1,
            grid=(4,),
            in_specs=[pl.BlockSpec(block, middle_block)] * 4 + [pl.BlockSpec(block, end_block)],
            out_specs=[pl.BlockSpec(block, middle_block), pl.BlockSpec(block, every_block)],
        ),
        out_shape=[jax.ShapeDtypeStruct(now.shape, now.dtype)] * 2,
        compiler_params=limits(32),
        cost_estimate=BRIEF,
        name="line_update",
    )(flags, now, got, pair, crossed, later)


class LineSums:
    def __init__(self, flags):
        self.flags = flags
        self.step = 0
        self.now = self.sent = self.pair = None
        self.outward = False
        self.flying = ()
        self.done = []

    def advance(self, later=None):
        if lax.axis_size("dp") != 4:
            if later is not None:
                total = lax.psum(later, "dp")
                self.sent = later
                self.done.append((total, total))
            return
        if self.outward:
            self.done.append((self.sent, self.flying[0]))
        self.outward = self.pair is not None
        sent = self.now if later is None else later
        if self.step == 0:
            self.sent = later
        elif self.now is None:
            self.sent = add_low(self.pair, self.flying[1])
            self.pair = None
            if later is not None:
                self.sent = jnp.where(self.flags[1] == 1, self.sent, later)
        elif self.pair is None:
            self.pair = add_low(self.now, self.flying[0])
            self.sent = sent
        else:
            self.pair, self.sent = line_update(
                self.flags, self.now, self.flying[0], self.pair, self.flying[1], sent
            )
        self.now = later
        self.step += 1
        self._start()

    def finish(self):
        if lax.axis_size("dp") == 4:
            self.done.append((self.sent, self.flying[0]))

    def _start(self):
        move = lax.ppermute(self.sent, "dp", [(0, 1), (3, 2), (1, 0), (2, 3)])
        if self.pair is None:
            self.flying = (move,)
        else:
            self.flying = (move, lax.ppermute(self.pair, "dp", [(1, 2), (2, 1)]))


def dp_part(values, distance):
    count = lax.axis_size("dp")
    return lax.ppermute(values, "dp", [(i, i ^ distance) for i in range(count)])


def dp_rest(values):
    distance = 2
    while distance < lax.axis_size("dp"):
        values = values + dp_part(values, distance)
        distance *= 2
    return values


def pick_kernel(*refs, count):
    out_ref = refs[-1]
    for at in range(count):

        @pl.when(pl.program_id(0) == at)
        def _():
            out_ref[...] = refs[at][...]


def pick(sources):
    rows, columns = sources[0][0].shape[1:]
    return pl.pallas_call(
        partial(pick_kernel, count=len(sources)),
        grid=(len(sources),),
        in_specs=[pl.BlockSpec((None, rows, columns), lambda i, at=at: (at, 0, 0)) for _, at in sources],
        out_specs=pl.BlockSpec((None, rows, columns), lambda i: (i, 0, 0)),
        out_shape=jax.ShapeDtypeStruct((len(sources), rows, columns), sources[0][0].dtype),
        compiler_params=limits(32),
        cost_estimate=BRIEF,
        name="pick",
    )(*[array for array, _ in sources])


def pick_at_kernel(flags_ref, in_ref, out_ref):
    out_ref[...] = in_ref[...]


def pick_at(flags, values, distance, tiles=2):
    _, rows, columns = values.shape
    size = rows // tiles
    return pl.pallas_call(
        pick_at_kernel,
        grid_spec=pltpu.PrefetchScalarGridSpec(
            num_scalar_prefetch=1,
            grid=(tiles,),
            in_specs=[
                pl.BlockSpec((None, size, columns), lambda i, f: (jnp.bitwise_xor(f[0], distance), i, 0))
            ],
            out_specs=pl.BlockSpec((size, columns), lambda i, f: (i, 0)),
        ),
        out_shape=jax.ShapeDtypeStruct((rows, columns), values.dtype),
        compiler_params=limits(32),
        cost_estimate=BRIEF,
        name="pick_at",
    )(flags, values)


def choose_kernel(flags_ref, middle_ref, end_ref, out_ref):
    @pl.when(flags_ref[1] == 1)
    def _():
        out_ref[...] = middle_ref[...]

    @pl.when(flags_ref[1] == 0)
    def _():
        out_ref[...] = end_ref[...]


def chosen(flags, pair):
    middle, end = pair
    block = (None, *middle.shape[1:])
    return pl.pallas_call(
        choose_kernel,
        grid_spec=pltpu.PrefetchScalarGridSpec(
            num_scalar_prefetch=1,
            grid=(middle.shape[0],),
            in_specs=[
                pl.BlockSpec(block, lambda i, f: (i * f[1], 0, 0)),
                pl.BlockSpec(block, lambda i, f: (i * (1 - f[1]), 0, 0)),
            ],
            out_specs=pl.BlockSpec(block, lambda i, f: (i, 0, 0)),
        ),
        out_shape=jax.ShapeDtypeStruct(middle.shape, middle.dtype),
        compiler_params=limits(32),
        cost_estimate=BRIEF,
        name="choose",
    )(flags, middle, end)


def pick_chosen_kernel(flags_ref, middle_ref, end_ref, out_ref):
    choose_kernel(flags_ref, middle_ref, end_ref, out_ref)


def pick_chosen(flags, pair, places):
    middle, end = pair
    block = (None, *middle.shape[1:])
    return pl.pallas_call(
        pick_chosen_kernel,
        grid_spec=pltpu.PrefetchScalarGridSpec(
            num_scalar_prefetch=1,
            grid=(len(places),),
            in_specs=[
                pl.BlockSpec(block, lambda i, f: (distance_at(i, places) * f[1], 0, 0)),
                pl.BlockSpec(block, lambda i, f: (distance_at(i, places) * (1 - f[1]), 0, 0)),
            ],
            out_specs=pl.BlockSpec(block, lambda i, f: (i, 0, 0)),
        ),
        out_shape=jax.ShapeDtypeStruct((len(places), *middle.shape[1:]), middle.dtype),
        compiler_params=limits(32),
        cost_estimate=BRIEF,
        name="pick_chosen",
    )(flags, middle, end)


def near_of_sum(flags, pair, fetched):
    kept = pick_chosen(flags, pair, (2,))
    return col_swap(pick([(kept, 0), (fetched, 1)]), 1)


def far_pair(blocks):
    return col_swap(pick([(blocks, 1), (blocks, 3)]), 2)


def near_pair(blocks, fetched):
    return col_swap(pick([(blocks, 2), (fetched, 1)]), 1)


def halves_kernel(flags_ref, in_ref, keep_ref, send_ref):
    part = keep_ref.shape[1]

    @pl.when(flags_ref[2] == 0)
    def _():
        keep_ref[...] = in_ref[:, :part]
        send_ref[...] = in_ref[:, part:]

    @pl.when(flags_ref[2] == 1)
    def _():
        keep_ref[...] = in_ref[:, part:]
        send_ref[...] = in_ref[:, :part]


def row_halves(flags, blocks):
    count, rows, columns = blocks.shape
    half = pl.BlockSpec((None, rows, columns // 2), lambda i, f: (i, 0, 0))
    return pl.pallas_call(
        halves_kernel,
        grid_spec=pltpu.PrefetchScalarGridSpec(
            num_scalar_prefetch=1,
            grid=(count,),
            in_specs=[pl.BlockSpec((None, rows, columns), lambda i, f: (i, 0, 0))],
            out_specs=[half, half],
        ),
        out_shape=[jax.ShapeDtypeStruct((count, rows, columns // 2), blocks.dtype)] * 2,
        compiler_params=limits(32),
        cost_estimate=BRIEF,
        name="row_halves",
    )(flags, blocks)


def pack_out_kernel(mine_ref, far_ref, near_ref, both_ref, out_ref):
    width = mine_ref.shape[1]
    for at, ref in enumerate((mine_ref, far_ref, near_ref, both_ref)):
        out_ref[:, at * width : (at + 1) * width] = ref[...]


def pack_out(blocks, fetched, passed):
    _, depth, width = blocks.shape
    tiles = 2
    return pl.pallas_call(
        pack_out_kernel,
        grid=(tiles,),
        in_specs=block_specs(depth // tiles, width),
        out_specs=pl.BlockSpec((depth // tiles, 4 * width), lambda i: (i, 0)),
        out_shape=jax.ShapeDtypeStruct((depth, 4 * width), blocks.dtype),
        compiler_params=limits(32),
        cost_estimate=BRIEF,
        name="pack_out",
    )(*block_values(blocks, fetched, passed))


def block_specs(size, count):
    return [
        pl.BlockSpec((None, size, count), lambda i, *_, at=at: (at, i, 0)) for at in (0, 0, 0, 1)
    ]


def block_values(blocks, fetched, passed):
    return blocks, fetched, passed, passed


def own_first(values, row_index):
    return jnp.where(row_index == 0, values, jnp.flip(values, 0))


def tile_blocks(refs, split):
    tile = pl.program_id(0)
    tiles = pl.num_programs(0)
    refs = list(refs)
    blocks = []
    for halves in split:
        if halves:
            top, low = refs.pop(0), refs.pop(0)
            blocks.append(jnp.where(tile < tiles // 2, top[...], low[...]))
        else:
            blocks.append(refs.pop(0)[...])
    return blocks, refs


def write_normed(blocks, gain_ref, out_ref, factor_ref):
    width = blocks[0].shape[1]
    total = jnp.zeros((blocks[0].shape[0], 1), jnp.float32)
    for block in blocks:
        values = block.astype(jnp.float32)
        total = total + jnp.sum(values * values, axis=1, keepdims=True)
    factor = lax.rsqrt(total * (1.0 / (width * len(blocks))) + EPS)
    for at, block in enumerate(blocks):
        span = slice(at * width, (at + 1) * width)
        out_ref[:, span] = (block.astype(jnp.float32) * factor * gain_ref[:, span]).astype(jnp.bfloat16)
    factor_ref[...] = jnp.broadcast_to(factor, factor_ref.shape)


def project_kernel(*refs, split):
    blocks, refs = tile_blocks(refs, split)
    gain_ref, weight_ref, normed_ref, factor_ref, raw_ref, step_ref = refs
    write_normed(blocks, gain_ref, normed_ref, factor_ref)
    raw = nn(normed_ref[...], weight_ref[...])
    main = raw_ref.shape[1]
    raw_ref[...] = raw[:, :main].astype(jnp.bfloat16)
    step_ref[...] = raw[:, main:]


def ffn_kernel(*refs, split):
    blocks, refs = tile_blocks(refs, split)
    gain_ref, weight_ref, grad_hidden_ref, normed_ref, factor_ref, hidden_ref, grad_ref, inner_ref = refs
    write_normed(blocks, gain_ref, normed_ref, factor_ref)
    low, wide = jnp.bfloat16, jnp.float32
    units = hidden_ref.shape[1]
    gate_up = nn(normed_ref[...], weight_ref[...])
    gate, up = gate_up[:, :units], gate_up[:, units:]
    sig = sigmoid_of(gate)
    silu = gate * sig
    hidden_ref[...] = (silu * up).astype(low)
    grad_hidden = grad_hidden_ref[...]
    grad_gate = (grad_hidden * up * sig * (1.0 + gate * (1.0 - sig))).astype(low)
    grad_up = (grad_hidden * silu).astype(low)
    grad_ref[:, :units] = grad_gate
    grad_ref[:, units:] = grad_up
    products = grad_gate.astype(wide) * gate + grad_up.astype(wide) * up
    inner = products[:, :LANES]
    for at in range(LANES, units, LANES):
        inner = inner + products[:, at : at + LANES]
    inner_ref[...] = inner


def meet_kernel(*refs, split):
    blocks, refs = tile_blocks(refs, split)
    weight_ref, out_ref, product_ref = refs
    width = blocks[0].shape[1]
    for at, block in enumerate(blocks):
        out_ref[:, at * width : (at + 1) * width] = block
    product_ref[...] = nt(out_ref[...], weight_ref[...]).astype(product_ref.dtype)


def tiled_call(kernel, name, pieces, operands, outs, tiles=4):
    tokens, width = pieces[0].shape
    size = tokens // tiles
    split = [isinstance(piece, tuple) for piece in pieces]
    specs, values = [], []
    for piece, halves in zip(pieces, split):
        if halves:
            specs.append(pl.BlockSpec((size, width), lambda i: (jnp.minimum(i, tiles // 2 - 1), 0)))
            specs.append(pl.BlockSpec((size, width), lambda i: (jnp.maximum(i - tiles // 2, 0), 0)))
            values.extend(piece)
        else:
            specs.append(pl.BlockSpec((size, width), lambda i: (i, 0)))
            values.append(piece)
    for value, is_whole in operands:
        specs.append(whole(value.shape) if is_whole else pl.BlockSpec((size, value.shape[1]), lambda i: (i, 0)))
        values.append(value)
    return pl.pallas_call(
        partial(kernel, split=split),
        grid=(tiles,),
        in_specs=specs,
        out_specs=[pl.BlockSpec((size, columns), lambda i: (i, 0)) for columns, _ in outs],
        out_shape=[jax.ShapeDtypeStruct((tokens, columns), dtype) for columns, dtype in outs],
        compiler_params=limits(56),
        cost_estimate=BRIEF,
        name=name,
    )(*values)


def weight_grad_kernel(former_0, former_1, latter_0, latter_1, *out_refs):
    total = tn(former_0[...], latter_0[...]) + tn(former_1[...], latter_1[...])
    at = 0
    for out_ref in out_refs:
        out_ref[...] = total[:, at : at + out_ref.shape[1]].astype(out_ref.dtype)
        at += out_ref.shape[1]


def weight_grad(former, latter, width, at=0, counts=None):
    length, depth = former[0].shape
    if counts is None:
        left = pl.BlockSpec((length, depth), lambda i: (0, 0))
        right = pl.BlockSpec((length, width), lambda i: (0, i))
        shapes = [(4, depth, width)]
    else:
        left = pl.BlockSpec((length, width), lambda i: (0, i))
        right = pl.BlockSpec((length, sum(counts)), lambda i: (0, at))
        shapes = [(4, width, count) for count in counts]
    out = pl.pallas_call(
        weight_grad_kernel,
        grid=(4,),
        in_specs=[left, left, right, right],
        out_specs=[pl.BlockSpec((None, *shape[1:]), lambda i: (i, 0, 0)) for shape in shapes],
        out_shape=[jax.ShapeDtypeStruct(shape, jnp.bfloat16) for shape in shapes],
        compiler_params=limits(56),
        cost_estimate=BRIEF,
        name="weight_grad",
    )(*former, *latter)
    return out[0] if len(out) == 1 else out


def spread_kernel(*refs, transposed):
    values, (weight_ref, far_ref, near_ref) = refs[:-3], refs[-3:]
    step = pl.program_id(0)
    total = None
    at = 0
    for ref in values:
        if transposed:
            part = nt(ref[...], weight_ref[:, at : at + ref.shape[1]])
            at += ref.shape[1]
        else:
            part = nn(ref[...], weight_ref[...])
        total = part if total is None else total + part
    total = total.astype(far_ref.dtype)

    @pl.when(step < 2)
    def _():
        far_ref[...] = total

    @pl.when(step >= 2)
    def _():
        near_ref[...] = total


def spread(values, weight, width, transposed):
    tokens = values[0].shape[0]

    def block_of(i):
        return (i + 2) % 4

    if transposed:
        weight_spec = pl.BlockSpec((width, weight.shape[1]), lambda i: (block_of(i), 0))
    else:
        weight_spec = pl.BlockSpec((weight.shape[0], width), lambda i: (0, block_of(i)))
    shape = jax.ShapeDtypeStruct((2, tokens, width), jnp.bfloat16)
    far, near = pl.pallas_call(
        partial(spread_kernel, transposed=transposed),
        grid=(4,),
        in_specs=[whole(v.shape) for v in values] + [weight_spec],
        out_specs=[
            pl.BlockSpec((None, tokens, width), lambda i: (jnp.minimum(i, 1), 0, 0)),
            pl.BlockSpec((None, tokens, width), lambda i: (jnp.maximum(i - 2, 0), 0, 0)),
        ],
        out_shape=[shape, shape],
        compiler_params=limits(56),
        cost_estimate=BRIEF,
        name="spread",
    )(*values, weight)
    return near, far


def cut_first_kernel(flags_ref, query_ref, gate_ref, conv_ref, step_ref, out_ref, *, distances, steps):
    at = 0
    for ref in (query_ref, gate_ref, conv_ref):
        out_ref[:, at : at + ref.shape[1]] = ref[...]
        at += ref.shape[1]
    place = jnp.bitwise_xor(flags_ref[0], distance_at(pl.program_id(0), distances))
    step = pltpu.roll(step_ref[...].astype(jnp.float32), (LANES - place * steps) % LANES, 1)
    lane = lax.broadcasted_iota(jnp.int32, step.shape, 1)
    out_ref[:, at:] = jnp.where(lane < steps, step, 0.0).astype(out_ref.dtype)


def distance_at(i, distances):
    value = distances[0]
    for at, distance in enumerate(distances[1:], 1):
        value = jnp.where(i == at, distance, value)
    return value


def cut_first(flags, query, gate, conv, step, distances, size, at_share):
    depth = gate.shape[0]
    widths = [array.shape[1] // 4 for array in (query, gate, conv)]
    steps = step.shape[1] // 4
    total = sum(widths) + LANES
    step = jnp.pad(step, ((0, 0), (0, LANES - step.shape[1])))

    def row(f):
        return f[3] if at_share else 0

    def column_index(i, f):
        return (row(f), jnp.bitwise_xor(f[0], distance_at(i, distances)))

    return pl.pallas_call(
        partial(cut_first_kernel, distances=distances, steps=steps),
        grid_spec=pltpu.PrefetchScalarGridSpec(
            num_scalar_prefetch=1,
            grid=(len(distances),),
            in_specs=[pl.BlockSpec((size, w), column_index) for w in widths]
            + [pl.BlockSpec((size, LANES), lambda i, f: (row(f), 0))],
            out_specs=pl.BlockSpec((None, size, total), lambda i, f: (i, 0, 0)),
        ),
        out_shape=jax.ShapeDtypeStruct((len(distances), size, total), gate.dtype),
        compiler_params=limits(32),
        cost_estimate=BRIEF,
        name="cut_first",
    )(flags, query, gate, conv, step)


def cut_rest_kernel(flags_ref, gate_ref, up_ref, down_ref, out_ref):
    at = 0
    for ref in (gate_ref, up_ref, down_ref):
        out_ref[:, at : at + ref.shape[1]] = ref[...]
        at += ref.shape[1]


def cut_rest(flags, gate, up, down, distances, size, at_share):
    units = gate.shape[1] // 4
    width = down.shape[1]
    total = 2 * units + width
    parts = units // size

    def column_index(i, f):
        return (f[3] if at_share else 0, jnp.bitwise_xor(f[0], distance_at(i, distances)))

    def row_index(i, f):
        place = jnp.bitwise_xor(f[0], distance_at(i, distances))
        return (place * parts + (f[3] if at_share else 0), 0)

    return pl.pallas_call(
        cut_rest_kernel,
        grid_spec=pltpu.PrefetchScalarGridSpec(
            num_scalar_prefetch=1,
            grid=(len(distances),),
            in_specs=[
                pl.BlockSpec((size, units), column_index),
                pl.BlockSpec((size, units), column_index),
                pl.BlockSpec((size, width), row_index),
            ],
            out_specs=pl.BlockSpec((None, size, total), lambda i, f: (i, 0, 0)),
        ),
        out_shape=jax.ShapeDtypeStruct((len(distances), size, total), gate.dtype),
        compiler_params=limits(32),
        cost_estimate=BRIEF,
        name="cut_rest",
    )(flags, gate, up, down)


def cut_out_kernel(flags_ref, mamba_ref, attn_ref, out_ref):
    out_ref[: mamba_ref.shape[0], :] = mamba_ref[...]
    out_ref[mamba_ref.shape[0] :, :] = attn_ref[...]


def cut_out(flags, mamba, attn):
    channels, query = mamba.shape[0] // 4, attn.shape[0] // 4
    width = mamba.shape[1]

    def row_index(i, f):
        return (jnp.bitwise_xor(f[0], distance_at(i, DISTANCES)), 0)

    return pl.pallas_call(
        cut_out_kernel,
        grid_spec=pltpu.PrefetchScalarGridSpec(
            num_scalar_prefetch=1,
            grid=(4,),
            in_specs=[pl.BlockSpec((channels, width), row_index), pl.BlockSpec((query, width), row_index)],
            out_specs=pl.BlockSpec((None, channels + query, width), lambda i, f: (i, 0, 0)),
        ),
        out_shape=jax.ShapeDtypeStruct((4, channels + query, width), mamba.dtype),
        compiler_params=limits(32),
        cost_estimate=BRIEF,
        name="cut_out",
    )(flags, mamba, attn)


def pack_first_kernel(*refs, places, begins):
    pieces, out_ref = refs[:-1], refs[-1]
    query = places.key - places.query
    channels = places.value - places.gate
    head = places.gate - places.key
    total = out_ref.shape[2]

    def place(at, ref, begin, count, to):
        out_ref[at, :, to : to + count] = ref[:, begin : begin + count]

    for at in range(4):
        alone, common = pieces[2 * at], pieces[2 * at + 1]
        begin = begins[2 * at + 1]
        place(at, alone, 0, query, places.query)
        place(at, alone, query, channels, places.gate)
        place(at, alone, query + channels, channels, places.conv)
        place(at, alone, query + 2 * channels, total - places.step, places.step)
        place(at, common, begin, head, places.key)
        place(at, common, begin + head, head, places.value)
        place(at, common, begin + 2 * head, places.conv - places.shared, places.shared)


def pack_first(sources, places, total):
    depth, dtype = sources[0][0].shape[1], sources[0][0].dtype
    tiles = 4
    size = depth // tiles
    out = pl.pallas_call(
        partial(pack_first_kernel, places=places, begins=[begin for _, _, begin in sources]),
        grid=(tiles,),
        in_specs=[
            pl.BlockSpec((None, size, v.shape[2]), lambda i, at=at: (at, i, 0)) for v, at, _ in sources
        ],
        out_specs=pl.BlockSpec((4, size, total), lambda i: (0, i, 0)),
        out_shape=jax.ShapeDtypeStruct((4, depth, total), dtype),
        compiler_params=limits(48),
        cost_estimate=BRIEF,
        name="pack_first",
    )(*[v for v, _, _ in sources])
    return out.reshape(4 * depth, total)


def pack_rest_kernel(mine_ref, far_ref, near_ref, both_ref, in_ref, down_ref):
    width = down_ref.shape[1] // 4
    inner = in_ref.shape[2]
    for at, ref in enumerate((mine_ref, far_ref, near_ref, both_ref)):
        in_ref[at] = ref[:, :inner]
        down_ref[:, at * width : (at + 1) * width] = ref[:, inner : inner + width]


def pack_rest(sources, width):
    _, depth, total = sources[0][0].shape
    dtype = sources[0][0].dtype
    inner = total - width
    tiles = 4
    size = depth // tiles
    into, down = pl.pallas_call(
        pack_rest_kernel,
        grid=(tiles,),
        in_specs=[
            pl.BlockSpec((None, size, total), lambda i, at=at: (at, i, 0)) for _, at in sources
        ],
        out_specs=[
            pl.BlockSpec((4, size, inner), lambda i: (0, i, 0)),
            pl.BlockSpec((size, 4 * width), lambda i: (i, 0)),
        ],
        out_shape=[
            jax.ShapeDtypeStruct((4, depth, inner), dtype),
            jax.ShapeDtypeStruct((depth, 4 * width), dtype),
        ],
        compiler_params=limits(32),
        cost_estimate=BRIEF,
        name="pack_rest",
    )(*[v for v, _ in sources])
    return into.reshape(4 * depth, inner), down


def collect_early_kernel(*refs, places):
    pieces, (out_ref, common_ref) = refs[:4], refs[4:]
    query = places.key - places.query
    key = jnp.zeros((out_ref.shape[1], places.gate - places.key), jnp.float32)
    value = jnp.zeros((out_ref.shape[1], places.shared - places.value), jnp.float32)
    for at, piece in enumerate(pieces):
        out_ref[at, :, :query] = piece[:, : places.key]
        out_ref[at, :, query:] = piece[:, places.gate : places.value]
        key = key + piece[:, places.key : places.gate].astype(jnp.float32)
        value = value + piece[:, places.value :].astype(jnp.float32)
    common_ref[:, : key.shape[1]] = key.astype(common_ref.dtype)
    common_ref[:, key.shape[1] :] = value.astype(common_ref.dtype)


def collect_early(blocks, fetched, passed, places):
    _, depth, count = blocks.shape
    alone = places.key - places.query + places.value - places.gate
    tiles = 2
    size = depth // tiles
    return pl.pallas_call(
        partial(collect_early_kernel, places=places),
        grid=(tiles,),
        in_specs=block_specs(size, count),
        out_specs=[
            pl.BlockSpec((4, size, alone), lambda i: (0, i, 0)),
            pl.BlockSpec((size, count - alone), lambda i: (i, 0)),
        ],
        out_shape=[
            jax.ShapeDtypeStruct((4, depth, alone), blocks.dtype),
            jax.ShapeDtypeStruct((depth, count - alone), blocks.dtype),
        ],
        compiler_params=limits(32),
        cost_estimate=BRIEF,
        name="collect_early",
    )(*block_values(blocks, fetched, passed))


def collect_late_kernel(*refs, channels):
    alone, shared, (common_ref, out_ref, step_ref) = refs[:4], refs[4:8], refs[8:]
    quarter = out_ref.shape[2] - channels
    wide = jnp.float32
    steps = jnp.zeros(step_ref.shape, wide)
    total = jnp.zeros((out_ref.shape[1], shared[0].shape[1]), wide)
    for at, piece in enumerate(alone):
        out_ref[at, :, :channels] = piece[:, :channels]
        step = piece[:, channels:].astype(wide)
        steps = steps + (pltpu.roll(step, at * 8, 1) if at else step)
        total = total + shared[at][...].astype(wide)
    step_ref[...] = steps
    for at in range(2):
        span = slice(at * quarter, (at + 1) * quarter)
        out_ref[at, :, channels:] = total[:, span].astype(out_ref.dtype)
        out_ref[at + 2, :, channels:] = common_ref[:, span]


def collect_late(alone, shared, common, channels):
    _, depth, count = alone[0].shape
    part = shared[0].shape[2]
    tiles = 2
    size = depth // tiles
    return pl.pallas_call(
        partial(collect_late_kernel, channels=channels),
        grid=(tiles,),
        in_specs=[
            *block_specs(size, count), *block_specs(size, part),
            pl.BlockSpec((size, common.shape[1]), lambda i: (i, 0)),
        ],
        out_specs=[
            pl.BlockSpec((4, size, channels + part // 2), lambda i: (0, i, 0)),
            pl.BlockSpec((size, LANES), lambda i: (i, 0)),
        ],
        out_shape=[
            jax.ShapeDtypeStruct((4, depth, channels + part // 2), alone[0].dtype),
            jax.ShapeDtypeStruct((depth, LANES), jnp.float32),
        ],
        compiler_params=limits(32),
        cost_estimate=BRIEF,
        name="collect_late",
    )(*block_values(*alone), *block_values(*shared), common)


def slot_of(flags, place):
    distance = jnp.bitwise_xor(flags[0], place)
    return 2 * jnp.bitwise_and(distance, 1) + distance // 2


def finalize_kernel(flags_ref, total_ref, last_ref, *out_refs, cuts):
    values = jnp.where(flags_ref[1] == 1, total_ref[...], last_ref[...])
    for (span, columns), out_ref in zip(cuts, out_refs):
        out_ref[...] = values[span, columns].astype(jnp.float32)


def finalize(flags, total, last, block, index, outs):
    return pl.pallas_call(
        partial(finalize_kernel, cuts=[(rows, columns) for _, _, _, rows, columns in outs]),
        grid_spec=pltpu.PrefetchScalarGridSpec(
            num_scalar_prefetch=1,
            grid=(4,),
            in_specs=[pl.BlockSpec(block, index)] * 2,
            out_specs=[pl.BlockSpec(out_block, out_index) for _, out_block, out_index, _, _ in outs],
        ),
        out_shape=[jax.ShapeDtypeStruct(shape, jnp.float32) for shape, _, _, _, _ in outs],
        compiler_params=limits(32),
        cost_estimate=BRIEF,
        name="finalize",
    )(flags, total, last)


def finalize_blocks_kernel(flags_ref, *refs, cuts):
    pieces, out_refs = refs[:4], refs[4:]
    slot = slot_of(flags_ref, pl.program_id(0))
    for at, piece in enumerate(pieces):

        @pl.when(slot == at)
        def _():
            for (rows, columns), out_ref in zip(cuts, out_refs):
                out_ref[...] = piece[rows, columns].astype(jnp.float32)


def finalize_blocks(flags, blocks, fetched, passed, outs):
    _, rows, columns = blocks.shape
    return pl.pallas_call(
        partial(finalize_blocks_kernel, cuts=[(rows, columns) for _, _, _, rows, columns in outs]),
        grid_spec=pltpu.PrefetchScalarGridSpec(
            num_scalar_prefetch=1,
            grid=(4,),
            in_specs=[
                pl.BlockSpec((None, rows, columns), lambda i, f, at=at: (at, 0, 0)) for at in (0, 0, 0, 1)
            ],
            out_specs=[pl.BlockSpec(out_block, out_index) for _, out_block, out_index, _, _ in outs],
        ),
        out_shape=[jax.ShapeDtypeStruct(shape, jnp.float32) for shape, _, _, _, _ in outs],
        compiler_params=limits(32),
        cost_estimate=BRIEF,
        name="finalize_blocks",
    )(flags, *block_values(blocks, fetched, passed))


def meet_gathered_kernel(flags_ref, *refs):
    meet_kernel(*refs, split=[False] * 4)


def meet_gathered(flags, gathered, weight, tiles=4):
    _, tokens, width = gathered.shape
    size = tokens // tiles

    def block_at(distance):
        return pl.BlockSpec((None, size, width), lambda i, f: (jnp.bitwise_xor(f[0], distance), i, 0))

    model, units = weight.shape[1], weight.shape[0]
    return pl.pallas_call(
        meet_gathered_kernel,
        grid_spec=pltpu.PrefetchScalarGridSpec(
            num_scalar_prefetch=1,
            grid=(tiles,),
            in_specs=[block_at(d) for d in DISTANCES] + [pl.BlockSpec(weight.shape, lambda i, f: (0, 0))],
            out_specs=[
                pl.BlockSpec((size, model), lambda i, f: (i, 0)),
                pl.BlockSpec((size, units), lambda i, f: (i, 0)),
            ],
        ),
        out_shape=[
            jax.ShapeDtypeStruct((tokens, model), jnp.bfloat16),
            jax.ShapeDtypeStruct((tokens, units), jnp.float32),
        ],
        compiler_params=limits(56),
        cost_estimate=BRIEF,
        name="meet_gathered",
    )(flags, *[gathered] * 4, weight)


def on_device(
    tokens,
    cotangent,
    segment_ids,
    norm1_gain,
    proj_gate,
    proj_conv,
    proj_step,
    proj_shared,
    proj_query,
    proj_key,
    proj_value,
    conv_weight,
    conv_bias,
    shared_conv,
    shared_bias,
    step_bias,
    decay_log,
    skip_gain,
    mamba_out_proj,
    attn_out_proj,
    norm2_gain,
    ffn_gate,
    ffn_up,
    ffn_down,
):
    low = jnp.bfloat16
    wide = jnp.float32
    me = lax.axis_index("col")
    row_index = lax.axis_index("row")
    length = segment_ids.shape[1]
    width = tokens.shape[1]
    model = width * len(DISTANCES)
    head_dim = proj_key.shape[1]
    channels = proj_gate.shape[1] // 4
    steps = proj_step.shape[1] // 4
    head_width = channels // steps
    units = ffn_gate.shape[1] // 4
    query_width = proj_query.shape[1] // 4
    part = proj_shared.shape[1]
    at_gate = query_width + head_dim
    at_value = at_gate + channels
    at_shared = at_value + head_dim
    at_conv = at_shared + 2 * part
    at_step = at_conv + channels
    places = Places(0, query_width, at_gate, at_value, at_shared, at_conv, at_step)
    line_place = lax.axis_index("dp")
    share = width // lax.axis_size("dp")
    flags = jnp.stack(
        [me, ((line_place == 1) | (line_place == 2)).astype(me.dtype), row_index, line_place]
    ).astype(jnp.int32)
    firsts = (proj_query, proj_gate, proj_conv, proj_step)
    rests = (ffn_gate, ffn_up, ffn_down)

    def along_line(values):
        return lax.all_gather(values, "dp", axis=1, tiled=True)

    shared_twin = row_swap(proj_shared)
    fetched = col_swap(cut_first(flags, *firsts, DISTANCES[1::2], share, True), 2)
    gains = jnp.stack([norm1_gain, norm2_gain])
    gains_far = col_swap(gains, 2)
    block, shared_twin, fetched, gains_far = together(tokens, shared_twin, fetched, gains_far)
    first = gather_start(block)
    far = along_line(fetched)
    common = jnp.concatenate(
        [
            proj_key, proj_value,
            jnp.where(row_index == 0, proj_shared, shared_twin),
            jnp.where(row_index == 0, shared_twin, proj_shared),
        ],
        axis=1,
    )[None]
    alone = cut_first(flags, *firsts, DISTANCES[::2], width, False)
    lone = alone.shape[2]
    near = col_swap(jnp.concatenate([alone[1:], common], axis=2), 1)
    common_far = col_swap(common, 2)
    segments = own_first(segment_ids, row_index)
    indices = jnp.arange(length, dtype=jnp.int32)
    same = segments[:, :, None] == segments[:, None, :]
    position = jnp.sum(same & (indices[:, None] > indices[None, :]), axis=2).astype(wide)
    remaining = jnp.sum(same & (indices[:, None] < indices[None, :]), axis=2).astype(wide)
    lane = jnp.arange(LANES)
    info = jnp.where(
        lane == 0,
        segments.astype(wide)[..., None],
        jnp.where(lane == 1, position[..., None], remaining[..., None]),
    )
    row_info = jnp.broadcast_to(segments.astype(wide)[:, None, :], (2, 8, length))
    half_dim = head_dim // 2
    frequency = ROPE_BASE ** (-2.0 * jnp.arange(half_dim, dtype=wide) / head_dim)
    angles = position[..., None] * frequency
    cosine, sine = jnp.cos(angles), jnp.sin(angles)
    cosine = jnp.concatenate([cosine, cosine], axis=2)
    sine = jnp.concatenate([-sine, sine], axis=2)
    head_rows = jnp.pad(
        jnp.stack([step_bias, jnp.exp(decay_log)]), ((0, 6), (0, LANES - steps))
    )
    gain1, gain2 = gains[0:1], gains[1:2]
    params = (
        conv_weight, conv_bias[None], shared_conv, shared_bias[None], head_rows,
        jnp.repeat(skip_gain, head_width)[None],
    )

    both = (0, 1)


    first, near, alone, info, row_info, cosine, sine, params = together(
        first, near, alone, info, row_info, cosine, sine, params
    )
    middle = gather_middle(block, first)
    gains = jnp.concatenate([gains, gains_far], axis=1)
    out_blocks = cut_out(flags, mamba_out_proj, attn_out_proj)
    rest_sent = cut_rest(flags, *rests, DISTANCES[1::2], share, True)
    rest_kept = cut_rest(flags, *rests, DISTANCES[::2], width, False)
    middle, far, common_far, out_blocks, rest_sent, rest_kept = together(
        middle, far, common_far, out_blocks, rest_sent, rest_kept
    )
    both_far = col_swap(jnp.concatenate([far[1:], common_far], axis=2), 1)
    out_fetched = far_pair(out_blocks)
    gains = jnp.concatenate([gains, col_swap(gains, 1)], axis=1)
    gain1, gain2 = gains[0:1], gains[1:2]
    token_own, token_other = gather_end(block, first, middle)
    both_far, gain1, gain2, token_other = together(both_far, gain1, gain2, token_other)
    weight_first = pack_first(
        [
            (alone, 0, 0), (common, 0, 0), (far, 0, 0), (common_far, 0, 0),
            (near, 0, 0), (near, 0, lone), (both_far, 0, 0), (both_far, 0, lone),
        ],
        places, at_step + LANES,
    )

    both = (0, 1)
    normed1, factor1, raw, step_raw, mixed, combined, states = [[None, None] for _ in range(7)]

    def project(s, pieces):
        normed1[s], factor1[s], raw[s], step_raw[s] = tiled_call(
            project_kernel, "project", pieces, [(gain1, True), (weight_first, True)],
            [(model, low), (LANES, wide), (at_step, low), (LANES, wide)],
        )
        return attention_forward(raw[s], places, cosine[s], sine[s], info[s], row_info[s])

    def mamba(s, attended):
        mixed[s], combined[s], states[s] = mamba_forward(
            raw[s], places, step_raw[s], info[s], row_info[s], params, attended, head_width
        )

    cot_y = row_swap(after(cotangent, weight_first))
    attended = project(1, token_other)
    attended, out_fetched, cot_y = together(attended, out_fetched, cot_y)
    out_passed = near_pair(out_blocks, out_fetched)
    fetched = col_swap(after(rest_sent, out_fetched), 2)
    mamba(1, attended)
    mixed[1], out_passed, fetched = together(mixed[1], out_passed, fetched)
    cot_col = lax.all_gather(after(cotangent, fetched), "col", axis=0)
    rest_far = along_line(fetched)
    weight_out = pack_out(out_blocks, out_fetched, out_passed)
    near, far = spread([mixed[1]], weight_out, width, False)
    far = col_swap(far, 1)
    near, far, token_own = together(near, far, token_own)
    rest_near = col_swap(rest_kept[1:], 1)
    top_near, top_far, low_send = fold(near, far, False)
    low_got, other_got = row_swap(low_send), col_swap(top_far, 2)
    attended = project(0, after(token_own, low_send))
    attended, low_got, other_got, rest_near = together(attended, low_got, other_got, rest_near)
    top_last = row_swap(add_low(top_near, other_got))
    mamba(0, attended)
    mixed[0], top_last = together(mixed[0], top_last)
    near, far = spread([mixed[0]], weight_out, width, False)
    far = col_swap(far, 1)
    near, far, cot_col = together(near, far, cot_col)
    own = fold(near, far, True)
    low_sent = add_low(own[3], low_got[1])
    own_got, low_last = col_swap(own[1], 2), col_swap(low_sent, 2)
    cot_xy = row_swap(pick_at(flags, after(cot_col, low_sent), 2))
    own_got, low_last, cot_xy = together(own_got, low_last, cot_xy)
    hidden1, block = sum_quarters(tokens, own, low_got, own_got, top_last, low_last)
    block, hidden1, rest_far = together(block, hidden1, rest_far)
    first = gather_start(block)
    rest_both = col_swap(rest_far[1:], 1)
    cot_cores = [col_swap(cot_y, 1), col_swap(cot_xy, 1)]
    weight_in, weight_down = pack_rest(
        [(rest_kept, 0), (rest_far, 0), (rest_near, 0), (rest_both, 0)], width
    )
    cot, grad_hidden = [None, None], [None, None]
    cot[0], grad_hidden[0] = meet_gathered(flags, cot_col, weight_down)
    first, weight_in, weight_down, cot_cores, cot[0], grad_hidden[0] = together(
        first, weight_in, weight_down, cot_cores, cot[0], grad_hidden[0]
    )
    middle = gather_middle(block, first)
    cot[1], grad_hidden[1] = tiled_call(
        meet_kernel, "meet_cotangent", [cot_y, cot_xy, *cot_cores], [(weight_down, True)],
        [(model, low), (units, wide)],
    )
    middle, cot, grad_hidden = together(middle, cot, grad_hidden)
    pieces = gather_end(block, first, middle)
    normed2, factor2, hidden, grad_in, inner = [[None, None] for _ in range(5)]

    def feed_forward(s, pieces):
        normed2[s], factor2[s], hidden[s], grad_in[s], products = tiled_call(
            ffn_kernel, "ffn", pieces, [(gain2, True), (weight_in, True), (grad_hidden[s], False)],
            [(model, low), (LANES, wide), (units, low), (2 * units, low), (LANES, wide)],
        )
        inner[s] = jnp.sum(products, axis=1).reshape(length // LANES, LANES)

    def piece_index(i, f):
        return (slot_of(f, i), 0, 0)

    def row_index_map(i, f):
        return (i, 0)

    def column_index_map(i, f):
        return (0, i)

    every = slice(None)
    line = LineSums(flags)
    feed_forward(1, pieces[1])
    near, far = spread([grad_in[1]], weight_in, width, True)
    far = col_swap(far, 1)
    feed_forward(0, after(pieces[0], near))
    near, far, hidden, inner, grad_in = together(near, far, hidden, inner, grad_in)
    top_near, top_far, low_send = fold(near, far, False)
    low_got, other_got = row_swap(low_send), col_swap(top_far, 2)
    inner_row = row_swap(inner[1])
    near, far = spread([after(grad_in[0], low_send)], weight_in, width, True)
    far = col_swap(far, 1)
    near, far = together(near, far)
    own = fold(near, far, True)
    own_got = col_swap(own[1], 2)
    down = weight_grad(after(hidden, own), cot, width)
    gate = weight_grad(after(normed2, down), grad_in, width, 0, [units])
    low_got, other_got, own_got, inner_row, down, own, gate = together(
        low_got, other_got, own_got, inner_row, down, own, gate
    )
    top_last = row_swap(add_low(top_near, other_got))
    low_last = col_swap(add_low(own[3], low_got[1]), 2)
    inner = inner[0] + inner_row
    inner_core = col_swap(inner, 1)
    line.advance(down)
    up = weight_grad(after(normed2, line.sent), grad_in, width, 1, [units])
    top_last, low_last, inner_core, up = together(top_last, low_last, inner_core, up)
    inner = inner + inner_core
    inner = inner + col_swap(inner, 2)
    inner2 = inner.reshape(length, 1)
    grad_normed2 = own_sum(own, low_got, own_got, top_last, low_last)
    own_factor = factor2[0][:, :1]
    back2 = (
        own_factor * norm2_gain * grad_normed2
        - hidden1 * (own_factor * own_factor * inner2 / model)
    )
    grad_gain2 = jnp.sum(grad_normed2 * hidden1 * own_factor, axis=0)
    grad_hidden1 = cotangent.astype(wide) + back2
    block, grad_hidden1, grad_gain2 = together(grad_hidden1.astype(low), grad_hidden1, grad_gain2)
    first = gather_start(block)
    output_shares = [spread([after(hidden[s], block)], weight_down, width, False) for s in both]
    first, output_shares, line.flying = together(first, output_shares, line.flying)
    line.advance(gate)
    middle = together(*gather_middle(block, first))
    pieces = gather_end(block, first, middle)
    output_far = [col_swap(output_shares[s][1], 1) for s in both]
    mix_grad, grad_mixed = [None, None], [None, None]
    for s in both:
        mix_grad[s], grad_mixed[s] = tiled_call(
            meet_kernel, "meet_mixed", pieces[s], [(weight_out, True)],
            [(model, low), (channels + query_width, low)],
        )
    out = weight_grad(mixed, mix_grad, width)
    early, late, sums, products, inner = [[None, None] for _ in range(5)]

    def mamba_step(s, *earlier):
        late[s], inner[s], sums[s] = mamba_backward(
            raw[s], places, step_raw[s], info[s], row_info[s], params, states[s],
            after(grad_mixed[s], *earlier), head_width,
        )

    for s in both:
        early[s], products[s] = attention_backward(
            raw[s], places, cosine[s], sine[s], info[s], row_info[s], combined[s],
            after(grad_mixed[s], out),
        )
    out, grad_mixed, early, output_far, line.flying = together(out, grad_mixed, early, output_far, line.flying)
    line.advance(up)
    output_other = add_low(output_shares[1][0], output_far[1])
    output_got = row_swap(output_other)
    early = after(early, line.sent, output_other)
    first = weight_grad(normed1, early, width, 0, [at_shared])
    first_far = far_pair(first)
    mamba_step(1, first)
    late[1], output_got, output_near, line.flying = together(
        late[1], output_got, output_far[0], line.flying
    )
    line.advance(out)
    first_far = after(first_far, line.sent)
    first_near = near_pair(first, first_far)
    output_sent = add_three(output_shares[0][0], output_near, output_got, 1)
    output_last = col_swap(output_sent, 2)
    down = line.done[0]
    down_sent = pick_chosen(flags, down, (1, 3))
    down_far = col_swap(down_sent, 2)
    mamba_step(0, line.sent, output_sent, down_sent)
    shared, last = weight_grad(normed1, late, width, 0, [2 * part, channels + LANES])
    shared, last, late, sums, inner, output_last, down_far, first_near, line.flying = together(
        shared, last, late, sums, inner, output_last, down_far, first_near, line.flying
    )
    shared_keep, shared_send = row_halves(flags, shared)
    shared_got = row_swap(shared_send)
    last_far = far_pair(last)
    down_near = near_of_sum(flags, down, down_far)
    first, common_sum = collect_early(first, first_far, first_near, places)
    line.advance(first)
    small_rows = length // width
    inner = [
        jnp.sum(inner[s] + products[s], axis=1).reshape(small_rows, width) for s in both
    ]
    small = jnp.concatenate(
        [(sums[0] + sums[1])[:13], grad_gain2[None], inner[0], inner[1], jnp.zeros((14, width), wide)],
        axis=0,
    )[:24]
    rank = jnp.arange(24)[:, None]
    taps = conv_weight.shape[0]
    is_shared = (rank > taps) & (rank < 2 * taps + 2)
    is_inner = (rank >= 14) & (rank < 14 + small_rows)
    is_gain = rank == 13
    last_far, shared_got, small, down_near = together(last_far, shared_got, small, down_near)
    shared = add_low(shared_keep, shared_got)
    shared_far = far_pair(shared)
    small_got = row_swap(small)
    last_near = near_pair(last, last_far)
    shared_far, last_near, small_got, line.flying = together(shared_far, last_near, small_got, line.flying)
    shared_near = together(near_pair(shared, shared_far))[0]
    last, step_sum = collect_late(
        (last, last_far, last_near), (shared, shared_far, shared_near), common_sum, channels
    )
    line.advance(last)
    small_other = jnp.concatenate(
        [small_got[:14], small_got[14 + small_rows : 14 + 2 * small_rows], small_got[14 + small_rows :]], axis=0
    )[:24]
    late, small, small_other = after((late, small, small_other), line.sent)
    gate, up = line.done[1], line.done[2]
    gate_far = col_swap(pick_chosen(flags, gate, (1, 3)), 2)
    up_far = col_swap(pick_chosen(flags, up, (1, 3)), 2)
    near, far = spread([early[1], late[1]], weight_first, width, True)
    own_near, own_far = spread([early[0], after(late[0], near)], weight_first, width, True)
    small = small + jnp.where(is_shared | is_gain | is_inner, small_other, 0.0)
    near, far, own_near, own_far, small, gate_far, up_far, line.flying = together(
        near, far, own_near, own_far, small, gate_far, up_far, line.flying
    )
    line.advance()
    far, own_far, small = after((far, own_far, small), line.sent)
    far, own_far, small_got = together(col_swap(far, 1), col_swap(own_far, 1), col_swap(small, 1))
    top_near, top_far, low_send = fold(near, far, False)
    low_got, other_got = row_swap(low_send), col_swap(top_far, 2)
    own = fold(own_near, own_far, True)
    own_got = col_swap(own[1], 2)
    small = small + jnp.where(is_shared | is_inner, small_got, 0.0)
    small_got = col_swap(small, 2)
    gate_near = near_of_sum(flags, gate, gate_far)
    up_near = near_of_sum(flags, up, up_far)
    low_got, other_got, own_got, small_got, gate_near, up_near, line.flying = together(
        low_got, other_got, own_got, small_got, gate_near, up_near, line.flying
    )
    line.advance()
    low_got, other_got, small, small_got = after((low_got, other_got, small, small_got), line.sent)
    top_last = row_swap(add_low(top_near, other_got))
    low_last = col_swap(add_low(own[3], low_got[1]), 2)
    out = line.done[3]
    out_far = col_swap(pick_chosen(flags, out, (1, 3)), 2)
    small = small + jnp.where(is_shared | is_inner, small_got, 0.0)
    total, final = line.done[4]
    alone = query_width + channels
    d_query, d_gate = finalize(
        flags, total, final, (None, width, alone), piece_index,
        [
            (proj_query.shape, (width, query_width), column_index_map, every, slice(0, query_width)),
            (proj_gate.shape, (width, channels), column_index_map, every, slice(query_width, None)),
        ],
    )
    (d_ffn_down,) = finalize_blocks(
        flags, pick_chosen(flags, down, (0,)), down_far, down_near,
        [(ffn_down.shape, (units, width), row_index_map, every, every)],
    )
    (d_ffn_gate,) = finalize_blocks(
        flags, pick_chosen(flags, gate, (0,)), gate_far, gate_near,
        [(ffn_gate.shape, (width, units), column_index_map, every, every)],
    )
    (d_ffn_up,) = finalize_blocks(
        flags, pick_chosen(flags, up, (0,)), up_far, up_near,
        [(ffn_up.shape, (width, units), column_index_map, every, every)],
    )
    output = (
        hidden1 + output_shares[0][0][0].astype(wide) + output_near[0].astype(wide)
        + output_got[0].astype(wide) + output_last.astype(wide)
    ).astype(low)
    top_last, low_last, out_far, d_query, d_gate, d_ffn_down, d_ffn_gate, d_ffn_up, output = together(
        top_last, low_last, out_far, d_query, d_gate, d_ffn_down, d_ffn_gate, d_ffn_up, output
    )
    out_near = near_of_sum(flags, out, out_far)
    inner1 = small[14 : 14 + small_rows].reshape(length, 1)
    grad_normed1 = own_sum(own, low_got, own_got, top_last, low_last)
    own_factor = factor1[0][:, :1]
    own_tokens = tokens.astype(wide)
    back1 = (
        own_factor * norm1_gain * grad_normed1
        - own_tokens * (own_factor * own_factor * inner1 / model)
    )
    grad_gain1 = jnp.sum(grad_normed1 * own_tokens * own_factor, axis=0)
    tokens_grad = (grad_hidden1 + back1).astype(low)
    gain_got = row_swap(grad_gain1[None])
    out_near, tokens_grad = together(out_near, tokens_grad)
    d_mamba_out, d_attn_out = finalize_blocks(
        flags, pick_chosen(flags, out, (0,)), out_far, out_near,
        [
            (mamba_out_proj.shape, (channels, width), row_index_map, slice(0, channels), every),
            (attn_out_proj.shape, (query_width, width), row_index_map, slice(channels, None), every),
        ],
    )
    gain_got, d_mamba_out, d_attn_out = together(gain_got, d_mamba_out, d_attn_out)
    small = jnp.concatenate(
        [
            small[:14], grad_gain1[None] + gain_got, jnp.zeros((1, width), wide),
            jnp.transpose(step_sum)[: 4 * 8],
        ],
        axis=0,
    )
    small_got = dp_part(small, 1)
    tokens_grad, small, small_got, line.flying = together(tokens_grad, small, small_got, line.flying)
    line.finish()
    total, final = line.done[5]
    (d_conv,) = finalize(
        flags, total, final, (None, width, channels + part // 2), piece_index,
        [(proj_conv.shape, (width, channels), column_index_map, every, slice(0, channels))],
    )
    sums = dp_rest(small + small_got)
    extra = jnp.where(flags[1] == 1, total[:, :, channels:], final[:, :, channels:]).astype(wide)
    d_shared = jnp.concatenate([extra[0], extra[1]], axis=1)
    d_key, d_value = extra[2], extra[3]
    step_sum = jnp.stack([sums[16 + p * 8 : 16 + p * 8 + steps] for p in (0, 2, 1, 3)])
    d_step = jnp.transpose(
        jnp.concatenate([lax.dynamic_index_in_dim(step_sum, me ^ d, 0, keepdims=False) for d in range(4)])
    )
    return (
        output, tokens_grad, sums[14], d_gate, d_conv, d_step, d_shared, d_query, d_key, d_value,
        sums[:taps, :channels], sums[taps, :channels], sums[taps + 1 : 2 * taps + 1],
        sums[2 * taps + 1],
        sums[11, :steps], sums[12, :steps],
        jnp.sum(sums[10, :channels].reshape(steps, head_width), axis=1),
        d_mamba_out, d_attn_out, sums[13], d_ffn_gate, d_ffn_up, d_ffn_down,
    )


def solution(mesh):
    return jax.shard_map(
        on_device,
        mesh=mesh,
        in_specs=(
            P(("dp", "row"), "col"),
            P(("dp", "row"), "col"),
            P("dp", None),
            P("col"),
            P("col", "row"),
            P("col", "row"),
            P("col", "row"),
            P("col", "row"),
            P("col", "row"),
            P("col", "row"),
            P("col", "row"),
            P(None, ("row", "col")),
            P(("row", "col")),
            P(),
            P(),
            P(("row", "col")),
            P(("row", "col")),
            P(("row", "col")),
            P("row", "col"),
            P("row", "col"),
            P("col"),
            P("col", "row"),
            P("col", "row"),
            P("row", "col"),
        ),
        out_specs=(
            P(("dp", "row"), "col"),
            P(("dp", "row"), "col"),
            P("col"),
            P("col", "row"),
            P("col", "row"),
            P("col", "row"),
            P("col", "row"),
            P("col", "row"),
            P("col", "row"),
            P("col", "row"),
            P(None, ("row", "col")),
            P(("row", "col")),
            P(),
            P(),
            P(("row", "col")),
            P(("row", "col")),
            P(("row", "col")),
            P("row", "col"),
            P("row", "col"),
            P("col"),
            P("col", "row"),
            P("col", "row"),
            P("row", "col"),
        ),
        check_vma=False,
    )
```
